32 devices in a mesh: dp: 8 (over z, x), mp: 4 (over y, core).
Axes of the slice: x: 2, y: 2, z: 4, core: 2. Of those that a mesh axis runs over, the one named last changes fastest.
Arguments:
- pixels: bfloat16 [256, 196, 768], P(('dp', 'mp')), may hold values from -6 to 6
- token_mask: int32 [256, 196], P('dp'), may hold values from 0 to 1, as said below
- counts: int32 [8], P('dp'), may hold values from 8 to 32, as said below
- labels: int32 [256], P(('dp', 'mp')), may hold values from 0 to 999
- pairs: int32 [256], P(('dp', 'mp')), may hold values from 0 to 255, as said below
- attn_in: float32 [2, 384, 3, 384], P(None, None, None, 'mp'), may hold values from -0.3125 to 0.3125
- attn_in_mean: float32 [2, 384, 3, 384], P(None, None, None, 'mp'), may hold values from -6.67572e-06 to 6.67572e-06
- attn_in_square: float32 [2, 384, 3, 384], P(None, None, None, 'mp'), may hold values from 9.300319e-14 to 3.7201275e-13
- attn_out: float32 [2, 384, 384], P(None, 'mp'), may hold values from -1 to 1
- attn_out_mean: float32 [2, 384, 384], P(None, 'mp'), may hold values from -6.67572e-06 to 6.67572e-06
- attn_out_square: float32 [2, 384, 384], P(None, 'mp'), may hold values from 9.300319e-14 to 3.7201275e-13
- mlp_in: float32 [2, 384, 1536], P(None, None, 'mp'), may hold values from -0.3125 to 0.3125
- mlp_in_mean: float32 [2, 384, 1536], P(None, None, 'mp'), may hold values from -6.67572e-06 to 6.67572e-06
- mlp_in_square: float32 [2, 384, 1536], P(None, None, 'mp'), may hold values from 9.300319e-14 to 3.7201275e-13
- mlp_out: float32 [2, 1536, 384], P(None, 'mp'), may hold values from -0.15625 to 0.15625
- mlp_out_mean: float32 [2, 1536, 384], P(None, 'mp'), may hold values from -6.67572e-06 to 6.67572e-06
- mlp_out_square: float32 [2, 1536, 384], P(None, 'mp'), may hold values from 9.300319e-14 to 3.7201275e-13
- tables: float32 [1964, 384], replicated, may hold values from -5 to 5
- tables_mean: float32 [1964, 384], replicated, may hold values from -6.67572e-06 to 6.67572e-06
- tables_square: float32 [1964, 384], replicated, may hold values from 9.300319e-14 to 3.7201275e-13
- vectors: float32 [20, 384], replicated, may hold values from -8 to 8
- vectors_mean: float32 [20, 384], replicated, may hold values from -3.0517578e-05 to 3.0517578e-05
- vectors_square: float32 [20, 384], replicated, may hold values from 2.3250796e-12 to 9.300318e-12
- talking: float32 [2, 8, 8], replicated, may hold values from -2 to 2
- talking_mean: float32 [2, 8, 8], replicated, may hold values from -6.67572e-06 to 6.67572e-06
- talking_square: float32 [2, 8, 8], replicated, may hold values from 9.300319e-14 to 3.7201275e-13
Outputs:
- attn_in_new: float32 [2, 384, 3, 384], P(None, None, None, 'mp')
- attn_in_mean_new: float32 [2, 384, 3, 384], P(None, None, None, 'mp')
- attn_in_square_new: float32 [2, 384, 3, 384], P(None, None, None, 'mp')
- attn_out_new: float32 [2, 384, 384], P(None, 'mp')
- attn_out_mean_new: float32 [2, 384, 384], P(None, 'mp')
- attn_out_square_new: float32 [2, 384, 384], P(None, 'mp')
- mlp_in_new: float32 [2, 384, 1536], P(None, None, 'mp')
- mlp_in_mean_new: float32 [2, 384, 1536], P(None, None, 'mp')
- mlp_in_square_new: float32 [2, 384, 1536], P(None, None, 'mp')
- mlp_out_new: float32 [2, 1536, 384], P(None, 'mp')
- mlp_out_mean_new: float32 [2, 1536, 384], P(None, 'mp')
- mlp_out_square_new: float32 [2, 1536, 384], P(None, 'mp')
- tables_new: float32 [1964, 384], replicated
- tables_mean_new: float32 [1964, 384], replicated
- tables_square_new: float32 [1964, 384], replicated
- vectors_new: float32 [20, 384], replicated
- vectors_mean_new: float32 [20, 384], replicated
- vectors_square_new: float32 [20, 384], replicated
- talking_new: float32 [2, 8, 8], replicated
- talking_mean_new: float32 [2, 8, 8], replicated
- talking_square_new: float32 [2, 8, 8], replicated
- attn_in_copy: bfloat16 [2, 384, 3, 384], P(None, None, None, 'mp')
- attn_out_copy: bfloat16 [2, 384, 384], P(None, 'mp')
- mlp_in_copy: bfloat16 [2, 384, 1536], P(None, None, 'mp')
- mlp_out_copy: bfloat16 [2, 1536, 384], P(None, 'mp')
- statistics: float32 [12], replicated
- clip_norm: float32 [], replicated
- norms: float32 [2, 13], replicated
The draws below stay inside these ranges and needn't reach their ends.
Inputs may be any that keep to these rules, and one draw needn't show every extreme that they name: The valid images of dp index d are the last counts[d] of its 32 slots; some index has all 32. `token_mask`: the first patch of every image is 1. `pairs`: each entry names a valid image other than its own row.
All inputs are finite; a program needn't handle non-finite values.
Results may differ from the reference program's by a relative error of at most 0.028.
Values may be sent and summed in bfloat16 or wider, within the bound.
A program may use at most 320 MiB of HBM per device.

```python
import math
import jax
import jax.numpy as jnp
from jax import lax

D = 384
HEADS = 8
FF = 1536
CLASSES = 1000
PIX = 768
P_SIZE = 196
IMG_DEV = 32
VECS = 20
STEP = 10
HEAD = 48
IMAGES = 256
ROWS = 1964
PARAMS = 4300928
N_DP = 8
N_MP = 4


def image_counts(key):
    inner = jax.random.fold_in(key, 7)
    first, second = jax.random.split(inner)
    rank = jnp.arange(N_DP)
    base = IMG_DEV // 3 + 2 * IMG_DEV // 3 * rank // max(N_DP - 1, 1)
    jitter = jax.random.randint(first, (N_DP,), -(IMG_DEV // 8), IMG_DEV // 8 + 1)
    values = jnp.clip(base + jitter, max(IMG_DEV // 4, 1), IMG_DEV)
    fullest = jax.random.randint(second, (), N_DP // 2, N_DP)
    return jnp.where(rank == fullest, IMG_DEV, values).astype(jnp.int32)


def draw_counts(key, part):
    return image_counts(key)


def draw_pairs(key, part):
    values = image_counts(key)
    key = jax.random.fold_in(key, 3)
    first, second = jax.random.split(key)
    local = IMG_DEV // N_MP
    spread = N_DP * N_MP
    index = jnp.arange(IMAGES)
    owner = index // local
    target = jnp.where(owner % 2 == 0, (owner + spread - 1) % spread, (owner + spread // 2) % spread)
    target_dp = target // N_MP
    target_mp = target % N_MP
    group_count = values[target_dp]
    in_block = jnp.clip(group_count - (IMG_DEV - (target_mp + 1) * local), 0, local)
    near = jax.random.randint(first, (IMAGES,), 0, jnp.maximum(in_block, 1))
    wide = jax.random.randint(second, (IMAGES,), 0, jnp.maximum(group_count, 1))
    near_pick = (target + 1) * local - 1 - near
    wide_pick = target_dp * IMG_DEV + IMG_DEV - 1 - wide
    picked = jnp.where(in_block > 0, near_pick, wide_pick)
    fallback = target_dp * IMG_DEV + IMG_DEV - 1 - jnp.where(IMG_DEV - 1 - (picked - target_dp * IMG_DEV) == 0, 1, 0)
    return jnp.where(picked == index, fallback, picked).astype(jnp.int32)


def draw_token_mask(key, part):
    key = jax.random.fold_in(key, 5)
    levels = jax.random.randint(key, (IMAGES, P_SIZE), 0, 4)
    first = jnp.arange(P_SIZE)[None, :] == 0
    return jnp.where(first, 1, (levels > 0).astype(jnp.int32)).astype(jnp.int32)


def draw_vectors(key, part):
    key = jax.random.fold_in(key, 11)
    first, second = jax.random.split(key)
    noise = jax.random.normal(first, (VECS, D), jnp.float32)
    spread = jax.random.uniform(second, (VECS, D), jnp.float32, 0.5, 1.0)
    ramp = 0.6 + 0.8 * jnp.arange(D, dtype=jnp.float32)[None, :] / D
    row = jnp.arange(VECS)[:, None]
    kind = row % 8
    gains = ramp * (1.0 + 0.15 * noise)
    biases = 0.2 * noise
    values = jnp.where((kind == 0) | (kind == 4), gains, jnp.where((kind == 3) | (kind == 7), spread, biases))
    values = jnp.where((row == 16) | (row == 19), biases, values)
    values = jnp.where(row == 18, gains, values)
    values = jnp.where(row == 17, noise, values)
    return values.astype(jnp.float32)


def draw_tables(key, part):
    key = jax.random.fold_in(key, 13)
    values = jax.random.normal(key, (PIX + P_SIZE + CLASSES, D), jnp.float32)
    row = jnp.arange(PIX + P_SIZE + CLASSES)[:, None]
    scale = jnp.where(row < PIX, PIX ** (-0.5), jnp.where(row < PIX + P_SIZE, 0.5, 1.5 * D ** (-0.5)))
    return (values * scale).astype(jnp.float32)


def set_ends(array, rng, low, top_value):
    spot = [jax.random.randint(jax.random.fold_in(rng, axis), (), 0, length) for axis, length in enumerate(array.shape)]
    longest = array.shape.index(max(array.shape))
    neighbour = spot[:longest] + [(spot[longest] + 1) % array.shape[longest]] + spot[longest + 1:]
    return array.at[tuple(spot)].set(low).at[tuple(neighbour)].set(top_value)


def block_levels(key, extent, cuts, low, high):
    loudness = 1.0
    for axis_at, blocks in cuts:
        draws = jax.random.uniform(jax.random.fold_in(jax.random.fold_in(key, 6), axis_at), (blocks,), jnp.float32, low / len(cuts), high / len(cuts))
        loudness = loudness * jnp.repeat(jnp.exp(draws), extent[axis_at] // blocks).reshape((-1,) + (1,) * (len(extent) - 1 - axis_at))
    return loudness


def centred(rng, dims, scale, bound, shards=(), held_as=jnp.bfloat16):
    values = scale * jax.random.normal(rng, dims, jnp.float32)
    if shards:
        values = values * block_levels(rng, dims, shards, -0.22, 0.18)
    return jnp.clip(values, -bound, bound).astype(held_as)


def setup_inputs(seed: int = 0) -> dict:
    seeds = jax.random.split(jax.random.key(seed), 27)
    return {
        "pixels": centred(seeds[0], (IMAGES, P_SIZE, PIX), 1.0, 6.0, ((0, 32),)),
        "token_mask": draw_token_mask(jax.random.fold_in(seeds[26], 71), 0),
        "counts": draw_counts(jax.random.fold_in(seeds[26], 71), 0),
        "labels": set_ends(jax.random.randint(seeds[3], (IMAGES,), 0, CLASSES), jax.random.fold_in(seeds[3], 1), 0, CLASSES - 1).astype(jnp.int32),
        "pairs": draw_pairs(jax.random.fold_in(seeds[26], 71), 0),
        "attn_in": centred(seeds[5], (2, D, 3, D), D ** -0.5, 0.3125, ((3, 4),), jnp.float32),
        "attn_in_mean": centred(seeds[6], (2, D, 3, D), (0.11 * 0.02 / PARAMS ** 0.5), 6.67572021484375e-06, ((3, 4),), jnp.float32),
        "attn_in_square": jnp.clip(jnp.exp(math.log(3.7201275046583326e-13) - 1.3862944 * jax.random.uniform(seeds[7], (2, D, 3, D), jnp.float32) ** block_levels(seeds[7], (2, D, 3, D), ((3, 4),), -0.2, 0.2)), 9.300318761645832e-14, 3.7201275046583326e-13),
        "attn_out": centred(seeds[8], (2, D, D), (D / P_SIZE ** 0.5) ** -0.5, 1.0, ((1, 4),), jnp.float32),
        "attn_out_mean": centred(seeds[9], (2, D, D), (0.11 * 0.02 / PARAMS ** 0.5), 6.67572021484375e-06, ((1, 4),), jnp.float32),
        "attn_out_square": jnp.clip(jnp.exp(math.log(3.7201275046583326e-13) - 1.3862944 * jax.random.uniform(seeds[10], (2, D, D), jnp.float32) ** block_levels(seeds[10], (2, D, D), ((1, 4),), -0.2, 0.2)), 9.300318761645832e-14, 3.7201275046583326e-13),
        "mlp_in": centred(seeds[11], (2, D, FF), D ** -0.5, 0.3125, ((2, 4),), jnp.float32),
        "mlp_in_mean": centred(seeds[12], (2, D, FF), (0.11 * 0.02 / PARAMS ** 0.5), 6.67572021484375e-06, ((2, 4),), jnp.float32),
        "mlp_in_square": jnp.clip(jnp.exp(math.log(3.7201275046583326e-13) - 1.3862944 * jax.random.uniform(seeds[13], (2, D, FF), jnp.float32) ** block_levels(seeds[13], (2, D, FF), ((2, 4),), -0.2, 0.2)), 9.300318761645832e-14, 3.7201275046583326e-13),
        "mlp_out": centred(seeds[14], (2, FF, D), FF ** -0.5, 0.15625, ((1, 4),), jnp.float32),
        "mlp_out_mean": centred(seeds[15], (2, FF, D), (0.11 * 0.02 / PARAMS ** 0.5), 6.67572021484375e-06, ((1, 4),), jnp.float32),
        "mlp_out_square": jnp.clip(jnp.exp(math.log(3.7201275046583326e-13) - 1.3862944 * jax.random.uniform(seeds[16], (2, FF, D), jnp.float32) ** block_levels(seeds[16], (2, FF, D), ((1, 4),), -0.2, 0.2)), 9.300318761645832e-14, 3.7201275046583326e-13),
        "tables": draw_tables(jax.random.fold_in(seeds[26], 71), 0),
        "tables_mean": centred(seeds[18], (ROWS, D), (0.11 * 0.02 / PARAMS ** 0.5), 6.67572021484375e-06, (), jnp.float32),
        "tables_square": jnp.clip(jnp.exp(jax.random.uniform(seeds[19], (ROWS, D), jnp.float32, math.log(9.300318761645832e-14), math.log(3.7201275046583326e-13))), 9.300318761645832e-14, 3.7201275046583326e-13),
        "vectors": draw_vectors(jax.random.fold_in(seeds[26], 71), 0),
        "vectors_mean": centred(seeds[21], (VECS, D), (0.55 * 0.02 / PARAMS ** 0.5), 3.0517578125e-05, (), jnp.float32),
        "vectors_square": jnp.clip(jnp.exp(jax.random.uniform(seeds[22], (VECS, D), jnp.float32, math.log(2.3250795819912407e-12), math.log(9.300318327964963e-12))), 2.3250795819912407e-12, 9.300318327964963e-12),
        "talking": centred(seeds[23], (2, HEADS, HEADS), HEADS ** -0.5, 2.0, (), jnp.float32),
        "talking_mean": centred(seeds[24], (2, HEADS, HEADS), (0.11 * 0.02 / PARAMS ** 0.5), 6.67572021484375e-06, (), jnp.float32),
        "talking_square": jnp.clip(jnp.exp(jax.random.uniform(seeds[25], (2, HEADS, HEADS), jnp.float32, math.log(9.300318761645832e-14), math.log(3.7201275046583326e-13))), 9.300318761645832e-14, 3.7201275046583326e-13),
    }


@jax.custom_vjp
def low(v):
    return lax.optimization_barrier(v.astype(jnp.bfloat16)).astype(jnp.float32)

@jax.custom_vjp
def low_back(v):
    return v

def low_keep(v):
    return (low(v), None)

def low_pass(kept, grad):
    return (grad,)

def back_keep(v):
    return (v, None)

def back_low(kept, grad):
    return (low(grad),)
low.defvjp(low_keep, low_pass)
low_back.defvjp(back_keep, back_low)
HIGH_PRECISION = lax.Precision.HIGHEST
BETA_ONE = 0.9
BETA_TWO = 0.999
ADAM_EPS = 1e-08
DECAY = 0.01
RATE = 0.5
RATE_VECTOR = 0.5
CLIP = 0.02
SIMILARITY_TEMP = 0.05
MASKED = -1000000000.0
NORM_EPS = 1e-06
LAYER_BOUNDS = ((0, 1), (1, 2))

def norm_rows(inputs, gain, bias):
    center = inputs - lax.optimization_barrier(jnp.mean(inputs, -1, keepdims=True))
    spread = lax.optimization_barrier(jnp.mean(center * center, -1, keepdims=True))
    return center * lax.rsqrt(spread + NORM_EPS) * gain + bias

def product(left, right):
    return lax.dot_general(left, right, (((left.ndim - 1,), (0,)), ((), ())), precision=HIGH_PRECISION)

def self_attend(packed, keep, talking):
    count = packed.shape[0]
    parts = packed.reshape(count, P_SIZE, 3, HEADS, HEAD)
    query, keys, values = (parts[:, :, 0], parts[:, :, 1], parts[:, :, 2])
    scores = low_back(jnp.einsum('nqhd,nkhd->nhqk', query, keys, precision=HIGH_PRECISION) * HEAD ** (-0.5))
    mixed = jnp.einsum('gh,nhqk->ngqk', talking[0], scores, precision=HIGH_PRECISION)
    mixed = jnp.where(keep[:, None, None, :], mixed, MASKED)
    probs = jax.nn.softmax(mixed, axis=-1)
    weights = low(jnp.einsum('hg,ngqk->nhqk', talking[1], probs, precision=HIGH_PRECISION))
    result = jnp.einsum('nhqk,nkhd->nqhd', weights, values, precision=HIGH_PRECISION)
    return low_back(low(result.reshape(count, P_SIZE, D)))

def feed_forward(resid, vectors, base, weight_up, weight_down):
    normed = low(norm_rows(resid, vectors[base + 4], vectors[base + 5]))
    inner = low_back(product(normed, low(weight_up)))
    active = low(jax.nn.gelu(inner, approximate=False))
    branch = vectors[base + 7] * (low_back(product(active, low(weight_down))) + vectors[base + 6])
    return (resid + branch, branch)

def self_block(resid, keep, params):
    attn_in, attn_out, mlp_in, mlp_out, tables, vectors, talking = params
    normed = low(norm_rows(resid, vectors[0], vectors[1]))
    packed = low_back(low(product(normed, low(attn_in[0]))))
    heads_out = self_attend(packed, keep, talking)
    branch = vectors[3] * (low_back(product(heads_out, low(attn_out[0]))) + vectors[2])
    middle = resid + branch
    final, mlp_branch = feed_forward(middle, vectors, 0, mlp_in[0], mlp_out[0])
    return (final, [branch, middle, mlp_branch, final])

def class_block(patches, keep, params):
    attn_in, attn_out, mlp_in, mlp_out, tables, vectors, talking = params
    count = patches.shape[0]
    token = jnp.broadcast_to(vectors[17], (count, 1, D))
    joined = jnp.concatenate([token, patches], axis=1)
    normed = low(norm_rows(joined, vectors[8], vectors[9]))
    weight_in = low(attn_in[1])
    query = low_back(low(product(normed[:, 0], weight_in[:, 0]))).reshape(count, HEADS, HEAD)
    keyval = low_back(low(product(normed, weight_in[:, 1:]))).reshape(count, P_SIZE + 1, 2, HEADS, HEAD)
    scores = low_back(jnp.einsum('nhd,nkhd->nhk', query, keyval[:, :, 0], precision=HIGH_PRECISION) * HEAD ** (-0.5))
    allowed = jnp.concatenate([jnp.ones((count, 1), bool), keep], axis=1)
    probs = low(jax.nn.softmax(jnp.where(allowed[:, None, :], scores, MASKED), axis=-1))
    result = jnp.einsum('nhk,nkhd->nhd', probs, keyval[:, :, 1], precision=HIGH_PRECISION).reshape(count, D)
    heads_out = low_back(low(result))
    branch = vectors[11] * (low_back(product(heads_out, low(attn_out[1]))) + vectors[10])
    middle = vectors[17] + branch
    final, mlp_branch = feed_forward(middle, vectors, 8, mlp_in[1], mlp_out[1])
    return (final, [branch, middle, mlp_branch, final])

def encode_group(pixel_values, keep, okay, params):
    tables, vectors = (params[4], params[5])
    embed = low_back(product(pixel_values, low(tables[:PIX]))) + vectors[16] + tables[PIX:PIX + P_SIZE]
    patches, self_parts = self_block(embed, keep, params)
    token, class_parts = class_block(patches, keep, params)
    feature = norm_rows(token, vectors[18], vectors[19])
    token_weight = keep.astype(jnp.float32) * okay[:, None]
    sums = [jnp.sum(lax.optimization_barrier(jnp.mean(part * part, -1)) * token_weight) for part in self_parts]
    sums = sums + [jnp.sum(lax.optimization_barrier(jnp.mean(part * part, -1)) * okay) for part in class_parts]
    return (feature, jnp.stack(sums))

def forward(params, pixel_values, keep, okay, labels, pairs):
    tables = params[4]
    group = math.gcd(IMAGES, 16)
    blocks = IMAGES // group

    def run(pieces):
        return encode_group(pieces[0], pieces[1], pieces[2], params)
    features, sums = lax.map(jax.checkpoint(run), (pixel_values.reshape(blocks, group, P_SIZE, PIX), keep.reshape(blocks, group, P_SIZE), okay.reshape(blocks, group)))
    features = features.reshape(IMAGES, D)
    logits = low_back(lax.dot_general(low(features), low(tables[PIX + P_SIZE:]), (((1,), (1,)), ((), ())), precision=HIGH_PRECISION))
    cross = jax.nn.logsumexp(logits, -1) - jnp.take_along_axis(logits, labels[:, None], 1)[:, 0]
    unit_embeddings = low(features * lax.rsqrt(lax.optimization_barrier(jnp.sum(features * features, -1, keepdims=True)) + NORM_EPS))
    similarity_scores = lax.dot_general(unit_embeddings, unit_embeddings, (((1,), (1,)), ((), ())), precision=HIGH_PRECISION) / SIMILARITY_TEMP
    index = jnp.arange(IMAGES)
    allowed = (okay[None, :] > 0) & (index[:, None] != index[None, :])
    similarity_scores = jnp.where(allowed, similarity_scores, MASKED)
    contrast = jax.nn.logsumexp(similarity_scores, -1) - jnp.take_along_axis(similarity_scores, pairs[:, None], 1)[:, 0]
    loss = jnp.sum(okay * (cross + contrast)) / jnp.sum(okay)
    return (loss, (lax.optimization_barrier(jnp.sum(sums, 0)), jnp.sum(okay * cross), jnp.sum(okay * contrast)))

def adam_parts(gradient, mean, square, factor):
    clipped = gradient * factor
    mean_new = BETA_ONE * mean + (1.0 - BETA_ONE) * clipped
    square_new = BETA_TWO * square + (1.0 - BETA_TWO) * clipped * clipped
    direction = mean_new / (1.0 - BETA_ONE ** STEP) / (jnp.sqrt(square_new / (1.0 - BETA_TWO ** STEP)) + ADAM_EPS)
    return (mean_new, square_new, direction)

def segment_squares(values, bounds):
    return jnp.stack([jnp.sum(values[lower:upper] * values[lower:upper]) for lower, upper in bounds])

def apply_trust(weight, update, bounds, weight_sq, update_sq):
    trust = jnp.sqrt(weight_sq / (update_sq + 1e-12))
    pieces = [weight[lower:upper] - RATE * trust[place] * update[lower:upper] for place, (lower, upper) in enumerate(bounds)]
    return jnp.concatenate(pieces, 0)

def reference(pixels, token_mask, counts, labels, pairs, attn_in, attn_in_mean, attn_in_square, attn_out, attn_out_mean, attn_out_square, mlp_in, mlp_in_mean, mlp_in_square, mlp_out, mlp_out_mean, mlp_out_square, tables, tables_mean, tables_square, vectors, vectors_mean, vectors_square, talking, talking_mean, talking_square):
    params = (attn_in, attn_out, mlp_in, mlp_out, tables, vectors, talking)
    means = (attn_in_mean, attn_out_mean, mlp_in_mean, mlp_out_mean, tables_mean, vectors_mean, talking_mean)
    squares = (attn_in_square, attn_out_square, mlp_in_square, mlp_out_square, tables_square, vectors_square, talking_square)
    index = jnp.arange(IMAGES)
    okay = (index % IMG_DEV >= IMG_DEV - counts[index // IMG_DEV]).astype(jnp.float32)
    keep = token_mask > 0
    pixel_values = pixels.astype(jnp.float32)

    def objective(weights):
        return forward(weights, pixel_values, keep, okay, labels, pairs)
    loss, pullback, extras = jax.vjp(objective, params, has_aux=True)
    grads = pullback(jnp.ones_like(loss))[0]
    sums, cross_sum, contrast_sum = extras
    total_sq = sum((jnp.sum(item * item) for item in grads))
    grad_norm = jnp.sqrt(total_sq)
    factor = CLIP / jnp.maximum(grad_norm, CLIP)
    table_bounds = ((0, PIX), (PIX, PIX + P_SIZE), (PIX + P_SIZE, ROWS))
    results = []
    copies = []
    weight_list = []
    update_list = []
    for place in range(7):
        mean_new, square_new, direction = adam_parts(grads[place], means[place], squares[place], factor)
        weight = params[place]
        if place == 5:
            renewed = weight - RATE_VECTOR * direction
        else:
            update = direction + DECAY * weight
            bounds = table_bounds if place == 4 else LAYER_BOUNDS
            weight_sq = segment_squares(weight, bounds)
            update_sq = segment_squares(update, bounds)
            renewed = apply_trust(weight, update, bounds, weight_sq, update_sq)
            weight_list.append(weight_sq)
            update_list.append(update_sq)
        results = results + [renewed, mean_new, square_new]
        if place < 4:
            copies.append(renewed.astype(jnp.bfloat16))
    count_img = jnp.sum(okay)
    count_tok = jnp.sum(keep.astype(jnp.float32) * okay[:, None])
    statistics = jnp.concatenate([jnp.stack([cross_sum, contrast_sum, count_img, count_tok]), jnp.sqrt(sums[:4] / count_tok), jnp.sqrt(sums[4:] / count_img)])
    norms = jnp.stack([jnp.sqrt(jnp.concatenate(weight_list)), jnp.sqrt(jnp.concatenate(update_list))])
    return (results[0], results[1], results[2], results[3], results[4], results[5], results[6], results[7], results[8], results[9], results[10], results[11], results[12], results[13], results[14], results[15], results[16], results[17], results[18], results[19], results[20], copies[0], copies[1], copies[2], copies[3], statistics, grad_norm, norms)
```

```python
import functools

import jax
import jax.numpy as jnp
from jax import lax
from jax.experimental import pallas as pl
from jax.experimental.pallas import tpu as pltpu
from jax.sharding import PartitionSpec as P

D = 384
HEADS = 8
HEAD = 48
PIX = 768
P_SIZE = 196
STEP = 10
SCALE = HEAD**-0.5
BETA_ONE = 0.9
BETA_TWO = 0.999
ADAM_EPS = 1e-08
DECAY = 0.01
RATE = 0.5
RATE_VECTOR = 0.5
CLIP = 0.02
TEMP = 0.05
MASKED = -1000000000.0
NORM_EPS = 1e-06
F32 = jnp.float32
BF = jnp.bfloat16
VMEM_LIMIT = 58 * 2**20
ANY = pl.BlockSpec(memory_space=pl.ANY)
MESH = pl.DeviceIdType.MESH
WHOLE = pl.BlockSpec(memory_space=pltpu.VMEM)


def nn(left, right):
    return lax.dot_general(left, right, (((1,), (0,)), ((), ())), preferred_element_type=F32)


def nt(left, right):
    return lax.dot_general(left, right, (((1,), (1,)), ((), ())), preferred_element_type=F32)


def tn(left, right):
    return lax.dot_general(left, right, (((0,), (0,)), ((), ())), preferred_element_type=F32)


def colsum(values):
    return jnp.sum(values, 0, keepdims=True)


def normalize(inputs):
    center = inputs - jnp.mean(inputs, -1, keepdims=True)
    spread = jnp.mean(center * center, -1, keepdims=True)
    inverse = lax.rsqrt(spread + NORM_EPS)
    return center * inverse, inverse


def normalize_back(unit, inverse, gain, incoming):
    scaled = incoming * gain
    return inverse * (
        scaled
        - jnp.mean(scaled, -1, keepdims=True)
        - unit * jnp.mean(scaled * unit, -1, keepdims=True)
    )


def gelu_parts(inner):
    size = jnp.abs(inner)
    t = 1.0 / (1.0 + (0.3275911 * 0.5**0.5) * size)
    bell = jnp.exp(-0.5 * inner * inner)
    poly = t * (
        0.5 * 0.254829592
        + t
        * (
            0.5 * -0.284496736
            + t * (0.5 * 1.421413741 + t * (0.5 * -1.453152027 + t * (0.5 * 1.061405429)))
        )
    )
    tail = poly * bell
    cumulative = jnp.where(inner >= 0, 1.0 - tail, tail)
    return inner * cumulative, cumulative + inner * bell * 0.3989422804014327


def head_mask():
    row = lax.broadcasted_iota(jnp.int32, (HEADS, D), 0)
    column = lax.broadcasted_iota(jnp.int32, (HEADS, D), 1)
    return ((column >= row * HEAD) & (column < row * HEAD + HEAD)).astype(F32)


def stat_lanes(parts, weight, first):
    lane = lax.broadcasted_iota(jnp.int32, (1, 128), 1)
    row = jnp.zeros((1, 128), F32)
    for place, values in enumerate(parts):
        total = jnp.sum(colsum(values * values * weight), keepdims=True)
        high = total.astype(BF).astype(F32)
        row = jnp.where(lane == first + 2 * place, high, row)
        row = jnp.where(lane == first + 2 * place + 1, total - high, row)
    return row


def part(ref, first, rows):
    shards_count = ref.shape[0]
    return ref[:, first : first + rows, :].reshape(shards_count * rows, ref.shape[2])


def self_attend_kernel(
    pixels, cols, vec, pos, wp, wattn, t1row, t2col,
    embed_out, q_out, k_out, v_out, prob_out, ho_out, raw_out, mid_out, stat_out,
):
    shard = wattn.shape[1] // 4
    x = nn(pixels[0], wp[...]) + vec[16:17, :] + pos[...]
    embed_out[0] = x
    unit, _ = normalize(x)
    normed = (unit * vec[0:1, :] + vec[1:2, :]).astype(BF)
    wv = part(wattn, 2 * shard, shard)
    q = nt(normed, part(wattn, 0, shard)).astype(BF)
    k = nt(normed, part(wattn, shard, shard)).astype(BF)
    q_out[0] = q
    k_out[0] = k
    v_out[0] = nt(normed, wv).astype(BF)
    v_flip = nt(wv, normed).astype(BF).astype(F32)
    bias = cols[0][:, 0:1]
    q_wide = q.astype(F32)
    heads_out = jnp.zeros((D, x.shape[0]), F32)
    for g in range(HEADS):
        mixed = nt(k, (q_wide * t1row[g : g + 1, :]).astype(BF)) + bias
        grown = jnp.exp(mixed - jnp.max(mixed, 0, keepdims=True))
        prob = (grown * (1.0 / jnp.sum(grown, 0, keepdims=True))).astype(BF)
        prob_out[0, g] = prob
        heads_out += nn((v_flip * t2col[:, g : g + 1]).astype(BF), prob)
    heads_out = heads_out.astype(BF)
    ho_out[0] = heads_out
    raw = tn(heads_out, part(wattn, 3 * shard, shard))
    raw_out[0] = raw.astype(BF)
    branch = vec[3:4, :] * (raw + vec[2:3, :])
    middle = x + branch
    mid_out[0] = middle
    stat_out[0] = stat_lanes((branch, middle), cols[0][:, 1:2], 8)


def feed_kernel(
    mid, cols, bias_row, base, stat, vec, wmlp, wcls,
    patch_out, act_out, slope_out, raw_out, cprob_out, cprob0_out, z_out, card_out, aux_out,
):
    hidden = wmlp.shape[1] // 2
    shard = wcls.shape[1] // 4
    mask = head_mask()

    @pl.when(pl.program_id(0) == 0)
    def _():
        unit, _ = normalize(jnp.broadcast_to(vec[17:18, :], (HEADS, D)))
        token = (unit * vec[8:9, :] + vec[9:10, :]).astype(BF)
        query = nt(token, part(wcls, 0, shard)).astype(BF).astype(F32)
        keys = nn((query * mask).astype(BF), part(wcls, shard, shard)) * SCALE
        aux_out[0:8, :] = keys
        aux_out[8:16, :] = token.astype(F32)
        aux_out[16:24, :] = query

    middle = mid[0]
    unit, _ = normalize(middle)
    normed = (unit * vec[4:5, :] + vec[5:6, :]).astype(BF)
    inner = nt(normed, part(wmlp, 0, hidden))
    active, slope = gelu_parts(inner)
    active = active.astype(BF)
    act_out[0] = active
    slope_out[0] = slope.astype(BF)
    raw = nn(active, part(wmlp, hidden, hidden))
    raw_out[0] = raw.astype(BF)
    branch = vec[7:8, :] * (raw + vec[6:7, :])
    patches = middle + branch
    patch_out[0] = patches
    first = 4 * pl.program_id(0)
    card_out[pl.ds(first + 3, 1), :] = (
        base[0] + stat[0] + stat_lanes((branch, patches), cols[0][:, 1:2], 12)
    )
    unit, _ = normalize(patches)
    normed = (unit * vec[8:9, :] + vec[9:10, :]).astype(BF)
    keys = aux_out[0:8, :]
    token = aux_out[8:16, :]
    scores = nt(keys.astype(BF), normed) + bias_row[0]
    score0 = jnp.sum(keys * token, -1, keepdims=True)
    top = jnp.maximum(jnp.max(scores, -1, keepdims=True), score0)
    grown = jnp.exp(scores - top)
    grown0 = jnp.exp(score0 - top)
    scale = 1.0 / (jnp.sum(grown, -1, keepdims=True) + grown0)
    cprob = grown * scale
    cprob0 = grown0 * scale
    cprob_out[0] = cprob
    cprob0_out[0] = jnp.broadcast_to(cprob0, (HEADS, 128))
    z = (nn(cprob.astype(BF), normed) + cprob0 * token).astype(BF)
    z_out[0] = z
    cheads = colsum(nt(z, part(wcls, 2 * shard, shard)) * mask)
    for piece in range(3):
        card_out[pl.ds(first + piece, 1), :] = cheads[:, 128 * piece : 128 * piece + 128]


def token_kernel(
    group, cards, vec, wcls, wmlp, head,
    dch_out, gout_out, gup_out, gdown_out, ghead_out, rows_out, stat_out,
):
    hidden = wmlp.shape[1] // 2
    shard = wcls.shape[1] // 4
    images = cards.shape[0] // 4
    cheads = jnp.concatenate(
        [cards[pl.ds(piece, images, stride=4), :] for piece in range(3)], 1
    ).astype(BF)
    card = cards[pl.ds(3, images, stride=4), :]
    labels = (card[:, 0:1] * 32.0 + card[:, 1:2]).astype(jnp.int32)
    pairs = (card[:, 2:3] * 32.0 + card[:, 3:4]).astype(jnp.int32)
    column = lax.broadcasted_iota(jnp.int32, (images, images), 1)
    row = lax.broadcasted_iota(jnp.int32, (images, images), 0)
    slot = lax.rem(lax.broadcasted_iota(jnp.int32, (images, 1), 0), group).astype(F32)
    okay = (slot >= group - card[:, 4:5]).astype(F32)
    okay_row = colsum(jnp.where(row == column, okay, 0.0))
    wo = part(wcls, 3 * shard, shard)
    wup = part(wmlp, 0, hidden)
    wdown = part(wmlp, hidden, hidden)
    count = jnp.sum(okay, keepdims=True)
    raw = nn(cheads, wo) + vec[10:11, :]
    branch = vec[11:12, :] * raw
    middle = vec[17:18, :] + branch
    unit2, inverse2 = normalize(middle)
    normed = (unit2 * vec[12:13, :] + vec[13:14, :]).astype(BF)
    inner = nt(normed, wup)
    active, slope = gelu_parts(inner)
    active = active.astype(BF)
    down = nn(active, wdown) + vec[14:15, :]
    mlp_branch = vec[15:16, :] * down
    token = middle + mlp_branch
    unit3, inverse3 = normalize(token)
    feature = unit3 * vec[18:19, :] + vec[19:20, :]
    feature_low = feature.astype(BF)
    logits = nt(feature_low, head[...])
    top = jnp.max(logits, -1, keepdims=True)
    grown = jnp.exp(logits - top)
    total = jnp.sum(grown, -1, keepdims=True)
    hot = lax.broadcasted_iota(jnp.int32, logits.shape, 1) == labels
    cross = jnp.log(total) + top - jnp.sum(jnp.where(hot, logits, 0.0), -1, keepdims=True)
    share = okay / count
    dlogits = (share * (grown / total - hot.astype(F32))).astype(BF)
    ghead_out[...] = tn(dlogits, feature_low)
    dfeature = nn(dlogits, head[...])

    length = lax.rsqrt(jnp.sum(feature * feature, -1, keepdims=True) + NORM_EPS)
    embed = (feature * length).astype(BF)
    sims = nt(embed, embed) / TEMP
    sims = jnp.where((okay_row > 0) & (row != column), sims, MASKED)
    top = jnp.max(sims, -1, keepdims=True)
    grown = jnp.exp(sims - top)
    total = jnp.sum(grown, -1, keepdims=True)
    hot = column == pairs
    contrast = jnp.log(total) + top - jnp.sum(jnp.where(hot, sims, 0.0), -1, keepdims=True)
    dsims = share * (grown / total - hot.astype(F32))
    high = dsims.astype(BF)
    low = (dsims - high.astype(F32)).astype(BF)
    dembed = (nn(high, embed) + nn(low, embed) + tn(high, embed) + tn(low, embed)) / TEMP
    dfeature += length * dembed - feature * (
        length * length * length * jnp.sum(dembed * feature, -1, keepdims=True)
    )

    dtoken = normalize_back(unit3, inverse3, vec[18:19, :], dfeature)
    rows_out[0:1, :] = jnp.zeros((1, D), F32)
    rows_out[1:2, :] = jnp.zeros((1, D), F32)
    rows_out[7:8, :] = colsum(dtoken * down)
    rows_out[6:7, :] = vec[15:16, :] * colsum(dtoken)
    ddown = (dtoken * vec[15:16, :]).astype(BF)
    gdown_out[...] = tn(active, ddown)
    dinner = (nt(ddown, wdown) * slope).astype(BF)
    gup_out[...] = tn(dinner, normed)
    dnormed = nn(dinner, wup)
    rows_out[4:5, :] = colsum(dnormed * unit2)
    rows_out[5:6, :] = colsum(dnormed)
    dmiddle = dtoken + normalize_back(unit2, inverse2, vec[12:13, :], dnormed)
    rows_out[3:4, :] = colsum(dmiddle * raw)
    rows_out[2:3, :] = vec[11:12, :] * colsum(dmiddle)
    rows_out[8:9, :] = colsum(dmiddle)
    rows_out[9:10, :] = colsum(dfeature * unit3)
    rows_out[10:11, :] = colsum(dfeature)
    dbranch = (dmiddle * vec[11:12, :]).astype(BF)
    gout_out[...] = tn(cheads, dbranch)
    dch_out[...] = nt(dbranch, wo).astype(BF)
    lane = lax.broadcasted_iota(jnp.int32, (1, 128), 1)
    self_sums = colsum(card)
    count_tokens = self_sums[:, 5:6]

    def squares(values):
        return jnp.sum(colsum(values * values * okay), keepdims=True)

    entries = [jnp.sum(okay * cross, keepdims=True), jnp.sum(okay * contrast, keepdims=True)]
    entries += [count, count_tokens]
    entries += [
        jnp.sqrt((self_sums[:, i : i + 1] + self_sums[:, i + 1 : i + 2]) / D / count_tokens)
        for i in (8, 10, 12, 14)
    ]
    entries += [
        jnp.sqrt(squares(item) / D / count) for item in (branch, middle, mlp_branch, token)
    ]
    line = jnp.zeros((1, 128), F32)
    for i, entry in enumerate(entries):
        line = jnp.where(lane == i, entry, line)
    stat_out[...] = jnp.broadcast_to(line, (8, 128))


def feed_back_kernel(
    dch, patch, mid, raw, act, slope, cprob, cprob0, z, aux, vec, wcls, wmlp,
    dmid_out, gmlp_out, gv_out, rows_out,
):
    hidden = wmlp.shape[1] // 2
    shard = wcls.shape[1] // 4
    count = wmlp.shape[0]
    mask = head_mask()

    @pl.when(pl.program_id(0) == 0)
    def _():
        gmlp_out[...] = jnp.zeros_like(gmlp_out)
        gv_out[...] = jnp.zeros_like(gv_out)
        rows_out[...] = jnp.zeros_like(rows_out)

    keys = aux[0:8, :]
    token = aux[8:16, :]
    unit, inverse = normalize(patch[0])
    normed = (unit * vec[8:9, :] + vec[9:10, :]).astype(BF)
    spread = (mask * dch[0].astype(F32)).astype(BF)
    dz = nn(spread, part(wcls, 2 * shard, shard))
    dz_low = dz.astype(BF)
    probs = cprob[0]
    prob0 = cprob0[0][:, 0:1]
    dprobs = nt(dz_low, normed)
    dprob0 = jnp.sum(dz * token, -1, keepdims=True)
    inside = jnp.sum(dprobs * probs, -1, keepdims=True) + dprob0 * prob0
    dscores = (probs * (dprobs - inside)).astype(BF)
    dscore0 = prob0 * (dprob0 - inside)
    dnormed = tn(
        jnp.concatenate([probs.astype(BF), dscores], 0),
        jnp.concatenate([dz_low, keys.astype(BF)], 0),
    )
    rows_out[8:16, :] += nn(dscores, normed) + dscore0 * token
    rows_out[6:7, :] += colsum(prob0 * dz + dscore0 * keys)
    gv_out[...] += tn(spread, z[0])
    rows_out[4:5, :] += colsum(dnormed * unit)
    rows_out[5:6, :] += colsum(dnormed)
    incoming = normalize_back(unit, inverse, vec[8:9, :], dnormed)

    unit, inverse = normalize(mid[0])
    normed = (unit * vec[4:5, :] + vec[5:6, :]).astype(BF)
    rows_out[3:4, :] += colsum(incoming * (raw[0].astype(F32) + vec[6:7, :]))
    rows_out[2:3, :] += vec[7:8, :] * colsum(incoming)
    ddown = (incoming * vec[7:8, :]).astype(BF)
    gmlp_out[:, hidden:, :] += tn(act[0], ddown).reshape(count, hidden, D)
    dinner = (nt(ddown, part(wmlp, hidden, hidden)) * slope[0].astype(F32)).astype(BF)
    gmlp_out[:, :hidden, :] += tn(dinner, normed).reshape(count, hidden, D)
    dnormed = nn(dinner, part(wmlp, 0, hidden))
    rows_out[0:1, :] += colsum(dnormed * unit)
    rows_out[1:2, :] += colsum(dnormed)
    dmid_out[0] = incoming + normalize_back(unit, inverse, vec[4:5, :], dnormed)


def self_back_kernel(
    dmid, pixels, embed, q, k, v, prob, ho, raw, vec, wattn, t1row, t1col, t2row,
    gattn_out, gpix_out, gpos_out, rows_out,
):
    shard = wattn.shape[1] // 4
    count = wattn.shape[0]

    @pl.when(pl.program_id(0) == 0)
    def _():
        gattn_out[...] = jnp.zeros_like(gattn_out)
        gpix_out[...] = jnp.zeros_like(gpix_out)
        gpos_out[...] = jnp.zeros_like(gpos_out)
        rows_out[...] = jnp.zeros_like(rows_out)

    wq = part(wattn, 0, shard)
    wk = part(wattn, shard, shard)
    wv = part(wattn, 2 * shard, shard)
    wo = part(wattn, 3 * shard, shard)
    incoming = dmid[0]
    rows_out[3:4, :] += colsum(incoming * (raw[0].astype(F32) + vec[2:3, :]))
    rows_out[2:3, :] += vec[3:4, :] * colsum(incoming)
    dbranch = (incoming * vec[3:4, :]).astype(BF)
    gattn_out[:, 3 * shard :, :] += nn(ho[0], dbranch).reshape(count, shard, D)
    dheads = nt(dbranch, wo).astype(BF)

    unit, inverse = normalize(embed[0])
    normed = (unit * vec[0:1, :] + vec[1:2, :]).astype(BF)
    q_low = q[0]
    k_wide = k[0].astype(F32)
    v_wide = v[0].astype(F32)
    k_flip = nt(wk, normed).astype(BF).astype(F32)
    dq = jnp.zeros((D, normed.shape[0]), F32)
    dk = jnp.zeros(normed.shape, F32)
    dv = jnp.zeros(normed.shape, F32)
    for g in range(HEADS):
        one = t1row[g : g + 1, :]
        two = t2row[g : g + 1, :]
        chance = prob[0, g]
        chance_wide = chance.astype(F32)
        dprob = nt((v_wide * two).astype(BF), dheads)
        dmixed = (chance_wide * (dprob - colsum(dprob * chance_wide))).astype(BF)
        dpost = nn(chance, dheads)
        dv += two * dpost
        rows_out[16 + g : 17 + g, :] += colsum(v_wide * dpost)
        dpre = nn(dmixed, q_low)
        dk += one * dpre
        rows_out[8 + g : 9 + g, :] += colsum(k_wide * dpre)
        dq += nn((k_flip * t1col[:, g : g + 1]).astype(BF), dmixed)
    dq = dq.astype(BF)
    dk = dk.astype(BF)
    dv = dv.astype(BF)
    gattn_out[:, :shard, :] += nn(dq, normed).reshape(count, shard, D)
    gattn_out[:, shard : 2 * shard, :] += tn(dk, normed).reshape(count, shard, D)
    gattn_out[:, 2 * shard : 3 * shard, :] += tn(dv, normed).reshape(count, shard, D)
    dnormed = tn(dq, wq) + nn(dk, wk) + nn(dv, wv)
    rows_out[0:1, :] += colsum(dnormed * unit)
    rows_out[1:2, :] += colsum(dnormed)
    dx = incoming + normalize_back(unit, inverse, vec[0:1, :], dnormed)
    gpos_out[...] += dx
    gpix_out[...] += tn(pixels[0], dx.astype(BF))


def per_image(*tail):
    return pl.BlockSpec((1, *tail), lambda n: (n, *(0 for _ in tail)))


def constant(*shape):
    return pl.BlockSpec(shape, lambda n: tuple(0 for _ in shape))


def shaped(*shape, dtype=F32):
    return jax.ShapeDtypeStruct(shape, dtype)


def params():
    return pltpu.CompilerParams(vmem_limit_bytes=VMEM_LIMIT, dimension_semantics=("arbitrary",))


def run_self_attend(pixels, cols, vec, pos, wp, wattn, t1row, t2col):
    count = pixels.shape[0]
    return pl.pallas_call(
        self_attend_kernel,
        grid=(count,),
        in_specs=[
            per_image(P_SIZE, PIX), per_image(P_SIZE, 2), constant(*vec.shape), constant(P_SIZE, D),
            constant(PIX, D), constant(*wattn.shape), constant(HEADS, D), constant(D, HEADS),
        ],
        out_specs=[
            per_image(P_SIZE, D), per_image(P_SIZE, D), per_image(P_SIZE, D), per_image(P_SIZE, D),
            per_image(HEADS, P_SIZE, P_SIZE), per_image(D, P_SIZE), per_image(P_SIZE, D),
            per_image(P_SIZE, D), per_image(1, 128),
        ],
        out_shape=[
            shaped(count, P_SIZE, D), shaped(count, P_SIZE, D, dtype=BF),
            shaped(count, P_SIZE, D, dtype=BF), shaped(count, P_SIZE, D, dtype=BF),
            shaped(count, HEADS, P_SIZE, P_SIZE, dtype=BF), shaped(count, D, P_SIZE, dtype=BF),
            shaped(count, P_SIZE, D, dtype=BF), shaped(count, P_SIZE, D), shaped(count, 1, 128),
        ],
        compiler_params=params(),
        name="self_attend",
    )(pixels, cols, vec, pos, wp, wattn, t1row, t2col)


def run_feed(mid, cols, bias_row, base, stat, vec, wmlp, wcls):
    count = mid.shape[0]
    wide = 2 * wmlp.shape[0] * wmlp.shape[1] // 4
    return pl.pallas_call(
        feed_kernel,
        grid=(count,),
        in_specs=[
            per_image(P_SIZE, D), per_image(P_SIZE, 2), per_image(1, P_SIZE), per_image(1, 128),
            per_image(1, 128), constant(*vec.shape), constant(*wmlp.shape), constant(*wcls.shape),
        ],
        out_specs=[
            per_image(P_SIZE, D), per_image(P_SIZE, wide), per_image(P_SIZE, wide),
            per_image(P_SIZE, D), per_image(HEADS, P_SIZE), per_image(HEADS, 128),
            per_image(HEADS, D), constant(4 * count, 128), constant(24, D),
        ],
        out_shape=[
            shaped(count, P_SIZE, D), shaped(count, P_SIZE, wide, dtype=BF),
            shaped(count, P_SIZE, wide, dtype=BF), shaped(count, P_SIZE, D, dtype=BF),
            shaped(count, HEADS, P_SIZE), shaped(count, HEADS, 128),
            shaped(count, HEADS, D, dtype=BF), shaped(4 * count, 128), shaped(24, D),
        ],
        compiler_params=params(),
        name="feed",
    )(mid, cols, bias_row, base, stat, vec, wmlp, wcls)


def run_token(group, cards, vec, wcls, wmlp, head):
    images = cards.shape[0] // 4
    wide = wmlp.shape[0] * wmlp.shape[1] // 2
    return pl.pallas_call(
        functools.partial(token_kernel, group),
        in_specs=[WHOLE] * 5,
        out_specs=[WHOLE] * 7,
        out_shape=[
            shaped(images, D, dtype=BF), shaped(D, D), shaped(wide, D), shaped(wide, D),
            shaped(*head.shape), shaped(16, D), shaped(8, 128),
        ],
        compiler_params=pltpu.CompilerParams(vmem_limit_bytes=VMEM_LIMIT),
        name="token_net",
    )(cards, vec, wcls, wmlp, head)


def run_feed_back(dch, patch, mid, raw, act, slope, cprob, cprob0, z, aux, vec, wcls, wmlp):
    count = mid.shape[0]
    wide = act.shape[2]
    return pl.pallas_call(
        feed_back_kernel,
        grid=(count,),
        in_specs=[
            per_image(1, D), per_image(P_SIZE, D), per_image(P_SIZE, D), per_image(P_SIZE, D),
            per_image(P_SIZE, wide), per_image(P_SIZE, wide), per_image(HEADS, P_SIZE),
            per_image(HEADS, 128), per_image(HEADS, D), constant(24, D), constant(*vec.shape),
            constant(*wcls.shape), constant(*wmlp.shape),
        ],
        out_specs=[
            per_image(P_SIZE, D), constant(*wmlp.shape), constant(D, D), constant(16, D),
        ],
        out_shape=[
            shaped(count, P_SIZE, D), shaped(*wmlp.shape), shaped(D, D), shaped(16, D),
        ],
        compiler_params=params(),
        name="feed_back",
    )(dch, patch, mid, raw, act, slope, cprob, cprob0, z, aux, vec, wcls, wmlp)


def run_self_back(dmid, pixels, embed, q, k, v, prob, ho, raw, vec, wattn, t1row, t1col, t2row):
    count = dmid.shape[0]
    return pl.pallas_call(
        self_back_kernel,
        grid=(count,),
        in_specs=[
            per_image(P_SIZE, D), per_image(P_SIZE, PIX), per_image(P_SIZE, D),
            per_image(P_SIZE, D), per_image(P_SIZE, D), per_image(P_SIZE, D),
            per_image(HEADS, P_SIZE, P_SIZE), per_image(D, P_SIZE), per_image(P_SIZE, D),
            constant(*vec.shape), constant(*wattn.shape), constant(HEADS, D), constant(D, HEADS),
            constant(HEADS, D),
        ],
        out_specs=[
            constant(*wattn.shape), constant(PIX, D), constant(P_SIZE, D), constant(24, D),
        ],
        out_shape=[shaped(*wattn.shape), shaped(PIX, D), shaped(P_SIZE, D), shaped(24, D)],
        compiler_params=params(),
        name="self_back",
    )(dmid, pixels, embed, q, k, v, prob, ho, raw, vec, wattn, t1row, t1col, t2row)


def peer_at(index, n_mp):
    return (lax.div(index, n_mp), lax.rem(index, n_mp))


def greet_all(me, n, n_mp):
    barrier = pltpu.get_barrier_semaphore()

    @pl.loop(1, n)
    def _(step):
        pl.semaphore_signal(
            barrier, inc=1, device_id=peer_at(lax.rem(me + step, n), n_mp), device_id_type=MESH
        )

    pl.semaphore_wait(barrier, n - 1)


def remote(src, dst, send_sem, recv_sem, device):
    return pltpu.make_async_remote_copy(
        src_ref=src, dst_ref=dst, send_sem=send_sem, recv_sem=recv_sem,
        device_id=device, device_id_type=MESH,
    )


def spread_to_all(me, n, n_mp, slots, rows, send_sem, recv_sem):
    def slot(index):
        return slots.at[pl.ds(pl.multiple_of(index * rows, rows), rows)]

    @pl.loop(1, n)
    def _(step):
        remote(
            slot(me), slot(me), send_sem.at[step], recv_sem.at[step],
            peer_at(lax.rem(me + step, n), n_mp),
        ).start()

    def finish():
        @pl.loop(1, n)
        def _(step):
            source = lax.rem(me + n - step, n)
            copy = remote(
                slot(me), slot(source), send_sem.at[step], recv_sem.at[step],
                peer_at(source, n_mp),
            )
            copy.wait_send()
            copy.wait_recv()

    return finish


def card_kernel(n_dp, n_mp, card, out, slots, send_sem, recv_sem):
    n = n_dp * n_mp
    me = lax.axis_index("dp") * n_mp + lax.axis_index("mp")
    rows = card.shape[0]
    greet_all(me, n, n_mp)
    slots[pl.ds(pl.multiple_of(me * rows, rows), rows), :] = card[...].astype(BF)
    spread_to_all(me, n, n_mp, slots, rows, send_sem, recv_sem)()
    out[...] = slots[...].astype(F32)


def run_cards(n_dp, n_mp, card):
    n = n_dp * n_mp
    return pl.pallas_call(
        functools.partial(card_kernel, n_dp, n_mp),
        in_specs=[WHOLE],
        out_specs=WHOLE,
        out_shape=shaped(n * card.shape[0], 128),
        scratch_shapes=[
            pltpu.VMEM((n * card.shape[0], 128), BF),
            pltpu.SemaphoreType.DMA((n,)),
            pltpu.SemaphoreType.DMA((n,)),
        ],
        compiler_params=pltpu.CompilerParams(
            vmem_limit_bytes=VMEM_LIMIT, collective_id=1, has_side_effects=True
        ),
        name="cards",
    )(card)


def weight_kernel(n_dp, n_mp, shard, out, near_send, near_recv, far_send, far_recv):
    dp = lax.axis_index("dp")
    mp = lax.axis_index("mp")
    n_y = n_mp // 2
    y = lax.div(mp, 2)
    core = lax.rem(mp, 2)
    sibling = (dp, y * 2 + 1 - core)
    barrier = pltpu.get_barrier_semaphore()
    pl.semaphore_signal(barrier, inc=1, device_id=sibling, device_id_type=MESH)
    for step in range(1, n_y):
        pl.semaphore_signal(
            barrier, inc=1, device_id=(dp, lax.rem(y + step, n_y) * 2 + core), device_id_type=MESH
        )
    pl.semaphore_wait(barrier, n_y)
    far = [
        remote(
            shard, out.at[mp], far_send.at[step], far_recv.at[step],
            (dp, lax.rem(y + step, n_y) * 2 + core),
        )
        for step in range(1, n_y)
    ]
    for copy in far:
        copy.start()
    near = [remote(shard, out.at[mp], near_send.at[0], near_recv.at[0], sibling)]
    near[0].start()
    out[pl.ds(mp, 1)] = shard[...][None]
    for step in range(1, n_y):
        source = lax.rem(y + n_y - step, n_y) * 2
        slot = source + core
        remote(
            shard, out.at[slot], far_send.at[step], far_recv.at[step], (dp, slot)
        ).wait_recv()
        copy = remote(
            out.at[slot], out.at[slot], near_send.at[step], near_recv.at[step], sibling
        )
        copy.start()
        near.append(copy)
    for copy in far:
        copy.wait_send()
    for step in range(n_y):
        slot = lax.rem(y + n_y - step, n_y) * 2 + 1 - core
        near[step].wait_send()
        remote(
            out.at[slot], out.at[slot], near_send.at[step], near_recv.at[step], sibling
        ).wait_recv()


def run_weights(n_dp, n_mp, rows):
    n_y = n_mp // 2
    return pl.pallas_call(
        functools.partial(weight_kernel, n_dp, n_mp),
        in_specs=[WHOLE],
        out_specs=WHOLE,
        out_shape=shaped(n_mp, *rows.shape, dtype=BF),
        scratch_shapes=[pltpu.SemaphoreType.DMA((n_y,))] * 4,
        compiler_params=pltpu.CompilerParams(
            vmem_limit_bytes=VMEM_LIMIT, collective_id=2, has_side_effects=True
        ),
        name="weights",
    )(rows)


def reduce_kernel(
    n_dp, n_mp, gattn, gmlp, gv, gpix, gpos, rows2, rows3,
    block_out, shared_out, square_out,
    blocks, commons, near_b, near_s, part_b, part_s, far_b, far_s, half_b, half_s, last_b, last_s,
    squares, near_sem, far_sem, last_sem, all_send, all_recv, block_sem, square_sem,
):
    n = n_dp * n_mp
    n_y = n_mp // 2
    dp = lax.axis_index("dp")
    mp = lax.axis_index("mp")
    me = dp * n_mp + mp
    y = lax.div(mp, 2)
    core = lax.rem(mp, 2)
    sibling = (dp, y * 2 + 1 - core)
    chunk_b = block_out.shape[0] // n_dp
    chunk_s = shared_out.shape[0] // n
    wide_s = chunk_s * n_dp

    greet_all(me, n, n_mp)

    first = 0
    for item in (gattn, gmlp, gv):
        size = item.shape[1]
        blocks[:, first : first + size, :] = item[...].astype(BF)
        first += size
    if first < blocks.shape[1]:
        blocks[:, first:, :] = jnp.zeros((n_mp, blocks.shape[1] - first, D), BF)
    commons[:PIX, :] = gpix[...].astype(BF)
    commons[PIX : PIX + P_SIZE + 12, :] = jnp.concatenate(
        [gpos[...], jnp.zeros((12, D), F32)], 0
    ).astype(BF)
    commons[PIX + 208 : PIX + 224, :] = rows2[...].astype(BF)
    commons[PIX + 224 : PIX + 256, :] = jnp.concatenate(
        [rows3[...], jnp.zeros((8, D), F32)], 0
    ).astype(BF)
    if commons.shape[0] > PIX + 256:
        commons[PIX + 256 :, :] = jnp.zeros((commons.shape[0] - PIX - 256, D), BF)

    def common(index, rows):
        return commons.at[pl.ds(pl.multiple_of(index * rows, rows), rows)]

    near = []
    for step in range(1, n_y + 1):
        place = lax.rem(y + step, n_y)
        give = place * 2 + 1 - core
        near.append(remote(blocks.at[give], near_b.at[place], near_sem.at[0, step], near_sem.at[1, step], sibling))
        near.append(remote(common(give, wide_s), near_s.at[place], near_sem.at[2, step], near_sem.at[3, step], sibling))
    for copy in near:
        copy.start()

    far = []
    for step in range(1, n_y + 1):
        place = lax.rem(y + step, n_y)
        near[2 * step - 2].wait_recv()
        near[2 * step - 1].wait_recv()
        keep = place * 2 + core
        part_b[pl.ds(place, 1)] = (
            blocks[pl.ds(keep, 1)].astype(F32) + near_b[pl.ds(place, 1)].astype(F32)
        ).astype(BF)
        part_s[pl.ds(place, 1)] = (
            commons[pl.ds(pl.multiple_of(keep * wide_s, wide_s), wide_s), :].astype(F32)[None]
            + near_s[pl.ds(place, 1)].astype(F32)
        ).astype(BF)
        if step < n_y:
            to = (dp, keep)
            far.append(remote(part_b.at[place], far_b.at[step - 1], far_sem.at[0, step], far_sem.at[1, step], to))
            far.append(remote(part_s.at[place], far_s.at[step - 1], far_sem.at[2, step], far_sem.at[3, step], to))
            far[-2].start()
            far[-1].start()
    total_b = part_b[pl.ds(y, 1)][0].astype(F32)
    total_s = part_s[pl.ds(y, 1)][0].astype(F32)
    for step in range(1, n_y):
        far[2 * step - 2].wait_recv()
        far[2 * step - 1].wait_recv()
        total_b += far_b[step - 1].astype(F32)
        total_s += far_s[step - 1].astype(F32)
    half_b[...] = total_b.astype(BF)
    half_s[...] = total_s.astype(BF)

    def rows_of(ref, index, rows):
        return ref.at[pl.ds(pl.multiple_of(index * rows, rows), rows)]

    last = []
    for step in range(1, n_dp):
        place = lax.rem(dp + step, n_dp)
        to = (place, mp)
        last.append(remote(rows_of(half_b, place, chunk_b), last_b.at[step - 1], last_sem.at[0, step], last_sem.at[1, step], to))
        last.append(remote(rows_of(half_s, place, chunk_s), last_s.at[step - 1], last_sem.at[2, step], last_sem.at[3, step], to))
    for copy in last:
        copy.start()
    total_b = half_b[pl.ds(pl.multiple_of(dp * chunk_b, chunk_b), chunk_b), :].astype(F32)
    total_s = half_s[pl.ds(pl.multiple_of(dp * chunk_s, chunk_s), chunk_s), :].astype(F32)
    for step in range(1, n_dp):
        last[2 * step - 2].wait_recv()
        last[2 * step - 1].wait_recv()
        total_b += last_b[step - 1].astype(F32)
        total_s += last_s[step - 1].astype(F32)
    block_out[pl.ds(pl.multiple_of(dp * chunk_b, chunk_b), chunk_b), :] = total_b.astype(BF)
    own = mp * n_dp + dp
    shared_out[pl.ds(pl.multiple_of(own * chunk_s, chunk_s), chunk_s), :] = total_s.astype(BF)

    back = []
    for step in range(1, n_dp):
        back.append(
            remote(
                rows_of(block_out, dp, chunk_b), rows_of(block_out, dp, chunk_b),
                block_sem.at[0, step], block_sem.at[1, step], (lax.rem(dp + step, n_dp), mp),
            )
        )
        back[-1].start()

    @pl.loop(1, n)
    def _(step):
        remote(
            rows_of(shared_out, own, chunk_s), rows_of(shared_out, own, chunk_s),
            all_send.at[step], all_recv.at[step], peer_at(lax.rem(me + step, n), n_mp),
        ).start()

    for step in range(1, n_dp):
        source = lax.rem(dp + n_dp - step, n_dp)
        remote(
            rows_of(block_out, dp, chunk_b), rows_of(block_out, source, chunk_b),
            block_sem.at[0, step], block_sem.at[1, step], (source, mp),
        ).wait_recv()

    sums = block_out[...].astype(F32)
    sums = colsum(sums * sums)
    squares[pl.ds(mp, 1)] = jnp.broadcast_to(
        sums[:, 0:128] + sums[:, 128:256] + sums[:, 256:384], (8, 128)
    )[None]
    tally = []
    for step in range(1, n_mp):
        tally.append(
            remote(
                squares.at[mp], squares.at[mp], square_sem.at[0, step], square_sem.at[1, step],
                (dp, lax.rem(mp + step, n_mp)),
            )
        )
        tally[-1].start()

    @pl.loop(1, n)
    def _(step):
        source = lax.rem(me + n - step, n)
        copy = remote(
            rows_of(shared_out, own, chunk_s),
            rows_of(shared_out, lax.rem(source, n_mp) * n_dp + lax.div(source, n_mp), chunk_s),
            all_send.at[step], all_recv.at[step], peer_at(source, n_mp),
        )
        copy.wait_send()
        copy.wait_recv()

    for step in range(1, n_mp):
        source = lax.rem(mp + n_mp - step, n_mp)
        tally[step - 1].wait_send()
        remote(
            squares.at[mp], squares.at[source], square_sem.at[0, step], square_sem.at[1, step],
            (dp, source),
        ).wait_recv()
    square_out[...] = jnp.sum(squares[...], 0)
    for copy in near + far + last + back:
        copy.wait_send()


def run_reduce(n_dp, n_mp, gattn, gmlp, gv, gpix, gpos, rows2, rows3):
    n = n_dp * n_mp
    n_y = n_mp // 2
    rows_b = gattn.shape[1] + gmlp.shape[1] + gv.shape[1]
    chunk_b = -(-rows_b // (16 * n_dp)) * 16
    rows_b = chunk_b * n_dp
    chunk_s = -(-(PIX + 256) // (16 * n)) * 16
    wide_s = chunk_s * n_dp
    y_less = max(n_y - 1, 1)
    dma = pltpu.SemaphoreType.DMA
    return pl.pallas_call(
        functools.partial(reduce_kernel, n_dp, n_mp),
        in_specs=[WHOLE] * 7,
        out_specs=[WHOLE] * 3,
        out_shape=[
            shaped(rows_b, D, dtype=BF), shaped(chunk_s * n, D, dtype=BF), shaped(8, 128),
        ],
        scratch_shapes=[
            pltpu.VMEM((n_mp, rows_b, D), BF), pltpu.VMEM((n * chunk_s, D), BF),
            pltpu.VMEM((n_y, rows_b, D), BF), pltpu.VMEM((n_y, wide_s, D), BF),
            pltpu.VMEM((n_y, rows_b, D), BF), pltpu.VMEM((n_y, wide_s, D), BF),
            pltpu.VMEM((y_less, rows_b, D), BF), pltpu.VMEM((y_less, wide_s, D), BF),
            pltpu.VMEM((rows_b, D), BF), pltpu.VMEM((wide_s, D), BF),
            pltpu.VMEM((n_dp - 1, chunk_b, D), BF), pltpu.VMEM((n_dp - 1, chunk_s, D), BF),
            pltpu.VMEM((n_mp, 8, 128), F32),
            dma((4, n_y + 1)), dma((4, n_y + 1)), dma((4, n_dp)), dma((n,)), dma((n,)),
            dma((2, n_dp)), dma((2, n_mp)),
        ],
        compiler_params=pltpu.CompilerParams(
            vmem_limit_bytes=VMEM_LIMIT, collective_id=3, has_side_effects=True
        ),
        name="reduce",
    )(gattn, gmlp, gv, gpix, gpos, rows2, rows3)


def adam_parts(gradient, mean, square, factor):
    clipped = gradient * factor
    mean_new = BETA_ONE * mean + (1.0 - BETA_ONE) * clipped
    square_new = BETA_TWO * square + (1.0 - BETA_TWO) * clipped * clipped
    direction = (
        mean_new
        / (1.0 - BETA_ONE**STEP)
        / (jnp.sqrt(square_new / (1.0 - BETA_TWO**STEP)) + ADAM_EPS)
    )
    return (mean_new, square_new, direction)


def layer_squares(values):
    return jnp.stack([jnp.sum(values[0] * values[0]), jnp.sum(values[1] * values[1])])


def trust_of(weight_sq, update_sq):
    return jnp.sqrt(weight_sq / (update_sq + 1e-12))


def per_layer(values, like):
    return values.reshape((2,) + (1,) * (like.ndim - 1))


def shards(
    pixels,
    token_mask,
    counts,
    labels,
    pairs,
    attn_in,
    attn_in_mean,
    attn_in_square,
    attn_out,
    attn_out_mean,
    attn_out_square,
    mlp_in,
    mlp_in_mean,
    mlp_in_square,
    mlp_out,
    mlp_out_mean,
    mlp_out_square,
    tables,
    tables_mean,
    tables_square,
    vectors,
    vectors_mean,
    vectors_square,
    talking,
    talking_mean,
    talking_square,
):
    local = pixels.shape[0]
    group = token_mask.shape[0]
    place_mp = lax.axis_index("mp")
    place_dp = lax.axis_index("dp")
    n_mp = lax.axis_size("mp")
    n_dp = lax.axis_size("dp")
    images = local * n_mp * n_dp
    place = place_dp * n_mp + place_mp
    hs = attn_in.shape[3]
    fs = mlp_in.shape[2]

    attn_rows = [
        jnp.concatenate(
            [attn_in[b].transpose(1, 2, 0).reshape(3 * hs, D), attn_out[b]], 0
        ).astype(BF)
        for b in range(2)
    ]
    mlp_rows = [jnp.concatenate([mlp_in[b].T, mlp_out[b]], 0).astype(BF) for b in range(2)]
    wattn = run_weights(n_dp, n_mp, attn_rows[0])
    wmlp = lax.all_gather(mlp_rows[0], "mp")
    wcls = lax.all_gather(attn_rows[1], "mp")
    wmlp_cls = lax.all_gather(mlp_rows[1], "mp")

    okay = lax.dynamic_slice_in_dim(
        (jnp.arange(group) >= group - counts[0]).astype(F32), place_mp * local, local, 0
    )
    keep = lax.dynamic_slice_in_dim(token_mask > 0, place_mp * local, local, 0)
    token_weight = keep.astype(F32) * okay[:, None]
    bias = jnp.where(keep, 0.0, MASKED).astype(F32)
    cols = jnp.stack([bias, token_weight], -1)
    digits = [labels // 32, labels % 32, pairs // 32, pairs % 32]
    digits = [item.astype(F32) for item in digits]
    digits += [jnp.broadcast_to(counts, (local,)).astype(F32), jnp.sum(token_weight, 1)]
    base = jnp.pad(jnp.stack(digits, 1), ((0, 0), (0, 128 - len(digits))))[:, None, :]

    spread_heads = functools.partial(jnp.repeat, repeats=HEAD, axis=1)
    t1row = spread_heads(talking[0]) * SCALE
    t1col = t1row.T
    t2row = spread_heads(talking[1].T)
    t2col = t2row.T
    wp = tables[:PIX].astype(BF)
    pos = tables[PIX : PIX + P_SIZE]
    head = tables[PIX + P_SIZE :].astype(BF)

    embed, q, k, v, prob, ho, raw0, middle, stat_a = run_self_attend(
        pixels, cols, vectors, pos, wp, wattn, t1row, t2col
    )
    patches, act, slope, raw1, cprob, cprob0, z, card, aux = run_feed(
        middle, cols, bias[:, None, :], base, stat_a, vectors, wmlp, wcls
    )
    cards = run_cards(n_dp, n_mp, card)
    dch, gout1, gup1, gdown1, ghead, rows1, stat = run_token(
        group, cards, vectors, wcls, wmlp_cls, head
    )
    dch = lax.dynamic_slice_in_dim(dch, place * local, local, 0).reshape(local, 1, D)
    dmid, gmlp, gv, rows2 = run_feed_back(
        dch, patches, middle, raw1, act, slope, cprob, cprob0, z, aux, vectors, wcls, wmlp
    )
    gattn, gpix, gpos, rows3 = run_self_back(
        dmid, pixels, embed, q, k, v, prob, ho, raw0, vectors, wattn, t1row, t1col, t2row
    )

    block, shared, block_sq = run_reduce(
        n_dp, n_mp, gattn, gmlp, gv.reshape(n_mp, hs, D), gpix, gpos, rows2, rows3
    )
    sharded = block.astype(F32)
    shared = shared[: PIX + 256].astype(F32)
    gpix = shared[:PIX]
    gpos = shared[PIX : PIX + P_SIZE]
    rows2 = shared[PIX + 208 : PIX + 224]
    rows3 = shared[PIX + 224 : PIX + 248]

    dkeys = rows2[8:16]
    token = aux[8:9]
    query = aux[16]
    wq1 = wcls[:, :hs].reshape(D, D)
    wk1 = wcls[:, hs : 2 * hs].reshape(D, D)
    dquery = SCALE * jnp.sum(wk1.astype(F32) * jnp.repeat(dkeys, HEAD, axis=0), 1)
    gq1 = dquery[:, None] * token
    gk1 = (SCALE * query)[:, None] * jnp.repeat(dkeys, HEAD, axis=0)
    dtoken = rows2[6] + jnp.sum(dquery[:, None] * wq1.astype(F32), 0)
    unit, inverse = normalize(vectors[17])
    grad_class_token = rows1[8] + normalize_back(unit, inverse, vectors[8], dtoken)
    grad_vectors = jnp.stack(
        [
            rows3[0], rows3[1], rows3[2], rows3[3], rows2[0], rows2[1], rows2[2], rows2[3],
            rows2[4] + dtoken * unit, rows2[5] + dtoken, rows1[2], rows1[3],
            rows1[4], rows1[5], rows1[6], rows1[7],
            jnp.sum(gpos, 0), grad_class_token, rows1[9], rows1[10],
        ]
    )
    by_head = rows3[8:24].reshape(2, HEADS, HEADS, HEAD).sum(-1)
    grad_talking = jnp.stack([by_head[0] * SCALE, by_head[1].T])

    def mine(rows, size):
        return lax.dynamic_slice_in_dim(rows, place_mp * size, size, 0)

    def unpack(rows):
        return rows.reshape(3, hs, D).transpose(2, 0, 1)

    class_rows = jnp.concatenate([mine(gq1, hs), mine(gk1, hs), sharded[4 * hs + 2 * fs : 5 * hs + 2 * fs]], 0)
    grads = (
        jnp.stack([unpack(sharded[: 3 * hs]), unpack(class_rows)]),
        jnp.stack([sharded[3 * hs : 4 * hs], mine(gout1, hs)]),
        jnp.stack([sharded[4 * hs : 4 * hs + fs].T, mine(gup1, fs).T]),
        jnp.stack([sharded[4 * hs + fs : 4 * hs + 2 * fs], mine(gdown1, fs)]),
    )
    grad_tables = jnp.concatenate([gpix, gpos, ghead], 0)

    weights = (attn_in, attn_out, mlp_in, mlp_out)
    means = (attn_in_mean, attn_out_mean, mlp_in_mean, mlp_out_mean)
    squares = (attn_in_square, attn_out_square, mlp_in_square, mlp_out_square)
    grad_norm = jnp.sqrt(
        jnp.sum(block_sq[0])
        + sum(jnp.sum(item * item) for item in (gq1, gk1, gout1, gup1, gdown1))
        + jnp.sum(grad_tables * grad_tables)
        + jnp.sum(grad_vectors * grad_vectors)
        + jnp.sum(grad_talking * grad_talking)
    )
    factor = CLIP / jnp.maximum(grad_norm, CLIP)
    moved = [adam_parts(grads[i], means[i], squares[i], factor) for i in range(4)]
    updates = [moved[i][2] + DECAY * weights[i] for i in range(4)]
    weight_sq, update_sq = lax.psum(
        (
            jnp.concatenate([layer_squares(item) for item in weights]),
            jnp.concatenate([layer_squares(item) for item in updates]),
        ),
        "mp",
    )
    trust = trust_of(weight_sq, update_sq)
    renewed = [
        weights[i] - RATE * per_layer(trust[2 * i : 2 * i + 2], weights[i]) * updates[i]
        for i in range(4)
    ]

    table_mean, table_square, table_direction = adam_parts(
        grad_tables, tables_mean, tables_square, factor
    )
    table_update = table_direction + DECAY * tables
    bounds = ((0, PIX), (PIX, PIX + P_SIZE), (PIX + P_SIZE, tables.shape[0]))

    def segments(values):
        by_row = jnp.sum(values * values, 1)
        return jnp.stack([jnp.sum(by_row[low:high]) for low, high in bounds])

    table_weight_sq = segments(tables)
    table_update_sq = segments(table_update)
    table_trust = trust_of(table_weight_sq, table_update_sq)
    row = jnp.arange(tables.shape[0])[:, None]
    row_trust = jnp.where(
        row < PIX, table_trust[0], jnp.where(row < PIX + P_SIZE, table_trust[1], table_trust[2])
    )
    tables_new = tables - RATE * row_trust * table_update

    vector_mean, vector_square, vector_direction = adam_parts(
        grad_vectors, vectors_mean, vectors_square, factor
    )
    vectors_new = vectors - RATE_VECTOR * vector_direction
    mixing_mean, mixing_square, mixing_direction = adam_parts(
        grad_talking, talking_mean, talking_square, factor
    )
    mixing_update = mixing_direction + DECAY * talking
    mixing_weight_sq = layer_squares(talking)
    mixing_update_sq = layer_squares(mixing_update)
    talking_new = talking - RATE * per_layer(
        trust_of(mixing_weight_sq, mixing_update_sq), talking
    ) * mixing_update
    norms = jnp.stack(
        [
            jnp.sqrt(jnp.concatenate([weight_sq, table_weight_sq, mixing_weight_sq])),
            jnp.sqrt(jnp.concatenate([update_sq, table_update_sq, mixing_update_sq])),
        ]
    )
    statistics = stat[0, :12]
    return (
        renewed[0],
        moved[0][0],
        moved[0][1],
        renewed[1],
        moved[1][0],
        moved[1][1],
        renewed[2],
        moved[2][0],
        moved[2][1],
        renewed[3],
        moved[3][0],
        moved[3][1],
        tables_new,
        table_mean,
        table_square,
        vectors_new,
        vector_mean,
        vector_square,
        talking_new,
        mixing_mean,
        mixing_square,
        renewed[0].astype(BF),
        renewed[1].astype(BF),
        renewed[2].astype(BF),
        renewed[3].astype(BF),
        statistics,
        grad_norm,
        norms,
    )


def solution(mesh):
    return jax.shard_map(
        shards,
        mesh=mesh,
        in_specs=(
            P(("dp", "mp"), None, None),
            P("dp", None),
            P("dp"),
            P(("dp", "mp")),
            P(("dp", "mp")),
            P(None, None, None, "mp"),
            P(None, None, None, "mp"),
            P(None, None, None, "mp"),
            P(None, "mp", None),
            P(None, "mp", None),
            P(None, "mp", None),
            P(None, None, "mp"),
            P(None, None, "mp"),
            P(None, None, "mp"),
            P(None, "mp", None),
            P(None, "mp", None),
            P(None, "mp", None),
            P(),
            P(),
            P(),
            P(),
            P(),
            P(),
            P(),
            P(),
            P(),
        ),
        out_specs=(
            P(None, None, None, "mp"),
            P(None, None, None, "mp"),
            P(None, None, None, "mp"),
            P(None, "mp", None),
            P(None, "mp", None),
            P(None, "mp", None),
            P(None, None, "mp"),
            P(None, None, "mp"),
            P(None, None, "mp"),
            P(None, "mp", None),
            P(None, "mp", None),
            P(None, "mp", None),
            P(),
            P(),
            P(),
            P(),
            P(),
            P(),
            P(),
            P(),
            P(),
            P(None, None, None, "mp"),
            P(None, "mp", None),
            P(None, None, "mp"),
            P(None, "mp", None),
            P(),
            P(),
            P(),
        ),
        check_vma=False,
    )
```

```python
import functools

import jax
import jax.numpy as jnp
from jax import lax
from jax.experimental import pallas as pl
from jax.experimental.pallas import tpu as pltpu
from jax.sharding import PartitionSpec as P

D = 384
HEADS = 8
HEAD = 48
PIX = 768
P_SIZE = 196
STEP = 10
SCALE = HEAD**-0.5
BETA_ONE = 0.9
BETA_TWO = 0.999
ADAM_EPS = 1e-08
DECAY = 0.01
RATE = 0.5
RATE_VECTOR = 0.5
CLIP = 0.02
TEMP = 0.05
MASKED = -1000000000.0
NORM_EPS = 1e-06
F32 = jnp.float32
BF = jnp.bfloat16
VMEM_LIMIT = 58 * 2**20
ANY = pl.BlockSpec(memory_space=pl.ANY)
MESH = pl.DeviceIdType.MESH
WHOLE = pl.BlockSpec(memory_space=pltpu.VMEM)


def nn(left, right):
    return lax.dot_general(left, right, (((1,), (0,)), ((), ())), preferred_element_type=F32)


def nt(left, right):
    return lax.dot_general(left, right, (((1,), (1,)), ((), ())), preferred_element_type=F32)


def tn(left, right):
    return lax.dot_general(left, right, (((0,), (0,)), ((), ())), preferred_element_type=F32)


def colsum(values):
    return jnp.sum(values, 0, keepdims=True)


def normalize(inputs):
    center = inputs - jnp.mean(inputs, -1, keepdims=True)
    spread = jnp.mean(center * center, -1, keepdims=True)
    inverse = lax.rsqrt(spread + NORM_EPS)
    return center * inverse, inverse


def normalize_back(unit, inverse, gain, incoming):
    scaled = incoming * gain
    return inverse * (
        scaled
        - jnp.mean(scaled, -1, keepdims=True)
        - unit * jnp.mean(scaled * unit, -1, keepdims=True)
    )


def gelu_parts(inner):
    size = jnp.abs(inner)
    t = 1.0 / (1.0 + (0.3275911 * 0.5**0.5) * size)
    bell = jnp.exp(-0.5 * inner * inner)
    poly = t * (
        0.5 * 0.254829592
        + t
        * (
            0.5 * -0.284496736
            + t * (0.5 * 1.421413741 + t * (0.5 * -1.453152027 + t * (0.5 * 1.061405429)))
        )
    )
    tail = poly * bell
    cumulative = jnp.where(inner >= 0, 1.0 - tail, tail)
    return inner * cumulative, cumulative + inner * bell * 0.3989422804014327


def head_mask():
    row = lax.broadcasted_iota(jnp.int32, (HEADS, D), 0)
    column = lax.broadcasted_iota(jnp.int32, (HEADS, D), 1)
    return ((column >= row * HEAD) & (column < row * HEAD + HEAD)).astype(F32)


def stat_lanes(parts, weight, first):
    lane = lax.broadcasted_iota(jnp.int32, (1, 128), 1)
    row = jnp.zeros((1, 128), F32)
    for place, values in enumerate(parts):
        total = jnp.sum(colsum(values * values * weight), keepdims=True)
        high = total.astype(BF).astype(F32)
        row = jnp.where(lane == first + 2 * place, high, row)
        row = jnp.where(lane == first + 2 * place + 1, total - high, row)
    return row


def part(ref, first, rows):
    shards_count = ref.shape[0]
    return ref[:, first : first + rows, :].reshape(shards_count * rows, ref.shape[2])


def pad_rows(rows, n_dp):
    return -(-rows // (16 * n_dp)) * 16 * n_dp


class Place:
    def __init__(self, n_dp, n_mp):
        self.n_dp, self.n_mp, self.n_y = n_dp, n_mp, n_mp // 2
        self.dp = lax.axis_index("dp")
        self.mp = lax.axis_index("mp")
        self.y = lax.div(self.mp, 2)
        self.core = lax.rem(self.mp, 2)
        self.sibling = (self.dp, self.y * 2 + 1 - self.core)

    def along_y(self, step):
        return lax.rem(self.y + step, self.n_y)

    def along_dp(self, step):
        return lax.rem(self.dp + step, self.n_dp)

    def greet(self):
        barrier = pltpu.get_barrier_semaphore()
        partners = [self.sibling]
        partners += [(self.dp, self.along_y(step) * 2 + self.core) for step in range(1, self.n_y)]
        partners += [(self.along_dp(step), self.mp) for step in range(1, self.n_dp)]
        for partner in partners:
            pl.semaphore_signal(barrier, inc=1, device_id=partner, device_id_type=MESH)
        return lambda: pl.semaphore_wait(barrier, len(partners))


class ShardSum:
    def __init__(self, place, rows, near, far, half, last, near_sem, far_sem, last_sem):
        self.place, self.rows, self.near, self.far = place, rows, near, far
        self.half, self.last = half, last
        self.near_sem, self.far_sem, self.last_sem = near_sem, far_sem, last_sem
        self.chunk = half.shape[0] // place.n_dp

    def near_copy(self, step):
        p = self.place
        y = p.along_y(step)
        return remote(
            self.rows.at[y * 2 + 1 - p.core], self.near.at[y],
            self.near_sem.at[0, step], self.near_sem.at[1, step], p.sibling,
        )

    def far_copy(self, step):
        p = self.place
        y = p.along_y(step)
        return remote(
            self.near.at[y], self.far.at[step - 1],
            self.far_sem.at[0, step], self.far_sem.at[1, step], (p.dp, y * 2 + p.core),
        )

    def last_copy(self, step):
        p = self.place
        to = p.along_dp(step)
        return remote(
            self.half.at[pl.ds(pl.multiple_of(to * self.chunk, self.chunk), self.chunk)],
            self.last.at[step - 1],
            self.last_sem.at[0, step], self.last_sem.at[1, step], (to, p.mp),
        )

    def start(self):
        for step in range(1, self.place.n_y + 1):
            self.near_copy(step).start()

    def near_to_far(self):
        p = self.place
        for step in range(1, p.n_y + 1):
            y = p.along_y(step)
            self.near_copy(step).wait_recv()
            self.near[pl.ds(y, 1)] = (
                self.rows[pl.ds(y * 2 + p.core, 1)].astype(F32) + self.near[pl.ds(y, 1)].astype(F32)
            ).astype(BF)
            if step < p.n_y:
                self.far_copy(step).start()

    def far_to_last(self):
        p = self.place
        total_rows = self.near[pl.ds(p.y, 1)][0].astype(F32)
        for step in range(1, p.n_y):
            self.far_copy(step).wait_recv()
            total_rows += self.far[step - 1].astype(F32)
        self.half[...] = total_rows.astype(BF)
        for step in range(1, p.n_dp):
            self.last_copy(step).start()

    def finish(self):
        p = self.place
        at = pl.ds(pl.multiple_of(p.dp * self.chunk, self.chunk), self.chunk)
        total_rows = self.half[at, :].astype(F32)
        for step in range(1, p.n_dp):
            self.last_copy(step).wait_recv()
            total_rows += self.last[step - 1].astype(F32)
        return total_rows.astype(BF)

    def wait_sends(self):
        p = self.place
        for step in range(1, p.n_y + 1):
            self.near_copy(step).wait_send()
            if step < p.n_y:
                self.far_copy(step).wait_send()
        for step in range(1, p.n_dp):
            self.last_copy(step).wait_send()


def sum_scratch(n_dp, n_mp, rows):
    n_y = n_mp // 2
    dma = pltpu.SemaphoreType.DMA
    return [
        pltpu.VMEM((n_y, rows, D), BF), pltpu.VMEM((max(n_y - 1, 1), rows, D), BF),
        pltpu.VMEM((rows, D), BF), pltpu.VMEM((n_dp - 1, rows // n_dp, D), BF),
        dma((2, n_y + 1)), dma((2, n_y + 1)), dma((2, n_dp)),
    ]


def remote(src, dst, send_sem, recv_sem, device):
    return pltpu.make_async_remote_copy(
        src_ref=src, dst_ref=dst, send_sem=send_sem, recv_sem=recv_sem,
        device_id=device, device_id_type=MESH,
    )


def self_attend_kernel(
    embed, cols, vec, wattn, t1row, t2col,
    q_out, k_out, v_out, prob_out, ho_out, raw_out, mid_out, stat_out,
):
    shard = wattn.shape[1] // 4
    x = embed[0]
    unit, _ = normalize(x)
    normed = (unit * vec[0:1, :] + vec[1:2, :]).astype(BF)
    wv = part(wattn, 2 * shard, shard)
    q = nt(normed, part(wattn, 0, shard)).astype(BF)
    k = nt(normed, part(wattn, shard, shard)).astype(BF)
    q_out[0] = q
    k_out[0] = k
    v_out[0] = nt(normed, wv).astype(BF)
    v_flip = nt(wv, normed).astype(BF).astype(F32)
    bias = cols[0][:, 0:1]
    q_wide = q.astype(F32)
    heads_out = jnp.zeros((D, x.shape[0]), F32)
    for g in range(HEADS):
        mixed = nt(k, (q_wide * t1row[g : g + 1, :]).astype(BF)) + bias
        grown = jnp.exp(mixed - jnp.max(mixed, 0, keepdims=True))
        prob = (grown * (1.0 / jnp.sum(grown, 0, keepdims=True))).astype(BF)
        prob_out[0, g] = prob
        heads_out += nn((v_flip * t2col[:, g : g + 1]).astype(BF), prob)
    heads_out = heads_out.astype(BF)
    ho_out[0] = heads_out
    raw = tn(heads_out, part(wattn, 3 * shard, shard))
    raw_out[0] = raw.astype(BF)
    branch = vec[3:4, :] * (raw + vec[2:3, :])
    middle = x + branch
    mid_out[0] = middle
    stat_out[0] = stat_lanes((branch, middle), cols[0][:, 1:2], 8)


def feed_kernel(
    mid, cols, bias_row, base, stat, vec, wmlp, wcls,
    patch_out, act_out, slope_out, raw_out, cprob_out, cprob0_out, z_out, card_out, aux_out,
):
    hidden = wmlp.shape[1] // 2
    shard = wcls.shape[1] // 4
    mask = head_mask()

    @pl.when(pl.program_id(0) == 0)
    def _():
        unit, _ = normalize(jnp.broadcast_to(vec[17:18, :], (HEADS, D)))
        token = (unit * vec[8:9, :] + vec[9:10, :]).astype(BF)
        query = nt(token, part(wcls, 0, shard)).astype(BF).astype(F32)
        keys = nn((query * mask).astype(BF), part(wcls, shard, shard)) * SCALE
        aux_out[0:8, :] = keys
        aux_out[8:16, :] = token.astype(F32)
        aux_out[16:24, :] = query

    middle = mid[0]
    unit, _ = normalize(middle)
    normed = (unit * vec[4:5, :] + vec[5:6, :]).astype(BF)
    inner = nt(normed, part(wmlp, 0, hidden))
    active, slope = gelu_parts(inner)
    active = active.astype(BF)
    act_out[0] = active
    slope_out[0] = slope.astype(BF)
    raw = nn(active, part(wmlp, hidden, hidden))
    raw_out[0] = raw.astype(BF)
    branch = vec[7:8, :] * (raw + vec[6:7, :])
    patches = middle + branch
    patch_out[0] = patches
    first = 4 * pl.program_id(0)
    card_out[pl.ds(first + 3, 1), :] = (
        base[0] + stat[0] + stat_lanes((branch, patches), cols[0][:, 1:2], 12)
    )
    unit, _ = normalize(patches)
    normed = (unit * vec[8:9, :] + vec[9:10, :]).astype(BF)
    keys = aux_out[0:8, :]
    token = aux_out[8:16, :]
    scores = nt(keys.astype(BF), normed) + bias_row[0]
    score0 = jnp.sum(keys * token, -1, keepdims=True)
    top = jnp.maximum(jnp.max(scores, -1, keepdims=True), score0)
    grown = jnp.exp(scores - top)
    grown0 = jnp.exp(score0 - top)
    scale = 1.0 / (jnp.sum(grown, -1, keepdims=True) + grown0)
    cprob = grown * scale
    cprob0 = grown0 * scale
    cprob_out[0] = cprob
    cprob0_out[0] = jnp.broadcast_to(cprob0, (HEADS, 128))
    z = (nn(cprob.astype(BF), normed) + cprob0 * token).astype(BF)
    z_out[0] = z
    cheads = colsum(nt(z, part(wcls, 2 * shard, shard)) * mask)
    for piece in range(3):
        card_out[pl.ds(first + piece, 1), :] = cheads[:, 128 * piece : 128 * piece + 128]


def token_kernel(
    group, cards, vec, wcls, wmlp, head,
    dch_out, gout_out, gup_out, gdown_out, ghead_out, rows_out, stat_out, dch_all,
):
    hidden = wmlp.shape[1] // 2
    shard = wcls.shape[1] // 4
    images = cards.shape[0] // 4
    cheads = jnp.concatenate(
        [cards[pl.ds(piece, images, stride=4), :] for piece in range(3)], 1
    ).astype(BF)
    card = cards[pl.ds(3, images, stride=4), :]
    labels = (card[:, 0:1] * 32.0 + card[:, 1:2]).astype(jnp.int32)
    pairs = (card[:, 2:3] * 32.0 + card[:, 3:4]).astype(jnp.int32)
    column = lax.broadcasted_iota(jnp.int32, (images, images), 1)
    row = lax.broadcasted_iota(jnp.int32, (images, images), 0)
    slot = lax.rem(lax.broadcasted_iota(jnp.int32, (images, 1), 0), group).astype(F32)
    okay = (slot >= group - card[:, 4:5]).astype(F32)
    okay_row = colsum(jnp.where(row == column, okay, 0.0))
    wo = part(wcls, 3 * shard, shard)
    wup = part(wmlp, 0, hidden)
    wdown = part(wmlp, hidden, hidden)
    count = jnp.sum(okay, keepdims=True)
    raw = nn(cheads, wo) + vec[10:11, :]
    branch = vec[11:12, :] * raw
    middle = vec[17:18, :] + branch
    unit2, inverse2 = normalize(middle)
    normed = (unit2 * vec[12:13, :] + vec[13:14, :]).astype(BF)
    inner = nt(normed, wup)
    active, slope = gelu_parts(inner)
    active = active.astype(BF)
    down = nn(active, wdown) + vec[14:15, :]
    mlp_branch = vec[15:16, :] * down
    token = middle + mlp_branch
    unit3, inverse3 = normalize(token)
    feature = unit3 * vec[18:19, :] + vec[19:20, :]
    feature_low = feature.astype(BF)
    logits = nt(feature_low, head[...])
    top = jnp.max(logits, -1, keepdims=True)
    grown = jnp.exp(logits - top)
    total = jnp.sum(grown, -1, keepdims=True)
    hot = lax.broadcasted_iota(jnp.int32, logits.shape, 1) == labels
    cross = jnp.log(total) + top - jnp.sum(jnp.where(hot, logits, 0.0), -1, keepdims=True)
    share = okay / count
    dlogits = (share * (grown / total - hot.astype(F32))).astype(BF)
    classes = head.shape[0]
    ghead = tn(dlogits, feature_low)
    ghead_out[0:8, :] = jnp.zeros((8, D), F32)
    ghead_out[classes:, :] = jnp.zeros((8, D), F32)
    ghead_out[4 : classes + 4, :] = ghead
    replicated_sq = colsum(ghead * ghead)
    dfeature = nn(dlogits, head[...])

    length = lax.rsqrt(jnp.sum(feature * feature, -1, keepdims=True) + NORM_EPS)
    embed = (feature * length).astype(BF)
    sims = nt(embed, embed) / TEMP
    sims = jnp.where((okay_row > 0) & (row != column), sims, MASKED)
    top = jnp.max(sims, -1, keepdims=True)
    grown = jnp.exp(sims - top)
    total = jnp.sum(grown, -1, keepdims=True)
    hot = column == pairs
    contrast = jnp.log(total) + top - jnp.sum(jnp.where(hot, sims, 0.0), -1, keepdims=True)
    dsims = share * (grown / total - hot.astype(F32))
    high = dsims.astype(BF)
    low = (dsims - high.astype(F32)).astype(BF)
    dembed = (nn(high, embed) + nn(low, embed) + tn(high, embed) + tn(low, embed)) / TEMP
    dfeature += length * dembed - feature * (
        length * length * length * jnp.sum(dembed * feature, -1, keepdims=True)
    )

    dtoken = normalize_back(unit3, inverse3, vec[18:19, :], dfeature)
    rows_out[0:1, :] = jnp.zeros((1, D), F32)
    rows_out[1:2, :] = jnp.zeros((1, D), F32)
    rows_out[7:8, :] = colsum(dtoken * down)
    rows_out[6:7, :] = vec[15:16, :] * colsum(dtoken)
    ddown = (dtoken * vec[15:16, :]).astype(BF)
    gdown = tn(active, ddown)
    gdown_out[...] = gdown
    replicated_sq += colsum(gdown * gdown)
    dinner = (nt(ddown, wdown) * slope).astype(BF)
    gup = tn(dinner, normed)
    gup_out[...] = gup
    replicated_sq += colsum(gup * gup)
    dnormed = nn(dinner, wup)
    rows_out[4:5, :] = colsum(dnormed * unit2)
    rows_out[5:6, :] = colsum(dnormed)
    dmiddle = dtoken + normalize_back(unit2, inverse2, vec[12:13, :], dnormed)
    rows_out[3:4, :] = colsum(dmiddle * raw)
    rows_out[2:3, :] = vec[11:12, :] * colsum(dmiddle)
    rows_out[8:9, :] = colsum(dmiddle)
    rows_out[9:10, :] = colsum(dfeature * unit3)
    rows_out[10:11, :] = colsum(dfeature)
    dbranch = (dmiddle * vec[11:12, :]).astype(BF)
    gout = tn(cheads, dbranch)
    gout_out[...] = gout
    replicated_sq += colsum(gout * gout)
    dch_all[...] = nt(dbranch, wo)
    local = dch_out.shape[0]
    place = lax.axis_index("dp") * lax.axis_size("mp") + lax.axis_index("mp")
    if local % 8 == 0:
        dch_out[...] = dch_all[pl.ds(pl.multiple_of(place * local, local), local), :]
    else:
        share_of = 8 // local
        start = pl.multiple_of(lax.div(place, share_of) * 8, 8)
        window = dch_all[pl.ds(start, 8), :]
        pick = lax.rem(place, share_of)
        dch_out[...] = sum(
            jnp.where(pick == i, window[i * local : (i + 1) * local, :], 0.0)
            for i in range(share_of)
        )
    lane = lax.broadcasted_iota(jnp.int32, (1, 128), 1)
    self_sums = colsum(card)
    count_tokens = self_sums[:, 5:6]

    def squares(values):
        return jnp.sum(colsum(values * values * okay), keepdims=True)

    entries = [jnp.sum(okay * cross, keepdims=True), jnp.sum(okay * contrast, keepdims=True)]
    entries += [count, count_tokens]
    entries += [
        jnp.sqrt((self_sums[:, i : i + 1] + self_sums[:, i + 1 : i + 2]) / D / count_tokens)
        for i in (8, 10, 12, 14)
    ]
    entries += [
        jnp.sqrt(squares(item) / D / count) for item in (branch, middle, mlp_branch, token)
    ]
    line = jnp.zeros((1, 128), F32)
    for i, entry in enumerate(entries):
        line = jnp.where(lane == i, entry, line)
    stat_out[0:1, :] = line
    stat_out[1:8, :] = jnp.broadcast_to(
        replicated_sq[:, 0:128] + replicated_sq[:, 128:256] + replicated_sq[:, 256:384], (7, 128)
    )


def feed_back_kernel(
    dch, patch, mid, raw, act, slope, cprob, cprob0, z, aux, vec, wcls, wmlp,
    dmid_out, gfeed_out, rows_out, gmlp_out, gv_out,
):
    hidden = wmlp.shape[1] // 2
    shard = wcls.shape[1] // 4
    count = wmlp.shape[0]
    mask = head_mask()

    @pl.when(pl.program_id(0) == 0)
    def _():
        gmlp_out[...] = jnp.zeros_like(gmlp_out)
        gv_out[...] = jnp.zeros_like(gv_out)
        rows_out[...] = jnp.zeros_like(rows_out)

    keys = aux[0:8, :]
    token = aux[8:16, :]
    unit, inverse = normalize(patch[0])
    normed = (unit * vec[8:9, :] + vec[9:10, :]).astype(BF)
    spread = (mask * dch[pl.ds(pl.program_id(0), 1), :]).astype(BF)
    dz = nn(spread, part(wcls, 2 * shard, shard))
    dz_low = dz.astype(BF)
    probs = cprob[0]
    prob0 = cprob0[0][:, 0:1]
    dprobs = nt(dz_low, normed)
    dprob0 = jnp.sum(dz * token, -1, keepdims=True)
    inside = jnp.sum(dprobs * probs, -1, keepdims=True) + dprob0 * prob0
    dscores = (probs * (dprobs - inside)).astype(BF)
    dscore0 = prob0 * (dprob0 - inside)
    dnormed = tn(
        jnp.concatenate([probs.astype(BF), dscores], 0),
        jnp.concatenate([dz_low, keys.astype(BF)], 0),
    )
    rows_out[8:16, :] += nn(dscores, normed) + dscore0 * token
    rows_out[6:7, :] += colsum(prob0 * dz + dscore0 * keys)
    gv_out[...] += tn(spread, z[0])
    rows_out[4:5, :] += colsum(dnormed * unit)
    rows_out[5:6, :] += colsum(dnormed)
    incoming = normalize_back(unit, inverse, vec[8:9, :], dnormed)

    unit, inverse = normalize(mid[0])
    normed = (unit * vec[4:5, :] + vec[5:6, :]).astype(BF)
    rows_out[3:4, :] += colsum(incoming * (raw[0].astype(F32) + vec[6:7, :]))
    rows_out[2:3, :] += vec[7:8, :] * colsum(incoming)
    ddown = (incoming * vec[7:8, :]).astype(BF)
    gmlp_out[:, hidden:, :] += tn(act[0], ddown).reshape(count, hidden, D)
    dinner = (nt(ddown, part(wmlp, hidden, hidden)) * slope[0].astype(F32)).astype(BF)
    gmlp_out[:, :hidden, :] += tn(dinner, normed).reshape(count, hidden, D)
    dnormed = nn(dinner, part(wmlp, 0, hidden))
    rows_out[0:1, :] += colsum(dnormed * unit)
    rows_out[1:2, :] += colsum(dnormed)
    dmid_out[0] = incoming + normalize_back(unit, inverse, vec[4:5, :], dnormed)

    @pl.when(pl.program_id(0) == pl.num_programs(0) - 1)
    def _():
        used = 2 * hidden + shard
        gfeed_out[:, : 2 * hidden, :] = gmlp_out[...].astype(BF)
        gfeed_out[:, 2 * hidden : used, :] = gv_out[...].astype(BF).reshape(count, shard, D)
        if used < gfeed_out.shape[1]:
            gfeed_out[:, used:, :] = jnp.zeros((count, gfeed_out.shape[1] - used, D), BF)


def self_back_kernel(
    n_dp, n_mp, dmid, pixels, embed, q, k, v, prob, ho, raw, vec, wattn, t1row, t1col, t2row, gfeed,
    gattn_out, gpix_out, gpos_out, rows_out, chunk_out, dx_all, dx_rows, *sum_buffers,
):
    shard = wattn.shape[1] // 4
    count = wattn.shape[0]
    images = dx_all.shape[0]
    feed = ShardSum(Place(n_dp, n_mp), gfeed, *sum_buffers)

    @pl.when(pl.program_id(0) == 0)
    def _():
        gattn_out[...] = jnp.zeros_like(gattn_out)
        gpos_out[...] = jnp.zeros_like(gpos_out)
        rows_out[...] = jnp.zeros_like(rows_out)
        feed.place.greet()()
        feed.start()

    @pl.when(pl.program_id(0) == 1)
    def _():
        feed.near_to_far()

    @pl.when(pl.program_id(0) == images // 2)
    def _():
        feed.far_to_last()

    wq = part(wattn, 0, shard)
    wk = part(wattn, shard, shard)
    wv = part(wattn, 2 * shard, shard)
    wo = part(wattn, 3 * shard, shard)
    incoming = dmid[0]
    rows_out[3:4, :] += colsum(incoming * (raw[0].astype(F32) + vec[2:3, :]))
    rows_out[2:3, :] += vec[3:4, :] * colsum(incoming)
    dbranch = (incoming * vec[3:4, :]).astype(BF)
    gattn_out[:, 3 * shard :, :] += nn(ho[0], dbranch).reshape(count, shard, D)
    dheads = nt(dbranch, wo).astype(BF)

    unit, inverse = normalize(embed[0])
    normed = (unit * vec[0:1, :] + vec[1:2, :]).astype(BF)
    q_low = q[0]
    k_wide = k[0].astype(F32)
    v_wide = v[0].astype(F32)
    k_flip = nt(wk, normed).astype(BF).astype(F32)
    dq = jnp.zeros((D, normed.shape[0]), F32)
    dk = jnp.zeros(normed.shape, F32)
    dv = jnp.zeros(normed.shape, F32)
    for g in range(HEADS):
        one = t1row[g : g + 1, :]
        two = t2row[g : g + 1, :]
        chance = prob[0, g]
        chance_wide = chance.astype(F32)
        dprob = nt((v_wide * two).astype(BF), dheads)
        dmixed = (chance_wide * (dprob - colsum(dprob * chance_wide))).astype(BF)
        dpost = nn(chance, dheads)
        dv += two * dpost
        rows_out[16 + g : 17 + g, :] += colsum(v_wide * dpost)
        dpre = nn(dmixed, q_low)
        dk += one * dpre
        rows_out[8 + g : 9 + g, :] += colsum(k_wide * dpre)
        dq += nn((k_flip * t1col[:, g : g + 1]).astype(BF), dmixed)
    dq = dq.astype(BF)
    dk = dk.astype(BF)
    dv = dv.astype(BF)
    gattn_out[:, :shard, :] += nn(dq, normed).reshape(count, shard, D)
    gattn_out[:, shard : 2 * shard, :] += tn(dk, normed).reshape(count, shard, D)
    gattn_out[:, 2 * shard : 3 * shard, :] += tn(dv, normed).reshape(count, shard, D)
    dnormed = tn(dq, wq) + nn(dk, wk) + nn(dv, wv)
    rows_out[0:1, :] += colsum(dnormed * unit)
    rows_out[1:2, :] += colsum(dnormed)
    dx = incoming + normalize_back(unit, inverse, vec[0:1, :], dnormed)
    gpos_out[...] += dx
    dx_all[pl.program_id(0)] = dx

    @pl.when(pl.program_id(0) == pl.num_programs(0) - 1)
    def _():
        for n in range(images):
            dx_rows[:, n, :] = dx_all[n]
        gpix_out[...] = tn(pixels[...], dx_rows[...].reshape(pixels.shape[0], D).astype(BF))
        chunk_out[...] = feed.finish()
        feed.wait_sends()


def per_image(*tail):
    return pl.BlockSpec((1, *tail), lambda n: (n, *(0 for _ in tail)))


def constant(*shape):
    return pl.BlockSpec(shape, lambda n: tuple(0 for _ in shape))


def shaped(*shape, dtype=F32):
    return jax.ShapeDtypeStruct(shape, dtype)


def params():
    return pltpu.CompilerParams(vmem_limit_bytes=VMEM_LIMIT, dimension_semantics=("arbitrary",))


def run_self_attend(embed, cols, vec, wattn, t1row, t2col):
    count = embed.shape[0]
    return pl.pallas_call(
        self_attend_kernel,
        grid=(count,),
        in_specs=[
            per_image(P_SIZE, D), per_image(P_SIZE, 2), constant(*vec.shape),
            constant(*wattn.shape), constant(HEADS, D), constant(D, HEADS),
        ],
        out_specs=[
            per_image(P_SIZE, D), per_image(P_SIZE, D), per_image(P_SIZE, D),
            per_image(HEADS, P_SIZE, P_SIZE), per_image(D, P_SIZE), per_image(P_SIZE, D),
            per_image(P_SIZE, D), per_image(1, 128),
        ],
        out_shape=[
            shaped(count, P_SIZE, D, dtype=BF),
            shaped(count, P_SIZE, D, dtype=BF), shaped(count, P_SIZE, D, dtype=BF),
            shaped(count, HEADS, P_SIZE, P_SIZE, dtype=BF), shaped(count, D, P_SIZE, dtype=BF),
            shaped(count, P_SIZE, D, dtype=BF), shaped(count, P_SIZE, D), shaped(count, 1, 128),
        ],
        compiler_params=params(),
        name="self_attend",
    )(embed, cols, vec, wattn, t1row, t2col)


def run_feed(mid, cols, bias_row, base, stat, vec, wmlp, wcls):
    count = mid.shape[0]
    wide = 2 * wmlp.shape[0] * wmlp.shape[1] // 4
    return pl.pallas_call(
        feed_kernel,
        grid=(count,),
        in_specs=[
            per_image(P_SIZE, D), per_image(P_SIZE, 2), per_image(1, P_SIZE), per_image(1, 128),
            per_image(1, 128), constant(*vec.shape), constant(*wmlp.shape), constant(*wcls.shape),
        ],
        out_specs=[
            per_image(P_SIZE, D), per_image(P_SIZE, wide), per_image(P_SIZE, wide),
            per_image(P_SIZE, D), per_image(HEADS, P_SIZE), per_image(HEADS, 128),
            per_image(HEADS, D), constant(4 * count, 128), constant(24, D),
        ],
        out_shape=[
            shaped(count, P_SIZE, D), shaped(count, P_SIZE, wide, dtype=BF),
            shaped(count, P_SIZE, wide, dtype=BF), shaped(count, P_SIZE, D, dtype=BF),
            shaped(count, HEADS, P_SIZE), shaped(count, HEADS, 128),
            shaped(count, HEADS, D, dtype=BF), shaped(4 * count, 128), shaped(24, D),
        ],
        compiler_params=params(),
        name="feed",
    )(mid, cols, bias_row, base, stat, vec, wmlp, wcls)


def run_token(group, local, cards, vec, wcls, wmlp, head):
    images = cards.shape[0] // 4
    wide = wmlp.shape[0] * wmlp.shape[1] // 2
    return pl.pallas_call(
        functools.partial(token_kernel, group),
        in_specs=[WHOLE] * 5,
        out_specs=[WHOLE] * 7,
        out_shape=[
            shaped(local, D), shaped(D, D), shaped(wide, D), shaped(wide, D),
            shaped(head.shape[0] + 8, D), shaped(16, D), shaped(8, 128),
        ],
        scratch_shapes=[pltpu.VMEM((images, D), F32)],
        compiler_params=pltpu.CompilerParams(vmem_limit_bytes=VMEM_LIMIT),
        name="token_net",
    )(cards, vec, wcls, wmlp, head)


def run_feed_back(n_dp, dch, patch, mid, raw, act, slope, cprob, cprob0, z, aux, vec, wcls, wmlp):
    count = mid.shape[0]
    wide = act.shape[2]
    feed = (wmlp.shape[0], pad_rows(wmlp.shape[1] + wcls.shape[1] // 4, n_dp), D)
    return pl.pallas_call(
        feed_back_kernel,
        grid=(count,),
        in_specs=[
            constant(count, D), per_image(P_SIZE, D), per_image(P_SIZE, D), per_image(P_SIZE, D),
            per_image(P_SIZE, wide), per_image(P_SIZE, wide), per_image(HEADS, P_SIZE),
            per_image(HEADS, 128), per_image(HEADS, D), constant(24, D), constant(*vec.shape),
            constant(*wcls.shape), constant(*wmlp.shape),
        ],
        out_specs=[
            per_image(P_SIZE, D), constant(*feed), constant(16, D),
        ],
        out_shape=[shaped(count, P_SIZE, D), shaped(*feed, dtype=BF), shaped(16, D)],
        scratch_shapes=[pltpu.VMEM(wmlp.shape, F32), pltpu.VMEM((D, D), F32)],
        compiler_params=params(),
        name="feed_back",
    )(dch, patch, mid, raw, act, slope, cprob, cprob0, z, aux, vec, wcls, wmlp)


def run_self_back(
    n_dp, n_mp, dmid, pixels, embed, q, k, v, prob, ho, raw, vec, wattn, t1row, t1col, t2row, gfeed
):
    count = dmid.shape[0]
    rows = gfeed.shape[1]
    return pl.pallas_call(
        functools.partial(self_back_kernel, n_dp, n_mp),
        grid=(count,),
        in_specs=[
            per_image(P_SIZE, D), constant(*pixels.shape), per_image(P_SIZE, D),
            per_image(P_SIZE, D), per_image(P_SIZE, D), per_image(P_SIZE, D),
            per_image(HEADS, P_SIZE, P_SIZE), per_image(D, P_SIZE), per_image(P_SIZE, D),
            constant(*vec.shape), constant(*wattn.shape), constant(HEADS, D), constant(D, HEADS),
            constant(HEADS, D), constant(*gfeed.shape),
        ],
        out_specs=[
            constant(*wattn.shape), constant(PIX, D), constant(P_SIZE, D), constant(24, D),
            constant(rows // n_dp, D),
        ],
        out_shape=[
            shaped(*wattn.shape), shaped(PIX, D), shaped(P_SIZE, D), shaped(24, D),
            shaped(rows // n_dp, D, dtype=BF),
        ],
        scratch_shapes=[pltpu.VMEM((count, P_SIZE, D), F32), pltpu.VMEM((P_SIZE, count, D), F32)]
        + sum_scratch(n_dp, n_mp, rows),
        compiler_params=pltpu.CompilerParams(
            vmem_limit_bytes=VMEM_LIMIT, dimension_semantics=("arbitrary",), collective_id=5,
            has_side_effects=True,
        ),
        name="self_back",
    )(dmid, pixels, embed, q, k, v, prob, ho, raw, vec, wattn, t1row, t1col, t2row, gfeed)


def peer_at(index, n_mp):
    return (lax.div(index, n_mp), lax.rem(index, n_mp))


def greet_all(me, n, n_mp):
    barrier = pltpu.get_barrier_semaphore()

    @pl.loop(1, n)
    def _(step):
        pl.semaphore_signal(
            barrier, inc=1, device_id=peer_at(lax.rem(me + step, n), n_mp), device_id_type=MESH
        )

    pl.semaphore_wait(barrier, n - 1)


def spread_to_all(me, n, n_mp, slots, rows, send_sem, recv_sem):
    def slot(index):
        return slots.at[pl.ds(pl.multiple_of(index * rows, rows), rows)]

    @pl.loop(1, n)
    def _(step):
        remote(
            slot(me), slot(me), send_sem.at[step], recv_sem.at[step],
            peer_at(lax.rem(me + step, n), n_mp),
        ).start()

    def finish():
        @pl.loop(1, n)
        def _(step):
            source = lax.rem(me + n - step, n)
            copy = remote(
                slot(me), slot(source), send_sem.at[step], recv_sem.at[step],
                peer_at(source, n_mp),
            )
            copy.wait_send()
            copy.wait_recv()

    return finish


def card_kernel(n_dp, n_mp, card, out, slots, send_sem, recv_sem):
    n = n_dp * n_mp
    me = lax.axis_index("dp") * n_mp + lax.axis_index("mp")
    rows = card.shape[0]
    greet_all(me, n, n_mp)
    slots[pl.ds(pl.multiple_of(me * rows, rows), rows), :] = card[...].astype(BF)
    spread_to_all(me, n, n_mp, slots, rows, send_sem, recv_sem)()
    out[...] = slots[...].astype(F32)


def run_cards(n_dp, n_mp, card):
    n = n_dp * n_mp
    return pl.pallas_call(
        functools.partial(card_kernel, n_dp, n_mp),
        in_specs=[WHOLE],
        out_specs=WHOLE,
        out_shape=shaped(n * card.shape[0], 128),
        scratch_shapes=[
            pltpu.VMEM((n * card.shape[0], 128), BF),
            pltpu.SemaphoreType.DMA((n,)),
            pltpu.SemaphoreType.DMA((n,)),
        ],
        compiler_params=pltpu.CompilerParams(
            vmem_limit_bytes=VMEM_LIMIT, collective_id=1, has_side_effects=True
        ),
        name="cards",
    )(card)


def start_kernel(
    n_dp, n_mp, attn_in, attn_out, pixels, tables, vec,
    out, embed_out,
    shard, wide_in, wide_out, patch_rows, pos_rows, by_patch, near_send, near_recv, far_send, far_recv, load_sem,
):
    dp = lax.axis_index("dp")
    mp = lax.axis_index("mp")
    n_y = n_mp // 2
    y = lax.div(mp, 2)
    core = lax.rem(mp, 2)
    sibling = (dp, y * 2 + 1 - core)
    load_patch = pltpu.make_async_copy(tables.at[pl.ds(0, PIX)], patch_rows, load_sem.at[0])
    load_pos = pltpu.make_async_copy(tables.at[pl.ds(PIX, 200)], pos_rows, load_sem.at[1])
    load_in = pltpu.make_async_copy(attn_in.at[0], wide_in, load_sem.at[2])
    load_out = pltpu.make_async_copy(attn_out.at[0], wide_out, load_sem.at[3])
    load_in.start()
    load_out.start()
    load_patch.start()
    load_pos.start()
    barrier = pltpu.get_barrier_semaphore()
    pl.semaphore_signal(barrier, inc=1, device_id=sibling, device_id_type=MESH)
    for step in range(1, n_y):
        pl.semaphore_signal(
            barrier, inc=1, device_id=(dp, lax.rem(y + step, n_y) * 2 + core), device_id_type=MESH
        )
    third = attn_in.shape[1]
    load_in.wait()
    load_out.wait()
    shard[:third, :] = wide_in[...].astype(BF)
    shard[third:, :] = wide_out[...].astype(BF)
    pl.semaphore_wait(barrier, n_y)
    far = [
        remote(
            shard, out.at[mp], far_send.at[step], far_recv.at[step],
            (dp, lax.rem(y + step, n_y) * 2 + core),
        )
        for step in range(1, n_y)
    ]
    for copy in far:
        copy.start()
    near = [remote(shard, out.at[mp], near_send.at[0], near_recv.at[0], sibling)]
    near[0].start()
    out[pl.ds(mp, 1)] = shard[...][None]

    load_patch.wait()
    wp = patch_rows[...].astype(BF)
    local = embed_out.shape[0]
    half = P_SIZE // 2
    for place in range(2):
        rows = slice(place * half * local, (place + 1) * half * local)
        by_patch[place * half : (place + 1) * half] = nn(pixels[rows, :], wp).reshape(half, local, D)

    for step in range(1, n_y):
        source = lax.rem(y + n_y - step, n_y) * 2
        slot = source + core
        remote(
            shard, out.at[slot], far_send.at[step], far_recv.at[step], (dp, slot)
        ).wait_recv()
        copy = remote(
            out.at[slot], out.at[slot], near_send.at[step], near_recv.at[step], sibling
        )
        copy.start()
        near.append(copy)
    load_pos.wait()
    offset = pos_rows[:P_SIZE, :] + vec[16:17, :]
    for n in range(local):
        embed_out[n] = by_patch[:, n, :] + offset
    for copy in far:
        copy.wait_send()
    for step in range(n_y):
        slot = lax.rem(y + n_y - step, n_y) * 2 + 1 - core
        near[step].wait_send()
        remote(
            out.at[slot], out.at[slot], near_send.at[step], near_recv.at[step], sibling
        ).wait_recv()


def run_start(n_dp, n_mp, local, attn_in, attn_out, pixels, tables, vec):
    n_y = n_mp // 2
    rows = attn_in.shape[1] + attn_out.shape[1]
    dma = pltpu.SemaphoreType.DMA
    return pl.pallas_call(
        functools.partial(start_kernel, n_dp, n_mp),
        in_specs=[ANY, ANY, WHOLE, ANY, WHOLE],
        out_specs=[WHOLE, WHOLE],
        out_shape=[shaped(n_mp, rows, D, dtype=BF), shaped(local, P_SIZE, D)],
        scratch_shapes=[
            pltpu.VMEM((rows, D), BF), pltpu.VMEM(attn_in.shape[1:], F32),
            pltpu.VMEM(attn_out.shape[1:], F32), pltpu.VMEM((PIX, D), F32),
            pltpu.VMEM((200, D), F32),
            pltpu.VMEM((P_SIZE, local, D), F32),
            dma((n_y,)), dma((n_y,)), dma((n_y,)), dma((n_y,)), dma((4,)),
        ],
        compiler_params=pltpu.CompilerParams(
            vmem_limit_bytes=VMEM_LIMIT, collective_id=2, has_side_effects=True
        ),
        name="start",
    )(attn_in, attn_out, pixels, tables, vec)


def reduce_kernel(
    n_dp, n_mp, gattn, chunk, gpix, gpos, rows2, rows3,
    block_out, shared_out, square_out,
    blocks, commons, squares, feed_sem, attn_sem, shared_sem, slab_sem, hand_sem, square_sem,
    *sum_buffers,
):
    p = Place(n_dp, n_mp)
    attn = ShardSum(p, blocks, *sum_buffers[:7])
    common = ShardSum(p, commons, *sum_buffers[7:])
    feed_rows = chunk.shape[0]
    rows_a = blocks.shape[1]
    wide = commons.shape[1]
    greeted = p.greet()

    used = gattn.shape[1]
    blocks[:, :used, :] = gattn[...].astype(BF)
    if used < rows_a:
        blocks[:, used:, :] = jnp.zeros((n_mp, rows_a - used, D), BF)
    commons[:3] = gpix[...].astype(BF).reshape(3, wide, D)
    commons[3] = jnp.concatenate(
        [
            gpos[...], jnp.zeros((12, D), F32), rows2[...], rows3[...], jnp.zeros((8, D), F32),
        ],
        0,
    ).astype(BF)
    if n_mp > 4:
        commons[4:] = jnp.zeros((n_mp - 4, wide, D), BF)

    def block_rows(index, first, rows):
        return block_out.at[pl.ds(pl.multiple_of(first + index * rows, rows), rows)]

    def shared_rows(index, rows):
        return shared_out.at[pl.ds(pl.multiple_of(index * rows, rows), rows)]

    def over_dp(view, sems):
        sends = [
            remote(view(p.dp), view(p.dp), sems.at[0, step], sems.at[1, step], (p.along_dp(step), p.mp))
            for step in range(1, n_dp)
        ]
        for copy in sends:
            copy.start()

        def arrive():
            for step in range(1, n_dp):
                source = p.along_dp(n_dp - step)
                remote(
                    view(p.dp), view(source), sems.at[0, step], sems.at[1, step], (source, p.mp)
                ).wait_recv()

        return sends, arrive

    greeted()
    attn.start()
    common.start()
    block_out[pl.ds(pl.multiple_of(rows_a + p.dp * feed_rows, 16), feed_rows), :] = chunk[...]
    sends, feed_arrive = over_dp(
        lambda index: block_out.at[
            pl.ds(pl.multiple_of(rows_a + index * feed_rows, 16), feed_rows)
        ],
        feed_sem,
    )
    attn.near_to_far()
    common.near_to_far()
    attn.far_to_last()
    common.far_to_last()
    size = attn.chunk
    block_out[pl.ds(pl.multiple_of(p.dp * size, size), size), :] = attn.finish()
    more, attn_arrive = over_dp(lambda index: block_rows(index, 0, size), attn_sem)
    sends += more
    size_s = common.chunk
    own = p.mp * n_dp + p.dp
    shared_out[pl.ds(pl.multiple_of(own * size_s, size_s), size_s), :] = common.finish()
    more, shared_arrive = over_dp(
        lambda index: shared_rows(p.mp * n_dp + index, size_s), shared_sem
    )
    sends += more
    shared_arrive()

    slab = shared_rows(p.mp, wide)
    for step in range(1, p.n_y):
        sends.append(
            remote(
                slab, slab, slab_sem.at[0, step], slab_sem.at[1, step],
                (p.dp, p.along_y(step) * 2 + p.core),
            )
        )
        sends[-1].start()
    sends.append(remote(slab, slab, hand_sem.at[0, 0], hand_sem.at[1, 0], p.sibling))
    sends[-1].start()

    feed_arrive()
    attn_arrive()
    sums = block_out[...].astype(F32)
    sums = colsum(sums * sums)
    squares[pl.ds(p.mp, 1)] = jnp.broadcast_to(
        sums[:, 0:128] + sums[:, 128:256] + sums[:, 256:384], (8, 128)
    )[None]

    for step in range(1, p.n_y):
        source = p.along_y(p.n_y - step) * 2 + p.core
        theirs = shared_rows(source, wide)
        remote(
            slab, theirs, slab_sem.at[0, step], slab_sem.at[1, step], (p.dp, source)
        ).wait_recv()
        sends.append(
            remote(theirs, theirs, hand_sem.at[0, step], hand_sem.at[1, step], p.sibling)
        )
        sends[-1].start()
    for step in range(1, p.n_y):
        sends.append(
            remote(
                squares.at[p.mp], squares.at[p.mp], square_sem.at[0, step],
                square_sem.at[1, step], (p.dp, p.along_y(step) * 2 + p.core),
            )
        )
        sends[-1].start()
    for step in range(1, p.n_y):
        source = p.along_y(p.n_y - step) * 2 + p.core
        remote(
            squares.at[p.mp], squares.at[source], square_sem.at[0, step], square_sem.at[1, step],
            (p.dp, source),
        ).wait_recv()
    mine = squares[pl.ds(p.core, 1)]
    for y in range(1, p.n_y):
        mine += squares[pl.ds(2 * y + p.core, 1)]
    squares[pl.ds(n_mp + p.core, 1)] = mine
    sends.append(
        remote(
            squares.at[n_mp + p.core], squares.at[n_mp + p.core], square_sem.at[0, 0],
            square_sem.at[1, 0], p.sibling,
        )
    )
    sends[-1].start()
    for step in range(p.n_y):
        theirs = shared_rows(p.along_y(p.n_y - step) * 2 + 1 - p.core, wide)
        remote(
            theirs, theirs, hand_sem.at[0, step], hand_sem.at[1, step], p.sibling
        ).wait_recv()
    remote(
        squares.at[n_mp + p.core], squares.at[n_mp + 1 - p.core], square_sem.at[0, 0],
        square_sem.at[1, 0], p.sibling,
    ).wait_recv()
    square_out[...] = squares[n_mp] + squares[n_mp + 1]
    for copy in sends:
        copy.wait_send()
    attn.wait_sends()
    common.wait_sends()


def run_reduce(n_dp, n_mp, gattn, chunk, gpix, gpos, rows2, rows3):
    n = n_dp * n_mp
    rows_a = pad_rows(gattn.shape[1], n_dp)
    chunk_s = -(-(PIX + 256) // (16 * n)) * 16
    wide = chunk_s * n_dp
    assert wide == 256
    dma = pltpu.SemaphoreType.DMA
    return pl.pallas_call(
        functools.partial(reduce_kernel, n_dp, n_mp),
        in_specs=[WHOLE] * 6,
        out_specs=[WHOLE] * 3,
        out_shape=[
            shaped(rows_a + chunk.shape[0] * n_dp, D, dtype=BF),
            shaped(wide * n_mp, D, dtype=BF), shaped(8, 128),
        ],
        scratch_shapes=[
            pltpu.VMEM((n_mp, rows_a, D), BF), pltpu.VMEM((n_mp, wide, D), BF),
            pltpu.VMEM((n_mp + 2, 8, 128), F32),
            dma((2, n_dp)), dma((2, n_dp)), dma((2, n_dp)),
            dma((2, n_mp)), dma((2, n_mp)), dma((2, n_mp)),
        ]
        + sum_scratch(n_dp, n_mp, rows_a)
        + sum_scratch(n_dp, n_mp, wide),
        compiler_params=pltpu.CompilerParams(
            vmem_limit_bytes=VMEM_LIMIT, collective_id=3, has_side_effects=True
        ),
        name="reduce",
    )(gattn, chunk, gpix, gpos, rows2, rows3)


def adam_parts(gradient, mean, square, factor):
    clipped = gradient * factor
    mean_new = BETA_ONE * mean + (1.0 - BETA_ONE) * clipped
    square_new = BETA_TWO * square + (1.0 - BETA_TWO) * clipped * clipped
    direction = (
        mean_new
        * (1.0 / (1.0 - BETA_ONE**STEP))
        / (jnp.sqrt(square_new * (1.0 / (1.0 - BETA_TWO**STEP))) + ADAM_EPS)
    )
    return (mean_new, square_new, direction)


def fold(values):
    squares = (values * values).reshape(values.shape[0] // 8, 8, values.shape[1]).sum(0)
    width = values.shape[1]
    if width % 128:
        return jnp.broadcast_to(jnp.sum(squares, 1, keepdims=True), (8, 128)) * (1.0 / 128)
    return sum(squares[:, i : i + 128] for i in range(0, width, 128))


def total(values):
    return jnp.sum(jnp.sum(values, 0, keepdims=True), 1, keepdims=True)


def moment_kernel(
    n_dp, block, shared, block_sq, gout1, gup1, gdown1, ghead, rows1, stat, aux, wcls,
    vec, vec_mean, vec_square, mix, mix_mean, mix_square, *rest,
):
    state = rest[:15]
    outs = rest[15:30]
    (
        vec_out, vec_mean_out, vec_square_out, mix_out, mix_mean_out, mix_square_out,
        misc_out, sums_out,
    ) = rest[30:38]
    held = rest[38:53]
    updates = rest[53:57]
    grad_q, grad_k, grad_flip, load_sem, save_sem, table_update = rest[57:]
    loads = [pltpu.make_async_copy(state[i], held[i], load_sem.at[i]) for i in range(15)]
    for copy in loads:
        copy.start()
    mp = lax.axis_index("mp")
    hs = state[3].shape[1]
    fs = state[9].shape[1]
    feed = pad_rows(4 * hs, n_dp)

    rows2 = shared[PIX + 208 : PIX + 224, :].astype(F32)
    rows3 = shared[PIX + 224 : PIX + 256, :].astype(F32)
    token = aux[8:9, :]
    wq = part(wcls, 0, hs)
    wk = part(wcls, hs, hs).astype(F32)
    query = nt(wq, aux[8:16, :].astype(BF))[:, 0:1].astype(BF).astype(F32)
    dkeys = jnp.concatenate(
        [jnp.broadcast_to(rows2[8 + h : 9 + h, :], (HEAD, D)) for h in range(HEADS)], 0
    )
    dquery = SCALE * jnp.sum(wk * dkeys, 1, keepdims=True)
    gq = dquery * token
    gk = (SCALE * query) * dkeys
    grad_q[...] = gq
    grad_k[...] = gk
    dtoken = rows2[6:7, :] + colsum(dquery * wq.astype(F32))
    unit, inverse = normalize(jnp.broadcast_to(vec[17:18, :], (8, D)))
    dcls = normalize_back(unit, inverse, vec[8:9, :], jnp.broadcast_to(dtoken, (8, D)))[0:1, :]
    dgain = rows2[4:5, :] + dtoken * unit[0:1, :]
    last = rows1[...]
    positions = shared[PIX : PIX + 208, :].astype(F32)
    grad_vec = jnp.concatenate(
        [
            rows3[0:4, :], rows2[0:4, :], dgain, rows2[5:6, :] + dtoken, last[2:8, :],
            colsum(positions), last[8:9, :] + dcls, last[9:11, :],
        ],
        0,
    )
    mask = head_mask()
    exact = functools.partial(
        lax.dot_general, dimension_numbers=(((1,), (1,)), ((), ())),
        preferred_element_type=F32, precision=lax.Precision.HIGHEST,
    )
    grad_mix = (exact(rows3[8:16, :], mask) * SCALE, exact(mask, rows3[16:24, :]))

    square = total(block_sq[0:1, :]) + total(stat[1:2, :]) + total(colsum(gq * gq + gk * gk))
    square += total(grad_vec * grad_vec)
    square += total(grad_mix[0] * grad_mix[0]) + total(grad_mix[1] * grad_mix[1])

    def square_rows(i, kept):
        rows = shared[pl.ds(pl.multiple_of(i * 16, 16), 16), :].astype(F32)
        return kept + fold(rows)

    square += total(lax.fori_loop(0, (PIX + 208) // 16, square_rows, jnp.zeros((8, 128), F32)))
    norm = jnp.sqrt(square)
    factor = CLIP / jnp.maximum(norm, CLIP)

    mean, second, direction = adam_parts(grad_vec, vec_mean[...], vec_square[...], factor)
    vec_mean_out[...] = mean
    vec_square_out[...] = second
    vec_out[...] = vec[...] - RATE_VECTOR * direction
    misc = [norm]
    weight_sums = []
    for b in range(2):
        mean, second, direction = adam_parts(grad_mix[b], mix_mean[b], mix_square[b], factor)
        mix_mean_out[b] = mean
        mix_square_out[b] = second
        update = direction + DECAY * mix[b]
        weight_sq = total(mix[b] * mix[b])
        update_sq = total(update * update)
        mix_out[b] = mix[b] - RATE * jnp.sqrt(weight_sq / (update_sq + 1e-12)) * update
        weight_sums.append(weight_sq)
        misc.append(update_sq)

    def sweep(grad, w, m, s, u, rows):
        chunk = 32 if rows % 32 == 0 else 16

        def step(i, kept):
            at = pl.ds(pl.multiple_of(i * chunk, chunk), chunk)
            weight = w[at, :]
            mean, second, direction = adam_parts(grad(i, chunk), m[at, :], s[at, :], factor)
            m[at, :] = mean
            s[at, :] = second
            update = direction + DECAY * weight
            u[at, :] = update
            return (kept[0] + fold(weight), kept[1] + fold(update))

        zero = jnp.zeros((8, 128), F32)
        return lax.fori_loop(0, rows // chunk, step, (zero, zero))

    def rows_from(ref, first):
        def read(i, chunk):
            at = pl.ds(pl.multiple_of(first + i * chunk, 16), chunk)
            return ref[at, :].astype(F32)

        return read

    saves = []

    def save(i, source):
        saves.append(pltpu.make_async_copy(source, outs[i], save_sem.at[i]))
        saves[-1].start()

    sums = []
    own_h = pl.multiple_of(mp * hs, hs)
    own_f = pl.multiple_of(mp * fs, fs)
    for kind in range(4):
        for copy in loads[3 * kind : 3 * kind + 3]:
            copy.wait()
        w, m, s = held[3 * kind : 3 * kind + 3]
        u = updates[kind]
        for b in range(2):
            views = (w.at[b], m.at[b], s.at[b], u.at[b])
            if kind == 0 and b == 0:
                sums.append(sweep(rows_from(block, 0), *views, 3 * hs))
            elif kind == 0:
                pieces = []
                for third, source in enumerate(
                    (
                        rows_from(grad_q, own_h),
                        rows_from(grad_k, own_h),
                        rows_from(block, feed + 2 * fs),
                    )
                ):
                    pieces.append(
                        sweep(
                            source, *(view.at[pl.ds(third * hs, hs)] for view in views), hs
                        )
                    )
                sums.append(
                    tuple(pieces[0][i] + pieces[1][i] + pieces[2][i] for i in range(2))
                )
            elif kind == 1:
                source = rows_from(gout1, own_h) if b else rows_from(block, 3 * hs)
                sums.append(sweep(source, *views, hs))
            elif kind == 2:
                if b:
                    grad_flip[...] = gup1[pl.ds(own_f, fs), :].T
                else:
                    grad_flip[...] = block[feed : feed + fs, :].astype(F32).T
                sums.append(sweep(rows_from(grad_flip, 0), *views, D))
            else:
                source = rows_from(gdown1, own_f) if b else rows_from(block, feed + fs)
                sums.append(sweep(source, *views, fs))
        save(3 * kind, u)
        save(3 * kind + 1, m)
        save(3 * kind + 2, s)
    for place, pair in enumerate(sums):
        sums_out[place : place + 1, :] = colsum(pair[1])
        sums_out[8 + place : 9 + place, :] = colsum(pair[0])

    for copy in loads[12:]:
        copy.wait()
    w, m, s = held[12:15]
    edge = PIX + P_SIZE - 4
    rows_all = w.shape[0]

    def slab(first, count, grad):
        at = slice(first, first + count)
        weight = w[at, :]
        mean, second, direction = adam_parts(grad, m[at, :], s[at, :], factor)
        m[at, :] = mean
        s[at, :] = second
        return weight, direction + DECAY * weight

    def run(first, count, source, offset):
        def step(i, kept):
            at = pl.ds(pl.multiple_of(first + i * 32, 16), 32)
            weight = w[at, :]
            grad = source[pl.ds(pl.multiple_of(offset + i * 32, 16), 32), :].astype(F32)
            mean, second, direction = adam_parts(grad, m[at, :], s[at, :], factor)
            m[at, :] = mean
            s[at, :] = second
            update = direction + DECAY * weight
            table_update[at, :] = update
            return (kept[0] + fold(weight), kept[1] + fold(update))

        zero = jnp.zeros((8, 128), F32)
        return lax.fori_loop(0, count // 32, step, (zero, zero))

    patch = run(0, PIX, shared, 0)
    place_rows = run(PIX, P_SIZE - 4, shared, PIX)
    body = (rows_all - edge - 16) // 32 * 32
    heads = run(edge + 16, body, ghead, 16)
    tile = lax.broadcasted_iota(jnp.int32, (16, 1), 0) < 4
    weight, update = slab(
        edge, 16, shared[edge : edge + 16, :].astype(F32) + ghead[0:16, :]
    )
    table_update[edge : edge + 16, :] = update
    left = edge + 16 + body
    tail_rows = rows_all - left
    tail_weight, tail_update = slab(left, tail_rows, ghead[16 + body : 16 + body + tail_rows, :])
    table_update[left:rows_all, :] = tail_update
    save(13, m)
    save(14, s)

    def masked(values, mask):
        return total(jnp.where(mask, values * values, 0.0))

    sq_w = [
        total(patch[0]), total(place_rows[0]) + masked(weight, tile),
        total(heads[0]) + masked(weight, ~tile) + total(tail_weight * tail_weight),
    ]
    sq_u = [
        total(patch[1]), total(place_rows[1]) + masked(update, tile),
        total(heads[1]) + masked(update, ~tile) + total(tail_update * tail_update),
    ]
    rates = [RATE * jnp.sqrt(sq_w[i] / (sq_u[i] + 1e-12)) for i in range(3)]

    def renew(first, count, rate):
        def step(i, _):
            at = pl.ds(pl.multiple_of(first + i * 32, 16), 32)
            w[at, :] = w[at, :] - rate * table_update[at, :]
            return 0

        lax.fori_loop(0, count // 32, step, 0)

    renew(0, PIX, rates[0])
    renew(PIX, P_SIZE - 4, rates[1])
    renew(edge + 16, body, rates[2])
    w[edge : edge + 16, :] = weight - jnp.where(tile, rates[1], rates[2]) * update
    w[left:rows_all, :] = tail_weight - rates[2] * tail_update
    save(12, w)

    lane = lax.broadcasted_iota(jnp.int32, (1, 128), 1)
    line = jnp.where(lane == 0, norm, 0.0)
    weight_line = jnp.zeros((1, 128), F32)
    update_line = jnp.zeros((1, 128), F32)
    for place, (first, second) in enumerate(
        zip(sq_w + weight_sums, sq_u + misc[1:])
    ):
        weight_line = jnp.where(lane == 8 + place, first, weight_line)
        update_line = jnp.where(lane == 8 + place, second, update_line)
    misc_out[0:1, :] = line
    misc_out[1:2, :] = weight_line
    misc_out[2:3, :] = update_line
    misc_out[3:8, :] = jnp.zeros((5, 128), F32)
    for copy in saves:
        copy.wait()


def run_moments(n_dp, grads, smalls, state):
    outs = []
    for i, item in enumerate(state):
        outs.append(jax.ShapeDtypeStruct(item.shape, F32))
    hs, fs = state[3].shape[1], state[9].shape[1]
    dma = pltpu.SemaphoreType.DMA
    return pl.pallas_call(
        functools.partial(moment_kernel, n_dp),
        in_specs=[WHOLE] * (len(grads) + len(smalls)) + [ANY] * 15,
        out_specs=[ANY] * 15 + [WHOLE] * 8,
        out_shape=outs
        + [jax.ShapeDtypeStruct(item.shape, F32) for item in smalls]
        + [shaped(8, 128), shaped(16, 128)],
        scratch_shapes=[pltpu.VMEM(item.shape, F32) for item in state]
        + [pltpu.VMEM(state[3 * kind].shape, F32) for kind in range(4)]
        + [
            pltpu.VMEM((D, D), F32), pltpu.VMEM((D, D), F32), pltpu.VMEM((D, fs), F32),
            dma((15,)), dma((15,)), pltpu.VMEM(state[12].shape, F32),
        ],
        compiler_params=pltpu.CompilerParams(vmem_limit_bytes=VMEM_LIMIT),
        name="moments",
    )(*grads, *smalls, *state)


def sums_kernel(n_mp, sums, out, slots, send_sem, recv_sem):
    dp = lax.axis_index("dp")
    mp = lax.axis_index("mp")
    barrier = pltpu.get_barrier_semaphore()
    for step in range(1, n_mp):
        pl.semaphore_signal(
            barrier, inc=1, device_id=(dp, lax.rem(mp + step, n_mp)), device_id_type=MESH
        )
    slots[pl.ds(mp, 1)] = sums[...][None]
    pl.semaphore_wait(barrier, n_mp - 1)
    copies = [
        remote(
            slots.at[mp], slots.at[mp], send_sem.at[step], recv_sem.at[step],
            (dp, lax.rem(mp + step, n_mp)),
        )
        for step in range(1, n_mp)
    ]
    for copy in copies:
        copy.start()
    for step in range(1, n_mp):
        source = lax.rem(mp + n_mp - step, n_mp)
        copies[step - 1].wait_send()
        remote(
            slots.at[mp], slots.at[source], send_sem.at[step], recv_sem.at[step], (dp, source)
        ).wait_recv()
    out[...] = jnp.sum(slots[...], 0)


def run_sums(n_mp, sums):
    return pl.pallas_call(
        functools.partial(sums_kernel, n_mp),
        in_specs=[WHOLE],
        out_specs=WHOLE,
        out_shape=shaped(*sums.shape),
        scratch_shapes=[
            pltpu.VMEM((n_mp, *sums.shape), F32),
            pltpu.SemaphoreType.DMA((n_mp,)),
            pltpu.SemaphoreType.DMA((n_mp,)),
        ],
        compiler_params=pltpu.CompilerParams(
            vmem_limit_bytes=VMEM_LIMIT, collective_id=4, has_side_effects=True
        ),
        name="sums",
    )(sums)


def renew_kernel(sums, misc, *rest):
    weights, updates = rest[:4], rest[4:8]
    new, copies, norms = rest[8:12], rest[12:16], rest[16]
    rates = []
    lane = lax.broadcasted_iota(jnp.int32, (1, 128), 1)
    weight_line, update_line = misc[1:2, :], misc[2:3, :]
    for place in range(8):
        update_sq = total(sums[place : place + 1, :])
        weight_sq = total(sums[8 + place : 9 + place, :])
        rates.append(RATE * jnp.sqrt(weight_sq / (update_sq + 1e-12)))
        weight_line = jnp.where(lane == place, weight_sq, weight_line)
        update_line = jnp.where(lane == place, update_sq, update_line)
    norms[0:1, :] = jnp.sqrt(weight_line)
    norms[1:2, :] = jnp.sqrt(update_line)
    norms[2:8, :] = jnp.zeros((6, 128), F32)
    for kind in range(4):
        rows = weights[kind].shape[1]
        chunk = 32 if rows % 32 == 0 else 16
        for b in range(2):
            w, u, out, low = weights[kind], updates[kind], new[kind], copies[kind]
            rate = rates[2 * kind + b]

            def step(i, _, b=b, w=w, u=u, out=out, low=low, rate=rate, chunk=chunk):
                at = pl.ds(pl.multiple_of(i * chunk, chunk), chunk)
                values = w[b, at, :] - rate * u[b, at, :]
                out[b, at, :] = values
                low[b, at, :] = values.astype(BF)
                return 0

            lax.fori_loop(0, rows // chunk, step, 0)


def run_renew(sums, misc, weights, updates):
    return pl.pallas_call(
        renew_kernel,
        in_specs=[WHOLE] * 10,
        out_specs=[WHOLE] * 9,
        out_shape=[shaped(*item.shape) for item in weights]
        + [shaped(*item.shape, dtype=BF) for item in weights]
        + [shaped(8, 128)],
        compiler_params=pltpu.CompilerParams(vmem_limit_bytes=VMEM_LIMIT),
        name="renew",
    )(sums, misc, *weights, *updates)


def shards(
    pixels,
    token_mask,
    counts,
    labels,
    pairs,
    attn_in,
    attn_in_mean,
    attn_in_square,
    attn_out,
    attn_out_mean,
    attn_out_square,
    mlp_in,
    mlp_in_mean,
    mlp_in_square,
    mlp_out,
    mlp_out_mean,
    mlp_out_square,
    tables,
    tables_mean,
    tables_square,
    vectors,
    vectors_mean,
    vectors_square,
    talking,
    talking_mean,
    talking_square,
):
    local = pixels.shape[0]
    group = token_mask.shape[0]
    place_mp = lax.axis_index("mp")
    n_mp = lax.axis_size("mp")
    n_dp = lax.axis_size("dp")
    hs = attn_in.shape[3]
    fs = mlp_in.shape[2]

    def as_rows(item):
        return item.transpose(0, 2, 3, 1).reshape(2, 3 * hs, D)

    def from_rows(item):
        return item.reshape(2, 3, hs, D).transpose(0, 3, 1, 2)

    attn_in, attn_in_mean, attn_in_square = map(as_rows, (attn_in, attn_in_mean, attn_in_square))
    mlp_rows = [jnp.concatenate([mlp_in[b].T, mlp_out[b]], 0).astype(BF) for b in range(2)]
    cls_rows = jnp.concatenate([attn_in[1], attn_out[1]], 0).astype(BF)
    wmlp = lax.all_gather(mlp_rows[0], "mp")
    wcls = lax.all_gather(cls_rows, "mp")
    wmlp_cls = lax.all_gather(mlp_rows[1], "mp")
    pixel_rows = pixels.transpose(1, 0, 2).reshape(P_SIZE * local, PIX)
    wattn, embed = run_start(
        n_dp, n_mp, local, attn_in, attn_out, pixel_rows, tables, vectors
    )

    okay = lax.dynamic_slice_in_dim(
        (jnp.arange(group) >= group - counts[0]).astype(F32), place_mp * local, local, 0
    )
    keep = lax.dynamic_slice_in_dim(token_mask > 0, place_mp * local, local, 0)
    token_weight = keep.astype(F32) * okay[:, None]
    bias = jnp.where(keep, 0.0, MASKED).astype(F32)
    cols = jnp.stack([bias, token_weight], -1)
    digits = [labels // 32, labels % 32, pairs // 32, pairs % 32]
    digits = [item.astype(F32) for item in digits]
    digits += [jnp.broadcast_to(counts, (local,)).astype(F32), jnp.sum(token_weight, 1)]
    base = jnp.pad(jnp.stack(digits, 1), ((0, 0), (0, 128 - len(digits))))[:, None, :]

    spread_heads = functools.partial(jnp.repeat, repeats=HEAD, axis=1)
    t1row = spread_heads(talking[0]) * SCALE
    t1col = t1row.T
    t2row = spread_heads(talking[1].T)
    t2col = t2row.T
    head = tables[PIX + P_SIZE :].astype(BF)

    q, k, v, prob, ho, raw0, middle, stat_a = run_self_attend(
        embed, cols, vectors, wattn, t1row, t2col
    )
    patches, act, slope, raw1, cprob, cprob0, z, card, aux = run_feed(
        middle, cols, bias[:, None, :], base, stat_a, vectors, wmlp, wcls
    )
    cards = run_cards(n_dp, n_mp, card)
    dch, gout1, gup1, gdown1, ghead, rows1, stat = run_token(
        group, local, cards, vectors, wcls, wmlp_cls, head
    )
    dmid, gfeed, rows2 = run_feed_back(
        n_dp, dch, patches, middle, raw1, act, slope, cprob, cprob0, z, aux, vectors, wcls, wmlp
    )
    gattn, gpix, gpos, rows3, chunk = run_self_back(
        n_dp, n_mp, dmid, pixel_rows, embed, q, k, v, prob, ho, raw0, vectors, wattn,
        t1row, t1col, t2row, gfeed,
    )

    block, shared, block_sq = run_reduce(
        n_dp, n_mp, gattn, chunk, gpix, gpos, rows2, rows3
    )
    state = (
        attn_in, attn_in_mean, attn_in_square, attn_out, attn_out_mean, attn_out_square,
        mlp_in, mlp_in_mean, mlp_in_square, mlp_out, mlp_out_mean, mlp_out_square,
        tables, tables_mean, tables_square,
    )
    smalls = (vectors, vectors_mean, vectors_square, talking, talking_mean, talking_square)
    moved = run_moments(
        n_dp, (block, shared, block_sq, gout1, gup1, gdown1, ghead, rows1, stat, aux, wcls),
        smalls, state,
    )
    sums = run_sums(n_mp, moved[22])
    renewed = run_renew(sums, moved[21], state[0:12:3], moved[0:12:3])
    norms = renewed[8][:2, :13]
    return (
        from_rows(renewed[0]),
        from_rows(moved[1]),
        from_rows(moved[2]),
        renewed[1],
        moved[4],
        moved[5],
        renewed[2],
        moved[7],
        moved[8],
        renewed[3],
        moved[10],
        moved[11],
        moved[12],
        moved[13],
        moved[14],
        *moved[15:21],
        from_rows(renewed[4]),
        renewed[5],
        renewed[6],
        renewed[7],
        stat[0, :12],
        moved[21][0, 0],
        norms,
    )


def solution(mesh):
    return jax.shard_map(
        shards,
        mesh=mesh,
        in_specs=(
            P(("dp", "mp"), None, None),
            P("dp", None),
            P("dp"),
            P(("dp", "mp")),
            P(("dp", "mp")),
            P(None, None, None, "mp"),
            P(None, None, None, "mp"),
            P(None, None, None, "mp"),
            P(None, "mp", None),
            P(None, "mp", None),
            P(None, "mp", None),
            P(None, None, "mp"),
            P(None, None, "mp"),
            P(None, None, "mp"),
            P(None, "mp", None),
            P(None, "mp", None),
            P(None, "mp", None),
            P(),
            P(),
            P(),
            P(),
            P(),
            P(),
            P(),
            P(),
            P(),
        ),
        out_specs=(
            P(None, None, None, "mp"),
            P(None, None, None, "mp"),
            P(None, None, None, "mp"),
            P(None, "mp", None),
            P(None, "mp", None),
            P(None, "mp", None),
            P(None, None, "mp"),
            P(None, None, "mp"),
            P(None, None, "mp"),
            P(None, "mp", None),
            P(None, "mp", None),
            P(None, "mp", None),
            P(),
            P(),
            P(),
            P(),
            P(),
            P(),
            P(),
            P(),
            P(),
            P(None, None, None, "mp"),
            P(None, "mp", None),
            P(None, None, "mp"),
            P(None, "mp", None),
            P(),
            P(),
            P(),
        ),
        check_vma=False,
    )
```

```python
import functools

import jax
import jax.numpy as jnp
from jax import lax
from jax.experimental import pallas as pl
from jax.experimental.pallas import tpu as pltpu
from jax.sharding import PartitionSpec as P

D = 384
HEADS = 8
HEAD = 48
PIX = 768
P_SIZE = 196
PAD = 208
WIDE = 256
STEP = 10
SCALE = HEAD**-0.5
BETA_ONE = 0.9
BETA_TWO = 0.999
ADAM_EPS = 1e-08
DECAY = 0.01
RATE = 0.5
RATE_VECTOR = 0.5
CLIP = 0.02
TEMP = 0.05
MASKED = -1000000000.0
NORM_EPS = 1e-06
F32 = jnp.float32
BF = jnp.bfloat16
VMEM_LIMIT = 58 * 2**20
ANY = pl.BlockSpec(memory_space=pl.ANY)
MESH = pl.DeviceIdType.MESH
WHOLE = pl.BlockSpec(memory_space=pltpu.VMEM)


def nn(left, right):
    return lax.dot_general(left, right, (((1,), (0,)), ((), ())), preferred_element_type=F32)


def nt(left, right):
    return lax.dot_general(left, right, (((1,), (1,)), ((), ())), preferred_element_type=F32)


def tn(left, right):
    return lax.dot_general(left, right, (((0,), (0,)), ((), ())), preferred_element_type=F32)


def colsum(values):
    return jnp.sum(values, 0, keepdims=True)


def normalize(inputs):
    center = inputs - jnp.mean(inputs, -1, keepdims=True)
    spread = jnp.mean(center * center, -1, keepdims=True)
    inverse = lax.rsqrt(spread + NORM_EPS)
    return center * inverse, inverse


def normalize_back(unit, inverse, gain, incoming):
    scaled = incoming * gain
    return inverse * (
        scaled
        - jnp.mean(scaled, -1, keepdims=True)
        - unit * jnp.mean(scaled * unit, -1, keepdims=True)
    )


def gelu_parts(inner):
    cumulative = 0.5 + 0.5 * lax.erf(inner * 0.5**0.5)
    bell = jnp.exp2(inner * inner * (-0.5 * 1.4426950408889634)) * 0.3989422804014327
    return inner * cumulative, cumulative + inner * bell


def head_mask(copies=1):
    row = lax.rem(lax.broadcasted_iota(jnp.int32, (copies * HEADS, D), 0), HEADS)
    column = lax.broadcasted_iota(jnp.int32, (copies * HEADS, D), 1)
    return ((column >= row * HEAD) & (column < row * HEAD + HEAD)).astype(F32)


def stat_lanes(parts, weight, first):
    lane = lax.broadcasted_iota(jnp.int32, (1, 128), 1)
    row = jnp.zeros((1, 128), F32)
    for place, values in enumerate(parts):
        total = jnp.sum(colsum(values * values * weight), keepdims=True)
        high = total.astype(BF).astype(F32)
        row = jnp.where(lane == first + 2 * place, high, row)
        row = jnp.where(lane == first + 2 * place + 1, total - high, row)
    return row


def part(ref, first, rows):
    shards_count = ref.shape[0]
    return ref[:, first : first + rows, :].reshape(shards_count * rows, ref.shape[2])


def pad_rows(rows, n_dp):
    return -(-rows // (16 * n_dp)) * 16 * n_dp


class Place:
    def __init__(self, n_dp, n_mp):
        self.n_dp, self.n_mp, self.n_y = n_dp, n_mp, n_mp // 2
        self.n_lo = 2 if n_dp < 16 else 4
        self.n_hi = n_dp // self.n_lo
        self.dp = lax.axis_index("dp")
        self.mp = lax.axis_index("mp")
        self.y = lax.div(self.mp, 2)
        self.core = lax.rem(self.mp, 2)
        self.high = lax.div(self.dp, self.n_lo)
        self.low = lax.rem(self.dp, self.n_lo)
        self.chunk = self.low * self.n_hi + self.high
        self.sibling = (self.dp, self.y * 2 + 1 - self.core)

    def along_y(self, step):
        return lax.rem(self.y + step, self.n_y)

    def along_lo(self, step):
        return lax.rem(self.low + step, self.n_lo)

    def along_hi(self, step):
        return lax.rem(self.high + step, self.n_hi)

    def at_lo(self, low):
        return (self.high * self.n_lo + low, self.mp)

    def at_hi(self, high):
        return (high * self.n_lo + self.low, self.mp)

    def near_partners(self):
        return [self.sibling] + [
            (self.dp, self.along_y(step) * 2 + self.core) for step in range(1, self.n_y)
        ]

    def low_partners(self):
        return [self.at_lo(self.along_lo(step)) for step in range(1, self.n_lo)]

    def dp_partners(self):
        return self.low_partners() + [self.at_hi(self.along_hi(step)) for step in range(1, self.n_hi)]


def greet(partners):
    barrier = pltpu.get_barrier_semaphore()
    for partner in partners:
        pl.semaphore_signal(barrier, inc=1, device_id=partner, device_id_type=MESH)
    return lambda: pl.semaphore_wait(barrier, len(partners))


def tile_rows(ref, first, rows):
    return ref.at[pl.ds(pl.multiple_of(first, 16), rows)]


class SpreadGather:
    def __init__(self, place, rows, out, far_sem, low_sem, near_sem):
        self.place, self.rows, self.out = place, rows, out
        self.far_sem, self.low_sem, self.near_sem = far_sem, low_sem, near_sem
        self.count = rows.shape[0] // place.n_lo

    def piece(self, ref, low):
        return tile_rows(ref, low * self.count, self.count)

    def far_copy(self, step, slot):
        p = self.place
        return remote(
            self.piece(self.rows, p.low), self.piece(self.out.at[slot], p.low),
            self.far_sem.at[0, step], self.far_sem.at[1, step],
            (p.dp, p.along_y(step) * 2 + p.core),
        )

    def low_copy(self, step, turn, low):
        p = self.place
        rows = self.piece(self.out.at[self.from_y(step) + p.core], low)
        at = (step - 1) * p.n_lo + turn
        return remote(
            rows, rows, self.low_sem.at[0, at], self.low_sem.at[1, at],
            p.at_lo(p.along_lo(turn)),
        )

    def near_copy(self, step, slot):
        return remote(
            self.rows if step == 0 else self.out.at[slot], self.out.at[slot],
            self.near_sem.at[0, step], self.near_sem.at[1, step], self.place.sibling,
        )

    def own_copy(self):
        return pltpu.make_async_copy(
            self.rows, self.out.at[self.place.mp], self.far_sem.at[0, 0]
        )

    def from_y(self, step):
        p = self.place
        return p.along_y(p.n_y - step) * 2

    def start(self):
        p = self.place
        for step in range(1, p.n_y):
            self.far_copy(step, p.mp).start()
        self.near_copy(0, p.mp).start()
        self.own_copy().start()

    def spread(self):
        p = self.place
        for step in range(1, p.n_y):
            self.far_copy(step, self.from_y(step) + p.core).wait_recv()
            for turn in range(1, p.n_lo):
                self.low_copy(step, turn, p.low).start()

    def forward(self):
        p = self.place
        for step in range(1, p.n_y):
            for turn in range(1, p.n_lo):
                self.low_copy(step, turn, p.along_lo(p.n_lo - turn)).wait_recv()
            self.near_copy(step, self.from_y(step) + p.core).start()

    def finish(self):
        p = self.place
        self.own_copy().wait()
        for step in range(1, p.n_y):
            self.far_copy(step, p.mp).wait_send()
            for turn in range(1, p.n_lo):
                self.low_copy(step, turn, p.low).wait_send()
        for step in range(p.n_y):
            self.near_copy(step, self.from_y(step) + p.core if step else p.mp).wait_send()
            self.near_copy(step, self.from_y(step) + 1 - p.core).wait_recv()


def spread_scratch(n_dp, n_mp):
    n_lo = 2 if n_dp < 16 else 4
    dma = pltpu.SemaphoreType.DMA
    return [dma((2, n_mp // 2)), dma((2, n_mp // 2 * n_lo)), dma((2, n_mp // 2))]


class Gather:
    def __init__(self, place, rows, out, far_sem, near_sem):
        self.place, self.rows, self.out = place, rows, out
        self.far_sem, self.near_sem = far_sem, near_sem

    def far_copy(self, step, slot):
        p = self.place
        return remote(
            self.rows, self.out.at[slot], self.far_sem.at[0, step], self.far_sem.at[1, step],
            (p.dp, p.along_y(step) * 2 + p.core),
        )

    def near_copy(self, step, slot):
        return remote(
            self.rows if step == 0 else self.out.at[slot], self.out.at[slot],
            self.near_sem.at[0, step], self.near_sem.at[1, step], self.place.sibling,
        )

    def own_copy(self):
        return pltpu.make_async_copy(
            self.rows, self.out.at[self.place.mp], self.far_sem.at[0, 0]
        )

    def from_y(self, step):
        p = self.place
        return p.along_y(p.n_y - step) * 2

    def start(self):
        p = self.place
        for step in range(1, p.n_y):
            self.far_copy(step, p.mp).start()
        self.near_copy(0, p.mp).start()
        self.own_copy().start()

    def forward(self):
        p = self.place
        for step in range(1, p.n_y):
            slot = self.from_y(step) + p.core
            self.far_copy(step, slot).wait_recv()
            self.near_copy(step, slot).start()

    def finish(self):
        p = self.place
        self.own_copy().wait()
        for step in range(1, p.n_y):
            self.far_copy(step, p.mp).wait_send()
        for step in range(p.n_y):
            self.near_copy(step, self.from_y(step) + p.core if step else p.mp).wait_send()
            self.near_copy(step, self.from_y(step) + 1 - p.core).wait_recv()


def gather_scratch(n_mp):
    dma = pltpu.SemaphoreType.DMA
    return [dma((2, n_mp // 2)), dma((2, n_mp // 2))]


class ShardSum:
    def __init__(
        self, place, rows, first, y_first, near, far, low, half, high,
        near_sem, far_sem, low_sem, high_sem,
    ):
        self.place, self.rows, self.first, self.y_first = place, rows, first, y_first
        self.near, self.far, self.low, self.half, self.high = near, far, low, half, high
        self.near_sem, self.far_sem = near_sem, far_sem
        self.low_sem, self.high_sem = low_sem, high_sem
        self.count = near.shape[1]
        self.wide = self.count // place.n_lo
        self.chunk = self.count // place.n_dp

    def near_copy(self, step):
        p = self.place
        y = p.along_y(step)
        return remote(
            self.rows.at[y * 2 + 1 - p.core, pl.ds(self.first, self.count)], self.near.at[y],
            self.near_sem.at[0, step], self.near_sem.at[1, step], p.sibling,
        )

    def far_copy(self, step):
        p = self.place
        y = p.along_y(step)
        rows = self.near.at[y]
        if not self.y_first:
            rows = tile_rows(rows, p.low * self.wide, self.wide)
        return remote(
            rows, self.far.at[step - 1],
            self.far_sem.at[0, step], self.far_sem.at[1, step], (p.dp, y * 2 + p.core),
        )

    def low_copy(self, step):
        p = self.place
        to = p.along_lo(step)
        at = pl.ds(pl.multiple_of(to * self.wide, 16), self.wide)
        rows = self.near.at[p.y, at] if self.y_first else self.near.at[:, at]
        return remote(
            rows, self.low.at[step - 1],
            self.low_sem.at[0, step], self.low_sem.at[1, step], p.at_lo(to),
        )

    def high_copy(self, step):
        p = self.place
        to = p.along_hi(step)
        return remote(
            tile_rows(self.half, to * self.chunk, self.chunk), self.high.at[step - 1],
            self.high_sem.at[0, step], self.high_sem.at[1, step], p.at_hi(to),
        )

    def start(self):
        for step in range(1, self.place.n_y + 1):
            self.near_copy(step).start()

    def second(self):
        p = self.place
        at = slice(self.first, self.first + self.count)
        for step in range(1, p.n_y + 1):
            y = p.along_y(step)
            self.near_copy(step).wait_recv()
            self.near[pl.ds(y, 1)] = (
                self.rows[pl.ds(y * 2 + p.core, 1), at, :].astype(F32)
                + self.near[pl.ds(y, 1)].astype(F32)
            ).astype(BF)
            if self.y_first and step < p.n_y:
                self.far_copy(step).start()
        if not self.y_first:
            for step in range(1, p.n_lo):
                self.low_copy(step).start()

    def third(self):
        p = self.place
        own = pl.ds(pl.multiple_of(p.low * self.wide, 16), self.wide)
        if self.y_first:
            sums = self.near[pl.ds(p.y, 1)].astype(F32)
            for step in range(1, p.n_y):
                self.far_copy(step).wait_recv()
                sums += self.far[step - 1].astype(F32)[None]
            self.near[pl.ds(p.y, 1)] = sums.astype(BF)
            for step in range(1, p.n_lo):
                self.low_copy(step).start()
        else:
            sums = self.near[:, own, :].astype(F32)
            for step in range(1, p.n_lo):
                self.low_copy(step).wait_recv()
                sums += self.low[step - 1].astype(F32)
            self.near[:, own, :] = sums.astype(BF)
            for step in range(1, p.n_y):
                self.far_copy(step).start()

    def fourth(self):
        p = self.place
        own = pl.ds(pl.multiple_of(p.low * self.wide, 16), self.wide)
        sums = self.near[pl.ds(p.y, 1), own, :][0].astype(F32)
        if self.y_first:
            for step in range(1, p.n_lo):
                self.low_copy(step).wait_recv()
                sums += self.low[step - 1].astype(F32)
        else:
            for step in range(1, p.n_y):
                self.far_copy(step).wait_recv()
                sums += self.far[step - 1].astype(F32)
        self.half[...] = sums.astype(BF)
        for step in range(1, p.n_hi):
            self.high_copy(step).start()

    def finish(self):
        p = self.place
        at = pl.ds(pl.multiple_of(p.high * self.chunk, 16), self.chunk)
        sums = self.half[at, :].astype(F32)
        for step in range(1, p.n_hi):
            self.high_copy(step).wait_recv()
            sums += self.high[step - 1].astype(F32)
        return sums.astype(BF)

    def wait_sends(self):
        p = self.place
        for step in range(1, p.n_y + 1):
            self.near_copy(step).wait_send()
            if step < p.n_y:
                self.far_copy(step).wait_send()
        for step in range(1, p.n_lo):
            self.low_copy(step).wait_send()
        for step in range(1, p.n_hi):
            self.high_copy(step).wait_send()


def sum_scratch(n_dp, n_mp, rows, y_first):
    n_y = n_mp // 2
    n_lo = 2 if n_dp < 16 else 4
    n_hi = n_dp // n_lo
    wide = rows // n_lo
    dma = pltpu.SemaphoreType.DMA
    far = (max(n_y - 1, 1), rows, D) if y_first else (max(n_y - 1, 1), wide, D)
    low = (n_lo - 1, wide, D) if y_first else (n_lo - 1, n_y, wide, D)
    return [
        pltpu.VMEM((n_y, rows, D), BF), pltpu.VMEM(far, BF), pltpu.VMEM(low, BF),
        pltpu.VMEM((wide, D), BF), pltpu.VMEM((n_hi - 1, rows // n_dp, D), BF),
        dma((2, n_y + 1)), dma((2, n_y + 1)), dma((2, n_lo)), dma((2, n_hi)),
    ]


SUM_BUFFERS = 9


def halves(rows, n_dp):
    unit = 16 * n_dp
    first = (rows // unit + 1) // 2 * unit
    return first, rows - first


class TableSum:
    def __init__(
        self, place, rows, out, near, low, part_rows, high, last, far, near_sem, low_sem, high_sem,
        far_sem, back_sem, hand_sem,
    ):
        self.place, self.rows, self.out = place, rows, out
        self.near, self.low, self.part, self.high = near, low, part_rows, high
        self.last, self.far = last, far
        self.near_sem, self.low_sem, self.high_sem = near_sem, low_sem, high_sem
        self.far_sem, self.back_sem, self.hand_sem = far_sem, back_sem, hand_sem
        self.chunk = high.shape[2]
        self.wide = low.shape[2]
        self.slab = place.core * place.n_y + place.y
        self.first = place.core * place.n_y

    def near_copy(self):
        p = self.place
        return remote(
            self.rows.at[pl.ds((1 - p.core) * p.n_y, p.n_y)], self.near,
            self.near_sem.at[0], self.near_sem.at[1], p.sibling,
        )

    def low_copy(self, step):
        p = self.place
        to = p.along_lo(step)
        return remote(
            self.near.at[:, pl.ds(pl.multiple_of(to * self.wide, 16), self.wide)],
            self.low.at[step - 1], self.low_sem.at[0, step], self.low_sem.at[1, step], p.at_lo(to),
        )

    def high_copy(self, step):
        p = self.place
        to = p.along_hi(step)
        return remote(
            self.part.at[:, pl.ds(pl.multiple_of(to * self.chunk, 16), self.chunk)],
            self.high.at[step - 1], self.high_sem.at[0, step], self.high_sem.at[1, step],
            p.at_hi(to),
        )

    def far_copy(self, step):
        p = self.place
        to = p.along_y(step)
        return remote(
            self.last.at[to], self.far.at[step - 1], self.far_sem.at[0, step],
            self.far_sem.at[1, step], (p.dp, to * 2 + p.core),
        )

    def start(self):
        self.near_copy().start()

    def near_to_low(self):
        p = self.place
        self.near_copy().wait_recv()
        self.near[...] = (
            self.rows[pl.ds(self.first, p.n_y)].astype(F32) + self.near[...].astype(F32)
        ).astype(BF)
        for step in range(1, p.n_lo):
            self.low_copy(step).start()

    def low_to_high(self):
        p = self.place
        at = pl.ds(pl.multiple_of(p.low * self.wide, 16), self.wide)
        sums = self.near[:, at, :].astype(F32)
        for step in range(1, p.n_lo):
            self.low_copy(step).wait_recv()
            sums += self.low[step - 1].astype(F32)
        self.part[...] = sums.astype(BF)
        for step in range(1, p.n_hi):
            self.high_copy(step).start()

    def high_to_far(self):
        p = self.place
        at = pl.ds(pl.multiple_of(p.high * self.chunk, 16), self.chunk)
        sums = self.part[:, at, :].astype(F32)
        for step in range(1, p.n_hi):
            self.high_copy(step).wait_recv()
            sums += self.high[step - 1].astype(F32)
        self.last[...] = sums.astype(BF)
        for step in range(1, p.n_y):
            self.far_copy(step).start()

    def chunk_at(self, slab, chunk):
        return self.out.at[slab, pl.ds(pl.multiple_of(chunk * self.chunk, 16), self.chunk)]

    def back_far(self, step, y):
        p = self.place
        rows = self.chunk_at(self.first + y, p.chunk)
        return remote(
            rows, rows, self.back_sem.at[0, step], self.back_sem.at[1, step],
            (p.dp, p.along_y(step) * 2 + p.core),
        )

    def back_high(self, step, chunk):
        p = self.place
        rows = self.chunk_at(pl.ds(self.first, p.n_y), chunk)
        return remote(
            rows, rows, self.back_sem.at[2, step], self.back_sem.at[3, step],
            p.at_hi(p.along_hi(step)),
        )

    def back_low(self, step, low):
        p = self.place
        rows = self.out.at[
            pl.ds(self.first, p.n_y), pl.ds(pl.multiple_of(low * self.wide, 16), self.wide)
        ]
        return remote(
            rows, rows, self.back_sem.at[4, step], self.back_sem.at[5, step],
            p.at_lo(p.along_lo(step)),
        )

    def hand_copy(self, core):
        p = self.place
        rows = self.out.at[pl.ds(core * p.n_y, p.n_y)]
        return remote(rows, rows, self.hand_sem.at[0], self.hand_sem.at[1], p.sibling)

    def turn(self):
        p = self.place
        sums = self.last[pl.ds(p.y, 1)][0].astype(F32)
        for step in range(1, p.n_y):
            self.far_copy(step).wait_recv()
            sums += self.far[step - 1].astype(F32)
        at = pl.ds(pl.multiple_of(p.chunk * self.chunk, 16), self.chunk)
        self.out[pl.ds(self.slab, 1), at, :] = sums.astype(BF)[None]
        for step in range(1, p.n_y):
            self.back_far(step, p.y).start()

    def far_to_high(self):
        p = self.place
        for step in range(1, p.n_y):
            self.back_far(step, p.along_y(p.n_y - step)).wait_recv()
        for step in range(1, p.n_hi):
            self.back_high(step, p.chunk).start()

    def high_to_low(self):
        p = self.place
        for step in range(1, p.n_hi):
            self.back_high(step, p.low * p.n_hi + p.along_hi(p.n_hi - step)).wait_recv()
        for step in range(1, p.n_lo):
            self.back_low(step, p.low).start()

    def low_to_near(self):
        p = self.place
        for step in range(1, p.n_lo):
            self.back_low(step, p.along_lo(p.n_lo - step)).wait_recv()
        self.hand_copy(p.core).start()

    def finish(self):
        p = self.place
        self.hand_copy(1 - p.core).wait_recv()
        self.near_copy().wait_send()
        self.hand_copy(p.core).wait_send()
        for step in range(1, p.n_lo):
            self.low_copy(step).wait_send()
            self.back_low(step, p.low).wait_send()
        for step in range(1, p.n_hi):
            self.high_copy(step).wait_send()
            self.back_high(step, p.chunk).wait_send()
        for step in range(1, p.n_y):
            self.far_copy(step).wait_send()
            self.back_far(step, p.y).wait_send()


def table_scratch(n_dp, n_mp, rows):
    n_y = n_mp // 2
    n_lo = 2 if n_dp < 16 else 4
    n_hi = n_dp // n_lo
    wide, chunk = rows // n_lo, rows // n_dp
    dma = pltpu.SemaphoreType.DMA
    return [
        pltpu.VMEM((n_y, rows, D), BF), pltpu.VMEM((n_lo - 1, n_y, wide, D), BF),
        pltpu.VMEM((n_y, wide, D), BF), pltpu.VMEM((n_hi - 1, n_y, chunk, D), BF),
        pltpu.VMEM((n_y, chunk, D), BF), pltpu.VMEM((max(n_y - 1, 1), chunk, D), BF),
        dma((2,)), dma((2, n_lo)), dma((2, n_hi)), dma((2, n_y)),
        dma((6, max(n_y, n_lo, n_hi))), dma((2,)),
    ]


class HandHigh:
    def __init__(self, place, rows, sems):
        self.place, self.rows, self.sems = place, rows, sems
        self.chunk = rows.shape[0] // place.n_hi

    def copy(self, step, source):
        p = self.place
        rows = tile_rows(self.rows, source * self.chunk, self.chunk)
        return remote(
            rows, rows, self.sems.at[0, step], self.sems.at[1, step], p.at_hi(p.along_hi(step))
        )

    def start(self, sums):
        p = self.place
        self.rows[pl.ds(pl.multiple_of(p.high * self.chunk, 16), self.chunk), :] = sums
        for step in range(1, p.n_hi):
            self.copy(step, p.high).start()

    def arrive(self):
        p = self.place
        for step in range(1, p.n_hi):
            self.copy(step, p.along_hi(p.n_hi - step)).wait_recv()

    def wait_sends(self):
        for step in range(1, self.place.n_hi):
            self.copy(step, self.place.high).wait_send()


class HandLow:
    def __init__(self, place, rows, first, count, sems):
        self.place, self.rows, self.first, self.sems = place, rows, first, sems
        self.run = count // place.n_lo

    def copy(self, step, source):
        p = self.place
        rows = tile_rows(self.rows, self.first + source * self.run, self.run)
        return remote(
            rows, rows, self.sems.at[0, step], self.sems.at[1, step], p.at_lo(p.along_lo(step))
        )

    def start(self, sums):
        p = self.place
        self.rows[pl.ds(pl.multiple_of(self.first + p.low * self.run, 16), self.run), :] = sums
        for step in range(1, p.n_lo):
            self.copy(step, p.low).start()

    def arrive(self):
        p = self.place
        for step in range(1, p.n_lo):
            self.copy(step, p.along_lo(p.n_lo - step)).wait_recv()

    def wait_sends(self):
        for step in range(1, self.place.n_lo):
            self.copy(step, self.place.low).wait_send()


def remote(src, dst, send_sem, recv_sem, device):
    return pltpu.make_async_remote_copy(
        src_ref=src, dst_ref=dst, send_sem=send_sem, recv_sem=recv_sem,
        device_id=device, device_id_type=MESH,
    )


def stack_heads(stack, rows, gains):
    for g in range(HEADS):
        stack[g * PAD : g * PAD + P_SIZE, :] = (rows * gains[g : g + 1, :]).astype(BF)


def column(cols, index):
    lane = lax.broadcasted_iota(jnp.int32, cols.shape, 1)
    return jnp.sum(jnp.where(lane == index, cols[...], 0.0), 1, keepdims=True)


def self_attend_kernel(
    n_dp, n_mp, embed, cols, vec, wattn, t1row, t2row, mlp_rows,
    q_out, k_out, v_out, prob_out, post_out, ho_out, raw_out, mid_out, stat_out, wmlp_out,
    stack, scores, *sems,
):
    shard = wattn.shape[1] // 4
    place = Place(n_dp, n_mp)
    gather = Gather(place, mlp_rows, wmlp_out, *sems)
    images = pl.num_programs(0)

    @pl.when(pl.program_id(0) == 0)
    def _():
        stack[...] = jnp.zeros_like(stack)
        greet(place.near_partners())()
        gather.start()

    @pl.when(pl.program_id(0) == images - 1)
    def _():
        gather.forward()

    x = embed[0]
    unit, _ = normalize(x)
    normed = (unit * vec[0:1, :] + vec[1:2, :]).astype(BF)
    q = nt(normed, part(wattn, 0, shard)).astype(BF)
    k = nt(normed, part(wattn, shard, shard)).astype(BF)
    v = nt(normed, part(wattn, 2 * shard, shard)).astype(BF)
    q_out[0] = q
    k_out[0] = k
    v_out[0] = v
    stack_heads(stack, q.astype(F32), t1row)
    scores[...] = nt(k, stack[...])
    bias = column(cols, pl.program_id(0))
    for first in range(0, HEADS * PAD, 128):
        mixed = scores[:, first : first + 128] + bias
        grown = jnp.exp(mixed - jnp.max(mixed, 0, keepdims=True))
        prob = grown * (1.0 / jnp.sum(grown, 0, keepdims=True))
        prob_out[0, :, first : first + 128] = prob.astype(BF)
    post = tn(prob_out[0], v)
    post_out[0] = post.astype(BF)
    heads_out = jnp.zeros(x.shape, F32)
    for g in range(HEADS):
        heads_out += post[g * PAD : g * PAD + P_SIZE, :] * t2row[g : g + 1, :]
    heads_out = heads_out.astype(BF)
    ho_out[0] = heads_out
    raw = nn(heads_out, part(wattn, 3 * shard, shard))
    raw_out[0] = raw.astype(BF)
    branch = vec[3:4, :] * (raw + vec[2:3, :])
    middle = x + branch
    mid_out[0] = middle
    weight = column(cols, pl.program_id(0) + cols.shape[1] // 2)
    stat_out[0] = stat_lanes((branch, middle), weight, 8)

    @pl.when(pl.program_id(0) == images - 1)
    def _():
        gather.finish()


def feed_kernel(
    n_dp, n_mp, mid, cols, bias_row, base, stat, vec, wmlp, cls_rows, up_rows, down_rows,
    patch_out, act_out, slope_out, raw_out, norm_out, cprob_out, cprob0_out, z_out, card_out,
    aux_out, wcls_out, wup_out, wdown_out, wcls, *sems,
):
    hidden = wmlp.shape[1] // 2
    shard = wcls.shape[1] // 4
    images = norm_out.shape[0]

    place = Place(n_dp, n_mp)
    gather_cls = SpreadGather(place, cls_rows, wcls, *sems[:3])
    gather_up = SpreadGather(place, up_rows, wup_out, *sems[3:6])
    gather_down = SpreadGather(place, down_rows, wdown_out, *sems[6:])

    def beside(step, *stages):
        @pl.when(pl.program_id(0) == step)
        def _():
            for stage in stages:
                stage()

    @pl.when(pl.program_id(0) == 0)
    def _():
        norm_out[...] = jnp.zeros_like(norm_out)
        greet(place.near_partners() + place.low_partners())()
        gather_cls.start()
        gather_up.start()
        gather_down.start()

    beside(images * 3 // 8, gather_cls.spread)
    beside(images // 2, gather_up.spread)
    beside(images * 5 // 8, gather_down.spread)
    beside(images * 3 // 4, gather_cls.forward)
    beside(images - 1, gather_up.forward, gather_cls.finish)

    middle = mid[0]
    unit, _ = normalize(middle)
    normed = (unit * vec[4:5, :] + vec[5:6, :]).astype(BF)
    inner = nt(normed, part(wmlp, 0, hidden))
    active, slope = gelu_parts(inner)
    active = active.astype(BF)
    act_out[0] = active
    slope_out[0] = slope.astype(BF)
    raw = nn(active, part(wmlp, hidden, hidden))
    raw_out[0] = raw.astype(BF)
    branch = vec[7:8, :] * (raw + vec[6:7, :])
    patches = middle + branch
    patch_out[0] = patches
    card_out[pl.ds(4 * pl.program_id(0) + 3, 1), :] = (
        base[pl.ds(pl.program_id(0), 1), :]
        + stat[0]
        + stat_lanes((branch, patches), column(cols, pl.program_id(0) + images), 12)
    )
    unit, _ = normalize(patches)
    norm_out[pl.ds(pl.program_id(0), 1), :P_SIZE, :] = (
        (unit * vec[8:9, :] + vec[9:10, :]).astype(BF)[None]
    )

    @pl.when(pl.program_id(0) == images - 1)
    def _():
        gather_down.forward()
        unit, _ = normalize(jnp.broadcast_to(vec[17:18, :], (HEADS, D)))
        token = (unit * vec[8:9, :] + vec[9:10, :]).astype(BF)
        query = nt(token, part(wcls, 0, shard)).astype(BF).astype(F32)
        keys = nn((query * head_mask()).astype(BF), part(wcls, shard, shard)) * SCALE
        token = token.astype(F32)
        aux_out[0:8, :] = keys
        aux_out[8:16, :] = token
        aux_out[16:24, :] = query
        scores = nt(keys.astype(BF), norm_out[...].reshape(images * WIDE, D)) + bias_row[...]
        score0 = jnp.sum(keys * token, -1, keepdims=True)
        for n in range(images):
            rows = slice(n * HEADS, (n + 1) * HEADS)
            mine = scores[:, n * WIDE : (n + 1) * WIDE]
            top = jnp.maximum(jnp.max(mine, -1, keepdims=True), score0)
            grown = jnp.exp(mine - top)
            grown0 = jnp.exp(score0 - top)
            scale = 1.0 / (jnp.sum(grown, -1, keepdims=True) + grown0)
            cprob = grown * scale
            cprob0 = grown0 * scale
            cprob_out[rows, :] = cprob
            cprob0_out[rows, :] = jnp.broadcast_to(cprob0, (HEADS, 128))
            z_out[rows, :] = nn(cprob.astype(BF), norm_out[n]) + cprob0 * token
        cheads = nt(z_out[...].astype(BF), part(wcls, 2 * shard, shard)) * head_mask(images)
        cheads = cheads.reshape(images, HEADS, D).sum(1)
        for piece in range(3):
            card_out[pl.ds(piece, images, stride=4), :] = cheads[:, 128 * piece : 128 * piece + 128]
        wcls_out[...] = wcls[...]
        gather_up.finish()
        gather_down.finish()


def card_token_kernel(n_dp, n_mp, group, card, vec, aux, *rest):
    far, outs, scratch = rest[:8], rest[8:18], rest[18:]
    dch_all, gout_all, gup_all, gdown_all, cards, slots, dp_sem, mp_sem, load_sem = scratch[:9]
    here = scratch[9:]
    loads = [
        pltpu.make_async_copy(far[i], here[i], load_sem.at[i]) for i in range(len(far))
    ]
    for copy in loads:
        copy.start()
    share_cards(n_dp, n_mp, card, cards, slots, dp_sem, mp_sem)
    for copy in loads:
        copy.wait()
    token_kernel(
        group, cards, vec, *here, aux, *outs, dch_all, gout_all, gup_all, gdown_all
    )


def token_kernel(
    group, cards, vec, wcls, wup_rows, wdown_rows, head, norm, cprob, cprob0, z, aux,
    left_out, right_out, gv_out, local_out, gout_out, gup_out, gdown_out, ghead_out, rows_out,
    stat_out, dch_all, gout_all, gup_all, gdown_all,
):
    hidden = wup_rows.shape[1]
    shard = wcls.shape[1] // 4
    images = cards.shape[0] // 4
    cheads = jnp.concatenate(
        [cards[pl.ds(piece, images, stride=4), :] for piece in range(3)], 1
    ).astype(BF)
    card = cards[pl.ds(3, images, stride=4), :]
    labels = (card[:, 0:1] * 32.0 + card[:, 1:2]).astype(jnp.int32)
    pairs = (card[:, 2:3] * 32.0 + card[:, 3:4]).astype(jnp.int32)
    column = lax.broadcasted_iota(jnp.int32, (images, images), 1)
    row = lax.broadcasted_iota(jnp.int32, (images, images), 0)
    slot = lax.rem(lax.broadcasted_iota(jnp.int32, (images, 1), 0), group).astype(F32)
    okay = (slot >= group - card[:, 4:5]).astype(F32)
    okay_row = colsum(jnp.where(row == column, okay, 0.0))
    wo = part(wcls, 3 * shard, shard)
    wup = part(wup_rows, 0, hidden)
    wdown = part(wdown_rows, 0, hidden)
    count = jnp.sum(okay, keepdims=True)
    raw = nn(cheads, wo) + vec[10:11, :]
    branch = vec[11:12, :] * raw
    middle = vec[17:18, :] + branch
    unit2, inverse2 = normalize(middle)
    normed = (unit2 * vec[12:13, :] + vec[13:14, :]).astype(BF)
    inner = nt(normed, wup)
    active, slope = gelu_parts(inner)
    active = active.astype(BF)
    down = nn(active, wdown) + vec[14:15, :]
    mlp_branch = vec[15:16, :] * down
    token = middle + mlp_branch
    unit3, inverse3 = normalize(token)
    feature = unit3 * vec[18:19, :] + vec[19:20, :]
    feature_low = feature.astype(BF)
    logits = nt(feature_low, head[...])
    top = jnp.max(logits, -1, keepdims=True)
    grown = jnp.exp(logits - top)
    total = jnp.sum(grown, -1, keepdims=True)
    hot = lax.broadcasted_iota(jnp.int32, logits.shape, 1) == labels
    cross = jnp.log(total) + top - jnp.sum(jnp.where(hot, logits, 0.0), -1, keepdims=True)
    share = okay / count
    dlogits = (share * (grown / total - hot.astype(F32))).astype(BF)
    classes = head.shape[0]
    ghead = tn(dlogits, feature_low)
    ghead_out[0:8, :] = jnp.zeros((8, D), F32)
    ghead_out[classes:, :] = jnp.zeros((8, D), F32)
    ghead_out[4 : classes + 4, :] = ghead
    replicated_sq = colsum(ghead * ghead)
    dfeature = nn(dlogits, head[...])

    length = lax.rsqrt(jnp.sum(feature * feature, -1, keepdims=True) + NORM_EPS)
    embed = (feature * length).astype(BF)
    sims = nt(embed, embed) / TEMP
    sims = jnp.where((okay_row > 0) & (row != column), sims, MASKED)
    top = jnp.max(sims, -1, keepdims=True)
    grown = jnp.exp(sims - top)
    total = jnp.sum(grown, -1, keepdims=True)
    hot = column == pairs
    contrast = jnp.log(total) + top - jnp.sum(jnp.where(hot, sims, 0.0), -1, keepdims=True)
    dsims = share * (grown / total - hot.astype(F32))
    high = dsims.astype(BF)
    low = (dsims - high.astype(F32)).astype(BF)
    dembed = (nn(high, embed) + nn(low, embed) + tn(high, embed) + tn(low, embed)) / TEMP
    dfeature += length * dembed - feature * (
        length * length * length * jnp.sum(dembed * feature, -1, keepdims=True)
    )

    dtoken = normalize_back(unit3, inverse3, vec[18:19, :], dfeature)
    rows_out[0:1, :] = jnp.zeros((1, D), F32)
    rows_out[1:2, :] = jnp.zeros((1, D), F32)
    rows_out[7:8, :] = colsum(dtoken * down)
    rows_out[6:7, :] = vec[15:16, :] * colsum(dtoken)
    ddown = (dtoken * vec[15:16, :]).astype(BF)
    gdown = tn(active, ddown)
    own_f = pl.multiple_of(lax.axis_index("mp") * hidden, hidden)
    gdown_all[...] = gdown
    gdown_out[...] = gdown_all[pl.ds(own_f, hidden), :]
    replicated_sq += colsum(gdown * gdown)
    dinner = (nt(ddown, wdown) * slope).astype(BF)
    gup = tn(dinner, normed)
    gup_all[...] = gup
    gup_out[...] = gup_all[pl.ds(own_f, hidden), :]
    replicated_sq += colsum(gup * gup)
    dnormed = nn(dinner, wup)
    rows_out[4:5, :] = colsum(dnormed * unit2)
    rows_out[5:6, :] = colsum(dnormed)
    dmiddle = dtoken + normalize_back(unit2, inverse2, vec[12:13, :], dnormed)
    rows_out[3:4, :] = colsum(dmiddle * raw)
    rows_out[2:3, :] = vec[11:12, :] * colsum(dmiddle)
    rows_out[8:9, :] = colsum(dmiddle)
    rows_out[9:10, :] = colsum(dfeature * unit3)
    rows_out[10:11, :] = colsum(dfeature)
    dbranch = (dmiddle * vec[11:12, :]).astype(BF)
    gout = tn(cheads, dbranch)
    gout_all[...] = gout
    own_h = pl.multiple_of(lax.axis_index("mp") * shard, shard)
    gout_out[...] = gout_all[pl.ds(own_h, shard), :]
    replicated_sq += colsum(gout * gout)
    dch_all[...] = nt(dbranch, wo)
    local = norm.shape[0]
    place = lax.axis_index("dp") * lax.axis_size("mp") + lax.axis_index("mp")
    if local % 8 == 0:
        dch = dch_all[pl.ds(pl.multiple_of(place * local, local), local), :]
    else:
        share_of = 8 // local
        start = pl.multiple_of(lax.div(place, share_of) * 8, 8)
        window = dch_all[pl.ds(start, 8), :]
        pick = lax.rem(place, share_of)
        dch = sum(
            jnp.where(pick == i, window[i * local : (i + 1) * local, :], 0.0)
            for i in range(share_of)
        )

    keys = aux[0:8, :]
    class_row = aux[8:16, :]
    mask = head_mask()
    spread = jnp.concatenate([mask * dch[n : n + 1, :] for n in range(local)], 0).astype(BF)
    dz = nn(spread, part(wcls, 2 * shard, shard))
    dz_low = dz.astype(BF)
    probs = cprob[...]
    prob0 = cprob0[...][:, 0:1]
    class_rows = jnp.concatenate([class_row] * local, 0)
    dprobs = jnp.concatenate(
        [nt(dz_low[n * HEADS : (n + 1) * HEADS, :], norm[n]) for n in range(local)], 0
    )
    dprob0 = jnp.sum(dz * class_rows, -1, keepdims=True)
    inside = jnp.sum(dprobs * probs, -1, keepdims=True) + dprob0 * prob0
    dscores = (probs * (dprobs - inside)).astype(BF)
    dscore0 = prob0 * (dprob0 - inside)
    gv_out[...] = tn(spread, z[...].astype(BF))
    local_out[0:8, :] = jnp.zeros((8, D), F32)
    dkeys = jnp.zeros((HEADS, D), F32)
    from_class = jnp.zeros((1, D), F32)
    for n in range(local):
        rows = slice(n * HEADS, (n + 1) * HEADS)
        dkeys += nn(dscores[rows, :], norm[n]) + dscore0[rows, :] * class_row
        from_class += colsum(prob0[rows, :] * dz[rows, :] + dscore0[rows, :] * keys)
        left_out[n] = jnp.concatenate([probs[rows, :].astype(BF), dscores[rows, :]], 0)
        right_out[n] = jnp.concatenate([dz_low[rows, :], keys.astype(BF)], 0)
    local_out[6:7, :] = from_class
    local_out[8:16, :] = dkeys
    lane = lax.broadcasted_iota(jnp.int32, (1, 128), 1)
    self_sums = colsum(card)
    count_tokens = self_sums[:, 5:6]

    def squares(values):
        return jnp.sum(colsum(values * values * okay), keepdims=True)

    entries = [jnp.sum(okay * cross, keepdims=True), jnp.sum(okay * contrast, keepdims=True)]
    entries += [count, count_tokens]
    entries += [
        jnp.sqrt((self_sums[:, i : i + 1] + self_sums[:, i + 1 : i + 2]) / D / count_tokens)
        for i in (8, 10, 12, 14)
    ]
    entries += [
        jnp.sqrt(squares(item) / D / count) for item in (branch, middle, mlp_branch, token)
    ]
    line = jnp.zeros((1, 128), F32)
    for i, entry in enumerate(entries):
        line = jnp.where(lane == i, entry, line)
    stat_out[0:1, :] = line
    stat_out[1:8, :] = jnp.broadcast_to(
        replicated_sq[:, 0:128] + replicated_sq[:, 128:256] + replicated_sq[:, 256:384], (7, 128)
    )


def feed_back_kernel(
    left, right, gv, local_rows, patch, mid, raw, act, slope, vec, wmlp,
    dmid_out, gfeed_out, rows_out, gmlp_out,
):
    hidden = wmlp.shape[1] // 2
    count = wmlp.shape[0]
    shard = D // count

    @pl.when(pl.program_id(0) == 0)
    def _():
        gmlp_out[...] = jnp.zeros_like(gmlp_out)
        rows_out[...] = local_rows[...]

    unit, inverse = normalize(patch[0])
    dnormed = tn(left[0], right[0])[:P_SIZE, :]
    rows_out[4:5, :] += colsum(dnormed * unit)
    rows_out[5:6, :] += colsum(dnormed)
    incoming = normalize_back(unit, inverse, vec[8:9, :], dnormed)

    unit, inverse = normalize(mid[0])
    normed = (unit * vec[4:5, :] + vec[5:6, :]).astype(BF)
    rows_out[3:4, :] += colsum(incoming * (raw[0].astype(F32) + vec[6:7, :]))
    rows_out[2:3, :] += vec[7:8, :] * colsum(incoming)
    ddown = (incoming * vec[7:8, :]).astype(BF)
    gmlp_out[:, hidden:, :] += tn(act[0], ddown).reshape(count, hidden, D)
    dinner = (nt(ddown, part(wmlp, hidden, hidden)) * slope[0].astype(F32)).astype(BF)
    gmlp_out[:, :hidden, :] += tn(dinner, normed).reshape(count, hidden, D)
    dnormed = nn(dinner, part(wmlp, 0, hidden))
    rows_out[0:1, :] += colsum(dnormed * unit)
    rows_out[1:2, :] += colsum(dnormed)
    dmid_out[0] = incoming + normalize_back(unit, inverse, vec[4:5, :], dnormed)

    @pl.when(pl.program_id(0) == pl.num_programs(0) - 1)
    def _():
        used = 2 * hidden + shard
        gfeed_out[:, : 2 * hidden, :] = gmlp_out[...].astype(BF)
        gfeed_out[:, 2 * hidden : used, :] = gv[...].astype(BF).reshape(count, shard, D)
        if used < gfeed_out.shape[1]:
            gfeed_out[:, used:, :] = jnp.zeros((count, gfeed_out.shape[1] - used, D), BF)


def self_back_kernel(
    n_dp, n_mp, dmid, pixels, embed, q, k, v, prob, post, ho, raw, vec, wattn, t1row, t2row, gfeed,
    gattn_out, gpix_out, gpos_out, rows_out, run_a_out, run_b_out,
    dx_all, dx_rows, stack_q, stack_h, slopes, run_a, run_b, hand_sem_a, hand_sem_b, *sum_buffers,
):
    shard = wattn.shape[1] // 4
    count = wattn.shape[0]
    images = dx_all.shape[0]
    place = Place(n_dp, n_mp)
    rows_a, _ = halves(gfeed.shape[1], n_dp)
    sum_a = ShardSum(place, gfeed, 0, True, *sum_buffers[:SUM_BUFFERS])
    sum_b = ShardSum(place, gfeed, rows_a, False, *sum_buffers[SUM_BUFFERS:])
    hand_a = HandHigh(place, run_a, hand_sem_a)
    hand_b = HandHigh(place, run_b, hand_sem_b)

    def beside(step, *stages):
        @pl.when(pl.program_id(0) == step)
        def _():
            for stage in stages:
                stage()

    @pl.when(pl.program_id(0) == 0)
    def _():
        gattn_out[...] = jnp.zeros_like(gattn_out)
        gpos_out[...] = jnp.zeros_like(gpos_out)
        rows_out[...] = jnp.zeros_like(rows_out)
        stack_q[...] = jnp.zeros_like(stack_q)
        stack_h[...] = jnp.zeros_like(stack_h)
        greet(place.near_partners() + place.dp_partners())()
        sum_a.start()
        sum_b.start()

    beside(1, sum_a.second, sum_b.second)
    beside(images * 3 // 8, sum_a.third, sum_b.third)
    beside(images // 2, sum_a.fourth, sum_b.fourth)

    wq = part(wattn, 0, shard)
    wk = part(wattn, shard, shard)
    wv = part(wattn, 2 * shard, shard)
    wo = part(wattn, 3 * shard, shard)
    incoming = dmid[0]
    rows_out[3:4, :] += colsum(incoming * (raw[0].astype(F32) + vec[2:3, :]))
    rows_out[2:3, :] += vec[3:4, :] * colsum(incoming)
    dbranch = (incoming * vec[3:4, :]).astype(BF)
    gattn_out[:, 3 * shard :, :] += tn(ho[0], dbranch).reshape(count, shard, D)
    dheads = nt(dbranch, wo).astype(BF).astype(F32)

    unit, inverse = normalize(embed[0])
    normed = (unit * vec[0:1, :] + vec[1:2, :]).astype(BF)
    beside(
        images * 3 // 4,
        lambda: hand_a.start(sum_a.finish()),
        lambda: hand_b.start(sum_b.finish()),
    )

    q_wide = q[0].astype(F32)
    stack_heads(stack_q, q_wide, t1row)
    stack_heads(stack_h, dheads, t2row)
    slopes[...] = nt(v[0], stack_h[...])
    dv = nn(prob[0], stack_h[...]).astype(BF)
    for first in range(0, HEADS * PAD, 128):
        at = slice(first, first + 128)
        chance = prob[0, :, at].astype(F32)
        dprob = slopes[:, at]
        slopes[:, at] = chance * (dprob - colsum(dprob * chance))
    dmixed = slopes[...].astype(BF)
    dk = nn(dmixed, stack_q[...]).astype(BF)
    dpre = tn(dmixed, k[0])
    dq = jnp.zeros(q_wide.shape, F32)
    for g in range(HEADS):
        rows = slice(g * PAD, g * PAD + P_SIZE)
        dq += dpre[rows, :] * t1row[g : g + 1, :]
        rows_out[8 + g : 9 + g, :] += colsum(q_wide * dpre[rows, :])
        rows_out[16 + g : 17 + g, :] += colsum(dheads * post[0, rows, :].astype(F32))
    dq = dq.astype(BF)
    gattn_out[:, :shard, :] += tn(dq, normed).reshape(count, shard, D)
    gattn_out[:, shard : 2 * shard, :] += tn(dk, normed).reshape(count, shard, D)
    gattn_out[:, 2 * shard : 3 * shard, :] += tn(dv, normed).reshape(count, shard, D)
    dnormed = nn(dq, wq) + nn(dk, wk) + nn(dv, wv)
    rows_out[0:1, :] += colsum(dnormed * unit)
    rows_out[1:2, :] += colsum(dnormed)
    dx = incoming + normalize_back(unit, inverse, vec[0:1, :], dnormed)
    gpos_out[...] += dx
    dx_all[pl.program_id(0)] = dx

    @pl.when(pl.program_id(0) == pl.num_programs(0) - 1)
    def _():
        for n in range(images):
            dx_rows[:, n, :] = dx_all[n]
        gpix_out[...] = tn(pixels[...], dx_rows[...].reshape(pixels.shape[0], D).astype(BF))
        for item in (hand_a, hand_b):
            item.arrive()
        run_a_out[...] = run_a[...]
        run_b_out[...] = run_b[...]
        for item in (sum_a, sum_b, hand_a, hand_b):
            item.wait_sends()


def per_image(*tail):
    return pl.BlockSpec((1, *tail), lambda n: (n, *(0 for _ in tail)))


def constant(*shape):
    return pl.BlockSpec(shape, lambda n: tuple(0 for _ in shape))


def shaped(*shape, dtype=F32):
    return jax.ShapeDtypeStruct(shape, dtype)


def params():
    return pltpu.CompilerParams(vmem_limit_bytes=VMEM_LIMIT, dimension_semantics=("arbitrary",))


def remote_params(collective_id):
    return pltpu.CompilerParams(
        vmem_limit_bytes=VMEM_LIMIT, dimension_semantics=("arbitrary",),
        collective_id=collective_id, has_side_effects=True,
    )


def run_self_attend(n_dp, n_mp, embed, cols, vec, wattn, t1row, t2row, mlp_rows):
    count = embed.shape[0]
    rows = per_image(P_SIZE, D)
    low = shaped(count, P_SIZE, D, dtype=BF)
    return pl.pallas_call(
        functools.partial(self_attend_kernel, n_dp, n_mp),
        grid=(count,),
        in_specs=[
            rows, constant(*cols.shape), constant(*vec.shape),
            constant(*wattn.shape), constant(HEADS, D), constant(HEADS, D),
            constant(*mlp_rows.shape),
        ],
        out_specs=[
            rows, rows, rows, per_image(P_SIZE, HEADS * PAD), per_image(HEADS * PAD, D),
            rows, rows, rows, per_image(1, 128), ANY,
        ],
        out_shape=[
            low, low, low, shaped(count, P_SIZE, HEADS * PAD, dtype=BF),
            shaped(count, HEADS * PAD, D, dtype=BF), low, low,
            shaped(count, P_SIZE, D), shaped(count, 1, 128),
            shaped(n_mp, *mlp_rows.shape, dtype=BF),
        ],
        scratch_shapes=[pltpu.VMEM((HEADS * PAD, D), BF), pltpu.VMEM((P_SIZE, HEADS * PAD), F32)]
        + gather_scratch(n_mp),
        compiler_params=remote_params(6),
        name="self_attend",
    )(embed, cols, vec, wattn, t1row, t2row, mlp_rows)


def run_feed(n_dp, n_mp, mid, cols, bias_row, base, stat, vec, wmlp, cls_rows, up_rows, down_rows):
    count = mid.shape[0]
    wide = 2 * wmlp.shape[0] * wmlp.shape[1] // 4
    return pl.pallas_call(
        functools.partial(feed_kernel, n_dp, n_mp),
        grid=(count,),
        in_specs=[
            per_image(P_SIZE, D), constant(*cols.shape), constant(1, count * WIDE),
            constant(*base.shape), per_image(1, 128), constant(*vec.shape), constant(*wmlp.shape),
            constant(*cls_rows.shape), constant(*up_rows.shape), constant(*down_rows.shape),
        ],
        out_specs=[
            per_image(P_SIZE, D), per_image(P_SIZE, wide), per_image(P_SIZE, wide),
            per_image(P_SIZE, D), constant(count, WIDE, D), constant(count * HEADS, WIDE),
            constant(count * HEADS, 128), constant(count * HEADS, D), constant(4 * count, 128),
            constant(24, D), constant(n_mp, *cls_rows.shape), ANY, ANY,
        ],
        out_shape=[
            shaped(count, P_SIZE, D), shaped(count, P_SIZE, wide, dtype=BF),
            shaped(count, P_SIZE, wide, dtype=BF), shaped(count, P_SIZE, D, dtype=BF),
            shaped(count, WIDE, D, dtype=BF), shaped(count * HEADS, WIDE),
            shaped(count * HEADS, 128), shaped(count * HEADS, D), shaped(4 * count, 128),
            shaped(24, D), shaped(n_mp, *cls_rows.shape, dtype=BF),
            shaped(n_mp, *up_rows.shape, dtype=BF), shaped(n_mp, *down_rows.shape, dtype=BF),
        ],
        scratch_shapes=[pltpu.VMEM((n_mp, *cls_rows.shape), BF)] + spread_scratch(n_dp, n_mp) * 3,
        compiler_params=remote_params(7),
        name="feed",
    )(mid, cols, bias_row, base, stat, vec, wmlp, cls_rows, up_rows, down_rows)


def run_token(n_dp, n_mp, group, card, vec, aux, wcls, wup, wdown, head, norm, cprob, cprob0, z):
    rows = card.shape[0]
    local = norm.shape[0]
    images = n_dp * n_mp * local
    hidden = wup.shape[1]
    shard = wcls.shape[1] // 4
    wide = wup.shape[0] * hidden
    dma = pltpu.SemaphoreType.DMA
    far = (wcls, wup, wdown, head, norm, cprob, cprob0, z)
    return pl.pallas_call(
        functools.partial(card_token_kernel, n_dp, n_mp, group),
        in_specs=[WHOLE] * 3 + [ANY] * 8,
        out_specs=[WHOLE] * 10,
        out_shape=[
            shaped(local, 2 * HEADS, WIDE, dtype=BF), shaped(local, 2 * HEADS, D, dtype=BF),
            shaped(D, D), shaped(16, D), shaped(shard, D), shaped(hidden, D), shaped(hidden, D),
            shaped(head.shape[0] + 8, D), shaped(16, D), shaped(8, 128),
        ],
        scratch_shapes=[
            pltpu.VMEM((images, D), F32), pltpu.VMEM((D, D), F32), pltpu.VMEM((wide, D), F32),
            pltpu.VMEM((wide, D), F32), pltpu.VMEM((n_dp * n_mp * rows, 128), F32),
            pltpu.VMEM((n_dp * n_mp * rows, 128), BF), dma((2, n_dp)), dma((2, n_mp)), dma((8,)),
        ]
        + [pltpu.VMEM(item.shape, item.dtype) for item in far],
        compiler_params=pltpu.CompilerParams(
            vmem_limit_bytes=VMEM_LIMIT, collective_id=1, has_side_effects=True
        ),
        name="token_net",
    )(card, vec, aux, *far)


def run_feed_back(n_dp, left, right, gv, local_rows, patch, mid, raw, act, slope, vec, wmlp):
    count = mid.shape[0]
    wide = act.shape[2]
    feed = (wmlp.shape[0], pad_rows(wmlp.shape[1] + D // wmlp.shape[0], n_dp), D)
    return pl.pallas_call(
        feed_back_kernel,
        grid=(count,),
        in_specs=[
            per_image(2 * HEADS, WIDE), per_image(2 * HEADS, D), constant(D, D), constant(16, D),
            per_image(P_SIZE, D), per_image(P_SIZE, D), per_image(P_SIZE, D),
            per_image(P_SIZE, wide), per_image(P_SIZE, wide), constant(*vec.shape),
            constant(*wmlp.shape),
        ],
        out_specs=[per_image(P_SIZE, D), constant(*feed), constant(16, D)],
        out_shape=[shaped(count, P_SIZE, D), shaped(*feed, dtype=BF), shaped(16, D)],
        scratch_shapes=[pltpu.VMEM(wmlp.shape, F32)],
        compiler_params=params(),
        name="feed_back",
    )(left, right, gv, local_rows, patch, mid, raw, act, slope, vec, wmlp)


def run_self_back(
    n_dp, n_mp, dmid, pixels, embed, q, k, v, prob, post, ho, raw, vec, wattn, t1row, t2row, gfeed
):
    count = dmid.shape[0]
    rows_a, rows_b = halves(gfeed.shape[1], n_dp)
    n_lo = 2 if n_dp < 16 else 4
    return pl.pallas_call(
        functools.partial(self_back_kernel, n_dp, n_mp),
        grid=(count,),
        in_specs=[
            per_image(P_SIZE, D), constant(*pixels.shape), per_image(P_SIZE, D),
            per_image(P_SIZE, D), per_image(P_SIZE, D), per_image(P_SIZE, D),
            per_image(P_SIZE, HEADS * PAD), per_image(HEADS * PAD, D), per_image(P_SIZE, D),
            per_image(P_SIZE, D), constant(*vec.shape), constant(*wattn.shape), constant(HEADS, D),
            constant(HEADS, D), constant(*gfeed.shape),
        ],
        out_specs=[
            constant(*wattn.shape), constant(PIX, D), constant(P_SIZE, D), constant(24, D),
            constant(rows_a // n_lo, D), constant(rows_b // n_lo, D),
        ],
        out_shape=[
            shaped(*wattn.shape), shaped(PIX, D), shaped(P_SIZE, D), shaped(24, D),
            shaped(rows_a // n_lo, D, dtype=BF), shaped(rows_b // n_lo, D, dtype=BF),
        ],
        scratch_shapes=[
            pltpu.VMEM((count, P_SIZE, D), F32), pltpu.VMEM((P_SIZE, count, D), F32),
            pltpu.VMEM((HEADS * PAD, D), BF), pltpu.VMEM((HEADS * PAD, D), BF),
            pltpu.VMEM((P_SIZE, HEADS * PAD), F32),
            pltpu.VMEM((rows_a // n_lo, D), BF), pltpu.VMEM((rows_b // n_lo, D), BF),
            pltpu.SemaphoreType.DMA((2, n_dp // n_lo)), pltpu.SemaphoreType.DMA((2, n_dp // n_lo)),
        ]
        + sum_scratch(n_dp, n_mp, rows_a, True)
        + sum_scratch(n_dp, n_mp, rows_b, False),
        compiler_params=pltpu.CompilerParams(
            vmem_limit_bytes=VMEM_LIMIT, dimension_semantics=("arbitrary",), collective_id=5,
            has_side_effects=True,
        ),
        name="self_back",
    )(dmid, pixels, embed, q, k, v, prob, post, ho, raw, vec, wattn, t1row, t2row, gfeed)


def share_cards(n_dp, n_mp, card, out, slots, dp_sem, mp_sem):
    dp = lax.axis_index("dp")
    mp = lax.axis_index("mp")
    rows = card.shape[0]
    barrier = pltpu.get_barrier_semaphore()
    others_dp = [(lax.rem(dp + step, n_dp), mp) for step in range(1, n_dp)]
    others_mp = [(dp, lax.rem(mp + step, n_mp)) for step in range(1, n_mp)]
    for partner in others_dp + others_mp:
        pl.semaphore_signal(barrier, inc=1, device_id=partner, device_id_type=MESH)
    own = tile_rows(slots, (mp * n_dp + dp) * rows, rows)
    slots[pl.ds(pl.multiple_of((mp * n_dp + dp) * rows, 16), rows), :] = card[...].astype(BF)
    pl.semaphore_wait(barrier, n_dp + n_mp - 2)
    sends = [
        remote(own, own, dp_sem.at[0, step], dp_sem.at[1, step], others_dp[step - 1])
        for step in range(1, n_dp)
    ]
    for copy in sends:
        copy.start()
    for step in range(1, n_dp):
        source = lax.rem(dp + n_dp - step, n_dp)
        theirs = tile_rows(slots, (mp * n_dp + source) * rows, rows)
        remote(own, theirs, dp_sem.at[0, step], dp_sem.at[1, step], (source, mp)).wait_recv()
    slab = tile_rows(slots, mp * n_dp * rows, n_dp * rows)
    for step in range(1, n_mp):
        sends.append(
            remote(slab, slab, mp_sem.at[0, step], mp_sem.at[1, step], others_mp[step - 1])
        )
        sends[-1].start()
    for step in range(1, n_mp):
        source = lax.rem(mp + n_mp - step, n_mp)
        theirs = tile_rows(slots, source * n_dp * rows, n_dp * rows)
        remote(slab, theirs, mp_sem.at[0, step], mp_sem.at[1, step], (dp, source)).wait_recv()
    for i in range(n_dp):
        for j in range(n_mp):
            to, source = (i * n_mp + j) * rows, (j * n_dp + i) * rows
            out[to : to + rows, :] = slots[source : source + rows, :].astype(F32)
    for copy in sends:
        copy.wait_send()


def start_kernel(
    n_dp, n_mp, group, attn_in, attn_out, mlp_in, mlp_out, pixels, tables, vec, mix, mask,
    counts, labels, pairs,
    out, mlp_rows, cls_rows, up_rows, down_rows, embed_out, head_out, t1_out, t2_out, cols_out, bias_out, base_out,
    head_rows, wide_up, wide_down, shard, wide_in, wide_out, patch_rows, pos_rows, by_patch, near_send, near_recv, far_send, far_recv, load_sem,
):
    dp = lax.axis_index("dp")
    mp = lax.axis_index("mp")
    n_y = n_mp // 2
    y = lax.div(mp, 2)
    core = lax.rem(mp, 2)
    sibling = (dp, y * 2 + 1 - core)
    load_patch = pltpu.make_async_copy(tables.at[pl.ds(0, PIX)], patch_rows, load_sem.at[0])
    load_pos = pltpu.make_async_copy(tables.at[pl.ds(PIX, 200)], pos_rows, load_sem.at[1])
    load_in = pltpu.make_async_copy(attn_in, wide_in, load_sem.at[2])
    load_out = pltpu.make_async_copy(attn_out, wide_out, load_sem.at[3])
    load_up = pltpu.make_async_copy(mlp_in, wide_up, load_sem.at[5])
    load_down = pltpu.make_async_copy(mlp_out, wide_down, load_sem.at[6])
    load_in.start()
    load_out.start()
    load_patch.start()
    load_pos.start()
    classes = head_out.shape[0]
    load_head = pltpu.make_async_copy(
        tables.at[pl.ds(PIX + P_SIZE - 4, classes + 4)], head_rows, load_sem.at[4]
    )
    load_up.start()
    load_down.start()
    load_head.start()
    barrier = pltpu.get_barrier_semaphore()
    pl.semaphore_signal(barrier, inc=1, device_id=sibling, device_id_type=MESH)
    for step in range(1, n_y):
        pl.semaphore_signal(
            barrier, inc=1, device_id=(dp, lax.rem(y + step, n_y) * 2 + core), device_id_type=MESH
        )
    third = attn_in.shape[1]
    load_in.wait()
    load_out.wait()
    shard[:third, :] = wide_in[0].astype(BF)
    shard[third:, :] = wide_out[0].astype(BF)
    pl.semaphore_wait(barrier, n_y)
    far = [
        remote(
            shard, out.at[mp], far_send.at[step], far_recv.at[step],
            (dp, lax.rem(y + step, n_y) * 2 + core),
        )
        for step in range(1, n_y)
    ]
    for copy in far:
        copy.start()
    near = [remote(shard, out.at[mp], near_send.at[0], near_recv.at[0], sibling)]
    near[0].start()
    out[pl.ds(mp, 1)] = shard[...][None]

    cls_rows[:third, :] = wide_in[1].astype(BF)
    cls_rows[third:, :] = wide_out[1].astype(BF)
    hidden = mlp_rows.shape[0] // 2
    load_up.wait()
    load_down.wait()
    mlp_rows[:hidden, :] = wide_up[0].T.astype(BF)
    mlp_rows[hidden:, :] = wide_down[0].astype(BF)
    up_rows[...] = wide_up[1].T.astype(BF)
    down_rows[...] = wide_down[1].astype(BF)

    images = mask.shape[0]
    lane = lax.broadcasted_iota(jnp.int32, (1, 128), 1)
    keep = (mask[...] > 0).astype(F32)
    bias = (1.0 - keep) * MASKED
    count = counts[0]
    okays = []
    bias_out[...] = jnp.full(bias_out.shape, MASKED, F32)
    for n in range(images):
        okays.append((jnp.full((1, 1), mp * images + n, jnp.int32) >= group - count).astype(F32))
        bias_out[:, n * WIDE : n * WIDE + P_SIZE] = bias[n : n + 1, :]
        tokens = jnp.sum(keep[n : n + 1, :], 1, keepdims=True) * okays[n]
        entries = (
            lax.div(labels[n], 32), lax.rem(labels[n], 32), lax.div(pairs[n], 32),
            lax.rem(pairs[n], 32), count,
        )
        line = jnp.where(lane == len(entries), tokens, 0.0)
        for place, entry in enumerate(entries):
            line = jnp.where(lane == place, entry.astype(F32), line)
        base_out[n : n + 1, :] = line
    cols_out[...] = jnp.concatenate([bias, keep * jnp.concatenate(okays, 0)], 0).T
    heads = head_mask()
    exact = functools.partial(
        lax.dot_general, preferred_element_type=F32, precision=lax.Precision.HIGHEST
    )
    t1_out[...] = exact(mix[0], heads, (((1,), (0,)), ((), ()))) * SCALE
    t2_out[...] = exact(mix[1], heads, (((0,), (0,)), ((), ())))

    load_patch.wait()
    wp = patch_rows[...].astype(BF)
    local = embed_out.shape[0]
    half = P_SIZE // 2
    for place in range(2):
        rows = slice(place * half * local, (place + 1) * half * local)
        by_patch[place * half : (place + 1) * half] = nn(pixels[rows, :], wp).reshape(half, local, D)

    for step in range(1, n_y):
        source = lax.rem(y + n_y - step, n_y) * 2
        slot = source + core
        remote(
            shard, out.at[slot], far_send.at[step], far_recv.at[step], (dp, slot)
        ).wait_recv()
        copy = remote(
            out.at[slot], out.at[slot], near_send.at[step], near_recv.at[step], sibling
        )
        copy.start()
        near.append(copy)
    load_pos.wait()
    offset = pos_rows[:P_SIZE, :] + vec[16:17, :]
    for n in range(local):
        embed_out[n] = by_patch[:, n, :] + offset
    load_head.wait()
    head_out[...] = head_rows[4:, :].astype(BF)
    for copy in far:
        copy.wait_send()
    for step in range(n_y):
        slot = lax.rem(y + n_y - step, n_y) * 2 + 1 - core
        near[step].wait_send()
        remote(
            out.at[slot], out.at[slot], near_send.at[step], near_recv.at[step], sibling
        ).wait_recv()


def run_start(
    n_dp, n_mp, group, attn_in, attn_out, mlp_in, mlp_out, pixels, tables, vec, mix, mask, counts,
    labels, pairs,
):
    local = labels.shape[0]
    classes = tables.shape[0] - PIX - P_SIZE
    scalars = pl.BlockSpec(memory_space=pltpu.SMEM)
    n_y = n_mp // 2
    rows = attn_in.shape[1] + attn_out.shape[1]
    hidden = mlp_in.shape[2]
    dma = pltpu.SemaphoreType.DMA
    return pl.pallas_call(
        functools.partial(start_kernel, n_dp, n_mp, group),
        in_specs=[ANY] * 4 + [WHOLE, ANY, WHOLE, WHOLE, WHOLE, scalars, scalars, scalars],
        out_specs=[WHOLE] * 12,
        out_shape=[
            shaped(n_mp, rows, D, dtype=BF), shaped(2 * hidden, D, dtype=BF),
            shaped(rows, D, dtype=BF), shaped(hidden, D, dtype=BF), shaped(hidden, D, dtype=BF),
            shaped(local, P_SIZE, D),
            shaped(classes, D, dtype=BF), shaped(HEADS, D), shaped(HEADS, D),
            shaped(P_SIZE, 2 * local), shaped(1, local * WIDE), shaped(local, 128),
        ],
        scratch_shapes=[
            pltpu.VMEM((classes + 4, D), F32), pltpu.VMEM(mlp_in.shape, F32),
            pltpu.VMEM(mlp_out.shape, F32),
            pltpu.VMEM((rows, D), BF), pltpu.VMEM(attn_in.shape, F32),
            pltpu.VMEM(attn_out.shape, F32), pltpu.VMEM((PIX, D), F32),
            pltpu.VMEM((200, D), F32),
            pltpu.VMEM((P_SIZE, local, D), F32),
            dma((n_y,)), dma((n_y,)), dma((n_y,)), dma((n_y,)), dma((7,)),
        ],
        compiler_params=pltpu.CompilerParams(
            vmem_limit_bytes=VMEM_LIMIT, collective_id=2, has_side_effects=True
        ),
        name="start",
    )(
        attn_in, attn_out, mlp_in, mlp_out, pixels, tables, vec, mix, mask, counts, labels, pairs
    )


def reduce_kernel(
    n_dp, n_mp, gattn, run_a, run_b, gpix, gpos, rows2, rows3,
    block_out, shared_out, square_out,
    blocks, commons, squares, attn_run, sem_a, sem_b, high_sem, low_sem, square_sem, *sum_buffers,
):
    p = Place(n_dp, n_mp)
    attn = ShardSum(p, blocks, 0, True, *sum_buffers[:SUM_BUFFERS])
    table = TableSum(p, commons, shared_out, *sum_buffers[SUM_BUFFERS:])
    rows_a = blocks.shape[1]
    wide = commons.shape[1]
    greeted = greet(p.near_partners() + p.dp_partners())

    used = gattn.shape[1]
    blocks[:, :used, :] = gattn[...].astype(BF)
    if used < rows_a:
        blocks[:, used:, :] = jnp.zeros((n_mp, rows_a - used, D), BF)
    commons[:3] = gpix[...].astype(BF).reshape(3, wide, D)
    commons[3] = jnp.concatenate(
        [
            gpos[...], jnp.zeros((12, D), F32), rows2[...], rows3[...], jnp.zeros((8, D), F32),
        ],
        0,
    ).astype(BF)
    if n_mp > 4:
        commons[4:] = jnp.zeros((n_mp - 4, wide, D), BF)

    rows_feed = p.n_lo * run_a.shape[0]
    hand_a = HandLow(p, block_out, rows_a, rows_feed, sem_a)
    hand_b = HandLow(p, block_out, rows_a + rows_feed, p.n_lo * run_b.shape[0], sem_b)
    hand_high = HandHigh(p, attn_run, high_sem)
    hand_low = HandLow(p, block_out, 0, rows_a, low_sem)

    greeted()
    attn.start()
    table.start()
    attn.second()
    table.near_to_low()
    hand_a.start(run_a[...])
    hand_b.start(run_b[...])
    table.low_to_high()
    attn.third()
    table.high_to_far()
    attn.fourth()
    table.turn()
    table.far_to_high()
    hand_high.start(attn.finish())
    table.high_to_low()
    hand_high.arrive()
    hand_low.start(attn_run[...])
    table.low_to_near()
    sends = []

    for item in (hand_a, hand_b, hand_low):
        item.arrive()
    sums = block_out[...].astype(F32)
    sums = colsum(sums * sums)
    squares[pl.ds(p.mp, 1)] = jnp.broadcast_to(
        sums[:, 0:128] + sums[:, 128:256] + sums[:, 256:384], (8, 128)
    )[None]

    for step in range(1, p.n_y):
        sends.append(
            remote(
                squares.at[p.mp], squares.at[p.mp], square_sem.at[0, step],
                square_sem.at[1, step], (p.dp, p.along_y(step) * 2 + p.core),
            )
        )
        sends[-1].start()
    for step in range(1, p.n_y):
        source = p.along_y(p.n_y - step) * 2 + p.core
        remote(
            squares.at[p.mp], squares.at[source], square_sem.at[0, step], square_sem.at[1, step],
            (p.dp, source),
        ).wait_recv()
    mine = squares[pl.ds(p.core, 1)]
    for y in range(1, p.n_y):
        mine += squares[pl.ds(2 * y + p.core, 1)]
    squares[pl.ds(n_mp + p.core, 1)] = mine
    sends.append(
        remote(
            squares.at[n_mp + p.core], squares.at[n_mp + p.core], square_sem.at[0, 0],
            square_sem.at[1, 0], p.sibling,
        )
    )
    sends[-1].start()
    table.finish()
    remote(
        squares.at[n_mp + p.core], squares.at[n_mp + 1 - p.core], square_sem.at[0, 0],
        square_sem.at[1, 0], p.sibling,
    ).wait_recv()
    square_out[...] = squares[n_mp] + squares[n_mp + 1]
    for copy in sends:
        copy.wait_send()
    for item in (attn, hand_a, hand_b, hand_high, hand_low):
        item.wait_sends()


def run_reduce(n_dp, n_mp, gattn, run_a, run_b, gpix, gpos, rows2, rows3):
    n = n_dp * n_mp
    rows_a = pad_rows(gattn.shape[1], n_dp)
    chunk_s = -(-(PIX + 256) // (16 * n)) * 16
    wide = chunk_s * n_dp
    assert wide == 256
    n_lo = 2 if n_dp < 16 else 4
    dma = pltpu.SemaphoreType.DMA
    return pl.pallas_call(
        functools.partial(reduce_kernel, n_dp, n_mp),
        in_specs=[WHOLE] * 7,
        out_specs=[WHOLE] * 3,
        out_shape=[
            shaped(rows_a + n_lo * (run_a.shape[0] + run_b.shape[0]), D, dtype=BF),
            shaped(n_mp, wide, D, dtype=BF), shaped(8, 128),
        ],
        scratch_shapes=[
            pltpu.VMEM((n_mp, rows_a, D), BF), pltpu.VMEM((n_mp, wide, D), BF),
            pltpu.VMEM((n_mp + 2, 8, 128), F32),
            pltpu.VMEM((rows_a // n_lo, D), BF),
            dma((2, n_lo)), dma((2, n_lo)), dma((2, n_dp // n_lo)), dma((2, n_lo)), dma((2, n_mp)),
        ]
        + sum_scratch(n_dp, n_mp, rows_a, True)
        + table_scratch(n_dp, n_mp, wide),
        compiler_params=pltpu.CompilerParams(
            vmem_limit_bytes=VMEM_LIMIT, collective_id=3, has_side_effects=True
        ),
        name="reduce",
    )(gattn, run_a, run_b, gpix, gpos, rows2, rows3)


def root(values):
    return values * lax.rsqrt(values)


def adam_parts(gradient, mean, square, factor):
    clipped = gradient * factor
    mean_new = BETA_ONE * mean + (1.0 - BETA_ONE) * clipped
    square_new = BETA_TWO * square + (1.0 - BETA_TWO) * clipped * clipped
    direction = (
        mean_new
        * (1.0 / (1.0 - BETA_ONE**STEP))
        / (root(square_new * (1.0 / (1.0 - BETA_TWO**STEP))) + ADAM_EPS)
    )
    return (mean_new, square_new, direction)


def fold(values):
    squares = (values * values).reshape(values.shape[0] // 8, 8, values.shape[1]).sum(0)
    width = values.shape[1]
    if width % 128:
        return jnp.broadcast_to(jnp.sum(squares, 1, keepdims=True), (8, 128)) * (1.0 / 128)
    return sum(squares[:, i : i + 128] for i in range(0, width, 128))


def total(values):
    return jnp.sum(jnp.sum(values, 0, keepdims=True), 1, keepdims=True)


def moment_sweep(factor, grad, w, m, s, u, rows):
    chunk = 32 if rows % 32 == 0 else 16

    def step(i, kept):
        at = pl.ds(pl.multiple_of(i * chunk, chunk), chunk)
        weight = w[at, :]
        mean, second, direction = adam_parts(grad(i, chunk), m[at, :], s[at, :], factor)
        m[at, :] = mean
        s[at, :] = second
        update = direction + DECAY * weight
        u[at, :] = update
        return (kept[0] + fold(weight), kept[1] + fold(update))

    zero = jnp.zeros((8, 128), F32)
    return lax.fori_loop(0, rows // chunk, step, (zero, zero))


def rows_from(ref, first):
    def read(i, chunk):
        at = pl.ds(pl.multiple_of(first + i * chunk, 16), chunk)
        return ref[at, :].astype(F32)

    return read


def moment_kernel(
    n_dp, block, shared, block_sq, gout1, gup1, gdown1, rows1, stat, aux, wcls,
    vec, vec_mean, vec_square, mix, mix_mean, mix_square, *rest,
):
    state = rest[:12]
    outs = rest[12:24]
    (
        vec_out, vec_mean_out, vec_square_out, mix_out, mix_mean_out, mix_square_out,
        misc_out, sums_out,
    ) = rest[24:32]
    held = rest[32:44]
    updates = rest[44:48]
    grad_q, grad_k, grad_flip, load_sem, save_sem = rest[48:]
    loads = [pltpu.make_async_copy(state[i], held[i], load_sem.at[i]) for i in range(12)]
    for copy in loads:
        copy.start()
    mp = lax.axis_index("mp")
    hs = state[3].shape[1]
    fs = state[9].shape[1]
    feed = pad_rows(4 * hs, n_dp)

    rows2 = shared[PIX + 208 : PIX + 224, :].astype(F32)
    rows3 = shared[PIX + 224 : PIX + 256, :].astype(F32)
    token = aux[8:9, :]
    wq = part(wcls, 0, hs)
    wk = part(wcls, hs, hs).astype(F32)
    query = nt(wq, aux[8:16, :].astype(BF))[:, 0:1].astype(BF).astype(F32)
    dkeys = jnp.concatenate(
        [jnp.broadcast_to(rows2[8 + h : 9 + h, :], (HEAD, D)) for h in range(HEADS)], 0
    )
    dquery = SCALE * jnp.sum(wk * dkeys, 1, keepdims=True)
    gq = dquery * token
    gk = (SCALE * query) * dkeys
    grad_q[...] = gq
    grad_k[...] = gk
    dtoken = rows2[6:7, :] + colsum(dquery * wq.astype(F32))
    unit, inverse = normalize(jnp.broadcast_to(vec[17:18, :], (8, D)))
    dcls = normalize_back(unit, inverse, vec[8:9, :], jnp.broadcast_to(dtoken, (8, D)))[0:1, :]
    dgain = rows2[4:5, :] + dtoken * unit[0:1, :]
    last = rows1[...]
    positions = shared[PIX : PIX + 208, :].astype(F32)
    grad_vec = jnp.concatenate(
        [
            rows3[0:4, :], rows2[0:4, :], dgain, rows2[5:6, :] + dtoken, last[2:8, :],
            colsum(positions), last[8:9, :] + dcls, last[9:11, :],
        ],
        0,
    )
    mask = head_mask()
    exact = functools.partial(
        lax.dot_general, dimension_numbers=(((1,), (1,)), ((), ())),
        preferred_element_type=F32, precision=lax.Precision.HIGHEST,
    )
    grad_mix = (exact(rows3[8:16, :], mask) * SCALE, exact(mask, rows3[16:24, :]))

    square = total(block_sq[0:1, :]) + total(stat[1:2, :]) + total(colsum(gq * gq + gk * gk))
    square += total(grad_vec * grad_vec)
    square += total(grad_mix[0] * grad_mix[0]) + total(grad_mix[1] * grad_mix[1])

    def square_rows(i, kept):
        rows = shared[pl.ds(pl.multiple_of(i * 16, 16), 16), :].astype(F32)
        return kept + fold(rows)

    square += total(lax.fori_loop(0, (PIX + 208) // 16, square_rows, jnp.zeros((8, 128), F32)))
    norm = jnp.sqrt(square)
    factor = CLIP / jnp.maximum(norm, CLIP)

    mean, second, direction = adam_parts(grad_vec, vec_mean[...], vec_square[...], factor)
    vec_mean_out[...] = mean
    vec_square_out[...] = second
    vec_out[...] = vec[...] - RATE_VECTOR * direction
    misc = []
    weight_sums = []
    for b in range(2):
        mean, second, direction = adam_parts(grad_mix[b], mix_mean[b], mix_square[b], factor)
        mix_mean_out[b] = mean
        mix_square_out[b] = second
        update = direction + DECAY * mix[b]
        weight_sq = total(mix[b] * mix[b])
        update_sq = total(update * update)
        mix_out[b] = mix[b] - RATE * jnp.sqrt(weight_sq / (update_sq + 1e-12)) * update
        weight_sums.append(weight_sq)
        misc.append(update_sq)

    def sweep(grad, w, m, s, u, rows):
        return moment_sweep(factor, grad, w, m, s, u, rows)

    saves = []

    def save(i, source):
        saves.append(pltpu.make_async_copy(source, outs[i], save_sem.at[i]))
        saves[-1].start()

    sums = []
    own_h = pl.multiple_of(mp * hs, hs)
    for kind in range(4):
        for copy in loads[3 * kind : 3 * kind + 3]:
            copy.wait()
        w, m, s = held[3 * kind : 3 * kind + 3]
        u = updates[kind]
        for b in range(2):
            views = (w.at[b], m.at[b], s.at[b], u.at[b])
            if kind == 0 and b == 0:
                sums.append(sweep(rows_from(block, 0), *views, 3 * hs))
            elif kind == 0:
                pieces = []
                for third, source in enumerate(
                    (
                        rows_from(grad_q, own_h),
                        rows_from(grad_k, own_h),
                        rows_from(block, feed + 2 * fs),
                    )
                ):
                    pieces.append(
                        sweep(
                            source, *(view.at[pl.ds(third * hs, hs)] for view in views), hs
                        )
                    )
                sums.append(
                    tuple(pieces[0][i] + pieces[1][i] + pieces[2][i] for i in range(2))
                )
            elif kind == 1:
                source = rows_from(gout1, 0) if b else rows_from(block, 3 * hs)
                sums.append(sweep(source, *views, hs))
            elif kind == 2:
                if b:
                    grad_flip[...] = gup1[...].T
                else:
                    grad_flip[...] = block[feed : feed + fs, :].astype(F32).T
                sums.append(sweep(rows_from(grad_flip, 0), *views, D))
            else:
                source = rows_from(gdown1, 0) if b else rows_from(block, feed + fs)
                sums.append(sweep(source, *views, fs))
        save(3 * kind, u)
        save(3 * kind + 1, m)
        save(3 * kind + 2, s)
    for place, pair in enumerate(sums):
        sums_out[place : place + 1, :] = colsum(pair[1])
        sums_out[8 + place : 9 + place, :] = colsum(pair[0])

    lane = lax.broadcasted_iota(jnp.int32, (1, 128), 1)
    misc_out[0:1, :] = jnp.broadcast_to(norm, (1, 128))
    weight_line = jnp.zeros((1, 128), F32)
    update_line = jnp.zeros((1, 128), F32)
    for b in range(2):
        weight_line = jnp.where(lane == 11 + b, weight_sums[b], weight_line)
        update_line = jnp.where(lane == 11 + b, misc[b], update_line)
    misc_out[1:2, :] = weight_line
    misc_out[2:3, :] = update_line
    misc_out[3:8, :] = jnp.zeros((5, 128), F32)
    for copy in saves:
        copy.wait()


def table_kernel(misc, shared, ghead, *rest):
    state, outs, misc_out = rest[:3], rest[3:6], rest[6]
    w, m, s, table_update, load_sem, save_sem = rest[7:]
    rows_all = w.shape[0]
    edge = PIX + P_SIZE - 4
    body = (rows_all - edge - 16) // 64 * 32
    middle = edge + 16 + body
    cuts = (0, PIX // 2, PIX, middle, rows_all)
    slabs = [pl.ds(low, high - low) for low, high in zip(cuts, cuts[1:])]
    loads = [
        [
            pltpu.make_async_copy(state[i].at[at], (w, m, s)[i].at[at], load_sem.at[i, place])
            for i in range(3)
        ]
        for place, at in enumerate(slabs)
    ]
    for group in loads:
        for copy in group:
            copy.start()
    factor = CLIP / jnp.maximum(misc[0:1, 0:1], CLIP)
    saves = []

    def arrive(place):
        for copy in loads[place]:
            copy.wait()

    def save(i, place):
        at = slabs[place]
        saves.append(
            pltpu.make_async_copy((w, m, s)[i].at[at], outs[i].at[at], save_sem.at[i, place])
        )
        saves[-1].start()

    def slab(first, count, grad):
        at = slice(first, first + count)
        weight = w[at, :]
        mean, second, direction = adam_parts(grad, m[at, :], s[at, :], factor)
        m[at, :] = mean
        s[at, :] = second
        update = direction + DECAY * weight
        table_update[at, :] = update
        return weight, update

    def run(first, count, source, offset):
        def at(ref, start):
            return ref.at[pl.ds(start, count)]

        return moment_sweep(
            factor, rows_from(source, offset), at(w, first), at(m, first), at(s, first),
            at(table_update, first), count,
        )

    def renew(first, count, rate):
        def step(i, _):
            at = pl.ds(pl.multiple_of(first + i * 32, 16), 32)
            w[at, :] = w[at, :] - rate * table_update[at, :]
            return 0

        lax.fori_loop(0, count // 32, step, 0)

    def rate_of(weight_sq, update_sq):
        return RATE * jnp.sqrt(weight_sq / (update_sq + 1e-12))

    def masked(values, mask):
        return total(jnp.where(mask, values * values, 0.0))

    arrive(0)
    first_half = run(0, PIX // 2, shared, 0)
    save(1, 0)
    save(2, 0)
    arrive(1)
    second_half = run(PIX // 2, PIX // 2, shared, PIX // 2)
    save(1, 1)
    save(2, 1)
    sq_w = [total(first_half[0] + second_half[0])]
    sq_u = [total(first_half[1] + second_half[1])]
    rates = [rate_of(sq_w[0], sq_u[0])]
    renew(0, PIX, rates[0])
    save(0, 0)
    save(0, 1)
    arrive(2)
    place_rows = run(PIX, P_SIZE - 4, shared, PIX)
    tile = lax.broadcasted_iota(jnp.int32, (16, 1), 0) < 4
    weight, update = slab(edge, 16, shared[edge : edge + 16, :].astype(F32) + ghead[0:16, :])
    heads = run(edge + 16, body, ghead, 16)
    save(1, 2)
    save(2, 2)
    arrive(3)
    rest_rows = (rows_all - middle) // 32 * 32
    more_heads = run(middle, rest_rows, ghead, 16 + body)
    left = middle + rest_rows
    tail_weight, tail_update = slab(
        left, rows_all - left, ghead[16 + left - edge - 16 : 16 + rows_all - edge - 16, :]
    )
    save(1, 3)
    save(2, 3)
    sq_w += [
        total(place_rows[0]) + masked(weight, tile),
        total(heads[0] + more_heads[0]) + masked(weight, ~tile) + total(tail_weight * tail_weight),
    ]
    sq_u += [
        total(place_rows[1]) + masked(update, tile),
        total(heads[1] + more_heads[1]) + masked(update, ~tile) + total(tail_update * tail_update),
    ]
    rates += [rate_of(sq_w[i], sq_u[i]) for i in (1, 2)]
    renew(PIX, P_SIZE - 4, rates[1])
    w[edge : edge + 16, :] = weight - jnp.where(tile, rates[1], rates[2]) * update
    renew(edge + 16, body, rates[2])
    save(0, 2)
    renew(middle, rest_rows, rates[2])
    w[left:rows_all, :] = tail_weight - rates[2] * tail_update
    save(0, 3)

    lane = lax.broadcasted_iota(jnp.int32, (1, 128), 1)
    weight_line = misc[1:2, :]
    update_line = misc[2:3, :]
    for place in range(3):
        weight_line = jnp.where(lane == 8 + place, sq_w[place], weight_line)
        update_line = jnp.where(lane == 8 + place, sq_u[place], update_line)
    misc_out[...] = misc[...]
    misc_out[1:2, :] = weight_line
    misc_out[2:3, :] = update_line
    for copy in saves:
        copy.wait()


def run_moments(n_dp, grads, smalls, state):
    outs = [jax.ShapeDtypeStruct(item.shape, F32) for item in state]
    fs = state[9].shape[1]
    dma = pltpu.SemaphoreType.DMA
    return pl.pallas_call(
        functools.partial(moment_kernel, n_dp),
        in_specs=[WHOLE] * (len(grads) + len(smalls)) + [ANY] * 12,
        out_specs=[ANY] * 12 + [WHOLE] * 8,
        out_shape=outs
        + [jax.ShapeDtypeStruct(item.shape, F32) for item in smalls]
        + [shaped(8, 128), shaped(16, 128)],
        scratch_shapes=[pltpu.VMEM(item.shape, F32) for item in state]
        + [pltpu.VMEM(state[3 * kind].shape, F32) for kind in range(4)]
        + [
            pltpu.VMEM((D, D), F32), pltpu.VMEM((D, D), F32), pltpu.VMEM((D, fs), F32),
            dma((12,)), dma((12,)),
        ],
        compiler_params=pltpu.CompilerParams(vmem_limit_bytes=VMEM_LIMIT),
        name="moments",
    )(*grads, *smalls, *state)


def run_tables(misc, shared, ghead, state):
    shape = state[0].shape
    dma = pltpu.SemaphoreType.DMA
    return pl.pallas_call(
        table_kernel,
        in_specs=[WHOLE] * 3 + [ANY] * 3,
        out_specs=[ANY] * 3 + [WHOLE],
        out_shape=[shaped(*shape)] * 3 + [shaped(8, 128)],
        scratch_shapes=[pltpu.VMEM(shape, F32)] * 4 + [dma((3, 4)), dma((3, 4))],
        cost_estimate=pl.CostEstimate(
            flops=40 * shape[0] * shape[1], bytes_accessed=28 * shape[0] * shape[1],
            transcendentals=2 * shape[0] * shape[1],
        ),
        compiler_params=pltpu.CompilerParams(vmem_limit_bytes=VMEM_LIMIT),
        name="tables",
    )(misc, shared, ghead, *state)


def renew_kernel(n_mp, misc, stat, *rest):
    theirs, rest = rest[:n_mp], rest[n_mp:]
    weights, updates = rest[:4], rest[4:8]
    new, copies = rest[8:12], rest[12:16]
    norms, norm_out, stat_out, slots = rest[16:]
    mp = lax.axis_index("mp")
    for step in range(n_mp):
        slots[pl.ds(lax.rem(mp + n_mp - step, n_mp), 1)] = theirs[step][...][None]
    sums = jnp.sum(slots[...], 0)
    rates = []
    lane = lax.broadcasted_iota(jnp.int32, (1, 128), 1)
    weight_line, update_line = misc[1:2, :], misc[2:3, :]
    for place in range(8):
        update_sq = total(sums[place : place + 1, :])
        weight_sq = total(sums[8 + place : 9 + place, :])
        rates.append(RATE * jnp.sqrt(weight_sq / (update_sq + 1e-12)))
        weight_line = jnp.where(lane == place, weight_sq, weight_line)
        update_line = jnp.where(lane == place, update_sq, update_line)
    norms[...] = jnp.sqrt(jnp.concatenate([weight_line, update_line], 0))[:, :13]
    norm_out[...] = misc[0:1, 0:1]
    stat_out[...] = stat[0:1, :12]
    for kind in range(4):
        rows = weights[kind].shape[1]
        chunk = 32 if rows % 32 == 0 else 16
        for b in range(2):
            w, u, out, low = weights[kind], updates[kind], new[kind], copies[kind]
            rate = rates[2 * kind + b]

            def step(i, _, b=b, w=w, u=u, out=out, low=low, rate=rate, chunk=chunk):
                at = pl.ds(pl.multiple_of(i * chunk, chunk), chunk)
                values = w[b, at, :] - rate * u[b, at, :]
                out[b, at, :] = values
                low[b, at, :] = values.astype(BF)
                return 0

            lax.fori_loop(0, rows // chunk, step, 0)


def run_renew(n_mp, misc, stat, sums, weights, updates):
    return pl.pallas_call(
        functools.partial(renew_kernel, n_mp),
        in_specs=[WHOLE] * (10 + n_mp),
        out_specs=[WHOLE] * 11,
        out_shape=[shaped(*item.shape) for item in weights]
        + [shaped(*item.shape, dtype=BF) for item in weights]
        + [shaped(2, 13), shaped(1, 1), shaped(1, 12)],
        scratch_shapes=[pltpu.VMEM((n_mp, 16, 128), F32)],
        compiler_params=pltpu.CompilerParams(vmem_limit_bytes=VMEM_LIMIT),
        name="renew",
    )(misc, stat, *sums, *weights, *updates)


def shards(
    pixels,
    token_mask,
    counts,
    labels,
    pairs,
    attn_in,
    attn_in_mean,
    attn_in_square,
    attn_out,
    attn_out_mean,
    attn_out_square,
    mlp_in,
    mlp_in_mean,
    mlp_in_square,
    mlp_out,
    mlp_out_mean,
    mlp_out_square,
    tables,
    tables_mean,
    tables_square,
    vectors,
    vectors_mean,
    vectors_square,
    talking,
    talking_mean,
    talking_square,
):
    local = pixels.shape[0]
    group = token_mask.shape[0]
    place_mp = lax.axis_index("mp")
    n_mp = lax.axis_size("mp")
    n_dp = lax.axis_size("dp")
    hs = attn_in.shape[3]
    fs = mlp_in.shape[2]

    def as_rows(item):
        return item.transpose(0, 2, 3, 1).reshape(2, 3 * hs, D)

    def from_rows(item):
        return item.reshape(2, 3, hs, D).transpose(0, 3, 1, 2)

    attn_in, attn_in_mean, attn_in_square = map(as_rows, (attn_in, attn_in_mean, attn_in_square))
    pixel_rows = pixels.transpose(1, 0, 2).reshape(P_SIZE * local, PIX)
    mask = lax.dynamic_slice_in_dim(token_mask, place_mp * local, local, 0)
    (
        wattn, mlp_rows, cls_rows, up_rows, down_rows, embed, head, t1row, t2row, cols, bias_row,
        base,
    ) = run_start(
        n_dp, n_mp, group, attn_in, attn_out, mlp_in, mlp_out, pixel_rows, tables, vectors,
        talking, mask, counts, labels, pairs,
    )
    q, k, v, prob, post, ho, raw0, middle, stat_a, wmlp = run_self_attend(
        n_dp, n_mp, embed, cols, vectors, wattn, t1row, t2row, mlp_rows
    )
    patches, act, slope, raw1, norm, cprob, cprob0, z, card, aux, wcls, wup, wdown = run_feed(
        n_dp, n_mp, middle, cols, bias_row, base, stat_a, vectors, wmlp, cls_rows, up_rows,
        down_rows,
    )
    left, right, gv, local_rows, gout1, gup1, gdown1, ghead, rows1, stat = run_token(
        n_dp, n_mp, group, card, vectors, aux, wcls, wup, wdown, head, norm, cprob, cprob0, z
    )
    dmid, gfeed, rows2 = run_feed_back(
        n_dp, left, right, gv, local_rows, patches, middle, raw1, act, slope, vectors, wmlp
    )
    gattn, gpix, gpos, rows3, run_a, run_b = run_self_back(
        n_dp, n_mp, dmid, pixel_rows, embed, q, k, v, prob, post, ho, raw0, vectors, wattn,
        t1row, t2row, gfeed,
    )

    block, shared, block_sq = run_reduce(
        n_dp, n_mp, gattn, run_a, run_b, gpix, gpos, rows2, rows3
    )
    shared = shared.reshape(-1, D)
    state = (
        attn_in, attn_in_mean, attn_in_square, attn_out, attn_out_mean, attn_out_square,
        mlp_in, mlp_in_mean, mlp_in_square, mlp_out, mlp_out_mean, mlp_out_square,
    )
    smalls = (vectors, vectors_mean, vectors_square, talking, talking_mean, talking_square)
    moved = run_moments(
        n_dp, (block, shared, block_sq, gout1, gup1, gdown1, rows1, stat, aux, wcls),
        smalls, state,
    )
    sums = [moved[19]]
    for step in range(1, n_mp):
        sums.append(lax.ppermute(moved[19], "mp", [(i, (i + step) % n_mp) for i in range(n_mp)]))
    table = run_tables(moved[18], shared, ghead, (tables, tables_mean, tables_square))
    renewed = run_renew(n_mp, table[3], stat, sums, state[0:12:3], moved[0:12:3])
    return (
        from_rows(renewed[0]),
        from_rows(moved[1]),
        from_rows(moved[2]),
        renewed[1],
        moved[4],
        moved[5],
        renewed[2],
        moved[7],
        moved[8],
        renewed[3],
        moved[10],
        moved[11],
        *table[:3],
        *moved[12:18],
        from_rows(renewed[4]),
        renewed[5],
        renewed[6],
        renewed[7],
        renewed[10].reshape(12),
        renewed[9].reshape(()),
        renewed[8],
    )


def solution(mesh):
    return jax.shard_map(
        shards,
        mesh=mesh,
        in_specs=(
            P(("dp", "mp"), None, None),
            P("dp", None),
            P("dp"),
            P(("dp", "mp")),
            P(("dp", "mp")),
            P(None, None, None, "mp"),
            P(None, None, None, "mp"),
            P(None, None, None, "mp"),
            P(None, "mp", None),
            P(None, "mp", None),
            P(None, "mp", None),
            P(None, None, "mp"),
            P(None, None, "mp"),
            P(None, None, "mp"),
            P(None, "mp", None),
            P(None, "mp", None),
            P(None, "mp", None),
            P(),
            P(),
            P(),
            P(),
            P(),
            P(),
            P(),
            P(),
            P(),
        ),
        out_specs=(
            P(None, None, None, "mp"),
            P(None, None, None, "mp"),
            P(None, None, None, "mp"),
            P(None, "mp", None),
            P(None, "mp", None),
            P(None, "mp", None),
            P(None, None, "mp"),
            P(None, None, "mp"),
            P(None, None, "mp"),
            P(None, "mp", None),
            P(None, "mp", None),
            P(None, "mp", None),
            P(),
            P(),
            P(),
            P(),
            P(),
            P(),
            P(),
            P(),
            P(),
            P(None, None, None, "mp"),
            P(None, "mp", None),
            P(None, None, "mp"),
            P(None, "mp", None),
            P(),
            P(),
            P(),
        ),
        check_vma=False,
    )
```

```python
import functools

import jax
import jax.numpy as jnp
from jax import lax
from jax.experimental import pallas as pl
from jax.experimental.pallas import tpu as pltpu
from jax.sharding import PartitionSpec as P

D = 384
HEADS = 8
HEAD = 48
PIX = 768
P_SIZE = 196
PAD = 208
WIDE = 256
STEP = 10
SCALE = HEAD**-0.5
BETA_ONE = 0.9
BETA_TWO = 0.999
ADAM_EPS = 1e-08
DECAY = 0.01
RATE = 0.5
RATE_VECTOR = 0.5
CLIP = 0.02
TEMP = 0.05
MASKED = -1000000000.0
NORM_EPS = 1e-06
F32 = jnp.float32
BF = jnp.bfloat16
VMEM_LIMIT = 58 * 2**20
ANY = pl.BlockSpec(memory_space=pl.ANY)
MESH = pl.DeviceIdType.MESH
WHOLE = pl.BlockSpec(memory_space=pltpu.VMEM)


def nn(left, right):
    return lax.dot_general(left, right, (((1,), (0,)), ((), ())), preferred_element_type=F32)


def nt(left, right):
    return lax.dot_general(left, right, (((1,), (1,)), ((), ())), preferred_element_type=F32)


def tn(left, right):
    return lax.dot_general(left, right, (((0,), (0,)), ((), ())), preferred_element_type=F32)


def colsum(values):
    return jnp.sum(values, 0, keepdims=True)


def normalize(inputs):
    center = inputs - jnp.mean(inputs, -1, keepdims=True)
    spread = jnp.mean(center * center, -1, keepdims=True)
    inverse = lax.rsqrt(spread + NORM_EPS)
    return center * inverse, inverse


def normalize_back(unit, inverse, gain, incoming):
    scaled = incoming * gain
    return inverse * (
        scaled
        - jnp.mean(scaled, -1, keepdims=True)
        - unit * jnp.mean(scaled * unit, -1, keepdims=True)
    )


def gelu_parts(inner):
    cumulative = 0.5 + 0.5 * lax.erf(inner * 0.5**0.5)
    bell = jnp.exp2(inner * inner * (-0.5 * 1.4426950408889634)) * 0.3989422804014327
    return inner * cumulative, cumulative + inner * bell


def head_mask(copies=1):
    row = lax.rem(lax.broadcasted_iota(jnp.int32, (copies * HEADS, D), 0), HEADS)
    column = lax.broadcasted_iota(jnp.int32, (copies * HEADS, D), 1)
    return ((column >= row * HEAD) & (column < row * HEAD + HEAD)).astype(F32)


def stat_lanes(parts, weight, first):
    lane = lax.broadcasted_iota(jnp.int32, (1, 128), 1)
    row = jnp.zeros((1, 128), F32)
    for place, values in enumerate(parts):
        total = jnp.sum(colsum(values * values * weight), keepdims=True)
        high = total.astype(BF).astype(F32)
        row = jnp.where(lane == first + 2 * place, high, row)
        row = jnp.where(lane == first + 2 * place + 1, total - high, row)
    return row


def part(ref, first, rows):
    shards_count = ref.shape[0]
    return ref[:, first : first + rows, :].reshape(shards_count * rows, ref.shape[2])


def pad_rows(rows, n_dp):
    return -(-rows // (16 * n_dp)) * 16 * n_dp


class Place:
    def __init__(self, n_dp, n_mp):
        self.n_dp, self.n_mp, self.n_y = n_dp, n_mp, n_mp // 2
        self.n_lo = 2 if n_dp < 16 else 4
        self.n_hi = n_dp // self.n_lo
        self.dp = lax.axis_index("dp")
        self.mp = lax.axis_index("mp")
        self.y = lax.div(self.mp, 2)
        self.core = lax.rem(self.mp, 2)
        self.high = lax.div(self.dp, self.n_lo)
        self.low = lax.rem(self.dp, self.n_lo)
        self.chunk = self.low * self.n_hi + self.high
        self.sibling = (self.dp, self.y * 2 + 1 - self.core)

    def along_y(self, step):
        return lax.rem(self.y + step, self.n_y)

    def along_lo(self, step):
        return lax.rem(self.low + step, self.n_lo)

    def along_hi(self, step):
        return lax.rem(self.high + step, self.n_hi)

    def at_lo(self, low):
        return (self.high * self.n_lo + low, self.mp)

    def at_hi(self, high):
        return (high * self.n_lo + self.low, self.mp)

    def near_partners(self):
        return [self.sibling] + [
            (self.dp, self.along_y(step) * 2 + self.core) for step in range(1, self.n_y)
        ]

    def low_partners(self):
        return [self.at_lo(self.along_lo(step)) for step in range(1, self.n_lo)]

    def dp_partners(self):
        return self.low_partners() + [self.at_hi(self.along_hi(step)) for step in range(1, self.n_hi)]


def greet(partners):
    barrier = pltpu.get_barrier_semaphore()
    for partner in partners:
        pl.semaphore_signal(barrier, inc=1, device_id=partner, device_id_type=MESH)
    return lambda: pl.semaphore_wait(barrier, len(partners))


def tile_rows(ref, first, rows):
    return ref.at[pl.ds(pl.multiple_of(first, 16), rows)]


class SpreadGather:
    def __init__(self, place, rows, out, far_sem, low_sem, near_sem):
        self.place, self.rows, self.out = place, rows, out
        self.far_sem, self.low_sem, self.near_sem = far_sem, low_sem, near_sem
        self.count = rows.shape[0] // place.n_lo

    def piece(self, ref, low):
        return tile_rows(ref, low * self.count, self.count)

    def far_copy(self, step, slot):
        p = self.place
        return remote(
            self.piece(self.rows, p.low), self.piece(self.out.at[slot], p.low),
            self.far_sem.at[0, step], self.far_sem.at[1, step],
            (p.dp, p.along_y(step) * 2 + p.core),
        )

    def low_copy(self, step, turn, low):
        p = self.place
        rows = self.piece(self.out.at[self.from_y(step) + p.core], low)
        at = (step - 1) * p.n_lo + turn
        return remote(
            rows, rows, self.low_sem.at[0, at], self.low_sem.at[1, at],
            p.at_lo(p.along_lo(turn)),
        )

    def near_copy(self, step, slot):
        return remote(
            self.rows if step == 0 else self.out.at[slot], self.out.at[slot],
            self.near_sem.at[0, step], self.near_sem.at[1, step], self.place.sibling,
        )

    def own_copy(self):
        return pltpu.make_async_copy(
            self.rows, self.out.at[self.place.mp], self.far_sem.at[0, 0]
        )

    def from_y(self, step):
        p = self.place
        return p.along_y(p.n_y - step) * 2

    def start(self):
        p = self.place
        for step in range(1, p.n_y):
            self.far_copy(step, p.mp).start()
        self.near_copy(0, p.mp).start()
        self.own_copy().start()

    def spread(self):
        p = self.place
        for step in range(1, p.n_y):
            self.far_copy(step, self.from_y(step) + p.core).wait_recv()
            for turn in range(1, p.n_lo):
                self.low_copy(step, turn, p.low).start()

    def forward(self):
        p = self.place
        for step in range(1, p.n_y):
            for turn in range(1, p.n_lo):
                self.low_copy(step, turn, p.along_lo(p.n_lo - turn)).wait_recv()
            self.near_copy(step, self.from_y(step) + p.core).start()

    def finish(self):
        p = self.place
        self.own_copy().wait()
        for step in range(1, p.n_y):
            self.far_copy(step, p.mp).wait_send()
            for turn in range(1, p.n_lo):
                self.low_copy(step, turn, p.low).wait_send()
        for step in range(p.n_y):
            self.near_copy(step, self.from_y(step) + p.core if step else p.mp).wait_send()
            self.near_copy(step, self.from_y(step) + 1 - p.core).wait_recv()


def spread_scratch(n_dp, n_mp):
    n_lo = 2 if n_dp < 16 else 4
    dma = pltpu.SemaphoreType.DMA
    return [dma((2, n_mp // 2)), dma((2, n_mp // 2 * n_lo)), dma((2, n_mp // 2))]


class Gather:
    def __init__(self, place, rows, out, far_sem, near_sem):
        self.place, self.rows, self.out = place, rows, out
        self.far_sem, self.near_sem = far_sem, near_sem

    def far_copy(self, step, slot):
        p = self.place
        return remote(
            self.rows, self.out.at[slot], self.far_sem.at[0, step], self.far_sem.at[1, step],
            (p.dp, p.along_y(step) * 2 + p.core),
        )

    def near_copy(self, step, slot):
        return remote(
            self.rows if step == 0 else self.out.at[slot], self.out.at[slot],
            self.near_sem.at[0, step], self.near_sem.at[1, step], self.place.sibling,
        )

    def own_copy(self):
        return pltpu.make_async_copy(
            self.rows, self.out.at[self.place.mp], self.far_sem.at[0, 0]
        )

    def from_y(self, step):
        p = self.place
        return p.along_y(p.n_y - step) * 2

    def start(self):
        p = self.place
        for step in range(1, p.n_y):
            self.far_copy(step, p.mp).start()
        self.near_copy(0, p.mp).start()
        self.own_copy().start()

    def forward(self):
        p = self.place
        for step in range(1, p.n_y):
            slot = self.from_y(step) + p.core
            self.far_copy(step, slot).wait_recv()
            self.near_copy(step, slot).start()

    def finish(self):
        p = self.place
        self.own_copy().wait()
        for step in range(1, p.n_y):
            self.far_copy(step, p.mp).wait_send()
        for step in range(p.n_y):
            self.near_copy(step, self.from_y(step) + p.core if step else p.mp).wait_send()
            self.near_copy(step, self.from_y(step) + 1 - p.core).wait_recv()


def gather_scratch(n_mp):
    dma = pltpu.SemaphoreType.DMA
    return [dma((2, n_mp // 2)), dma((2, n_mp // 2))]


class ShardSum:
    def __init__(
        self, place, rows, first, y_first, near, far, low, half, high,
        near_sem, far_sem, low_sem, high_sem,
    ):
        self.place, self.rows, self.first, self.y_first = place, rows, first, y_first
        self.near, self.far, self.low, self.half, self.high = near, far, low, half, high
        self.near_sem, self.far_sem = near_sem, far_sem
        self.low_sem, self.high_sem = low_sem, high_sem
        self.count = near.shape[1]
        self.wide = self.count // place.n_lo
        self.chunk = self.count // place.n_dp

    def near_copy(self, step):
        p = self.place
        y = p.along_y(step)
        return remote(
            self.rows.at[y * 2 + 1 - p.core, pl.ds(self.first, self.count)], self.near.at[y],
            self.near_sem.at[0, step], self.near_sem.at[1, step], p.sibling,
        )

    def far_copy(self, step):
        p = self.place
        y = p.along_y(step)
        rows = self.near.at[y]
        if not self.y_first:
            rows = tile_rows(rows, p.low * self.wide, self.wide)
        return remote(
            rows, self.far.at[step - 1],
            self.far_sem.at[0, step], self.far_sem.at[1, step], (p.dp, y * 2 + p.core),
        )

    def low_copy(self, step):
        p = self.place
        to = p.along_lo(step)
        at = pl.ds(pl.multiple_of(to * self.wide, 16), self.wide)
        rows = self.near.at[p.y, at] if self.y_first else self.near.at[:, at]
        return remote(
            rows, self.low.at[step - 1],
            self.low_sem.at[0, step], self.low_sem.at[1, step], p.at_lo(to),
        )

    def high_copy(self, step):
        p = self.place
        to = p.along_hi(step)
        return remote(
            tile_rows(self.half, to * self.chunk, self.chunk), self.high.at[step - 1],
            self.high_sem.at[0, step], self.high_sem.at[1, step], p.at_hi(to),
        )

    def start(self):
        for step in range(1, self.place.n_y + 1):
            self.near_copy(step).start()

    def second(self):
        p = self.place
        at = slice(self.first, self.first + self.count)
        for step in range(1, p.n_y + 1):
            y = p.along_y(step)
            self.near_copy(step).wait_recv()
            self.near[pl.ds(y, 1)] = (
                self.rows[pl.ds(y * 2 + p.core, 1), at, :].astype(F32)
                + self.near[pl.ds(y, 1)].astype(F32)
            ).astype(BF)
            if self.y_first and step < p.n_y:
                self.far_copy(step).start()
        if not self.y_first:
            for step in range(1, p.n_lo):
                self.low_copy(step).start()

    def third(self):
        p = self.place
        own = pl.ds(pl.multiple_of(p.low * self.wide, 16), self.wide)
        if self.y_first:
            sums = self.near[pl.ds(p.y, 1)].astype(F32)
            for step in range(1, p.n_y):
                self.far_copy(step).wait_recv()
                sums += self.far[step - 1].astype(F32)[None]
            self.near[pl.ds(p.y, 1)] = sums.astype(BF)
            for step in range(1, p.n_lo):
                self.low_copy(step).start()
        else:
            sums = self.near[:, own, :].astype(F32)
            for step in range(1, p.n_lo):
                self.low_copy(step).wait_recv()
                sums += self.low[step - 1].astype(F32)
            self.near[:, own, :] = sums.astype(BF)
            for step in range(1, p.n_y):
                self.far_copy(step).start()

    def fourth(self):
        p = self.place
        own = pl.ds(pl.multiple_of(p.low * self.wide, 16), self.wide)
        sums = self.near[pl.ds(p.y, 1), own, :][0].astype(F32)
        if self.y_first:
            for step in range(1, p.n_lo):
                self.low_copy(step).wait_recv()
                sums += self.low[step - 1].astype(F32)
        else:
            for step in range(1, p.n_y):
                self.far_copy(step).wait_recv()
                sums += self.far[step - 1].astype(F32)
        self.half[...] = sums.astype(BF)
        for step in range(1, p.n_hi):
            self.high_copy(step).start()

    def finish(self):
        p = self.place
        at = pl.ds(pl.multiple_of(p.high * self.chunk, 16), self.chunk)
        sums = self.half[at, :].astype(F32)
        for step in range(1, p.n_hi):
            self.high_copy(step).wait_recv()
            sums += self.high[step - 1].astype(F32)
        return sums.astype(BF)

    def wait_sends(self):
        p = self.place
        for step in range(1, p.n_y + 1):
            self.near_copy(step).wait_send()
            if step < p.n_y:
                self.far_copy(step).wait_send()
        for step in range(1, p.n_lo):
            self.low_copy(step).wait_send()
        for step in range(1, p.n_hi):
            self.high_copy(step).wait_send()


def sum_scratch(n_dp, n_mp, rows, y_first):
    n_y = n_mp // 2
    n_lo = 2 if n_dp < 16 else 4
    n_hi = n_dp // n_lo
    wide = rows // n_lo
    dma = pltpu.SemaphoreType.DMA
    far = (max(n_y - 1, 1), rows, D) if y_first else (max(n_y - 1, 1), wide, D)
    low = (n_lo - 1, wide, D) if y_first else (n_lo - 1, n_y, wide, D)
    return [
        pltpu.VMEM((n_y, rows, D), BF), pltpu.VMEM(far, BF), pltpu.VMEM(low, BF),
        pltpu.VMEM((wide, D), BF), pltpu.VMEM((n_hi - 1, rows // n_dp, D), BF),
        dma((2, n_y + 1)), dma((2, n_y + 1)), dma((2, n_lo)), dma((2, n_hi)),
    ]


SUM_BUFFERS = 9


def halves(rows, n_dp):
    unit = 16 * n_dp
    first = (rows // unit + 1) // 2 * unit
    return first, rows - first


class TableSum:
    def __init__(
        self, place, rows, out, near, low, part_rows, high, last, far, near_sem, low_sem, high_sem,
        far_sem, back_sem, hand_sem,
    ):
        self.place, self.rows, self.out = place, rows, out
        self.near, self.low, self.part, self.high = near, low, part_rows, high
        self.last, self.far = last, far
        self.near_sem, self.low_sem, self.high_sem = near_sem, low_sem, high_sem
        self.far_sem, self.back_sem, self.hand_sem = far_sem, back_sem, hand_sem
        self.chunk = high.shape[2]
        self.wide = low.shape[2]
        self.slab = place.core * place.n_y + place.y
        self.first = place.core * place.n_y

    def near_copy(self):
        p = self.place
        return remote(
            self.rows.at[pl.ds((1 - p.core) * p.n_y, p.n_y)], self.near,
            self.near_sem.at[0], self.near_sem.at[1], p.sibling,
        )

    def low_copy(self, step):
        p = self.place
        to = p.along_lo(step)
        return remote(
            self.near.at[:, pl.ds(pl.multiple_of(to * self.wide, 16), self.wide)],
            self.low.at[step - 1], self.low_sem.at[0, step], self.low_sem.at[1, step], p.at_lo(to),
        )

    def high_copy(self, step):
        p = self.place
        to = p.along_hi(step)
        return remote(
            self.part.at[:, pl.ds(pl.multiple_of(to * self.chunk, 16), self.chunk)],
            self.high.at[step - 1], self.high_sem.at[0, step], self.high_sem.at[1, step],
            p.at_hi(to),
        )

    def far_copy(self, step):
        p = self.place
        to = p.along_y(step)
        return remote(
            self.last.at[to], self.far.at[step - 1], self.far_sem.at[0, step],
            self.far_sem.at[1, step], (p.dp, to * 2 + p.core),
        )

    def start(self):
        self.near_copy().start()

    def near_to_low(self):
        p = self.place
        self.near_copy().wait_recv()
        self.near[...] = (
            self.rows[pl.ds(self.first, p.n_y)].astype(F32) + self.near[...].astype(F32)
        ).astype(BF)
        for step in range(1, p.n_lo):
            self.low_copy(step).start()

    def low_to_high(self):
        p = self.place
        at = pl.ds(pl.multiple_of(p.low * self.wide, 16), self.wide)
        sums = self.near[:, at, :].astype(F32)
        for step in range(1, p.n_lo):
            self.low_copy(step).wait_recv()
            sums += self.low[step - 1].astype(F32)
        self.part[...] = sums.astype(BF)
        for step in range(1, p.n_hi):
            self.high_copy(step).start()

    def high_to_far(self):
        p = self.place
        at = pl.ds(pl.multiple_of(p.high * self.chunk, 16), self.chunk)
        sums = self.part[:, at, :].astype(F32)
        for step in range(1, p.n_hi):
            self.high_copy(step).wait_recv()
            sums += self.high[step - 1].astype(F32)
        self.last[...] = sums.astype(BF)
        for step in range(1, p.n_y):
            self.far_copy(step).start()

    def chunk_at(self, slab, chunk):
        return self.out.at[slab, pl.ds(pl.multiple_of(chunk * self.chunk, 16), self.chunk)]

    def back_far(self, step, y):
        p = self.place
        rows = self.chunk_at(self.first + y, p.chunk)
        return remote(
            rows, rows, self.back_sem.at[0, step], self.back_sem.at[1, step],
            (p.dp, p.along_y(step) * 2 + p.core),
        )

    def back_high(self, step, chunk):
        p = self.place
        rows = self.chunk_at(pl.ds(self.first, p.n_y), chunk)
        return remote(
            rows, rows, self.back_sem.at[2, step], self.back_sem.at[3, step],
            p.at_hi(p.along_hi(step)),
        )

    def back_low(self, step, low):
        p = self.place
        rows = self.out.at[
            pl.ds(self.first, p.n_y), pl.ds(pl.multiple_of(low * self.wide, 16), self.wide)
        ]
        return remote(
            rows, rows, self.back_sem.at[4, step], self.back_sem.at[5, step],
            p.at_lo(p.along_lo(step)),
        )

    def hand_copy(self, core):
        p = self.place
        rows = self.out.at[pl.ds(core * p.n_y, p.n_y)]
        return remote(rows, rows, self.hand_sem.at[0], self.hand_sem.at[1], p.sibling)

    def turn(self):
        p = self.place
        sums = self.last[pl.ds(p.y, 1)][0].astype(F32)
        for step in range(1, p.n_y):
            self.far_copy(step).wait_recv()
            sums += self.far[step - 1].astype(F32)
        at = pl.ds(pl.multiple_of(p.chunk * self.chunk, 16), self.chunk)
        self.out[pl.ds(self.slab, 1), at, :] = sums.astype(BF)[None]
        for step in range(1, p.n_y):
            self.back_far(step, p.y).start()

    def far_to_high(self):
        p = self.place
        for step in range(1, p.n_y):
            self.back_far(step, p.along_y(p.n_y - step)).wait_recv()
        for step in range(1, p.n_hi):
            self.back_high(step, p.chunk).start()

    def high_to_low(self):
        p = self.place
        for step in range(1, p.n_hi):
            self.back_high(step, p.low * p.n_hi + p.along_hi(p.n_hi - step)).wait_recv()
        for step in range(1, p.n_lo):
            self.back_low(step, p.low).start()

    def low_to_near(self):
        p = self.place
        for step in range(1, p.n_lo):
            self.back_low(step, p.along_lo(p.n_lo - step)).wait_recv()
        self.hand_copy(p.core).start()

    def finish(self):
        p = self.place
        self.hand_copy(1 - p.core).wait_recv()
        self.near_copy().wait_send()
        self.hand_copy(p.core).wait_send()
        for step in range(1, p.n_lo):
            self.low_copy(step).wait_send()
            self.back_low(step, p.low).wait_send()
        for step in range(1, p.n_hi):
            self.high_copy(step).wait_send()
            self.back_high(step, p.chunk).wait_send()
        for step in range(1, p.n_y):
            self.far_copy(step).wait_send()
            self.back_far(step, p.y).wait_send()


def table_scratch(n_dp, n_mp, rows):
    n_y = n_mp // 2
    n_lo = 2 if n_dp < 16 else 4
    n_hi = n_dp // n_lo
    wide, chunk = rows // n_lo, rows // n_dp
    dma = pltpu.SemaphoreType.DMA
    return [
        pltpu.VMEM((n_y, rows, D), BF), pltpu.VMEM((n_lo - 1, n_y, wide, D), BF),
        pltpu.VMEM((n_y, wide, D), BF), pltpu.VMEM((n_hi - 1, n_y, chunk, D), BF),
        pltpu.VMEM((n_y, chunk, D), BF), pltpu.VMEM((max(n_y - 1, 1), chunk, D), BF),
        dma((2,)), dma((2, n_lo)), dma((2, n_hi)), dma((2, n_y)),
        dma((6, max(n_y, n_lo, n_hi))), dma((2,)),
    ]


class HandHigh:
    def __init__(self, place, rows, sems):
        self.place, self.rows, self.sems = place, rows, sems
        self.chunk = rows.shape[0] // place.n_hi

    def copy(self, step, source):
        p = self.place
        rows = tile_rows(self.rows, source * self.chunk, self.chunk)
        return remote(
            rows, rows, self.sems.at[0, step], self.sems.at[1, step], p.at_hi(p.along_hi(step))
        )

    def start(self, sums):
        p = self.place
        self.rows[pl.ds(pl.multiple_of(p.high * self.chunk, 16), self.chunk), :] = sums
        for step in range(1, p.n_hi):
            self.copy(step, p.high).start()

    def arrive(self):
        p = self.place
        for step in range(1, p.n_hi):
            self.copy(step, p.along_hi(p.n_hi - step)).wait_recv()

    def wait_sends(self):
        for step in range(1, self.place.n_hi):
            self.copy(step, self.place.high).wait_send()


class HandLow:
    def __init__(self, place, rows, first, count, sems):
        self.place, self.rows, self.first, self.sems = place, rows, first, sems
        self.run = count // place.n_lo

    def copy(self, step, source):
        p = self.place
        rows = tile_rows(self.rows, self.first + source * self.run, self.run)
        return remote(
            rows, rows, self.sems.at[0, step], self.sems.at[1, step], p.at_lo(p.along_lo(step))
        )

    def start(self, sums):
        p = self.place
        self.rows[pl.ds(pl.multiple_of(self.first + p.low * self.run, 16), self.run), :] = sums
        for step in range(1, p.n_lo):
            self.copy(step, p.low).start()

    def arrive(self):
        p = self.place
        for step in range(1, p.n_lo):
            self.copy(step, p.along_lo(p.n_lo - step)).wait_recv()

    def wait_sends(self):
        for step in range(1, self.place.n_lo):
            self.copy(step, self.place.low).wait_send()


def remote(src, dst, send_sem, recv_sem, device):
    return pltpu.make_async_remote_copy(
        src_ref=src, dst_ref=dst, send_sem=send_sem, recv_sem=recv_sem,
        device_id=device, device_id_type=MESH,
    )


def stack_heads(stack, rows, gains):
    for g in range(HEADS):
        stack[g * PAD : g * PAD + P_SIZE, :] = (rows * gains[g : g + 1, :]).astype(BF)


def column(cols, index):
    lane = lax.broadcasted_iota(jnp.int32, cols.shape, 1)
    return jnp.sum(jnp.where(lane == index, cols[...], 0.0), 1, keepdims=True)


def self_attend_kernel(
    n_dp, n_mp, embed, cols, vec, wattn, t1row, t2row, mlp_rows,
    q_out, k_out, v_out, prob_out, post_out, ho_out, raw_out, mid_out, stat_out, wmlp_out,
    stack, scores, *sems,
):
    shard = wattn.shape[1] // 4
    place = Place(n_dp, n_mp)
    gather = Gather(place, mlp_rows, wmlp_out, *sems)
    images = pl.num_programs(0)

    @pl.when(pl.program_id(0) == 0)
    def _():
        stack[...] = jnp.zeros_like(stack)
        greet(place.near_partners())()
        gather.start()

    @pl.when(pl.program_id(0) == images - 1)
    def _():
        gather.forward()

    x = embed[0]
    unit, _ = normalize(x)
    normed = (unit * vec[0:1, :] + vec[1:2, :]).astype(BF)
    q = nt(normed, part(wattn, 0, shard)).astype(BF)
    k = nt(normed, part(wattn, shard, shard)).astype(BF)
    v = nt(normed, part(wattn, 2 * shard, shard)).astype(BF)
    q_out[0] = q
    k_out[0] = k
    v_out[0] = v
    stack_heads(stack, q.astype(F32), t1row)
    scores[...] = nt(k, stack[...])
    bias = column(cols, pl.program_id(0))
    for first in range(0, HEADS * PAD, 128):
        mixed = scores[:, first : first + 128] + bias
        grown = jnp.exp(mixed - jnp.max(mixed, 0, keepdims=True))
        prob = grown * (1.0 / jnp.sum(grown, 0, keepdims=True))
        prob_out[0, :, first : first + 128] = prob.astype(BF)
    post = tn(prob_out[0], v)
    post_out[0] = post.astype(BF)
    heads_out = jnp.zeros(x.shape, F32)
    for g in range(HEADS):
        heads_out += post[g * PAD : g * PAD + P_SIZE, :] * t2row[g : g + 1, :]
    heads_out = heads_out.astype(BF)
    ho_out[0] = heads_out
    raw = nn(heads_out, part(wattn, 3 * shard, shard))
    raw_out[0] = raw.astype(BF)
    branch = vec[3:4, :] * (raw + vec[2:3, :])
    middle = x + branch
    mid_out[0] = middle
    weight = column(cols, pl.program_id(0) + cols.shape[1] // 2)
    stat_out[0] = stat_lanes((branch, middle), weight, 8)

    @pl.when(pl.program_id(0) == images - 1)
    def _():
        gather.finish()


def feed_kernel(
    n_dp, n_mp, mid, cols, bias_row, base, stat, vec, wmlp, cls_rows, up_rows, down_rows,
    patch_out, act_out, slope_out, raw_out, norm_out, cprob_out, cprob0_out, z_out, card_out,
    aux_out, wcls_out, wup_out, wdown_out, wcls, *sems,
):
    hidden = wmlp.shape[1] // 2
    shard = wcls.shape[1] // 4
    images = norm_out.shape[0]

    place = Place(n_dp, n_mp)
    gather_cls = SpreadGather(place, cls_rows, wcls, *sems[:3])
    gather_up = SpreadGather(place, up_rows, wup_out, *sems[3:6])
    gather_down = SpreadGather(place, down_rows, wdown_out, *sems[6:])

    def beside(step, *stages):
        @pl.when(pl.program_id(0) == step)
        def _():
            for stage in stages:
                stage()

    @pl.when(pl.program_id(0) == 0)
    def _():
        norm_out[...] = jnp.zeros_like(norm_out)
        greet(place.near_partners() + place.low_partners())()
        gather_cls.start()
        gather_up.start()
        gather_down.start()

    beside(images * 3 // 8, gather_cls.spread)
    beside(images // 2, gather_up.spread)
    beside(images * 5 // 8, gather_down.spread)
    beside(images * 3 // 4, gather_cls.forward)
    beside(images - 1, gather_up.forward, gather_cls.finish)

    middle = mid[0]
    unit, _ = normalize(middle)
    normed = (unit * vec[4:5, :] + vec[5:6, :]).astype(BF)
    inner = nt(normed, part(wmlp, 0, hidden))
    active, slope = gelu_parts(inner)
    active = active.astype(BF)
    act_out[0] = active
    slope_out[0] = slope.astype(BF)
    raw = nn(active, part(wmlp, hidden, hidden))
    raw_out[0] = raw.astype(BF)
    branch = vec[7:8, :] * (raw + vec[6:7, :])
    patches = middle + branch
    patch_out[0] = patches
    card_out[pl.ds(4 * pl.program_id(0) + 3, 1), :] = (
        base[pl.ds(pl.program_id(0), 1), :]
        + stat[0]
        + stat_lanes((branch, patches), column(cols, pl.program_id(0) + images), 12)
    )
    unit, _ = normalize(patches)
    norm_out[pl.ds(pl.program_id(0), 1), :P_SIZE, :] = (
        (unit * vec[8:9, :] + vec[9:10, :]).astype(BF)[None]
    )

    @pl.when(pl.program_id(0) == images - 1)
    def _():
        gather_down.forward()
        unit, _ = normalize(jnp.broadcast_to(vec[17:18, :], (HEADS, D)))
        token = (unit * vec[8:9, :] + vec[9:10, :]).astype(BF)
        query = nt(token, part(wcls, 0, shard)).astype(BF).astype(F32)
        keys = nn((query * head_mask()).astype(BF), part(wcls, shard, shard)) * SCALE
        token = token.astype(F32)
        aux_out[0:8, :] = keys
        aux_out[8:16, :] = token
        aux_out[16:24, :] = query
        scores = nt(keys.astype(BF), norm_out[...].reshape(images * WIDE, D)) + bias_row[...]
        score0 = jnp.sum(keys * token, -1, keepdims=True)
        for n in range(images):
            rows = slice(n * HEADS, (n + 1) * HEADS)
            mine = scores[:, n * WIDE : (n + 1) * WIDE]
            top = jnp.maximum(jnp.max(mine, -1, keepdims=True), score0)
            grown = jnp.exp(mine - top)
            grown0 = jnp.exp(score0 - top)
            scale = 1.0 / (jnp.sum(grown, -1, keepdims=True) + grown0)
            cprob = grown * scale
            cprob0 = grown0 * scale
            cprob_out[rows, :] = cprob
            cprob0_out[rows, :] = jnp.broadcast_to(cprob0, (HEADS, 128))
            z_out[rows, :] = nn(cprob.astype(BF), norm_out[n]) + cprob0 * token
        cheads = nt(z_out[...].astype(BF), part(wcls, 2 * shard, shard)) * head_mask(images)
        cheads = cheads.reshape(images, HEADS, D).sum(1)
        for piece in range(3):
            card_out[pl.ds(piece, images, stride=4), :] = cheads[:, 128 * piece : 128 * piece + 128]
        wcls_out[...] = wcls[...]
        gather_up.finish()
        gather_down.finish()


def card_token_kernel(n_dp, n_mp, group, card, vec, aux, *rest):
    far, outs, scratch = rest[:8], rest[8:18], rest[18:]
    dch_all, gout_all, gup_all, gdown_all, cards, slots, dp_sem, mp_sem, load_sem = scratch[:9]
    here = scratch[9:]
    loads = [
        pltpu.make_async_copy(far[i], here[i], load_sem.at[i]) for i in range(len(far))
    ]
    for copy in loads:
        copy.start()
    share_cards(n_dp, n_mp, card, cards, slots, dp_sem, mp_sem)
    for copy in loads:
        copy.wait()
    token_kernel(
        group, cards, vec, *here, aux, *outs, dch_all, gout_all, gup_all, gdown_all
    )


def token_kernel(
    group, cards, vec, wcls, wup_rows, wdown_rows, head, norm, cprob, cprob0, z, aux,
    left_out, right_out, gv_out, local_out, gout_out, gup_out, gdown_out, ghead_out, rows_out,
    stat_out, dch_all, gout_all, gup_all, gdown_all,
):
    hidden = wup_rows.shape[1]
    shard = wcls.shape[1] // 4
    images = cards.shape[0] // 4
    cheads = jnp.concatenate(
        [cards[pl.ds(piece, images, stride=4), :] for piece in range(3)], 1
    ).astype(BF)
    card = cards[pl.ds(3, images, stride=4), :]
    labels = (card[:, 0:1] * 32.0 + card[:, 1:2]).astype(jnp.int32)
    pairs = (card[:, 2:3] * 32.0 + card[:, 3:4]).astype(jnp.int32)
    column = lax.broadcasted_iota(jnp.int32, (images, images), 1)
    row = lax.broadcasted_iota(jnp.int32, (images, images), 0)
    slot = lax.rem(lax.broadcasted_iota(jnp.int32, (images, 1), 0), group).astype(F32)
    okay = (slot >= group - card[:, 4:5]).astype(F32)
    okay_row = colsum(jnp.where(row == column, okay, 0.0))
    wo = part(wcls, 3 * shard, shard)
    wup = part(wup_rows, 0, hidden)
    wdown = part(wdown_rows, 0, hidden)
    count = jnp.sum(okay, keepdims=True)
    raw = nn(cheads, wo) + vec[10:11, :]
    branch = vec[11:12, :] * raw
    middle = vec[17:18, :] + branch
    unit2, inverse2 = normalize(middle)
    normed = (unit2 * vec[12:13, :] + vec[13:14, :]).astype(BF)
    inner = nt(normed, wup)
    active, slope = gelu_parts(inner)
    active = active.astype(BF)
    down = nn(active, wdown) + vec[14:15, :]
    mlp_branch = vec[15:16, :] * down
    token = middle + mlp_branch
    unit3, inverse3 = normalize(token)
    feature = unit3 * vec[18:19, :] + vec[19:20, :]
    feature_low = feature.astype(BF)
    logits = nt(feature_low, head[...])
    top = jnp.max(logits, -1, keepdims=True)
    grown = jnp.exp(logits - top)
    total = jnp.sum(grown, -1, keepdims=True)
    hot = lax.broadcasted_iota(jnp.int32, logits.shape, 1) == labels
    cross = jnp.log(total) + top - jnp.sum(jnp.where(hot, logits, 0.0), -1, keepdims=True)
    share = okay / count
    dlogits = (share * (grown / total - hot.astype(F32))).astype(BF)
    classes = head.shape[0]
    ghead = tn(dlogits, feature_low)
    ghead_out[0:8, :] = jnp.zeros((8, D), F32)
    ghead_out[classes:, :] = jnp.zeros((8, D), F32)
    ghead_out[4 : classes + 4, :] = ghead
    replicated_sq = colsum(ghead * ghead)
    dfeature = nn(dlogits, head[...])

    length = lax.rsqrt(jnp.sum(feature * feature, -1, keepdims=True) + NORM_EPS)
    embed = (feature * length).astype(BF)
    sims = nt(embed, embed) / TEMP
    sims = jnp.where((okay_row > 0) & (row != column), sims, MASKED)
    top = jnp.max(sims, -1, keepdims=True)
    grown = jnp.exp(sims - top)
    total = jnp.sum(grown, -1, keepdims=True)
    hot = column == pairs
    contrast = jnp.log(total) + top - jnp.sum(jnp.where(hot, sims, 0.0), -1, keepdims=True)
    dsims = share * (grown / total - hot.astype(F32))
    high = dsims.astype(BF)
    low = (dsims - high.astype(F32)).astype(BF)
    dembed = (nn(high, embed) + nn(low, embed) + tn(high, embed) + tn(low, embed)) / TEMP
    dfeature += length * dembed - feature * (
        length * length * length * jnp.sum(dembed * feature, -1, keepdims=True)
    )

    dtoken = normalize_back(unit3, inverse3, vec[18:19, :], dfeature)
    rows_out[0:1, :] = jnp.zeros((1, D), F32)
    rows_out[1:2, :] = jnp.zeros((1, D), F32)
    rows_out[7:8, :] = colsum(dtoken * down)
    rows_out[6:7, :] = vec[15:16, :] * colsum(dtoken)
    ddown = (dtoken * vec[15:16, :]).astype(BF)
    gdown = tn(active, ddown)
    own_f = pl.multiple_of(lax.axis_index("mp") * hidden, hidden)
    gdown_all[...] = gdown
    gdown_out[...] = gdown_all[pl.ds(own_f, hidden), :]
    replicated_sq += colsum(gdown * gdown)
    dinner = (nt(ddown, wdown) * slope).astype(BF)
    gup = tn(dinner, normed)
    gup_all[...] = gup
    gup_out[...] = gup_all[pl.ds(own_f, hidden), :]
    replicated_sq += colsum(gup * gup)
    dnormed = nn(dinner, wup)
    rows_out[4:5, :] = colsum(dnormed * unit2)
    rows_out[5:6, :] = colsum(dnormed)
    dmiddle = dtoken + normalize_back(unit2, inverse2, vec[12:13, :], dnormed)
    rows_out[3:4, :] = colsum(dmiddle * raw)
    rows_out[2:3, :] = vec[11:12, :] * colsum(dmiddle)
    rows_out[8:9, :] = colsum(dmiddle)
    rows_out[9:10, :] = colsum(dfeature * unit3)
    rows_out[10:11, :] = colsum(dfeature)
    dbranch = (dmiddle * vec[11:12, :]).astype(BF)
    gout = tn(cheads, dbranch)
    gout_all[...] = gout
    own_h = pl.multiple_of(lax.axis_index("mp") * shard, shard)
    gout_out[...] = gout_all[pl.ds(own_h, shard), :]
    replicated_sq += colsum(gout * gout)
    dch_all[...] = nt(dbranch, wo)
    local = norm.shape[0]
    place = lax.axis_index("dp") * lax.axis_size("mp") + lax.axis_index("mp")
    if local % 8 == 0:
        dch = dch_all[pl.ds(pl.multiple_of(place * local, local), local), :]
    else:
        share_of = 8 // local
        start = pl.multiple_of(lax.div(place, share_of) * 8, 8)
        window = dch_all[pl.ds(start, 8), :]
        pick = lax.rem(place, share_of)
        dch = sum(
            jnp.where(pick == i, window[i * local : (i + 1) * local, :], 0.0)
            for i in range(share_of)
        )

    keys = aux[0:8, :]
    class_row = aux[8:16, :]
    mask = head_mask()
    spread = jnp.concatenate([mask * dch[n : n + 1, :] for n in range(local)], 0).astype(BF)
    dz = nn(spread, part(wcls, 2 * shard, shard))
    dz_low = dz.astype(BF)
    probs = cprob[...]
    prob0 = cprob0[...][:, 0:1]
    class_rows = jnp.concatenate([class_row] * local, 0)
    dprobs = jnp.concatenate(
        [nt(dz_low[n * HEADS : (n + 1) * HEADS, :], norm[n]) for n in range(local)], 0
    )
    dprob0 = jnp.sum(dz * class_rows, -1, keepdims=True)
    inside = jnp.sum(dprobs * probs, -1, keepdims=True) + dprob0 * prob0
    dscores = (probs * (dprobs - inside)).astype(BF)
    dscore0 = prob0 * (dprob0 - inside)
    gv_out[...] = tn(spread, z[...].astype(BF))
    local_out[0:8, :] = jnp.zeros((8, D), F32)
    dkeys = jnp.zeros((HEADS, D), F32)
    from_class = jnp.zeros((1, D), F32)
    for n in range(local):
        rows = slice(n * HEADS, (n + 1) * HEADS)
        dkeys += nn(dscores[rows, :], norm[n]) + dscore0[rows, :] * class_row
        from_class += colsum(prob0[rows, :] * dz[rows, :] + dscore0[rows, :] * keys)
        left_out[n] = jnp.concatenate([probs[rows, :].astype(BF), dscores[rows, :]], 0)
        right_out[n] = jnp.concatenate([dz_low[rows, :], keys.astype(BF)], 0)
    local_out[6:7, :] = from_class
    local_out[8:16, :] = dkeys
    lane = lax.broadcasted_iota(jnp.int32, (1, 128), 1)
    self_sums = colsum(card)
    count_tokens = self_sums[:, 5:6]

    def squares(values):
        return jnp.sum(colsum(values * values * okay), keepdims=True)

    entries = [jnp.sum(okay * cross, keepdims=True), jnp.sum(okay * contrast, keepdims=True)]
    entries += [count, count_tokens]
    entries += [
        jnp.sqrt((self_sums[:, i : i + 1] + self_sums[:, i + 1 : i + 2]) / D / count_tokens)
        for i in (8, 10, 12, 14)
    ]
    entries += [
        jnp.sqrt(squares(item) / D / count) for item in (branch, middle, mlp_branch, token)
    ]
    line = jnp.zeros((1, 128), F32)
    for i, entry in enumerate(entries):
        line = jnp.where(lane == i, entry, line)
    stat_out[0:1, :] = line
    stat_out[1:8, :] = jnp.broadcast_to(
        replicated_sq[:, 0:128] + replicated_sq[:, 128:256] + replicated_sq[:, 256:384], (7, 128)
    )


def feed_back_kernel(
    left, right, gv, local_rows, patch, mid, raw, act, slope, vec, wmlp,
    dmid_out, gfeed_out, rows_out, gmlp_out,
):
    hidden = wmlp.shape[1] // 2
    count = wmlp.shape[0]
    shard = D // count

    @pl.when(pl.program_id(0) == 0)
    def _():
        gmlp_out[...] = jnp.zeros_like(gmlp_out)
        rows_out[...] = local_rows[...]

    unit, inverse = normalize(patch[0])
    dnormed = tn(left[0], right[0])[:P_SIZE, :]
    rows_out[4:5, :] += colsum(dnormed * unit)
    rows_out[5:6, :] += colsum(dnormed)
    incoming = normalize_back(unit, inverse, vec[8:9, :], dnormed)

    unit, inverse = normalize(mid[0])
    normed = (unit * vec[4:5, :] + vec[5:6, :]).astype(BF)
    rows_out[3:4, :] += colsum(incoming * (raw[0].astype(F32) + vec[6:7, :]))
    rows_out[2:3, :] += vec[7:8, :] * colsum(incoming)
    ddown = (incoming * vec[7:8, :]).astype(BF)
    gmlp_out[:, hidden:, :] += tn(act[0], ddown).reshape(count, hidden, D)
    dinner = (nt(ddown, part(wmlp, hidden, hidden)) * slope[0].astype(F32)).astype(BF)
    gmlp_out[:, :hidden, :] += tn(dinner, normed).reshape(count, hidden, D)
    dnormed = nn(dinner, part(wmlp, 0, hidden))
    rows_out[0:1, :] += colsum(dnormed * unit)
    rows_out[1:2, :] += colsum(dnormed)
    dmid_out[0] = incoming + normalize_back(unit, inverse, vec[4:5, :], dnormed)

    @pl.when(pl.program_id(0) == pl.num_programs(0) - 1)
    def _():
        used = 2 * hidden + shard
        gfeed_out[:, : 2 * hidden, :] = gmlp_out[...].astype(BF)
        gfeed_out[:, 2 * hidden : used, :] = gv[...].astype(BF).reshape(count, shard, D)
        if used < gfeed_out.shape[1]:
            gfeed_out[:, used:, :] = jnp.zeros((count, gfeed_out.shape[1] - used, D), BF)


def self_back_kernel(
    n_dp, n_mp, dmid, pixels, embed, q, k, v, prob, post, ho, raw, vec, wattn, t1row, t2row, gfeed,
    rows_feed, block_far, shared_far, square_out,
    gattn_out, gpos_out, rows_out, dx_all, dx_rows, stack_q, stack_h, slopes,
    blocks_out, commons_out, block_here, shared_here, save_sem, *sum_buffers,
):
    shard = wattn.shape[1] // 4
    count = wattn.shape[0]
    images = dx_all.shape[0]
    place = Place(n_dp, n_mp)
    rows_a, _ = halves(gfeed.shape[1], n_dp)
    sum_a = ShardSum(place, gfeed, 0, True, *sum_buffers[:SUM_BUFFERS])
    sum_b = ShardSum(
        place, gfeed, rows_a, False, *sum_buffers[SUM_BUFFERS : 2 * SUM_BUFFERS]
    )

    def beside(step, *stages):
        @pl.when(pl.program_id(0) == step)
        def _():
            for stage in stages:
                stage()

    @pl.when(pl.program_id(0) == 0)
    def _():
        gattn_out[...] = jnp.zeros_like(gattn_out)
        gpos_out[...] = jnp.zeros_like(gpos_out)
        rows_out[...] = jnp.zeros_like(rows_out)
        stack_q[...] = jnp.zeros_like(stack_q)
        stack_h[...] = jnp.zeros_like(stack_h)
        greet(place.near_partners() + place.dp_partners())()
        sum_a.start()
        sum_b.start()

    beside(1, sum_a.second, sum_b.second)
    beside(images * 3 // 8, sum_a.third, sum_b.third)
    beside(images * 5 // 8, sum_a.fourth, sum_b.fourth)

    wq = part(wattn, 0, shard)
    wk = part(wattn, shard, shard)
    wv = part(wattn, 2 * shard, shard)
    wo = part(wattn, 3 * shard, shard)
    incoming = dmid[0]
    rows_out[3:4, :] += colsum(incoming * (raw[0].astype(F32) + vec[2:3, :]))
    rows_out[2:3, :] += vec[3:4, :] * colsum(incoming)
    dbranch = (incoming * vec[3:4, :]).astype(BF)
    gattn_out[:, 3 * shard :, :] += tn(ho[0], dbranch).reshape(count, shard, D)
    dheads = nt(dbranch, wo).astype(BF).astype(F32)

    unit, inverse = normalize(embed[0])
    normed = (unit * vec[0:1, :] + vec[1:2, :]).astype(BF)
    q_wide = q[0].astype(F32)
    stack_heads(stack_q, q_wide, t1row)
    stack_heads(stack_h, dheads, t2row)
    slopes[...] = nt(v[0], stack_h[...])
    dv = nn(prob[0], stack_h[...]).astype(BF)
    for first in range(0, HEADS * PAD, 128):
        at = slice(first, first + 128)
        chance = prob[0, :, at].astype(F32)
        dprob = slopes[:, at]
        slopes[:, at] = chance * (dprob - colsum(dprob * chance))
    dmixed = slopes[...].astype(BF)
    dk = nn(dmixed, stack_q[...]).astype(BF)
    dpre = tn(dmixed, k[0])
    dq = jnp.zeros(q_wide.shape, F32)
    for g in range(HEADS):
        rows = slice(g * PAD, g * PAD + P_SIZE)
        dq += dpre[rows, :] * t1row[g : g + 1, :]
        rows_out[8 + g : 9 + g, :] += colsum(q_wide * dpre[rows, :])
        rows_out[16 + g : 17 + g, :] += colsum(dheads * post[0, rows, :].astype(F32))
    dq = dq.astype(BF)
    gattn_out[:, :shard, :] += tn(dq, normed).reshape(count, shard, D)
    gattn_out[:, shard : 2 * shard, :] += tn(dk, normed).reshape(count, shard, D)
    gattn_out[:, 2 * shard : 3 * shard, :] += tn(dv, normed).reshape(count, shard, D)
    dnormed = nn(dq, wq) + nn(dk, wk) + nn(dv, wv)
    rows_out[0:1, :] += colsum(dnormed * unit)
    rows_out[1:2, :] += colsum(dnormed)
    dx = incoming + normalize_back(unit, inverse, vec[0:1, :], dnormed)
    gpos_out[...] += dx
    dx_all[pl.program_id(0)] = dx

    @pl.when(pl.program_id(0) == pl.num_programs(0) - 1)
    def _():
        for n in range(images):
            dx_rows[:, n, :] = dx_all[n]
        gpix = tn(pixels[...], dx_rows[...].reshape(pixels.shape[0], D).astype(BF))
        used = gattn_out.shape[1]
        blocks_out[:, :used, :] = gattn_out[...].astype(BF)
        if used < blocks_out.shape[1]:
            blocks_out[:, used:, :] = jnp.zeros((count, blocks_out.shape[1] - used, D), BF)
        wide = commons_out.shape[1]
        commons_out[:3] = gpix.astype(BF).reshape(3, wide, D)
        commons_out[3] = jnp.concatenate(
            [
                gpos_out[...], jnp.zeros((12, D), F32), rows_feed[...], rows_out[...],
                jnp.zeros((8, D), F32),
            ],
            0,
        ).astype(BF)
        if count > 4:
            commons_out[4:] = jnp.zeros((count - 4, wide, D), BF)
        reduce_rows(
            place, blocks_out, commons_out, sum_a.finish(), sum_b.finish(), block_here,
            shared_here, square_out, *sum_buffers[2 * SUM_BUFFERS :],
        )
        saves = [
            pltpu.make_async_copy(block_here, block_far, save_sem.at[0]),
            pltpu.make_async_copy(shared_here, shared_far, save_sem.at[1]),
        ]
        for copy in saves:
            copy.start()
        sum_a.wait_sends()
        sum_b.wait_sends()
        for copy in saves:
            copy.wait()


def table_rows(n_dp, n_mp):
    return -(-(PIX + 256) // (16 * n_dp * n_mp)) * 16 * n_dp


def per_image(*tail):
    return pl.BlockSpec((1, *tail), lambda n: (n, *(0 for _ in tail)))


def constant(*shape):
    return pl.BlockSpec(shape, lambda n: tuple(0 for _ in shape))


def shaped(*shape, dtype=F32):
    return jax.ShapeDtypeStruct(shape, dtype)


def params():
    return pltpu.CompilerParams(vmem_limit_bytes=VMEM_LIMIT, dimension_semantics=("arbitrary",))


def remote_params(collective_id):
    return pltpu.CompilerParams(
        vmem_limit_bytes=VMEM_LIMIT, dimension_semantics=("arbitrary",),
        collective_id=collective_id, has_side_effects=True,
    )


def run_self_attend(n_dp, n_mp, embed, cols, vec, wattn, t1row, t2row, mlp_rows):
    count = embed.shape[0]
    rows = per_image(P_SIZE, D)
    low = shaped(count, P_SIZE, D, dtype=BF)
    return pl.pallas_call(
        functools.partial(self_attend_kernel, n_dp, n_mp),
        grid=(count,),
        in_specs=[
            rows, constant(*cols.shape), constant(*vec.shape),
            constant(*wattn.shape), constant(HEADS, D), constant(HEADS, D),
            constant(*mlp_rows.shape),
        ],
        out_specs=[
            rows, rows, rows, per_image(P_SIZE, HEADS * PAD), per_image(HEADS * PAD, D),
            rows, rows, rows, per_image(1, 128), ANY,
        ],
        out_shape=[
            low, low, low, shaped(count, P_SIZE, HEADS * PAD, dtype=BF),
            shaped(count, HEADS * PAD, D, dtype=BF), low, low,
            shaped(count, P_SIZE, D), shaped(count, 1, 128),
            shaped(n_mp, *mlp_rows.shape, dtype=BF),
        ],
        scratch_shapes=[pltpu.VMEM((HEADS * PAD, D), BF), pltpu.VMEM((P_SIZE, HEADS * PAD), F32)]
        + gather_scratch(n_mp),
        compiler_params=remote_params(6),
        name="self_attend",
    )(embed, cols, vec, wattn, t1row, t2row, mlp_rows)


def run_feed(n_dp, n_mp, mid, cols, bias_row, base, stat, vec, wmlp, cls_rows, up_rows, down_rows):
    count = mid.shape[0]
    wide = 2 * wmlp.shape[0] * wmlp.shape[1] // 4
    return pl.pallas_call(
        functools.partial(feed_kernel, n_dp, n_mp),
        grid=(count,),
        in_specs=[
            per_image(P_SIZE, D), constant(*cols.shape), constant(1, count * WIDE),
            constant(*base.shape), per_image(1, 128), constant(*vec.shape), constant(*wmlp.shape),
            constant(*cls_rows.shape), constant(*up_rows.shape), constant(*down_rows.shape),
        ],
        out_specs=[
            per_image(P_SIZE, D), per_image(P_SIZE, wide), per_image(P_SIZE, wide),
            per_image(P_SIZE, D), constant(count, WIDE, D), constant(count * HEADS, WIDE),
            constant(count * HEADS, 128), constant(count * HEADS, D), constant(4 * count, 128),
            constant(24, D), constant(n_mp, *cls_rows.shape), ANY, ANY,
        ],
        out_shape=[
            shaped(count, P_SIZE, D), shaped(count, P_SIZE, wide, dtype=BF),
            shaped(count, P_SIZE, wide, dtype=BF), shaped(count, P_SIZE, D, dtype=BF),
            shaped(count, WIDE, D, dtype=BF), shaped(count * HEADS, WIDE),
            shaped(count * HEADS, 128), shaped(count * HEADS, D), shaped(4 * count, 128),
            shaped(24, D), shaped(n_mp, *cls_rows.shape, dtype=BF),
            shaped(n_mp, *up_rows.shape, dtype=BF), shaped(n_mp, *down_rows.shape, dtype=BF),
        ],
        scratch_shapes=[pltpu.VMEM((n_mp, *cls_rows.shape), BF)] + spread_scratch(n_dp, n_mp) * 3,
        compiler_params=remote_params(7),
        name="feed",
    )(mid, cols, bias_row, base, stat, vec, wmlp, cls_rows, up_rows, down_rows)


def run_token(n_dp, n_mp, group, card, vec, aux, wcls, wup, wdown, head, norm, cprob, cprob0, z):
    rows = card.shape[0]
    local = norm.shape[0]
    images = n_dp * n_mp * local
    hidden = wup.shape[1]
    shard = wcls.shape[1] // 4
    wide = wup.shape[0] * hidden
    dma = pltpu.SemaphoreType.DMA
    far = (wcls, wup, wdown, head, norm, cprob, cprob0, z)
    return pl.pallas_call(
        functools.partial(card_token_kernel, n_dp, n_mp, group),
        in_specs=[WHOLE] * 3 + [ANY] * 8,
        out_specs=[WHOLE] * 10,
        out_shape=[
            shaped(local, 2 * HEADS, WIDE, dtype=BF), shaped(local, 2 * HEADS, D, dtype=BF),
            shaped(D, D), shaped(16, D), shaped(shard, D), shaped(hidden, D), shaped(hidden, D),
            shaped(head.shape[0] + 8, D), shaped(16, D), shaped(8, 128),
        ],
        scratch_shapes=[
            pltpu.VMEM((images, D), F32), pltpu.VMEM((D, D), F32), pltpu.VMEM((wide, D), F32),
            pltpu.VMEM((wide, D), F32), pltpu.VMEM((n_dp * n_mp * rows, 128), F32),
            pltpu.VMEM((n_dp * n_mp * rows, 128), BF), dma((2, n_dp)), dma((2, n_mp)), dma((8,)),
        ]
        + [pltpu.VMEM(item.shape, item.dtype) for item in far],
        compiler_params=pltpu.CompilerParams(
            vmem_limit_bytes=VMEM_LIMIT, collective_id=1, has_side_effects=True
        ),
        name="token_net",
    )(card, vec, aux, *far)


def run_feed_back(n_dp, left, right, gv, local_rows, patch, mid, raw, act, slope, vec, wmlp):
    count = mid.shape[0]
    wide = act.shape[2]
    feed = (wmlp.shape[0], pad_rows(wmlp.shape[1] + D // wmlp.shape[0], n_dp), D)
    return pl.pallas_call(
        feed_back_kernel,
        grid=(count,),
        in_specs=[
            per_image(2 * HEADS, WIDE), per_image(2 * HEADS, D), constant(D, D), constant(16, D),
            per_image(P_SIZE, D), per_image(P_SIZE, D), per_image(P_SIZE, D),
            per_image(P_SIZE, wide), per_image(P_SIZE, wide), constant(*vec.shape),
            constant(*wmlp.shape),
        ],
        out_specs=[per_image(P_SIZE, D), constant(*feed), constant(16, D)],
        out_shape=[shaped(count, P_SIZE, D), shaped(*feed, dtype=BF), shaped(16, D)],
        scratch_shapes=[pltpu.VMEM(wmlp.shape, F32)],
        compiler_params=params(),
        name="feed_back",
    )(left, right, gv, local_rows, patch, mid, raw, act, slope, vec, wmlp)


def run_self_back(
    n_dp, n_mp, dmid, pixels, embed, q, k, v, prob, post, ho, raw, vec, wattn, t1row, t2row, gfeed,
    rows_feed,
):
    count = dmid.shape[0]
    rows_a, rows_b = halves(gfeed.shape[1], n_dp)
    blocks = (n_mp, pad_rows(wattn.shape[1], n_dp), D)
    commons = (n_mp, table_rows(n_dp, n_mp), D)
    rows = blocks[1] + rows_a + rows_b
    n_lo = 2 if n_dp < 16 else 4
    return pl.pallas_call(
        functools.partial(self_back_kernel, n_dp, n_mp),
        grid=(count,),
        in_specs=[
            per_image(P_SIZE, D), constant(*pixels.shape), per_image(P_SIZE, D),
            per_image(P_SIZE, D), per_image(P_SIZE, D), per_image(P_SIZE, D),
            per_image(P_SIZE, HEADS * PAD), per_image(HEADS * PAD, D), per_image(P_SIZE, D),
            per_image(P_SIZE, D), constant(*vec.shape), constant(*wattn.shape), constant(HEADS, D),
            constant(HEADS, D), constant(*gfeed.shape), constant(16, D),
        ],
        out_specs=[
            ANY, ANY, constant(8, 128),
        ],
        out_shape=[
            shaped(rows, D, dtype=BF), shaped(*commons, dtype=BF), shaped(8, 128),
        ],
        scratch_shapes=[
            pltpu.VMEM(wattn.shape, F32), pltpu.VMEM((P_SIZE, D), F32), pltpu.VMEM((24, D), F32),
            pltpu.VMEM((count, P_SIZE, D), F32), pltpu.VMEM((P_SIZE, count, D), F32),
            pltpu.VMEM((HEADS * PAD, D), BF), pltpu.VMEM((HEADS * PAD, D), BF),
            pltpu.VMEM((P_SIZE, HEADS * PAD), F32),
            pltpu.VMEM(blocks, BF), pltpu.VMEM(commons, BF), pltpu.VMEM((rows, D), BF),
            pltpu.VMEM(commons, BF), pltpu.SemaphoreType.DMA((2,)),
        ]
        + sum_scratch(n_dp, n_mp, rows_a, True)
        + sum_scratch(n_dp, n_mp, rows_b, False)
        + reduce_scratch(
            n_dp, n_mp, blocks[1], commons[1], (rows_a // n_lo, rows_b // n_lo)
        ),
        compiler_params=pltpu.CompilerParams(
            vmem_limit_bytes=VMEM_LIMIT, dimension_semantics=("arbitrary",), collective_id=5,
            has_side_effects=True,
        ),
        name="self_back",
    )(dmid, pixels, embed, q, k, v, prob, post, ho, raw, vec, wattn, t1row, t2row, gfeed, rows_feed)


def share_cards(n_dp, n_mp, card, out, slots, dp_sem, mp_sem):
    dp = lax.axis_index("dp")
    mp = lax.axis_index("mp")
    rows = card.shape[0]
    barrier = pltpu.get_barrier_semaphore()
    others_dp = [(lax.rem(dp + step, n_dp), mp) for step in range(1, n_dp)]
    others_mp = [(dp, lax.rem(mp + step, n_mp)) for step in range(1, n_mp)]
    for partner in others_dp + others_mp:
        pl.semaphore_signal(barrier, inc=1, device_id=partner, device_id_type=MESH)
    own = tile_rows(slots, (mp * n_dp + dp) * rows, rows)
    slots[pl.ds(pl.multiple_of((mp * n_dp + dp) * rows, 16), rows), :] = card[...].astype(BF)
    pl.semaphore_wait(barrier, n_dp + n_mp - 2)
    sends = [
        remote(own, own, dp_sem.at[0, step], dp_sem.at[1, step], others_dp[step - 1])
        for step in range(1, n_dp)
    ]
    for copy in sends:
        copy.start()
    for step in range(1, n_dp):
        source = lax.rem(dp + n_dp - step, n_dp)
        theirs = tile_rows(slots, (mp * n_dp + source) * rows, rows)
        remote(own, theirs, dp_sem.at[0, step], dp_sem.at[1, step], (source, mp)).wait_recv()
    slab = tile_rows(slots, mp * n_dp * rows, n_dp * rows)
    for step in range(1, n_mp):
        sends.append(
            remote(slab, slab, mp_sem.at[0, step], mp_sem.at[1, step], others_mp[step - 1])
        )
        sends[-1].start()
    for step in range(1, n_mp):
        source = lax.rem(mp + n_mp - step, n_mp)
        theirs = tile_rows(slots, source * n_dp * rows, n_dp * rows)
        remote(slab, theirs, mp_sem.at[0, step], mp_sem.at[1, step], (dp, source)).wait_recv()
    for i in range(n_dp):
        for j in range(n_mp):
            to, source = (i * n_mp + j) * rows, (j * n_dp + i) * rows
            out[to : to + rows, :] = slots[source : source + rows, :].astype(F32)
    for copy in sends:
        copy.wait_send()


def start_kernel(
    n_dp, n_mp, group, attn_in, attn_out, mlp_in, mlp_out, pixels, tables, vec, mix, mask,
    counts, labels, pairs,
    out, mlp_rows, cls_rows, up_rows, down_rows, embed_far, head_out, t1_out, t2_out, cols_out, bias_out, base_out,
    embed_out, head_rows, wide_up, wide_down, shard, wide_in, wide_out, patch_rows, pos_rows, by_patch, near_send, near_recv, far_send, far_recv, load_sem,
):
    dp = lax.axis_index("dp")
    mp = lax.axis_index("mp")
    n_y = n_mp // 2
    y = lax.div(mp, 2)
    core = lax.rem(mp, 2)
    sibling = (dp, y * 2 + 1 - core)
    load_patch = pltpu.make_async_copy(tables.at[pl.ds(0, PIX)], patch_rows, load_sem.at[0])
    load_pos = pltpu.make_async_copy(tables.at[pl.ds(PIX, 200)], pos_rows, load_sem.at[1])
    load_in = pltpu.make_async_copy(attn_in, wide_in, load_sem.at[2])
    load_out = pltpu.make_async_copy(attn_out, wide_out, load_sem.at[3])
    load_up = pltpu.make_async_copy(mlp_in, wide_up, load_sem.at[5])
    load_down = pltpu.make_async_copy(mlp_out, wide_down, load_sem.at[6])
    load_in.start()
    load_out.start()
    load_patch.start()
    load_pos.start()
    classes = head_out.shape[0]
    load_head = pltpu.make_async_copy(
        tables.at[pl.ds(PIX + P_SIZE - 4, classes + 4)], head_rows, load_sem.at[4]
    )
    load_up.start()
    load_down.start()
    load_head.start()
    barrier = pltpu.get_barrier_semaphore()
    pl.semaphore_signal(barrier, inc=1, device_id=sibling, device_id_type=MESH)
    for step in range(1, n_y):
        pl.semaphore_signal(
            barrier, inc=1, device_id=(dp, lax.rem(y + step, n_y) * 2 + core), device_id_type=MESH
        )
    third = attn_in.shape[1]
    load_in.wait()
    load_out.wait()
    shard[:third, :] = wide_in[0].astype(BF)
    shard[third:, :] = wide_out[0].astype(BF)
    pl.semaphore_wait(barrier, n_y)
    far = [
        remote(
            shard, out.at[mp], far_send.at[step], far_recv.at[step],
            (dp, lax.rem(y + step, n_y) * 2 + core),
        )
        for step in range(1, n_y)
    ]
    for copy in far:
        copy.start()
    near = [remote(shard, out.at[mp], near_send.at[0], near_recv.at[0], sibling)]
    near[0].start()
    out[pl.ds(mp, 1)] = shard[...][None]

    cls_rows[:third, :] = wide_in[1].astype(BF)
    cls_rows[third:, :] = wide_out[1].astype(BF)
    hidden = mlp_rows.shape[0] // 2
    load_up.wait()
    load_down.wait()
    mlp_rows[:hidden, :] = wide_up[0].T.astype(BF)
    mlp_rows[hidden:, :] = wide_down[0].astype(BF)
    up_rows[...] = wide_up[1].T.astype(BF)
    down_rows[...] = wide_down[1].astype(BF)

    images = mask.shape[0]
    lane = lax.broadcasted_iota(jnp.int32, (1, 128), 1)
    keep = (mask[...] > 0).astype(F32)
    bias = (1.0 - keep) * MASKED
    count = counts[0]
    okays = []
    bias_out[...] = jnp.full(bias_out.shape, MASKED, F32)
    for n in range(images):
        okays.append((jnp.full((1, 1), mp * images + n, jnp.int32) >= group - count).astype(F32))
        bias_out[:, n * WIDE : n * WIDE + P_SIZE] = bias[n : n + 1, :]
        tokens = jnp.sum(keep[n : n + 1, :], 1, keepdims=True) * okays[n]
        entries = (
            lax.div(labels[n], 32), lax.rem(labels[n], 32), lax.div(pairs[n], 32),
            lax.rem(pairs[n], 32), count,
        )
        line = jnp.where(lane == len(entries), tokens, 0.0)
        for place, entry in enumerate(entries):
            line = jnp.where(lane == place, entry.astype(F32), line)
        base_out[n : n + 1, :] = line
    cols_out[...] = jnp.concatenate([bias, keep * jnp.concatenate(okays, 0)], 0).T
    heads = head_mask()
    exact = functools.partial(
        lax.dot_general, preferred_element_type=F32, precision=lax.Precision.HIGHEST
    )
    t1_out[...] = exact(mix[0], heads, (((1,), (0,)), ((), ()))) * SCALE
    t2_out[...] = exact(mix[1], heads, (((0,), (0,)), ((), ())))

    load_patch.wait()
    wp = patch_rows[...].astype(BF)
    local = embed_out.shape[0]
    half = P_SIZE // 2
    for place in range(2):
        rows = slice(place * half * local, (place + 1) * half * local)
        by_patch[place * half : (place + 1) * half] = nn(pixels[rows, :], wp).reshape(half, local, D)

    for step in range(1, n_y):
        source = lax.rem(y + n_y - step, n_y) * 2
        slot = source + core
        remote(
            shard, out.at[slot], far_send.at[step], far_recv.at[step], (dp, slot)
        ).wait_recv()
        copy = remote(
            out.at[slot], out.at[slot], near_send.at[step], near_recv.at[step], sibling
        )
        copy.start()
        near.append(copy)
    load_pos.wait()
    offset = pos_rows[:P_SIZE, :] + vec[16:17, :]
    for n in range(local):
        embed_out[n] = by_patch[:, n, :] + offset
    save_embed = pltpu.make_async_copy(embed_out, embed_far, load_sem.at[7])
    save_embed.start()
    load_head.wait()
    head_out[...] = head_rows[4:, :].astype(BF)
    save_embed.wait()
    for copy in far:
        copy.wait_send()
    for step in range(n_y):
        slot = lax.rem(y + n_y - step, n_y) * 2 + 1 - core
        near[step].wait_send()
        remote(
            out.at[slot], out.at[slot], near_send.at[step], near_recv.at[step], sibling
        ).wait_recv()


def run_start(
    n_dp, n_mp, group, attn_in, attn_out, mlp_in, mlp_out, pixels, tables, vec, mix, mask, counts,
    labels, pairs,
):
    local = labels.shape[0]
    classes = tables.shape[0] - PIX - P_SIZE
    scalars = pl.BlockSpec(memory_space=pltpu.SMEM)
    n_y = n_mp // 2
    rows = attn_in.shape[1] + attn_out.shape[1]
    hidden = mlp_in.shape[2]
    dma = pltpu.SemaphoreType.DMA
    return pl.pallas_call(
        functools.partial(start_kernel, n_dp, n_mp, group),
        in_specs=[ANY] * 4 + [WHOLE, ANY, WHOLE, WHOLE, WHOLE, scalars, scalars, scalars],
        out_specs=[WHOLE] * 5 + [ANY] + [WHOLE] * 6,
        out_shape=[
            shaped(n_mp, rows, D, dtype=BF), shaped(2 * hidden, D, dtype=BF),
            shaped(rows, D, dtype=BF), shaped(hidden, D, dtype=BF), shaped(hidden, D, dtype=BF),
            shaped(local, P_SIZE, D),
            shaped(classes, D, dtype=BF), shaped(HEADS, D), shaped(HEADS, D),
            shaped(P_SIZE, 2 * local), shaped(1, local * WIDE), shaped(local, 128),
        ],
        scratch_shapes=[
            pltpu.VMEM((local, P_SIZE, D), F32),
            pltpu.VMEM((classes + 4, D), F32), pltpu.VMEM(mlp_in.shape, F32),
            pltpu.VMEM(mlp_out.shape, F32),
            pltpu.VMEM((rows, D), BF), pltpu.VMEM(attn_in.shape, F32),
            pltpu.VMEM(attn_out.shape, F32), pltpu.VMEM((PIX, D), F32),
            pltpu.VMEM((200, D), F32),
            pltpu.VMEM((P_SIZE, local, D), F32),
            dma((n_y,)), dma((n_y,)), dma((n_y,)), dma((n_y,)), dma((8,)),
        ],
        compiler_params=pltpu.CompilerParams(
            vmem_limit_bytes=VMEM_LIMIT, collective_id=2, has_side_effects=True
        ),
        name="start",
    )(
        attn_in, attn_out, mlp_in, mlp_out, pixels, tables, vec, mix, mask, counts, labels, pairs
    )


def reduce_rows(
    p, blocks, commons, chunk_a, chunk_b,
    block_out, shared_out, square_out,
    squares, attn_run, run_a, run_b, sem_a, sem_b, high_a, high_b, high_sem, low_sem, square_sem,
    *sum_buffers,
):
    n_mp = p.n_mp
    attn = ShardSum(p, blocks, 0, True, *sum_buffers[:SUM_BUFFERS])
    table = TableSum(p, commons, shared_out, *sum_buffers[SUM_BUFFERS:])
    rows_a = blocks.shape[1]
    rows_feed = p.n_lo * run_a.shape[0]
    hand_a = HandLow(p, block_out, rows_a, rows_feed, sem_a)
    hand_b = HandLow(p, block_out, rows_a + rows_feed, p.n_lo * run_b.shape[0], sem_b)
    wide_a = HandHigh(p, run_a, high_a)
    wide_b = HandHigh(p, run_b, high_b)
    hand_high = HandHigh(p, attn_run, high_sem)
    hand_low = HandLow(p, block_out, 0, rows_a, low_sem)

    attn.start()
    table.start()
    wide_a.start(chunk_a)
    wide_b.start(chunk_b)
    attn.second()
    table.near_to_low()
    table.low_to_high()
    attn.third()
    wide_a.arrive()
    hand_a.start(run_a[...])
    wide_b.arrive()
    hand_b.start(run_b[...])
    table.high_to_far()
    attn.fourth()
    table.turn()
    table.far_to_high()
    hand_high.start(attn.finish())
    table.high_to_low()
    hand_high.arrive()
    hand_low.start(attn_run[...])
    table.low_to_near()
    sends = []

    for item in (hand_a, hand_b, hand_low):
        item.arrive()
    sums = block_out[...].astype(F32)
    sums = colsum(sums * sums)
    squares[pl.ds(p.mp, 1)] = jnp.broadcast_to(
        sums[:, 0:128] + sums[:, 128:256] + sums[:, 256:384], (8, 128)
    )[None]

    for step in range(1, p.n_y):
        sends.append(
            remote(
                squares.at[p.mp], squares.at[p.mp], square_sem.at[0, step],
                square_sem.at[1, step], (p.dp, p.along_y(step) * 2 + p.core),
            )
        )
        sends[-1].start()
    for step in range(1, p.n_y):
        source = p.along_y(p.n_y - step) * 2 + p.core
        remote(
            squares.at[p.mp], squares.at[source], square_sem.at[0, step], square_sem.at[1, step],
            (p.dp, source),
        ).wait_recv()
    mine = squares[pl.ds(p.core, 1)]
    for y in range(1, p.n_y):
        mine += squares[pl.ds(2 * y + p.core, 1)]
    squares[pl.ds(n_mp + p.core, 1)] = mine
    sends.append(
        remote(
            squares.at[n_mp + p.core], squares.at[n_mp + p.core], square_sem.at[0, 0],
            square_sem.at[1, 0], p.sibling,
        )
    )
    sends[-1].start()
    table.finish()
    remote(
        squares.at[n_mp + p.core], squares.at[n_mp + 1 - p.core], square_sem.at[0, 0],
        square_sem.at[1, 0], p.sibling,
    ).wait_recv()
    square_out[...] = squares[n_mp] + squares[n_mp + 1]
    for copy in sends:
        copy.wait_send()
    for item in (attn, wide_a, wide_b, hand_a, hand_b, hand_high, hand_low):
        item.wait_sends()


def reduce_scratch(n_dp, n_mp, rows_a, wide, feed):
    assert wide == 256
    n_lo = 2 if n_dp < 16 else 4
    n_hi = n_dp // n_lo
    dma = pltpu.SemaphoreType.DMA
    return (
        [
            pltpu.VMEM((n_mp + 2, 8, 128), F32), pltpu.VMEM((rows_a // n_lo, D), BF),
            pltpu.VMEM((feed[0], D), BF), pltpu.VMEM((feed[1], D), BF),
            dma((2, n_lo)), dma((2, n_lo)), dma((2, n_hi)), dma((2, n_hi)), dma((2, n_hi)),
            dma((2, n_lo)), dma((2, n_mp)),
        ]
        + sum_scratch(n_dp, n_mp, rows_a, True)
        + table_scratch(n_dp, n_mp, wide)
    )


def root(values):
    return values * lax.rsqrt(values)


def adam_parts(gradient, mean, square, factor):
    clipped = gradient * factor
    mean_new = BETA_ONE * mean + (1.0 - BETA_ONE) * clipped
    square_new = BETA_TWO * square + (1.0 - BETA_TWO) * clipped * clipped
    direction = (
        mean_new
        * (1.0 / (1.0 - BETA_ONE**STEP))
        / (root(square_new * (1.0 / (1.0 - BETA_TWO**STEP))) + ADAM_EPS)
    )
    return (mean_new, square_new, direction)


def fold(values):
    squares = (values * values).reshape(values.shape[0] // 8, 8, values.shape[1]).sum(0)
    width = values.shape[1]
    if width % 128:
        return jnp.broadcast_to(jnp.sum(squares, 1, keepdims=True), (8, 128)) * (1.0 / 128)
    return sum(squares[:, i : i + 128] for i in range(0, width, 128))


def total(values):
    return jnp.sum(jnp.sum(values, 0, keepdims=True), 1, keepdims=True)


def moment_sweep(factor, grad, w, m, s, u, rows):
    chunk = 32 if rows % 32 == 0 else 16

    def step(i, kept):
        at = pl.ds(pl.multiple_of(i * chunk, chunk), chunk)
        weight = w[at, :]
        mean, second, direction = adam_parts(grad(i, chunk), m[at, :], s[at, :], factor)
        m[at, :] = mean
        s[at, :] = second
        update = direction + DECAY * weight
        u[at, :] = update
        return (kept[0] + fold(weight), kept[1] + fold(update))

    zero = jnp.zeros((8, 128), F32)
    return lax.fori_loop(0, rows // chunk, step, (zero, zero))


def rows_from(ref, first):
    def read(i, chunk):
        at = pl.ds(pl.multiple_of(first + i * chunk, 16), chunk)
        return ref[at, :].astype(F32)

    return read


def moment_kernel(
    n_dp, block_sq, gout1, rows1, stat, aux, vec, vec_mean, vec_square, mix, mix_mean, mix_square,
    *rest,
):
    large, rest = rest[:5], rest[5:]
    state = rest[:12]
    outs = rest[12:24]
    (
        vec_out, vec_mean_out, vec_square_out, mix_out, mix_mean_out, mix_square_out,
        misc_out, sums_out,
    ) = rest[24:32]
    held = rest[32:44]
    updates = rest[44:48]
    grad_q, grad_k, grad_flip, load_sem, save_sem = rest[48:53]
    large_here = rest[53:]
    first_loads = [
        pltpu.make_async_copy(large[i], large_here[i], load_sem.at[12 + i]) for i in range(5)
    ]
    loads = [pltpu.make_async_copy(state[i], held[i], load_sem.at[i]) for i in range(12)]
    for copy in first_loads + loads:
        copy.start()
    for copy in first_loads:
        copy.wait()
    block, shared, wcls, gup1, gdown1 = large_here
    mp = lax.axis_index("mp")
    hs = state[3].shape[1]
    fs = state[9].shape[1]
    feed = pad_rows(4 * hs, n_dp)

    rows2 = shared[PIX + 208 : PIX + 224, :].astype(F32)
    rows3 = shared[PIX + 224 : PIX + 256, :].astype(F32)
    token = aux[8:9, :]
    wq = part(wcls, 0, hs)
    wk = part(wcls, hs, hs).astype(F32)
    query = nt(wq, aux[8:16, :].astype(BF))[:, 0:1].astype(BF).astype(F32)
    dkeys = jnp.concatenate(
        [jnp.broadcast_to(rows2[8 + h : 9 + h, :], (HEAD, D)) for h in range(HEADS)], 0
    )
    dquery = SCALE * jnp.sum(wk * dkeys, 1, keepdims=True)
    gq = dquery * token
    gk = (SCALE * query) * dkeys
    grad_q[...] = gq
    grad_k[...] = gk
    dtoken = rows2[6:7, :] + colsum(dquery * wq.astype(F32))
    unit, inverse = normalize(jnp.broadcast_to(vec[17:18, :], (8, D)))
    dcls = normalize_back(unit, inverse, vec[8:9, :], jnp.broadcast_to(dtoken, (8, D)))[0:1, :]
    dgain = rows2[4:5, :] + dtoken * unit[0:1, :]
    last = rows1[...]
    positions = shared[PIX : PIX + 208, :].astype(F32)
    grad_vec = jnp.concatenate(
        [
            rows3[0:4, :], rows2[0:4, :], dgain, rows2[5:6, :] + dtoken, last[2:8, :],
            colsum(positions), last[8:9, :] + dcls, last[9:11, :],
        ],
        0,
    )
    mask = head_mask()
    exact = functools.partial(
        lax.dot_general, dimension_numbers=(((1,), (1,)), ((), ())),
        preferred_element_type=F32, precision=lax.Precision.HIGHEST,
    )
    grad_mix = (exact(rows3[8:16, :], mask) * SCALE, exact(mask, rows3[16:24, :]))

    square = total(block_sq[0:1, :]) + total(stat[1:2, :]) + total(colsum(gq * gq + gk * gk))
    square += total(grad_vec * grad_vec)
    square += total(grad_mix[0] * grad_mix[0]) + total(grad_mix[1] * grad_mix[1])

    def square_rows(i, kept):
        rows = shared[pl.ds(pl.multiple_of(i * 16, 16), 16), :].astype(F32)
        return kept + fold(rows)

    square += total(lax.fori_loop(0, (PIX + 208) // 16, square_rows, jnp.zeros((8, 128), F32)))
    norm = jnp.sqrt(square)
    factor = CLIP / jnp.maximum(norm, CLIP)

    mean, second, direction = adam_parts(grad_vec, vec_mean[...], vec_square[...], factor)
    vec_mean_out[...] = mean
    vec_square_out[...] = second
    vec_out[...] = vec[...] - RATE_VECTOR * direction
    misc = []
    weight_sums = []
    for b in range(2):
        mean, second, direction = adam_parts(grad_mix[b], mix_mean[b], mix_square[b], factor)
        mix_mean_out[b] = mean
        mix_square_out[b] = second
        update = direction + DECAY * mix[b]
        weight_sq = total(mix[b] * mix[b])
        update_sq = total(update * update)
        mix_out[b] = mix[b] - RATE * jnp.sqrt(weight_sq / (update_sq + 1e-12)) * update
        weight_sums.append(weight_sq)
        misc.append(update_sq)

    def sweep(grad, w, m, s, u, rows):
        return moment_sweep(factor, grad, w, m, s, u, rows)

    saves = []

    def save(i, source):
        saves.append(pltpu.make_async_copy(source, outs[i], save_sem.at[i]))
        saves[-1].start()

    sums = []
    own_h = pl.multiple_of(mp * hs, hs)
    for kind in range(4):
        for copy in loads[3 * kind : 3 * kind + 3]:
            copy.wait()
        w, m, s = held[3 * kind : 3 * kind + 3]
        u = updates[kind]
        for b in range(2):
            views = (w.at[b], m.at[b], s.at[b], u.at[b])
            if kind == 0 and b == 0:
                sums.append(sweep(rows_from(block, 0), *views, 3 * hs))
            elif kind == 0:
                pieces = []
                for third, source in enumerate(
                    (
                        rows_from(grad_q, own_h),
                        rows_from(grad_k, own_h),
                        rows_from(block, feed + 2 * fs),
                    )
                ):
                    pieces.append(
                        sweep(
                            source, *(view.at[pl.ds(third * hs, hs)] for view in views), hs
                        )
                    )
                sums.append(
                    tuple(pieces[0][i] + pieces[1][i] + pieces[2][i] for i in range(2))
                )
            elif kind == 1:
                source = rows_from(gout1, 0) if b else rows_from(block, 3 * hs)
                sums.append(sweep(source, *views, hs))
            elif kind == 2:
                if b:
                    grad_flip[...] = gup1[...].T
                else:
                    grad_flip[...] = block[feed : feed + fs, :].astype(F32).T
                sums.append(sweep(rows_from(grad_flip, 0), *views, D))
            else:
                source = rows_from(gdown1, 0) if b else rows_from(block, feed + fs)
                sums.append(sweep(source, *views, fs))
        save(3 * kind, u)
        save(3 * kind + 1, m)
        save(3 * kind + 2, s)
    for place, pair in enumerate(sums):
        sums_out[place : place + 1, :] = colsum(pair[1])
        sums_out[8 + place : 9 + place, :] = colsum(pair[0])

    lane = lax.broadcasted_iota(jnp.int32, (1, 128), 1)
    misc_out[0:1, :] = jnp.broadcast_to(norm, (1, 128))
    weight_line = jnp.zeros((1, 128), F32)
    update_line = jnp.zeros((1, 128), F32)
    for b in range(2):
        weight_line = jnp.where(lane == 11 + b, weight_sums[b], weight_line)
        update_line = jnp.where(lane == 11 + b, misc[b], update_line)
    misc_out[1:2, :] = weight_line
    misc_out[2:3, :] = update_line
    misc_out[3:8, :] = jnp.zeros((5, 128), F32)
    for copy in saves:
        copy.wait()


def table_kernel(misc, shared, ghead, *rest):
    state, outs, misc_out = rest[:3], rest[3:6], rest[6]
    w, m, s, table_update, load_sem, save_sem = rest[7:]
    rows_all = w.shape[0]
    edge = PIX + P_SIZE - 4
    body = (rows_all - edge - 16) // 64 * 32
    middle = edge + 16 + body
    cuts = (0, PIX // 2, PIX, middle, rows_all)
    slabs = [pl.ds(low, high - low) for low, high in zip(cuts, cuts[1:])]
    loads = [
        [
            pltpu.make_async_copy(state[i].at[at], (w, m, s)[i].at[at], load_sem.at[i, place])
            for i in range(3)
        ]
        for place, at in enumerate(slabs)
    ]
    for group in loads:
        for copy in group:
            copy.start()
    factor = CLIP / jnp.maximum(misc[0:1, 0:1], CLIP)
    saves = []

    def arrive(place):
        for copy in loads[place]:
            copy.wait()

    def save(i, place):
        at = slabs[place]
        saves.append(
            pltpu.make_async_copy((w, m, s)[i].at[at], outs[i].at[at], save_sem.at[i, place])
        )
        saves[-1].start()

    def slab(first, count, grad):
        at = slice(first, first + count)
        weight = w[at, :]
        mean, second, direction = adam_parts(grad, m[at, :], s[at, :], factor)
        m[at, :] = mean
        s[at, :] = second
        update = direction + DECAY * weight
        table_update[at, :] = update
        return weight, update

    def run(first, count, source, offset):
        def at(ref, start):
            return ref.at[pl.ds(start, count)]

        return moment_sweep(
            factor, rows_from(source, offset), at(w, first), at(m, first), at(s, first),
            at(table_update, first), count,
        )

    def renew(first, count, rate):
        def step(i, _):
            at = pl.ds(pl.multiple_of(first + i * 32, 16), 32)
            w[at, :] = w[at, :] - rate * table_update[at, :]
            return 0

        lax.fori_loop(0, count // 32, step, 0)

    def rate_of(weight_sq, update_sq):
        return RATE * jnp.sqrt(weight_sq / (update_sq + 1e-12))

    def masked(values, mask):
        return total(jnp.where(mask, values * values, 0.0))

    arrive(0)
    first_half = run(0, PIX // 2, shared, 0)
    save(1, 0)
    save(2, 0)
    arrive(1)
    second_half = run(PIX // 2, PIX // 2, shared, PIX // 2)
    save(1, 1)
    save(2, 1)
    sq_w = [total(first_half[0] + second_half[0])]
    sq_u = [total(first_half[1] + second_half[1])]
    rates = [rate_of(sq_w[0], sq_u[0])]
    renew(0, PIX, rates[0])
    save(0, 0)
    save(0, 1)
    arrive(2)
    place_rows = run(PIX, P_SIZE - 4, shared, PIX)
    tile = lax.broadcasted_iota(jnp.int32, (16, 1), 0) < 4
    weight, update = slab(edge, 16, shared[edge : edge + 16, :].astype(F32) + ghead[0:16, :])
    heads = run(edge + 16, body, ghead, 16)
    save(1, 2)
    save(2, 2)
    arrive(3)
    rest_rows = (rows_all - middle) // 32 * 32
    more_heads = run(middle, rest_rows, ghead, 16 + body)
    left = middle + rest_rows
    tail_weight, tail_update = slab(
        left, rows_all - left, ghead[16 + left - edge - 16 : 16 + rows_all - edge - 16, :]
    )
    save(1, 3)
    save(2, 3)
    sq_w += [
        total(place_rows[0]) + masked(weight, tile),
        total(heads[0] + more_heads[0]) + masked(weight, ~tile) + total(tail_weight * tail_weight),
    ]
    sq_u += [
        total(place_rows[1]) + masked(update, tile),
        total(heads[1] + more_heads[1]) + masked(update, ~tile) + total(tail_update * tail_update),
    ]
    rates += [rate_of(sq_w[i], sq_u[i]) for i in (1, 2)]
    renew(PIX, P_SIZE - 4, rates[1])
    w[edge : edge + 16, :] = weight - jnp.where(tile, rates[1], rates[2]) * update
    renew(edge + 16, body, rates[2])
    save(0, 2)
    renew(middle, rest_rows, rates[2])
    w[left:rows_all, :] = tail_weight - rates[2] * tail_update
    save(0, 3)

    lane = lax.broadcasted_iota(jnp.int32, (1, 128), 1)
    weight_line = misc[1:2, :]
    update_line = misc[2:3, :]
    for place in range(3):
        weight_line = jnp.where(lane == 8 + place, sq_w[place], weight_line)
        update_line = jnp.where(lane == 8 + place, sq_u[place], update_line)
    misc_out[...] = misc[...]
    misc_out[1:2, :] = weight_line
    misc_out[2:3, :] = update_line
    for copy in saves:
        copy.wait()


def run_moments(n_dp, grads, smalls, large, state):
    outs = [jax.ShapeDtypeStruct(item.shape, F32) for item in state]
    fs = state[9].shape[1]
    dma = pltpu.SemaphoreType.DMA
    return pl.pallas_call(
        functools.partial(moment_kernel, n_dp),
        in_specs=[WHOLE] * (len(grads) + len(smalls)) + [ANY] * 17,
        out_specs=[ANY] * 12 + [WHOLE] * 8,
        out_shape=outs
        + [jax.ShapeDtypeStruct(item.shape, F32) for item in smalls]
        + [shaped(8, 128), shaped(16, 128)],
        scratch_shapes=[pltpu.VMEM(item.shape, F32) for item in state]
        + [pltpu.VMEM(state[3 * kind].shape, F32) for kind in range(4)]
        + [
            pltpu.VMEM((D, D), F32), pltpu.VMEM((D, D), F32), pltpu.VMEM((D, fs), F32),
            dma((17,)), dma((12,)),
        ]
        + [pltpu.VMEM(item.shape, item.dtype) for item in large],
        compiler_params=pltpu.CompilerParams(vmem_limit_bytes=VMEM_LIMIT),
        name="moments",
    )(*grads, *smalls, *large, *state)


def run_tables(misc, shared, ghead, state):
    shape = state[0].shape
    dma = pltpu.SemaphoreType.DMA
    return pl.pallas_call(
        table_kernel,
        in_specs=[WHOLE] * 3 + [ANY] * 3,
        out_specs=[ANY] * 3 + [WHOLE],
        out_shape=[shaped(*shape)] * 3 + [shaped(8, 128)],
        scratch_shapes=[pltpu.VMEM(shape, F32)] * 4 + [dma((3, 4)), dma((3, 4))],
        cost_estimate=pl.CostEstimate(
            flops=40 * shape[0] * shape[1], bytes_accessed=28 * shape[0] * shape[1],
            transcendentals=2 * shape[0] * shape[1],
        ),
        compiler_params=pltpu.CompilerParams(vmem_limit_bytes=VMEM_LIMIT),
        name="tables",
    )(misc, shared, ghead, *state)


def renew_kernel(n_mp, misc, stat, *rest):
    theirs, rest = rest[:n_mp], rest[n_mp:]
    weights, updates = rest[:4], rest[4:8]
    new, copies = rest[8:12], rest[12:16]
    norms, norm_out, stat_out = rest[16:19]
    here, changes, lows = rest[19:23], rest[23:27], rest[27:31]
    slots, load_sem, save_sem = rest[31:]
    loads = [
        (
            pltpu.make_async_copy(weights[kind], here[kind], load_sem.at[0, kind]),
            pltpu.make_async_copy(updates[kind], changes[kind], load_sem.at[1, kind]),
        )
        for kind in range(4)
    ]
    for pair in loads[::-1]:
        for copy in pair:
            copy.start()
    mp = lax.axis_index("mp")
    for step in range(n_mp):
        slots[pl.ds(lax.rem(mp + n_mp - step, n_mp), 1)] = theirs[step][...][None]
    sums = jnp.sum(slots[...], 0)
    rates = []
    lane = lax.broadcasted_iota(jnp.int32, (1, 128), 1)
    weight_line, update_line = misc[1:2, :], misc[2:3, :]
    for place in range(8):
        update_sq = total(sums[place : place + 1, :])
        weight_sq = total(sums[8 + place : 9 + place, :])
        rates.append(RATE * jnp.sqrt(weight_sq / (update_sq + 1e-12)))
        weight_line = jnp.where(lane == place, weight_sq, weight_line)
        update_line = jnp.where(lane == place, update_sq, update_line)
    norms[...] = jnp.sqrt(jnp.concatenate([weight_line, update_line], 0))[:, :13]
    norm_out[...] = misc[0:1, 0:1]
    stat_out[...] = stat[0:1, :12]
    saves = []
    for kind in (3, 2, 1, 0):
        w, u, low = here[kind], changes[kind], lows[kind]
        rows = w.shape[1]
        chunk = 32 if rows % 32 == 0 else 16
        for copy in loads[kind]:
            copy.wait()
        for b in range(2):
            rate = rates[2 * kind + b]

            def step(i, _, b=b, w=w, u=u, low=low, rate=rate, chunk=chunk):
                at = pl.ds(pl.multiple_of(i * chunk, chunk), chunk)
                values = w[b, at, :] - rate * u[b, at, :]
                w[b, at, :] = values
                low[b, at, :] = values.astype(BF)
                return 0

            lax.fori_loop(0, rows // chunk, step, 0)
        saves.append(pltpu.make_async_copy(w, new[kind], save_sem.at[0, kind]))
        saves.append(pltpu.make_async_copy(low, copies[kind], save_sem.at[1, kind]))
        for copy in saves[-2:]:
            copy.start()
    for copy in saves:
        copy.wait()


def run_renew(n_mp, misc, stat, sums, weights, updates):
    dma = pltpu.SemaphoreType.DMA
    return pl.pallas_call(
        functools.partial(renew_kernel, n_mp),
        in_specs=[WHOLE] * (2 + n_mp) + [ANY] * 8,
        out_specs=[ANY] * 8 + [WHOLE] * 3,
        out_shape=[shaped(*item.shape) for item in weights]
        + [shaped(*item.shape, dtype=BF) for item in weights]
        + [shaped(2, 13), shaped(1, 1), shaped(1, 12)],
        scratch_shapes=[pltpu.VMEM(item.shape, F32) for item in weights]
        + [pltpu.VMEM(item.shape, F32) for item in weights]
        + [pltpu.VMEM(item.shape, BF) for item in weights]
        + [pltpu.VMEM((n_mp, 16, 128), F32), dma((2, 4)), dma((2, 4))],
        compiler_params=pltpu.CompilerParams(vmem_limit_bytes=VMEM_LIMIT),
        name="renew",
    )(misc, stat, *sums, *weights, *updates)


def shards(
    pixels,
    token_mask,
    counts,
    labels,
    pairs,
    attn_in,
    attn_in_mean,
    attn_in_square,
    attn_out,
    attn_out_mean,
    attn_out_square,
    mlp_in,
    mlp_in_mean,
    mlp_in_square,
    mlp_out,
    mlp_out_mean,
    mlp_out_square,
    tables,
    tables_mean,
    tables_square,
    vectors,
    vectors_mean,
    vectors_square,
    talking,
    talking_mean,
    talking_square,
):
    local = pixels.shape[0]
    group = token_mask.shape[0]
    place_mp = lax.axis_index("mp")
    n_mp = lax.axis_size("mp")
    n_dp = lax.axis_size("dp")
    hs = attn_in.shape[3]
    fs = mlp_in.shape[2]

    def as_rows(item):
        return item.transpose(0, 2, 3, 1).reshape(2, 3 * hs, D)

    def from_rows(item):
        return item.reshape(2, 3, hs, D).transpose(0, 3, 1, 2)

    attn_in, attn_in_mean, attn_in_square = map(as_rows, (attn_in, attn_in_mean, attn_in_square))
    pixel_rows = pixels.transpose(1, 0, 2).reshape(P_SIZE * local, PIX)
    mask = lax.dynamic_slice_in_dim(token_mask, place_mp * local, local, 0)
    (
        wattn, mlp_rows, cls_rows, up_rows, down_rows, embed, head, t1row, t2row, cols, bias_row,
        base,
    ) = run_start(
        n_dp, n_mp, group, attn_in, attn_out, mlp_in, mlp_out, pixel_rows, tables, vectors,
        talking, mask, counts, labels, pairs,
    )
    q, k, v, prob, post, ho, raw0, middle, stat_a, wmlp = run_self_attend(
        n_dp, n_mp, embed, cols, vectors, wattn, t1row, t2row, mlp_rows
    )
    patches, act, slope, raw1, norm, cprob, cprob0, z, card, aux, wcls, wup, wdown = run_feed(
        n_dp, n_mp, middle, cols, bias_row, base, stat_a, vectors, wmlp, cls_rows, up_rows,
        down_rows,
    )
    left, right, gv, local_rows, gout1, gup1, gdown1, ghead, rows1, stat = run_token(
        n_dp, n_mp, group, card, vectors, aux, wcls, wup, wdown, head, norm, cprob, cprob0, z
    )
    dmid, gfeed, rows2 = run_feed_back(
        n_dp, left, right, gv, local_rows, patches, middle, raw1, act, slope, vectors, wmlp
    )
    block, shared, block_sq = run_self_back(
        n_dp, n_mp, dmid, pixel_rows, embed, q, k, v, prob, post, ho, raw0, vectors, wattn,
        t1row, t2row, gfeed, rows2,
    )

    shared = shared.reshape(-1, D)
    state = (
        attn_in, attn_in_mean, attn_in_square, attn_out, attn_out_mean, attn_out_square,
        mlp_in, mlp_in_mean, mlp_in_square, mlp_out, mlp_out_mean, mlp_out_square,
    )
    smalls = (vectors, vectors_mean, vectors_square, talking, talking_mean, talking_square)
    moved = run_moments(
        n_dp, (block_sq, gout1, rows1, stat, aux), smalls, (block, shared, wcls, gup1, gdown1),
        state,
    )
    sums = [moved[19]]
    for step in range(1, n_mp):
        sums.append(lax.ppermute(moved[19], "mp", [(i, (i + step) % n_mp) for i in range(n_mp)]))
    table = run_tables(moved[18], shared, ghead, (tables, tables_mean, tables_square))
    renewed = run_renew(n_mp, table[3], stat, sums, state[0:12:3], moved[0:12:3])
    return (
        from_rows(renewed[0]),
        from_rows(moved[1]),
        from_rows(moved[2]),
        renewed[1],
        moved[4],
        moved[5],
        renewed[2],
        moved[7],
        moved[8],
        renewed[3],
        moved[10],
        moved[11],
        *table[:3],
        *moved[12:18],
        from_rows(renewed[4]),
        renewed[5],
        renewed[6],
        renewed[7],
        renewed[10].reshape(12),
        renewed[9].reshape(()),
        renewed[8],
    )


def solution(mesh):
    return jax.shard_map(
        shards,
        mesh=mesh,
        in_specs=(
            P(("dp", "mp"), None, None),
            P("dp", None),
            P("dp"),
            P(("dp", "mp")),
            P(("dp", "mp")),
            P(None, None, None, "mp"),
            P(None, None, None, "mp"),
            P(None, None, None, "mp"),
            P(None, "mp", None),
            P(None, "mp", None),
            P(None, "mp", None),
            P(None, None, "mp"),
            P(None, None, "mp"),
            P(None, None, "mp"),
            P(None, "mp", None),
            P(None, "mp", None),
            P(None, "mp", None),
            P(),
            P(),
            P(),
            P(),
            P(),
            P(),
            P(),
            P(),
            P(),
        ),
        out_specs=(
            P(None, None, None, "mp"),
            P(None, None, None, "mp"),
            P(None, None, None, "mp"),
            P(None, "mp", None),
            P(None, "mp", None),
            P(None, "mp", None),
            P(None, None, "mp"),
            P(None, None, "mp"),
            P(None, None, "mp"),
            P(None, "mp", None),
            P(None, "mp", None),
            P(None, "mp", None),
            P(),
            P(),
            P(),
            P(),
            P(),
            P(),
            P(),
            P(),
            P(),
            P(None, None, None, "mp"),
            P(None, "mp", None),
            P(None, None, "mp"),
            P(None, "mp", None),
            P(),
            P(),
            P(),
        ),
        check_vma=False,
    )
```

```python
import functools

import jax
import jax.numpy as jnp
from jax import lax
from jax.experimental import pallas as pl
from jax.experimental.pallas import tpu as pltpu
from jax.sharding import PartitionSpec as P

D = 384
HEADS = 8
HEAD = 48
PIX = 768
P_SIZE = 196
PAD = 208
WIDE = 256
STEP = 10
SCALE = HEAD**-0.5
BETA_ONE = 0.9
BETA_TWO = 0.999
ADAM_EPS = 1e-08
DECAY = 0.01
RATE = 0.5
RATE_VECTOR = 0.5
CLIP = 0.02
TEMP = 0.05
MASKED = -1000000000.0
NORM_EPS = 1e-06
F32 = jnp.float32
BF = jnp.bfloat16
VMEM_LIMIT = 58 * 2**20
ANY = pl.BlockSpec(memory_space=pl.ANY)
MESH = pl.DeviceIdType.MESH
WHOLE = pl.BlockSpec(memory_space=pltpu.VMEM)


def nn(left, right):
    return lax.dot_general(left, right, (((1,), (0,)), ((), ())), preferred_element_type=F32)


def nt(left, right):
    return lax.dot_general(left, right, (((1,), (1,)), ((), ())), preferred_element_type=F32)


def tn(left, right):
    return lax.dot_general(left, right, (((0,), (0,)), ((), ())), preferred_element_type=F32)


def colsum(values):
    return jnp.sum(values, 0, keepdims=True)


def normalize(inputs):
    center = inputs - jnp.mean(inputs, -1, keepdims=True)
    spread = jnp.mean(center * center, -1, keepdims=True)
    inverse = lax.rsqrt(spread + NORM_EPS)
    return center * inverse, inverse


def normalize_back(unit, inverse, gain, incoming):
    scaled = incoming * gain
    return inverse * (
        scaled
        - jnp.mean(scaled, -1, keepdims=True)
        - unit * jnp.mean(scaled * unit, -1, keepdims=True)
    )


def gelu_parts(inner):
    cumulative = 0.5 + 0.5 * lax.erf(inner * 0.5**0.5)
    bell = jnp.exp2(inner * inner * (-0.5 * 1.4426950408889634)) * 0.3989422804014327
    return inner * cumulative, cumulative + inner * bell


def head_mask(copies=1):
    row = lax.rem(lax.broadcasted_iota(jnp.int32, (copies * HEADS, D), 0), HEADS)
    column = lax.broadcasted_iota(jnp.int32, (copies * HEADS, D), 1)
    return ((column >= row * HEAD) & (column < row * HEAD + HEAD)).astype(F32)


def stat_lanes(parts, weight, first):
    lane = lax.broadcasted_iota(jnp.int32, (1, 128), 1)
    row = jnp.zeros((1, 128), F32)
    for place, values in enumerate(parts):
        total = jnp.sum(colsum(values * values * weight), keepdims=True)
        high = total.astype(BF).astype(F32)
        row = jnp.where(lane == first + 2 * place, high, row)
        row = jnp.where(lane == first + 2 * place + 1, total - high, row)
    return row


def part(ref, first, rows):
    shards_count = ref.shape[0]
    return ref[:, first : first + rows, :].reshape(shards_count * rows, ref.shape[2])


def pad_rows(rows, n_dp):
    return -(-rows // (16 * n_dp)) * 16 * n_dp


class Place:
    def __init__(self, n_dp, n_mp):
        self.n_dp, self.n_mp, self.n_y = n_dp, n_mp, n_mp // 2
        self.n_lo = 2 if n_dp < 16 else 4
        self.n_hi = n_dp // self.n_lo
        self.dp = lax.axis_index("dp")
        self.mp = lax.axis_index("mp")
        self.y = lax.div(self.mp, 2)
        self.core = lax.rem(self.mp, 2)
        self.high = lax.div(self.dp, self.n_lo)
        self.low = lax.rem(self.dp, self.n_lo)
        self.chunk = self.low * self.n_hi + self.high
        self.sibling = (self.dp, self.y * 2 + 1 - self.core)

    def along_y(self, step):
        return lax.rem(self.y + step, self.n_y)

    def along_lo(self, step):
        return lax.rem(self.low + step, self.n_lo)

    def along_hi(self, step):
        return lax.rem(self.high + step, self.n_hi)

    def at_lo(self, low):
        return (self.high * self.n_lo + low, self.mp)

    def at_hi(self, high):
        return (high * self.n_lo + self.low, self.mp)

    def near_partners(self):
        return [self.sibling] + [
            (self.dp, self.along_y(step) * 2 + self.core) for step in range(1, self.n_y)
        ]

    def all_partners(self):
        partners = [(lax.rem(self.dp + step, self.n_dp), self.mp) for step in range(1, self.n_dp)]
        return partners + [
            (self.dp, lax.rem(self.mp + step, self.n_mp)) for step in range(1, self.n_mp)
        ]

    def low_partners(self):
        return [self.at_lo(self.along_lo(step)) for step in range(1, self.n_lo)]

    def dp_partners(self):
        return self.low_partners() + [self.at_hi(self.along_hi(step)) for step in range(1, self.n_hi)]


def greet(partners):
    barrier = pltpu.get_barrier_semaphore()
    for partner in partners:
        pl.semaphore_signal(barrier, inc=1, device_id=partner, device_id_type=MESH)
    return lambda: pl.semaphore_wait(barrier, len(partners))


def tile_rows(ref, first, rows):
    return ref.at[pl.ds(pl.multiple_of(first, 16), rows)]


class SpreadGather:
    def __init__(self, place, rows, out, far_sem, low_sem, near_sem):
        self.place, self.rows, self.out = place, rows, out
        self.far_sem, self.low_sem, self.near_sem = far_sem, low_sem, near_sem
        self.count = rows.shape[0] // place.n_lo

    def piece(self, ref, low):
        return tile_rows(ref, low * self.count, self.count)

    def far_copy(self, step, slot):
        p = self.place
        return remote(
            self.piece(self.rows, p.low), self.piece(self.out.at[slot], p.low),
            self.far_sem.at[0, step], self.far_sem.at[1, step],
            (p.dp, p.along_y(step) * 2 + p.core),
        )

    def low_copy(self, step, turn, low):
        p = self.place
        rows = self.piece(self.out.at[self.from_y(step) + p.core], low)
        at = (step - 1) * p.n_lo + turn
        return remote(
            rows, rows, self.low_sem.at[0, at], self.low_sem.at[1, at],
            p.at_lo(p.along_lo(turn)),
        )

    def near_copy(self, step, slot):
        return remote(
            self.rows if step == 0 else self.out.at[slot], self.out.at[slot],
            self.near_sem.at[0, step], self.near_sem.at[1, step], self.place.sibling,
        )

    def own_copy(self):
        return pltpu.make_async_copy(
            self.rows, self.out.at[self.place.mp], self.far_sem.at[0, 0]
        )

    def from_y(self, step):
        p = self.place
        return p.along_y(p.n_y - step) * 2

    def start(self):
        p = self.place
        for step in range(1, p.n_y):
            self.far_copy(step, p.mp).start()
        self.near_copy(0, p.mp).start()
        self.own_copy().start()

    def spread(self):
        p = self.place
        for step in range(1, p.n_y):
            self.far_copy(step, self.from_y(step) + p.core).wait_recv()
            for turn in range(1, p.n_lo):
                self.low_copy(step, turn, p.low).start()

    def forward(self):
        p = self.place
        for step in range(1, p.n_y):
            for turn in range(1, p.n_lo):
                self.low_copy(step, turn, p.along_lo(p.n_lo - turn)).wait_recv()
            self.near_copy(step, self.from_y(step) + p.core).start()

    def finish(self):
        p = self.place
        self.own_copy().wait()
        for step in range(1, p.n_y):
            self.far_copy(step, p.mp).wait_send()
            for turn in range(1, p.n_lo):
                self.low_copy(step, turn, p.low).wait_send()
        for step in range(p.n_y):
            self.near_copy(step, self.from_y(step) + p.core if step else p.mp).wait_send()
            self.near_copy(step, self.from_y(step) + 1 - p.core).wait_recv()


def spread_scratch(n_dp, n_mp):
    n_lo = 2 if n_dp < 16 else 4
    dma = pltpu.SemaphoreType.DMA
    return [dma((2, n_mp // 2)), dma((2, n_mp // 2 * n_lo)), dma((2, n_mp // 2))]


class Gather:
    def __init__(self, place, rows, out, far_sem, near_sem):
        self.place, self.rows, self.out = place, rows, out
        self.far_sem, self.near_sem = far_sem, near_sem

    def far_copy(self, step, slot):
        p = self.place
        return remote(
            self.rows, self.out.at[slot], self.far_sem.at[0, step], self.far_sem.at[1, step],
            (p.dp, p.along_y(step) * 2 + p.core),
        )

    def near_copy(self, step, slot):
        return remote(
            self.rows if step == 0 else self.out.at[slot], self.out.at[slot],
            self.near_sem.at[0, step], self.near_sem.at[1, step], self.place.sibling,
        )

    def own_copy(self):
        return pltpu.make_async_copy(
            self.rows, self.out.at[self.place.mp], self.far_sem.at[0, 0]
        )

    def from_y(self, step):
        p = self.place
        return p.along_y(p.n_y - step) * 2

    def start(self):
        p = self.place
        for step in range(1, p.n_y):
            self.far_copy(step, p.mp).start()
        self.near_copy(0, p.mp).start()
        self.own_copy().start()

    def forward(self):
        p = self.place
        for step in range(1, p.n_y):
            slot = self.from_y(step) + p.core
            self.far_copy(step, slot).wait_recv()
            self.near_copy(step, slot).start()

    def finish(self):
        p = self.place
        self.own_copy().wait()
        for step in range(1, p.n_y):
            self.far_copy(step, p.mp).wait_send()
        for step in range(p.n_y):
            self.near_copy(step, self.from_y(step) + p.core if step else p.mp).wait_send()
            self.near_copy(step, self.from_y(step) + 1 - p.core).wait_recv()


def gather_scratch(n_mp):
    dma = pltpu.SemaphoreType.DMA
    return [dma((2, n_mp // 2)), dma((2, n_mp // 2))]


class ShardSum:
    def __init__(
        self, place, rows, first, y_first, near, far, low, half, high,
        near_sem, far_sem, low_sem, high_sem,
    ):
        self.place, self.rows, self.first, self.y_first = place, rows, first, y_first
        self.near, self.far, self.low, self.half, self.high = near, far, low, half, high
        self.near_sem, self.far_sem = near_sem, far_sem
        self.low_sem, self.high_sem = low_sem, high_sem
        self.count = near.shape[1]
        self.wide = self.count // place.n_lo
        self.chunk = self.count // place.n_dp

    def near_copy(self, step):
        p = self.place
        y = p.along_y(step)
        return remote(
            self.rows.at[y * 2 + 1 - p.core, pl.ds(self.first, self.count)], self.near.at[y],
            self.near_sem.at[0, step], self.near_sem.at[1, step], p.sibling,
        )

    def far_copy(self, step):
        p = self.place
        y = p.along_y(step)
        rows = self.near.at[y]
        if not self.y_first:
            rows = tile_rows(rows, p.low * self.wide, self.wide)
        return remote(
            rows, self.far.at[step - 1],
            self.far_sem.at[0, step], self.far_sem.at[1, step], (p.dp, y * 2 + p.core),
        )

    def low_copy(self, step):
        p = self.place
        to = p.along_lo(step)
        at = pl.ds(pl.multiple_of(to * self.wide, 16), self.wide)
        rows = self.near.at[p.y, at] if self.y_first else self.near.at[:, at]
        return remote(
            rows, self.low.at[step - 1],
            self.low_sem.at[0, step], self.low_sem.at[1, step], p.at_lo(to),
        )

    def high_copy(self, step):
        p = self.place
        to = p.along_hi(step)
        return remote(
            tile_rows(self.half, to * self.chunk, self.chunk), self.high.at[step - 1],
            self.high_sem.at[0, step], self.high_sem.at[1, step], p.at_hi(to),
        )

    def start(self):
        for step in range(1, self.place.n_y + 1):
            self.near_copy(step).start()

    def second(self):
        p = self.place
        at = slice(self.first, self.first + self.count)
        for step in range(1, p.n_y + 1):
            y = p.along_y(step)
            self.near_copy(step).wait_recv()
            self.near[pl.ds(y, 1)] = (
                self.rows[pl.ds(y * 2 + p.core, 1), at, :].astype(F32)
                + self.near[pl.ds(y, 1)].astype(F32)
            ).astype(BF)
            if self.y_first and step < p.n_y:
                self.far_copy(step).start()
        if not self.y_first:
            for step in range(1, p.n_lo):
                self.low_copy(step).start()

    def third(self):
        p = self.place
        own = pl.ds(pl.multiple_of(p.low * self.wide, 16), self.wide)
        if self.y_first:
            sums = self.near[pl.ds(p.y, 1)].astype(F32)
            for step in range(1, p.n_y):
                self.far_copy(step).wait_recv()
                sums += self.far[step - 1].astype(F32)[None]
            self.near[pl.ds(p.y, 1)] = sums.astype(BF)
            for step in range(1, p.n_lo):
                self.low_copy(step).start()
        else:
            sums = self.near[:, own, :].astype(F32)
            for step in range(1, p.n_lo):
                self.low_copy(step).wait_recv()
                sums += self.low[step - 1].astype(F32)
            self.near[:, own, :] = sums.astype(BF)
            for step in range(1, p.n_y):
                self.far_copy(step).start()

    def fourth(self):
        p = self.place
        own = pl.ds(pl.multiple_of(p.low * self.wide, 16), self.wide)
        sums = self.near[pl.ds(p.y, 1), own, :][0].astype(F32)
        if self.y_first:
            for step in range(1, p.n_lo):
                self.low_copy(step).wait_recv()
                sums += self.low[step - 1].astype(F32)
        else:
            for step in range(1, p.n_y):
                self.far_copy(step).wait_recv()
                sums += self.far[step - 1].astype(F32)
        self.half[...] = sums.astype(BF)
        for step in range(1, p.n_hi):
            self.high_copy(step).start()

    def finish(self):
        p = self.place
        at = pl.ds(pl.multiple_of(p.high * self.chunk, 16), self.chunk)
        sums = self.half[at, :].astype(F32)
        for step in range(1, p.n_hi):
            self.high_copy(step).wait_recv()
            sums += self.high[step - 1].astype(F32)
        return sums.astype(BF)

    def wait_sends(self):
        p = self.place
        for step in range(1, p.n_y + 1):
            self.near_copy(step).wait_send()
            if step < p.n_y:
                self.far_copy(step).wait_send()
        for step in range(1, p.n_lo):
            self.low_copy(step).wait_send()
        for step in range(1, p.n_hi):
            self.high_copy(step).wait_send()


def sum_scratch(n_dp, n_mp, rows, y_first):
    n_y = n_mp // 2
    n_lo = 2 if n_dp < 16 else 4
    n_hi = n_dp // n_lo
    wide = rows // n_lo
    dma = pltpu.SemaphoreType.DMA
    far = (max(n_y - 1, 1), rows, D) if y_first else (max(n_y - 1, 1), wide, D)
    low = (n_lo - 1, wide, D) if y_first else (n_lo - 1, n_y, wide, D)
    return [
        pltpu.VMEM((n_y, rows, D), BF), pltpu.VMEM(far, BF), pltpu.VMEM(low, BF),
        pltpu.VMEM((wide, D), BF), pltpu.VMEM((n_hi - 1, rows // n_dp, D), BF),
        dma((2, n_y + 1)), dma((2, n_y + 1)), dma((2, n_lo)), dma((2, n_hi)),
    ]


SUM_BUFFERS = 9


def halves(rows, n_dp):
    unit = 16 * n_dp
    first = (rows // unit + 1) // 2 * unit
    return first, rows - first


class TableSum:
    def __init__(
        self, place, rows, out, near, low, part_rows, high, last, far, near_sem, low_sem, high_sem,
        far_sem, back_sem, hand_sem,
    ):
        self.place, self.rows, self.out = place, rows, out
        self.near, self.low, self.part, self.high = near, low, part_rows, high
        self.last, self.far = last, far
        self.near_sem, self.low_sem, self.high_sem = near_sem, low_sem, high_sem
        self.far_sem, self.back_sem, self.hand_sem = far_sem, back_sem, hand_sem
        self.chunk = high.shape[2]
        self.wide = low.shape[2]
        self.slab = place.core * place.n_y + place.y
        self.first = place.core * place.n_y

    def near_copy(self):
        p = self.place
        return remote(
            self.rows.at[pl.ds((1 - p.core) * p.n_y, p.n_y)], self.near,
            self.near_sem.at[0], self.near_sem.at[1], p.sibling,
        )

    def low_copy(self, step):
        p = self.place
        to = p.along_lo(step)
        return remote(
            self.near.at[:, pl.ds(pl.multiple_of(to * self.wide, 16), self.wide)],
            self.low.at[step - 1], self.low_sem.at[0, step], self.low_sem.at[1, step], p.at_lo(to),
        )

    def high_copy(self, step):
        p = self.place
        to = p.along_hi(step)
        return remote(
            self.part.at[:, pl.ds(pl.multiple_of(to * self.chunk, 16), self.chunk)],
            self.high.at[step - 1], self.high_sem.at[0, step], self.high_sem.at[1, step],
            p.at_hi(to),
        )

    def far_copy(self, step):
        p = self.place
        to = p.along_y(step)
        return remote(
            self.last.at[to], self.far.at[step - 1], self.far_sem.at[0, step],
            self.far_sem.at[1, step], (p.dp, to * 2 + p.core),
        )

    def start(self):
        self.near_copy().start()

    def near_to_low(self):
        p = self.place
        self.near_copy().wait_recv()
        self.near[...] = (
            self.rows[pl.ds(self.first, p.n_y)].astype(F32) + self.near[...].astype(F32)
        ).astype(BF)
        for step in range(1, p.n_lo):
            self.low_copy(step).start()

    def low_to_high(self):
        p = self.place
        at = pl.ds(pl.multiple_of(p.low * self.wide, 16), self.wide)
        sums = self.near[:, at, :].astype(F32)
        for step in range(1, p.n_lo):
            self.low_copy(step).wait_recv()
            sums += self.low[step - 1].astype(F32)
        self.part[...] = sums.astype(BF)
        for step in range(1, p.n_hi):
            self.high_copy(step).start()

    def high_to_far(self):
        p = self.place
        at = pl.ds(pl.multiple_of(p.high * self.chunk, 16), self.chunk)
        sums = self.part[:, at, :].astype(F32)
        for step in range(1, p.n_hi):
            self.high_copy(step).wait_recv()
            sums += self.high[step - 1].astype(F32)
        self.last[...] = sums.astype(BF)
        for step in range(1, p.n_y):
            self.far_copy(step).start()

    def chunk_at(self, slab, chunk):
        return self.out.at[slab, pl.ds(pl.multiple_of(chunk * self.chunk, 16), self.chunk)]

    def back_far(self, step, y):
        p = self.place
        rows = self.chunk_at(self.first + y, p.chunk)
        return remote(
            rows, rows, self.back_sem.at[0, step], self.back_sem.at[1, step],
            (p.dp, p.along_y(step) * 2 + p.core),
        )

    def back_high(self, step, chunk):
        p = self.place
        rows = self.chunk_at(pl.ds(self.first, p.n_y), chunk)
        return remote(
            rows, rows, self.back_sem.at[2, step], self.back_sem.at[3, step],
            p.at_hi(p.along_hi(step)),
        )

    def back_low(self, step, low):
        p = self.place
        rows = self.out.at[
            pl.ds(self.first, p.n_y), pl.ds(pl.multiple_of(low * self.wide, 16), self.wide)
        ]
        return remote(
            rows, rows, self.back_sem.at[4, step], self.back_sem.at[5, step],
            p.at_lo(p.along_lo(step)),
        )

    def hand_copy(self, core):
        p = self.place
        rows = self.out.at[pl.ds(core * p.n_y, p.n_y)]
        return remote(rows, rows, self.hand_sem.at[0], self.hand_sem.at[1], p.sibling)

    def turn(self):
        p = self.place
        sums = self.last[pl.ds(p.y, 1)][0].astype(F32)
        for step in range(1, p.n_y):
            self.far_copy(step).wait_recv()
            sums += self.far[step - 1].astype(F32)
        at = pl.ds(pl.multiple_of(p.chunk * self.chunk, 16), self.chunk)
        self.out[pl.ds(self.slab, 1), at, :] = sums.astype(BF)[None]
        for step in range(1, p.n_y):
            self.back_far(step, p.y).start()

    def far_to_high(self):
        p = self.place
        for step in range(1, p.n_y):
            self.back_far(step, p.along_y(p.n_y - step)).wait_recv()
        for step in range(1, p.n_hi):
            self.back_high(step, p.chunk).start()

    def high_to_low(self):
        p = self.place
        for step in range(1, p.n_hi):
            self.back_high(step, p.low * p.n_hi + p.along_hi(p.n_hi - step)).wait_recv()
        for step in range(1, p.n_lo):
            self.back_low(step, p.low).start()

    def low_to_near(self):
        p = self.place
        for step in range(1, p.n_lo):
            self.back_low(step, p.along_lo(p.n_lo - step)).wait_recv()
        self.hand_copy(p.core).start()

    def finish(self):
        p = self.place
        self.hand_copy(1 - p.core).wait_recv()
        self.near_copy().wait_send()
        self.hand_copy(p.core).wait_send()
        for step in range(1, p.n_lo):
            self.low_copy(step).wait_send()
            self.back_low(step, p.low).wait_send()
        for step in range(1, p.n_hi):
            self.high_copy(step).wait_send()
            self.back_high(step, p.chunk).wait_send()
        for step in range(1, p.n_y):
            self.far_copy(step).wait_send()
            self.back_far(step, p.y).wait_send()


def table_scratch(n_dp, n_mp, rows):
    n_y = n_mp // 2
    n_lo = 2 if n_dp < 16 else 4
    n_hi = n_dp // n_lo
    wide, chunk = rows // n_lo, rows // n_dp
    dma = pltpu.SemaphoreType.DMA
    return [
        pltpu.VMEM((n_y, rows, D), BF), pltpu.VMEM((n_lo - 1, n_y, wide, D), BF),
        pltpu.VMEM((n_y, wide, D), BF), pltpu.VMEM((n_hi - 1, n_y, chunk, D), BF),
        pltpu.VMEM((n_y, chunk, D), BF), pltpu.VMEM((max(n_y - 1, 1), chunk, D), BF),
        dma((2,)), dma((2, n_lo)), dma((2, n_hi)), dma((2, n_y)),
        dma((6, max(n_y, n_lo, n_hi))), dma((2,)),
    ]


class HandHigh:
    def __init__(self, place, rows, sems):
        self.place, self.rows, self.sems = place, rows, sems
        self.chunk = rows.shape[0] // place.n_hi

    def copy(self, step, source):
        p = self.place
        rows = tile_rows(self.rows, source * self.chunk, self.chunk)
        return remote(
            rows, rows, self.sems.at[0, step], self.sems.at[1, step], p.at_hi(p.along_hi(step))
        )

    def start(self, sums):
        p = self.place
        self.rows[pl.ds(pl.multiple_of(p.high * self.chunk, 16), self.chunk), :] = sums
        for step in range(1, p.n_hi):
            self.copy(step, p.high).start()

    def arrive(self):
        p = self.place
        for step in range(1, p.n_hi):
            self.copy(step, p.along_hi(p.n_hi - step)).wait_recv()

    def wait_sends(self):
        for step in range(1, self.place.n_hi):
            self.copy(step, self.place.high).wait_send()


class HandLow:
    def __init__(self, place, rows, first, count, sems):
        self.place, self.rows, self.first, self.sems = place, rows, first, sems
        self.run = count // place.n_lo

    def copy(self, step, source):
        p = self.place
        rows = tile_rows(self.rows, self.first + source * self.run, self.run)
        return remote(
            rows, rows, self.sems.at[0, step], self.sems.at[1, step], p.at_lo(p.along_lo(step))
        )

    def start(self, sums):
        p = self.place
        self.rows[pl.ds(pl.multiple_of(self.first + p.low * self.run, 16), self.run), :] = sums
        for step in range(1, p.n_lo):
            self.copy(step, p.low).start()

    def arrive(self):
        p = self.place
        for step in range(1, p.n_lo):
            self.copy(step, p.along_lo(p.n_lo - step)).wait_recv()

    def wait_sends(self):
        for step in range(1, self.place.n_lo):
            self.copy(step, self.place.low).wait_send()


def remote(src, dst, send_sem, recv_sem, device):
    return pltpu.make_async_remote_copy(
        src_ref=src, dst_ref=dst, send_sem=send_sem, recv_sem=recv_sem,
        device_id=device, device_id_type=MESH,
    )


def stack_heads(stack, rows, gains):
    for g in range(HEADS):
        stack[g * PAD : g * PAD + P_SIZE, :] = (rows * gains[g : g + 1, :]).astype(BF)


def column(cols, index):
    lane = lax.broadcasted_iota(jnp.int32, cols.shape, 1)
    return jnp.sum(jnp.where(lane == index, cols[...], 0.0), 1, keepdims=True)


def self_attend_kernel(
    n_dp, n_mp, embed, cols, vec, wattn, t1row, t2row, mlp_rows,
    q_out, k_out, v_out, prob_out, post_out, ho_out, raw_out, mid_out, stat_out, wmlp_out,
    stack, scores, *sems,
):
    shard = wattn.shape[1] // 4
    place = Place(n_dp, n_mp)
    gather = Gather(place, mlp_rows, wmlp_out, *sems)
    images = pl.num_programs(0)

    @pl.when(pl.program_id(0) == 0)
    def _():
        stack[...] = jnp.zeros_like(stack)
        greet(place.near_partners())()
        gather.start()

    @pl.when(pl.program_id(0) == images - 1)
    def _():
        gather.forward()

    x = embed[0]
    unit, _ = normalize(x)
    normed = (unit * vec[0:1, :] + vec[1:2, :]).astype(BF)
    q = nt(normed, part(wattn, 0, shard)).astype(BF)
    k = nt(normed, part(wattn, shard, shard)).astype(BF)
    v = nt(normed, part(wattn, 2 * shard, shard)).astype(BF)
    q_out[0] = q
    k_out[0] = k
    v_out[0] = v
    stack_heads(stack, q.astype(F32), t1row)
    scores[...] = nt(k, stack[...])
    bias = column(cols, pl.program_id(0))
    for first in range(0, HEADS * PAD, 128):
        mixed = scores[:, first : first + 128] + bias
        grown = jnp.exp(mixed - jnp.max(mixed, 0, keepdims=True))
        prob = grown * (1.0 / jnp.sum(grown, 0, keepdims=True))
        prob_out[0, :, first : first + 128] = prob.astype(BF)
    post = tn(prob_out[0], v)
    post_out[0] = post.astype(BF)
    heads_out = jnp.zeros(x.shape, F32)
    for g in range(HEADS):
        heads_out += post[g * PAD : g * PAD + P_SIZE, :] * t2row[g : g + 1, :]
    heads_out = heads_out.astype(BF)
    ho_out[0] = heads_out
    raw = nn(heads_out, part(wattn, 3 * shard, shard))
    raw_out[0] = raw.astype(BF)
    branch = vec[3:4, :] * (raw + vec[2:3, :])
    middle = x + branch
    mid_out[0] = middle
    weight = column(cols, pl.program_id(0) + cols.shape[1] // 2)
    stat_out[0] = stat_lanes((branch, middle), weight, 8)

    @pl.when(pl.program_id(0) == images - 1)
    def _():
        gather.finish()


def feed_kernel(
    n_dp, n_mp, group, mid, cols, bias_row, base, stat, vec, wmlp, cls_rows, up_rows, down_rows,
    head_far,
    patch_out, act_out, slope_out, raw_out, aux_out, wcls_out, *rest,
):
    token_outs, rest = rest[:10], rest[10:]
    norm_out, cprob_out, cprob0_out, z_out, card_out, wup_out, wdown_out, wcls, head = rest[:9]
    token_scratch, (cards, slots, dp_sem, mp_sem, head_sem), sems = rest[9:13], rest[13:18], rest[18:]
    hidden = wmlp.shape[1] // 2
    shard = wcls.shape[1] // 4
    images = norm_out.shape[0]
    place = Place(n_dp, n_mp)
    load_head = pltpu.make_async_copy(head_far, head, head_sem.at[0])
    gather_cls = SpreadGather(place, cls_rows, wcls, *sems[:3])
    gather_up = SpreadGather(place, up_rows, wup_out, *sems[3:6])
    gather_down = SpreadGather(place, down_rows, wdown_out, *sems[6:])

    def beside(step, *stages):
        @pl.when(pl.program_id(0) == step)
        def _():
            for stage in stages:
                stage()

    @pl.when(pl.program_id(0) == 0)
    def _():
        norm_out[...] = jnp.zeros_like(norm_out)
        load_head.start()
        greet(place.all_partners())()
        gather_cls.start()
        gather_up.start()
        gather_down.start()

    beside(images * 3 // 8, gather_cls.spread)
    beside(images // 2, gather_up.spread)
    beside(images * 5 // 8, gather_down.spread)
    beside(images * 3 // 4, gather_cls.forward)
    beside(images - 1, gather_up.forward, gather_cls.finish)

    middle = mid[0]
    unit, _ = normalize(middle)
    normed = (unit * vec[4:5, :] + vec[5:6, :]).astype(BF)
    inner = nt(normed, part(wmlp, 0, hidden))
    active, slope = gelu_parts(inner)
    active = active.astype(BF)
    act_out[0] = active
    slope_out[0] = slope.astype(BF)
    raw = nn(active, part(wmlp, hidden, hidden))
    raw_out[0] = raw.astype(BF)
    branch = vec[7:8, :] * (raw + vec[6:7, :])
    patches = middle + branch
    patch_out[0] = patches
    card_out[pl.ds(4 * pl.program_id(0) + 3, 1), :] = (
        base[pl.ds(pl.program_id(0), 1), :]
        + stat[0]
        + stat_lanes((branch, patches), column(cols, pl.program_id(0) + images), 12)
    )
    unit, _ = normalize(patches)
    norm_out[pl.ds(pl.program_id(0), 1), :P_SIZE, :] = (
        (unit * vec[8:9, :] + vec[9:10, :]).astype(BF)[None]
    )

    @pl.when(pl.program_id(0) == images - 1)
    def _():
        unit, _ = normalize(jnp.broadcast_to(vec[17:18, :], (HEADS, D)))
        token = (unit * vec[8:9, :] + vec[9:10, :]).astype(BF)
        query = nt(token, part(wcls, 0, shard)).astype(BF).astype(F32)
        keys = nn((query * head_mask()).astype(BF), part(wcls, shard, shard)) * SCALE
        token = token.astype(F32)
        aux_out[0:8, :] = keys
        aux_out[8:16, :] = token
        aux_out[16:24, :] = query
        scores = nt(keys.astype(BF), norm_out[...].reshape(images * WIDE, D)) + bias_row[...]
        score0 = jnp.sum(keys * token, -1, keepdims=True)
        for n in range(images):
            rows = slice(n * HEADS, (n + 1) * HEADS)
            mine = scores[:, n * WIDE : (n + 1) * WIDE]
            top = jnp.maximum(jnp.max(mine, -1, keepdims=True), score0)
            grown = jnp.exp(mine - top)
            grown0 = jnp.exp(score0 - top)
            scale = 1.0 / (jnp.sum(grown, -1, keepdims=True) + grown0)
            cprob = grown * scale
            cprob0 = grown0 * scale
            cprob_out[rows, :] = cprob
            cprob0_out[rows, :] = jnp.broadcast_to(cprob0, (HEADS, 128))
            z_out[rows, :] = nn(cprob.astype(BF), norm_out[n]) + cprob0 * token
        cheads = nt(z_out[...].astype(BF), part(wcls, 2 * shard, shard)) * head_mask(images)
        cheads = cheads.reshape(images, HEADS, D).sum(1)
        for piece in range(3):
            card_out[pl.ds(piece, images, stride=4), :] = cheads[:, 128 * piece : 128 * piece + 128]
        gather_down.forward()
        share_cards(n_dp, n_mp, card_out, cards, slots, dp_sem, mp_sem)
        wcls_out[...] = wcls[...]
        gather_up.finish()
        gather_down.finish()
        load_head.wait()
        token_kernel(
            group, cards, vec, wcls, wup_out, wdown_out, head, norm_out, cprob_out, cprob0_out,
            z_out, aux_out, *token_outs, *token_scratch,
        )


def token_kernel(
    group, cards, vec, wcls, wup_rows, wdown_rows, head, norm, cprob, cprob0, z, aux,
    left_out, right_out, gv_out, local_out, gout_out, gup_out, gdown_out, ghead_out, rows_out,
    stat_out, dch_all, gout_all, gup_all, gdown_all,
):
    hidden = wup_rows.shape[1]
    shard = wcls.shape[1] // 4
    images = cards.shape[0] // 4
    cheads = jnp.concatenate(
        [cards[pl.ds(piece, images, stride=4), :] for piece in range(3)], 1
    ).astype(BF)
    card = cards[pl.ds(3, images, stride=4), :]
    labels = (card[:, 0:1] * 32.0 + card[:, 1:2]).astype(jnp.int32)
    pairs = (card[:, 2:3] * 32.0 + card[:, 3:4]).astype(jnp.int32)
    column = lax.broadcasted_iota(jnp.int32, (images, images), 1)
    row = lax.broadcasted_iota(jnp.int32, (images, images), 0)
    slot = lax.rem(lax.broadcasted_iota(jnp.int32, (images, 1), 0), group).astype(F32)
    okay = (slot >= group - card[:, 4:5]).astype(F32)
    okay_row = colsum(jnp.where(row == column, okay, 0.0))
    wo = part(wcls, 3 * shard, shard)
    wup = part(wup_rows, 0, hidden)
    wdown = part(wdown_rows, 0, hidden)
    count = jnp.sum(okay, keepdims=True)
    raw = nn(cheads, wo) + vec[10:11, :]
    branch = vec[11:12, :] * raw
    middle = vec[17:18, :] + branch
    unit2, inverse2 = normalize(middle)
    normed = (unit2 * vec[12:13, :] + vec[13:14, :]).astype(BF)
    inner = nt(normed, wup)
    active, slope = gelu_parts(inner)
    active = active.astype(BF)
    down = nn(active, wdown) + vec[14:15, :]
    mlp_branch = vec[15:16, :] * down
    token = middle + mlp_branch
    unit3, inverse3 = normalize(token)
    feature = unit3 * vec[18:19, :] + vec[19:20, :]
    feature_low = feature.astype(BF)
    logits = nt(feature_low, head[...])
    top = jnp.max(logits, -1, keepdims=True)
    grown = jnp.exp(logits - top)
    total = jnp.sum(grown, -1, keepdims=True)
    hot = lax.broadcasted_iota(jnp.int32, logits.shape, 1) == labels
    cross = jnp.log(total) + top - jnp.sum(jnp.where(hot, logits, 0.0), -1, keepdims=True)
    share = okay / count
    dlogits = (share * (grown / total - hot.astype(F32))).astype(BF)
    classes = head.shape[0]
    ghead = tn(dlogits, feature_low)
    ghead_out[0:8, :] = jnp.zeros((8, D), F32)
    ghead_out[classes:, :] = jnp.zeros((8, D), F32)
    ghead_out[4 : classes + 4, :] = ghead
    replicated_sq = colsum(ghead * ghead)
    dfeature = nn(dlogits, head[...])

    length = lax.rsqrt(jnp.sum(feature * feature, -1, keepdims=True) + NORM_EPS)
    embed = (feature * length).astype(BF)
    sims = nt(embed, embed) / TEMP
    sims = jnp.where((okay_row > 0) & (row != column), sims, MASKED)
    top = jnp.max(sims, -1, keepdims=True)
    grown = jnp.exp(sims - top)
    total = jnp.sum(grown, -1, keepdims=True)
    hot = column == pairs
    contrast = jnp.log(total) + top - jnp.sum(jnp.where(hot, sims, 0.0), -1, keepdims=True)
    dsims = share * (grown / total - hot.astype(F32))
    high = dsims.astype(BF)
    low = (dsims - high.astype(F32)).astype(BF)
    dembed = (nn(high, embed) + nn(low, embed) + tn(high, embed) + tn(low, embed)) / TEMP
    dfeature += length * dembed - feature * (
        length * length * length * jnp.sum(dembed * feature, -1, keepdims=True)
    )

    dtoken = normalize_back(unit3, inverse3, vec[18:19, :], dfeature)
    rows_out[0:1, :] = jnp.zeros((1, D), F32)
    rows_out[1:2, :] = jnp.zeros((1, D), F32)
    rows_out[7:8, :] = colsum(dtoken * down)
    rows_out[6:7, :] = vec[15:16, :] * colsum(dtoken)
    ddown = (dtoken * vec[15:16, :]).astype(BF)
    gdown = tn(active, ddown)
    own_f = pl.multiple_of(lax.axis_index("mp") * hidden, hidden)
    gdown_all[...] = gdown
    gdown_out[...] = gdown_all[pl.ds(own_f, hidden), :]
    replicated_sq += colsum(gdown * gdown)
    dinner = (nt(ddown, wdown) * slope).astype(BF)
    gup = tn(dinner, normed)
    gup_all[...] = gup
    gup_out[...] = gup_all[pl.ds(own_f, hidden), :]
    replicated_sq += colsum(gup * gup)
    dnormed = nn(dinner, wup)
    rows_out[4:5, :] = colsum(dnormed * unit2)
    rows_out[5:6, :] = colsum(dnormed)
    dmiddle = dtoken + normalize_back(unit2, inverse2, vec[12:13, :], dnormed)
    rows_out[3:4, :] = colsum(dmiddle * raw)
    rows_out[2:3, :] = vec[11:12, :] * colsum(dmiddle)
    rows_out[8:9, :] = colsum(dmiddle)
    rows_out[9:10, :] = colsum(dfeature * unit3)
    rows_out[10:11, :] = colsum(dfeature)
    dbranch = (dmiddle * vec[11:12, :]).astype(BF)
    gout = tn(cheads, dbranch)
    gout_all[...] = gout
    own_h = pl.multiple_of(lax.axis_index("mp") * shard, shard)
    gout_out[...] = gout_all[pl.ds(own_h, shard), :]
    replicated_sq += colsum(gout * gout)
    dch_all[...] = nt(dbranch, wo)
    local = norm.shape[0]
    place = lax.axis_index("dp") * lax.axis_size("mp") + lax.axis_index("mp")
    if local % 8 == 0:
        dch = dch_all[pl.ds(pl.multiple_of(place * local, local), local), :]
    else:
        share_of = 8 // local
        start = pl.multiple_of(lax.div(place, share_of) * 8, 8)
        window = dch_all[pl.ds(start, 8), :]
        pick = lax.rem(place, share_of)
        dch = sum(
            jnp.where(pick == i, window[i * local : (i + 1) * local, :], 0.0)
            for i in range(share_of)
        )

    keys = aux[0:8, :]
    class_row = aux[8:16, :]
    mask = head_mask()
    spread = jnp.concatenate([mask * dch[n : n + 1, :] for n in range(local)], 0).astype(BF)
    dz = nn(spread, part(wcls, 2 * shard, shard))
    dz_low = dz.astype(BF)
    probs = cprob[...]
    prob0 = cprob0[...][:, 0:1]
    class_rows = jnp.concatenate([class_row] * local, 0)
    dprobs = jnp.concatenate(
        [nt(dz_low[n * HEADS : (n + 1) * HEADS, :], norm[n]) for n in range(local)], 0
    )
    dprob0 = jnp.sum(dz * class_rows, -1, keepdims=True)
    inside = jnp.sum(dprobs * probs, -1, keepdims=True) + dprob0 * prob0
    dscores = (probs * (dprobs - inside)).astype(BF)
    dscore0 = prob0 * (dprob0 - inside)
    gv_out[...] = tn(spread, z[...].astype(BF))
    local_out[0:8, :] = jnp.zeros((8, D), F32)
    dkeys = jnp.zeros((HEADS, D), F32)
    from_class = jnp.zeros((1, D), F32)
    for n in range(local):
        rows = slice(n * HEADS, (n + 1) * HEADS)
        dkeys += nn(dscores[rows, :], norm[n]) + dscore0[rows, :] * class_row
        from_class += colsum(prob0[rows, :] * dz[rows, :] + dscore0[rows, :] * keys)
        left_out[n] = jnp.concatenate([probs[rows, :].astype(BF), dscores[rows, :]], 0)
        right_out[n] = jnp.concatenate([dz_low[rows, :], keys.astype(BF)], 0)
    local_out[6:7, :] = from_class
    local_out[8:16, :] = dkeys
    lane = lax.broadcasted_iota(jnp.int32, (1, 128), 1)
    self_sums = colsum(card)
    count_tokens = self_sums[:, 5:6]

    def squares(values):
        return jnp.sum(colsum(values * values * okay), keepdims=True)

    entries = [jnp.sum(okay * cross, keepdims=True), jnp.sum(okay * contrast, keepdims=True)]
    entries += [count, count_tokens]
    entries += [
        jnp.sqrt((self_sums[:, i : i + 1] + self_sums[:, i + 1 : i + 2]) / D / count_tokens)
        for i in (8, 10, 12, 14)
    ]
    entries += [
        jnp.sqrt(squares(item) / D / count) for item in (branch, middle, mlp_branch, token)
    ]
    line = jnp.zeros((1, 128), F32)
    for i, entry in enumerate(entries):
        line = jnp.where(lane == i, entry, line)
    stat_out[0:1, :] = line
    stat_out[1:8, :] = jnp.broadcast_to(
        replicated_sq[:, 0:128] + replicated_sq[:, 128:256] + replicated_sq[:, 256:384], (7, 128)
    )


def feed_back_kernel(
    left, right, gv, local_rows, patch, mid, raw, act, slope, vec, wmlp,
    dmid_out, gfeed_out, rows_out, gmlp_out,
):
    hidden = wmlp.shape[1] // 2
    count = wmlp.shape[0]
    shard = D // count

    @pl.when(pl.program_id(0) == 0)
    def _():
        gmlp_out[...] = jnp.zeros_like(gmlp_out)
        rows_out[...] = local_rows[...]

    unit, inverse = normalize(patch[0])
    dnormed = tn(left[0], right[0])[:P_SIZE, :]
    rows_out[4:5, :] += colsum(dnormed * unit)
    rows_out[5:6, :] += colsum(dnormed)
    incoming = normalize_back(unit, inverse, vec[8:9, :], dnormed)

    unit, inverse = normalize(mid[0])
    normed = (unit * vec[4:5, :] + vec[5:6, :]).astype(BF)
    rows_out[3:4, :] += colsum(incoming * (raw[0].astype(F32) + vec[6:7, :]))
    rows_out[2:3, :] += vec[7:8, :] * colsum(incoming)
    ddown = (incoming * vec[7:8, :]).astype(BF)
    gmlp_out[:, hidden:, :] += tn(act[0], ddown).reshape(count, hidden, D)
    dinner = (nt(ddown, part(wmlp, hidden, hidden)) * slope[0].astype(F32)).astype(BF)
    gmlp_out[:, :hidden, :] += tn(dinner, normed).reshape(count, hidden, D)
    dnormed = nn(dinner, part(wmlp, 0, hidden))
    rows_out[0:1, :] += colsum(dnormed * unit)
    rows_out[1:2, :] += colsum(dnormed)
    dmid_out[0] = incoming + normalize_back(unit, inverse, vec[4:5, :], dnormed)

    @pl.when(pl.program_id(0) == pl.num_programs(0) - 1)
    def _():
        used = 2 * hidden + shard
        gfeed_out[:, : 2 * hidden, :] = gmlp_out[...].astype(BF)
        gfeed_out[:, 2 * hidden : used, :] = gv[...].astype(BF).reshape(count, shard, D)
        if used < gfeed_out.shape[1]:
            gfeed_out[:, used:, :] = jnp.zeros((count, gfeed_out.shape[1] - used, D), BF)


def self_back_kernel(
    n_dp, n_mp, dmid, pixels, embed, q, k, v, prob, post, ho, raw, vec, wattn, t1row, t2row, gfeed,
    rows_feed, block_far, shared_far, square_out,
    gattn_out, gpos_out, rows_out, dx_all, dx_rows, stack_q, stack_h, slopes,
    blocks_out, commons_out, block_here, shared_here, save_sem, *sum_buffers,
):
    shard = wattn.shape[1] // 4
    count = wattn.shape[0]
    images = dx_all.shape[0]
    place = Place(n_dp, n_mp)
    rows_a, _ = halves(gfeed.shape[1], n_dp)
    sum_a = ShardSum(place, gfeed, 0, True, *sum_buffers[:SUM_BUFFERS])
    sum_b = ShardSum(
        place, gfeed, rows_a, False, *sum_buffers[SUM_BUFFERS : 2 * SUM_BUFFERS]
    )

    def beside(step, *stages):
        @pl.when(pl.program_id(0) == step)
        def _():
            for stage in stages:
                stage()

    @pl.when(pl.program_id(0) == 0)
    def _():
        gattn_out[...] = jnp.zeros_like(gattn_out)
        gpos_out[...] = jnp.zeros_like(gpos_out)
        rows_out[...] = jnp.zeros_like(rows_out)
        stack_q[...] = jnp.zeros_like(stack_q)
        stack_h[...] = jnp.zeros_like(stack_h)
        greet(place.near_partners() + place.dp_partners())()
        sum_a.start()
        sum_b.start()

    beside(1, sum_a.second, sum_b.second)
    beside(images * 3 // 8, sum_a.third, sum_b.third)
    beside(images * 5 // 8, sum_a.fourth, sum_b.fourth)

    wq = part(wattn, 0, shard)
    wk = part(wattn, shard, shard)
    wv = part(wattn, 2 * shard, shard)
    wo = part(wattn, 3 * shard, shard)
    incoming = dmid[0]
    rows_out[3:4, :] += colsum(incoming * (raw[0].astype(F32) + vec[2:3, :]))
    rows_out[2:3, :] += vec[3:4, :] * colsum(incoming)
    dbranch = (incoming * vec[3:4, :]).astype(BF)
    gattn_out[:, 3 * shard :, :] += tn(ho[0], dbranch).reshape(count, shard, D)
    dheads = nt(dbranch, wo).astype(BF).astype(F32)

    unit, inverse = normalize(embed[0])
    normed = (unit * vec[0:1, :] + vec[1:2, :]).astype(BF)
    q_wide = q[0].astype(F32)
    stack_heads(stack_q, q_wide, t1row)
    stack_heads(stack_h, dheads, t2row)
    slopes[...] = nt(v[0], stack_h[...])
    dv = nn(prob[0], stack_h[...]).astype(BF)
    for first in range(0, HEADS * PAD, 128):
        at = slice(first, first + 128)
        chance = prob[0, :, at].astype(F32)
        dprob = slopes[:, at]
        slopes[:, at] = chance * (dprob - colsum(dprob * chance))
    dmixed = slopes[...].astype(BF)
    dk = nn(dmixed, stack_q[...]).astype(BF)
    dpre = tn(dmixed, k[0])
    dq = jnp.zeros(q_wide.shape, F32)
    for g in range(HEADS):
        rows = slice(g * PAD, g * PAD + P_SIZE)
        dq += dpre[rows, :] * t1row[g : g + 1, :]
        rows_out[8 + g : 9 + g, :] += colsum(q_wide * dpre[rows, :])
        rows_out[16 + g : 17 + g, :] += colsum(dheads * post[0, rows, :].astype(F32))
    dq = dq.astype(BF)
    gattn_out[:, :shard, :] += tn(dq, normed).reshape(count, shard, D)
    gattn_out[:, shard : 2 * shard, :] += tn(dk, normed).reshape(count, shard, D)
    gattn_out[:, 2 * shard : 3 * shard, :] += tn(dv, normed).reshape(count, shard, D)
    dnormed = nn(dq, wq) + nn(dk, wk) + nn(dv, wv)
    rows_out[0:1, :] += colsum(dnormed * unit)
    rows_out[1:2, :] += colsum(dnormed)
    dx = incoming + normalize_back(unit, inverse, vec[0:1, :], dnormed)
    gpos_out[...] += dx
    dx_all[pl.program_id(0)] = dx

    @pl.when(pl.program_id(0) == pl.num_programs(0) - 1)
    def _():
        for n in range(images):
            dx_rows[:, n, :] = dx_all[n]
        gpix = tn(pixels[...], dx_rows[...].reshape(pixels.shape[0], D).astype(BF))
        used = gattn_out.shape[1]
        blocks_out[:, :used, :] = gattn_out[...].astype(BF)
        if used < blocks_out.shape[1]:
            blocks_out[:, used:, :] = jnp.zeros((count, blocks_out.shape[1] - used, D), BF)
        wide = commons_out.shape[1]
        commons_out[:3] = gpix.astype(BF).reshape(3, wide, D)
        commons_out[3] = jnp.concatenate(
            [
                gpos_out[...], jnp.zeros((12, D), F32), rows_feed[...], rows_out[...],
                jnp.zeros((8, D), F32),
            ],
            0,
        ).astype(BF)
        if count > 4:
            commons_out[4:] = jnp.zeros((count - 4, wide, D), BF)
        reduce_rows(
            place, blocks_out, commons_out, sum_a.finish(), sum_b.finish(), block_here,
            shared_here, square_out, *sum_buffers[2 * SUM_BUFFERS :],
        )
        saves = [
            pltpu.make_async_copy(block_here, block_far, save_sem.at[0]),
            pltpu.make_async_copy(shared_here, shared_far, save_sem.at[1]),
        ]
        for copy in saves:
            copy.start()
        sum_a.wait_sends()
        sum_b.wait_sends()
        for copy in saves:
            copy.wait()


def table_rows(n_dp, n_mp):
    return -(-(PIX + 256) // (16 * n_dp * n_mp)) * 16 * n_dp


def per_image(*tail):
    return pl.BlockSpec((1, *tail), lambda n: (n, *(0 for _ in tail)))


def constant(*shape):
    return pl.BlockSpec(shape, lambda n: tuple(0 for _ in shape))


def shaped(*shape, dtype=F32):
    return jax.ShapeDtypeStruct(shape, dtype)


def params():
    return pltpu.CompilerParams(vmem_limit_bytes=VMEM_LIMIT, dimension_semantics=("arbitrary",))


def remote_params(collective_id):
    return pltpu.CompilerParams(
        vmem_limit_bytes=VMEM_LIMIT, dimension_semantics=("arbitrary",),
        collective_id=collective_id, has_side_effects=True,
    )


def run_self_attend(n_dp, n_mp, embed, cols, vec, wattn, t1row, t2row, mlp_rows):
    count = embed.shape[0]
    rows = per_image(P_SIZE, D)
    low = shaped(count, P_SIZE, D, dtype=BF)
    return pl.pallas_call(
        functools.partial(self_attend_kernel, n_dp, n_mp),
        grid=(count,),
        in_specs=[
            rows, constant(*cols.shape), constant(*vec.shape),
            constant(*wattn.shape), constant(HEADS, D), constant(HEADS, D),
            constant(*mlp_rows.shape),
        ],
        out_specs=[
            rows, rows, rows, per_image(P_SIZE, HEADS * PAD), per_image(HEADS * PAD, D),
            rows, rows, rows, per_image(1, 128), ANY,
        ],
        out_shape=[
            low, low, low, shaped(count, P_SIZE, HEADS * PAD, dtype=BF),
            shaped(count, HEADS * PAD, D, dtype=BF), low, low,
            shaped(count, P_SIZE, D), shaped(count, 1, 128),
            shaped(n_mp, *mlp_rows.shape, dtype=BF),
        ],
        scratch_shapes=[pltpu.VMEM((HEADS * PAD, D), BF), pltpu.VMEM((P_SIZE, HEADS * PAD), F32)]
        + gather_scratch(n_mp),
        compiler_params=remote_params(6),
        name="self_attend",
    )(embed, cols, vec, wattn, t1row, t2row, mlp_rows)


def run_feed(
    n_dp, n_mp, group, mid, cols, bias_row, base, stat, vec, wmlp, cls_rows, up_rows, down_rows, head
):
    count = mid.shape[0]
    shard, hidden = cls_rows.shape[0] // 4, up_rows.shape[0]
    wide = n_mp * hidden
    everyone = n_dp * n_mp * count
    wcls = (n_mp, *cls_rows.shape)
    half = (n_mp, *up_rows.shape)
    dma = pltpu.SemaphoreType.DMA
    token_outs = [
        shaped(count, 2 * HEADS, WIDE, dtype=BF), shaped(count, 2 * HEADS, D, dtype=BF),
        shaped(D, D), shaped(16, D), shaped(shard, D), shaped(hidden, D), shaped(hidden, D),
        shaped(head.shape[0] + 8, D), shaped(16, D), shaped(8, 128),
    ]
    return pl.pallas_call(
        functools.partial(feed_kernel, n_dp, n_mp, group),
        grid=(count,),
        in_specs=[
            per_image(P_SIZE, D), constant(*cols.shape), constant(1, count * WIDE),
            constant(*base.shape), per_image(1, 128), constant(*vec.shape), constant(*wmlp.shape),
            constant(*cls_rows.shape), constant(*up_rows.shape), constant(*down_rows.shape), ANY,
        ],
        out_specs=[
            per_image(P_SIZE, D), per_image(P_SIZE, wide), per_image(P_SIZE, wide),
            per_image(P_SIZE, D), constant(24, D), constant(*wcls),
        ]
        + [constant(*item.shape) for item in token_outs],
        out_shape=[
            shaped(count, P_SIZE, D), shaped(count, P_SIZE, wide, dtype=BF),
            shaped(count, P_SIZE, wide, dtype=BF), shaped(count, P_SIZE, D, dtype=BF),
            shaped(24, D), shaped(*wcls, dtype=BF),
        ]
        + token_outs,
        scratch_shapes=[
            pltpu.VMEM((count, WIDE, D), BF), pltpu.VMEM((count * HEADS, WIDE), F32),
            pltpu.VMEM((count * HEADS, 128), F32), pltpu.VMEM((count * HEADS, D), F32),
            pltpu.VMEM((4 * count, 128), F32), pltpu.VMEM(half, BF), pltpu.VMEM(half, BF),
            pltpu.VMEM(wcls, BF), pltpu.VMEM(head.shape, BF),
            pltpu.VMEM((everyone, D), F32), pltpu.VMEM((D, D), F32), pltpu.VMEM((wide, D), F32),
            pltpu.VMEM((wide, D), F32),
            pltpu.VMEM((4 * everyone, 128), F32), pltpu.VMEM((4 * everyone, 128), BF),
            dma((2, n_dp)), dma((2, n_mp)), dma((1,)),
        ]
        + spread_scratch(n_dp, n_mp) * 3,
        compiler_params=remote_params(7),
        name="feed",
    )(
        mid, cols, bias_row, base, stat, vec, wmlp, cls_rows, up_rows, down_rows, head
    )


def run_feed_back(n_dp, left, right, gv, local_rows, patch, mid, raw, act, slope, vec, wmlp):
    count = mid.shape[0]
    wide = act.shape[2]
    feed = (wmlp.shape[0], pad_rows(wmlp.shape[1] + D // wmlp.shape[0], n_dp), D)
    return pl.pallas_call(
        feed_back_kernel,
        grid=(count,),
        in_specs=[
            per_image(2 * HEADS, WIDE), per_image(2 * HEADS, D), constant(D, D), constant(16, D),
            per_image(P_SIZE, D), per_image(P_SIZE, D), per_image(P_SIZE, D),
            per_image(P_SIZE, wide), per_image(P_SIZE, wide), constant(*vec.shape),
            constant(*wmlp.shape),
        ],
        out_specs=[per_image(P_SIZE, D), constant(*feed), constant(16, D)],
        out_shape=[shaped(count, P_SIZE, D), shaped(*feed, dtype=BF), shaped(16, D)],
        scratch_shapes=[pltpu.VMEM(wmlp.shape, F32)],
        compiler_params=params(),
        name="feed_back",
    )(left, right, gv, local_rows, patch, mid, raw, act, slope, vec, wmlp)


def run_self_back(
    n_dp, n_mp, dmid, pixels, embed, q, k, v, prob, post, ho, raw, vec, wattn, t1row, t2row, gfeed,
    rows_feed,
):
    count = dmid.shape[0]
    rows_a, rows_b = halves(gfeed.shape[1], n_dp)
    blocks = (n_mp, pad_rows(wattn.shape[1], n_dp), D)
    commons = (n_mp, table_rows(n_dp, n_mp), D)
    rows = blocks[1] + rows_a + rows_b
    n_lo = 2 if n_dp < 16 else 4
    return pl.pallas_call(
        functools.partial(self_back_kernel, n_dp, n_mp),
        grid=(count,),
        in_specs=[
            per_image(P_SIZE, D), constant(*pixels.shape), per_image(P_SIZE, D),
            per_image(P_SIZE, D), per_image(P_SIZE, D), per_image(P_SIZE, D),
            per_image(P_SIZE, HEADS * PAD), per_image(HEADS * PAD, D), per_image(P_SIZE, D),
            per_image(P_SIZE, D), constant(*vec.shape), constant(*wattn.shape), constant(HEADS, D),
            constant(HEADS, D), constant(*gfeed.shape), constant(16, D),
        ],
        out_specs=[
            ANY, ANY, constant(8, 128),
        ],
        out_shape=[
            shaped(rows, D, dtype=BF), shaped(*commons, dtype=BF), shaped(8, 128),
        ],
        scratch_shapes=[
            pltpu.VMEM(wattn.shape, F32), pltpu.VMEM((P_SIZE, D), F32), pltpu.VMEM((24, D), F32),
            pltpu.VMEM((count, P_SIZE, D), F32), pltpu.VMEM((P_SIZE, count, D), F32),
            pltpu.VMEM((HEADS * PAD, D), BF), pltpu.VMEM((HEADS * PAD, D), BF),
            pltpu.VMEM((P_SIZE, HEADS * PAD), F32),
            pltpu.VMEM(blocks, BF), pltpu.VMEM(commons, BF), pltpu.VMEM((rows, D), BF),
            pltpu.VMEM(commons, BF), pltpu.SemaphoreType.DMA((2,)),
        ]
        + sum_scratch(n_dp, n_mp, rows_a, True)
        + sum_scratch(n_dp, n_mp, rows_b, False)
        + reduce_scratch(
            n_dp, n_mp, blocks[1], commons[1], (rows_a // n_lo, rows_b // n_lo)
        ),
        compiler_params=pltpu.CompilerParams(
            vmem_limit_bytes=VMEM_LIMIT, dimension_semantics=("arbitrary",), collective_id=5,
            has_side_effects=True,
        ),
        name="self_back",
    )(dmid, pixels, embed, q, k, v, prob, post, ho, raw, vec, wattn, t1row, t2row, gfeed, rows_feed)


def share_cards(n_dp, n_mp, card, out, slots, dp_sem, mp_sem):
    dp = lax.axis_index("dp")
    mp = lax.axis_index("mp")
    rows = card.shape[0]
    others_dp = [(lax.rem(dp + step, n_dp), mp) for step in range(1, n_dp)]
    others_mp = [(dp, lax.rem(mp + step, n_mp)) for step in range(1, n_mp)]
    own = tile_rows(slots, (mp * n_dp + dp) * rows, rows)
    slots[pl.ds(pl.multiple_of((mp * n_dp + dp) * rows, 16), rows), :] = card[...].astype(BF)
    sends = [
        remote(own, own, dp_sem.at[0, step], dp_sem.at[1, step], others_dp[step - 1])
        for step in range(1, n_dp)
    ]
    for copy in sends:
        copy.start()
    for step in range(1, n_dp):
        source = lax.rem(dp + n_dp - step, n_dp)
        theirs = tile_rows(slots, (mp * n_dp + source) * rows, rows)
        remote(own, theirs, dp_sem.at[0, step], dp_sem.at[1, step], (source, mp)).wait_recv()
    slab = tile_rows(slots, mp * n_dp * rows, n_dp * rows)
    for step in range(1, n_mp):
        sends.append(
            remote(slab, slab, mp_sem.at[0, step], mp_sem.at[1, step], others_mp[step - 1])
        )
        sends[-1].start()
    for step in range(1, n_mp):
        source = lax.rem(mp + n_mp - step, n_mp)
        theirs = tile_rows(slots, source * n_dp * rows, n_dp * rows)
        remote(slab, theirs, mp_sem.at[0, step], mp_sem.at[1, step], (dp, source)).wait_recv()
    for i in range(n_dp):
        for j in range(n_mp):
            to, source = (i * n_mp + j) * rows, (j * n_dp + i) * rows
            out[to : to + rows, :] = slots[source : source + rows, :].astype(F32)
    for copy in sends:
        copy.wait_send()


def start_kernel(
    n_dp, n_mp, group, attn_in, attn_out, mlp_in, mlp_out, pixels, tables, vec, mix, mask,
    counts, labels, pairs,
    out, mlp_rows, cls_rows, up_rows, down_rows, embed_far, head_out, t1_out, t2_out, cols_out, bias_out, base_out,
    embed_out, head_rows, wide_up, wide_down, shard, wide_in, wide_out, patch_rows, pos_rows, by_patch, near_send, near_recv, far_send, far_recv, load_sem,
):
    dp = lax.axis_index("dp")
    mp = lax.axis_index("mp")
    n_y = n_mp // 2
    y = lax.div(mp, 2)
    core = lax.rem(mp, 2)
    sibling = (dp, y * 2 + 1 - core)
    load_patch = pltpu.make_async_copy(tables.at[pl.ds(0, PIX)], patch_rows, load_sem.at[0])
    load_pos = pltpu.make_async_copy(tables.at[pl.ds(PIX, 200)], pos_rows, load_sem.at[1])
    load_in = pltpu.make_async_copy(attn_in, wide_in, load_sem.at[2])
    load_out = pltpu.make_async_copy(attn_out, wide_out, load_sem.at[3])
    load_up = pltpu.make_async_copy(mlp_in, wide_up, load_sem.at[5])
    load_down = pltpu.make_async_copy(mlp_out, wide_down, load_sem.at[6])
    load_in.start()
    load_out.start()
    load_patch.start()
    load_pos.start()
    classes = head_out.shape[0]
    load_head = pltpu.make_async_copy(
        tables.at[pl.ds(PIX + P_SIZE - 4, classes + 4)], head_rows, load_sem.at[4]
    )
    load_up.start()
    load_down.start()
    load_head.start()
    barrier = pltpu.get_barrier_semaphore()
    pl.semaphore_signal(barrier, inc=1, device_id=sibling, device_id_type=MESH)
    for step in range(1, n_y):
        pl.semaphore_signal(
            barrier, inc=1, device_id=(dp, lax.rem(y + step, n_y) * 2 + core), device_id_type=MESH
        )
    third = attn_in.shape[1]
    load_in.wait()
    load_out.wait()
    shard[:third, :] = wide_in[0].astype(BF)
    shard[third:, :] = wide_out[0].astype(BF)
    pl.semaphore_wait(barrier, n_y)
    far = [
        remote(
            shard, out.at[mp], far_send.at[step], far_recv.at[step],
            (dp, lax.rem(y + step, n_y) * 2 + core),
        )
        for step in range(1, n_y)
    ]
    for copy in far:
        copy.start()
    near = [remote(shard, out.at[mp], near_send.at[0], near_recv.at[0], sibling)]
    near[0].start()
    out[pl.ds(mp, 1)] = shard[...][None]

    cls_rows[:third, :] = wide_in[1].astype(BF)
    cls_rows[third:, :] = wide_out[1].astype(BF)
    hidden = mlp_rows.shape[0] // 2
    load_up.wait()
    load_down.wait()
    mlp_rows[:hidden, :] = wide_up[0].T.astype(BF)
    mlp_rows[hidden:, :] = wide_down[0].astype(BF)
    up_rows[...] = wide_up[1].T.astype(BF)
    down_rows[...] = wide_down[1].astype(BF)

    images = mask.shape[0]
    lane = lax.broadcasted_iota(jnp.int32, (1, 128), 1)
    keep = (mask[...] > 0).astype(F32)
    bias = (1.0 - keep) * MASKED
    count = counts[0]
    okays = []
    bias_out[...] = jnp.full(bias_out.shape, MASKED, F32)
    for n in range(images):
        okays.append((jnp.full((1, 1), mp * images + n, jnp.int32) >= group - count).astype(F32))
        bias_out[:, n * WIDE : n * WIDE + P_SIZE] = bias[n : n + 1, :]
        tokens = jnp.sum(keep[n : n + 1, :], 1, keepdims=True) * okays[n]
        entries = (
            lax.div(labels[n], 32), lax.rem(labels[n], 32), lax.div(pairs[n], 32),
            lax.rem(pairs[n], 32), count,
        )
        line = jnp.where(lane == len(entries), tokens, 0.0)
        for place, entry in enumerate(entries):
            line = jnp.where(lane == place, entry.astype(F32), line)
        base_out[n : n + 1, :] = line
    cols_out[...] = jnp.concatenate([bias, keep * jnp.concatenate(okays, 0)], 0).T
    heads = head_mask()
    exact = functools.partial(
        lax.dot_general, preferred_element_type=F32, precision=lax.Precision.HIGHEST
    )
    t1_out[...] = exact(mix[0], heads, (((1,), (0,)), ((), ()))) * SCALE
    t2_out[...] = exact(mix[1], heads, (((0,), (0,)), ((), ())))

    load_patch.wait()
    wp = patch_rows[...].astype(BF)
    local = embed_out.shape[0]
    half = P_SIZE // 2
    for place in range(2):
        rows = slice(place * half * local, (place + 1) * half * local)
        by_patch[place * half : (place + 1) * half] = nn(pixels[rows, :], wp).reshape(half, local, D)

    for step in range(1, n_y):
        source = lax.rem(y + n_y - step, n_y) * 2
        slot = source + core
        remote(
            shard, out.at[slot], far_send.at[step], far_recv.at[step], (dp, slot)
        ).wait_recv()
        copy = remote(
            out.at[slot], out.at[slot], near_send.at[step], near_recv.at[step], sibling
        )
        copy.start()
        near.append(copy)
    load_pos.wait()
    offset = pos_rows[:P_SIZE, :] + vec[16:17, :]
    for n in range(local):
        embed_out[n] = by_patch[:, n, :] + offset
    save_embed = pltpu.make_async_copy(embed_out, embed_far, load_sem.at[7])
    save_embed.start()
    load_head.wait()
    head_out[...] = head_rows[4:, :].astype(BF)
    save_embed.wait()
    for copy in far:
        copy.wait_send()
    for step in range(n_y):
        slot = lax.rem(y + n_y - step, n_y) * 2 + 1 - core
        near[step].wait_send()
        remote(
            out.at[slot], out.at[slot], near_send.at[step], near_recv.at[step], sibling
        ).wait_recv()


def run_start(
    n_dp, n_mp, group, attn_in, attn_out, mlp_in, mlp_out, pixels, tables, vec, mix, mask, counts,
    labels, pairs,
):
    local = labels.shape[0]
    classes = tables.shape[0] - PIX - P_SIZE
    scalars = pl.BlockSpec(memory_space=pltpu.SMEM)
    n_y = n_mp // 2
    rows = attn_in.shape[1] + attn_out.shape[1]
    hidden = mlp_in.shape[2]
    dma = pltpu.SemaphoreType.DMA
    return pl.pallas_call(
        functools.partial(start_kernel, n_dp, n_mp, group),
        in_specs=[ANY] * 4 + [WHOLE, ANY, WHOLE, WHOLE, WHOLE, scalars, scalars, scalars],
        out_specs=[WHOLE] * 5 + [ANY] + [WHOLE] * 6,
        out_shape=[
            shaped(n_mp, rows, D, dtype=BF), shaped(2 * hidden, D, dtype=BF),
            shaped(rows, D, dtype=BF), shaped(hidden, D, dtype=BF), shaped(hidden, D, dtype=BF),
            shaped(local, P_SIZE, D),
            shaped(classes, D, dtype=BF), shaped(HEADS, D), shaped(HEADS, D),
            shaped(P_SIZE, 2 * local), shaped(1, local * WIDE), shaped(local, 128),
        ],
        scratch_shapes=[
            pltpu.VMEM((local, P_SIZE, D), F32),
            pltpu.VMEM((classes + 4, D), F32), pltpu.VMEM(mlp_in.shape, F32),
            pltpu.VMEM(mlp_out.shape, F32),
            pltpu.VMEM((rows, D), BF), pltpu.VMEM(attn_in.shape, F32),
            pltpu.VMEM(attn_out.shape, F32), pltpu.VMEM((PIX, D), F32),
            pltpu.VMEM((200, D), F32),
            pltpu.VMEM((P_SIZE, local, D), F32),
            dma((n_y,)), dma((n_y,)), dma((n_y,)), dma((n_y,)), dma((8,)),
        ],
        compiler_params=pltpu.CompilerParams(
            vmem_limit_bytes=VMEM_LIMIT, collective_id=2, has_side_effects=True
        ),
        name="start",
    )(
        attn_in, attn_out, mlp_in, mlp_out, pixels, tables, vec, mix, mask, counts, labels, pairs
    )


def reduce_rows(
    p, blocks, commons, chunk_a, chunk_b,
    block_out, shared_out, square_out,
    squares, attn_run, run_a, run_b, sem_a, sem_b, high_a, high_b, high_sem, low_sem, square_sem,
    *sum_buffers,
):
    n_mp = p.n_mp
    attn = ShardSum(p, blocks, 0, True, *sum_buffers[:SUM_BUFFERS])
    table = TableSum(p, commons, shared_out, *sum_buffers[SUM_BUFFERS:])
    rows_a = blocks.shape[1]
    rows_feed = p.n_lo * run_a.shape[0]
    hand_a = HandLow(p, block_out, rows_a, rows_feed, sem_a)
    hand_b = HandLow(p, block_out, rows_a + rows_feed, p.n_lo * run_b.shape[0], sem_b)
    wide_a = HandHigh(p, run_a, high_a)
    wide_b = HandHigh(p, run_b, high_b)
    hand_high = HandHigh(p, attn_run, high_sem)
    hand_low = HandLow(p, block_out, 0, rows_a, low_sem)

    attn.start()
    table.start()
    wide_a.start(chunk_a)
    wide_b.start(chunk_b)
    attn.second()
    table.near_to_low()
    table.low_to_high()
    attn.third()
    wide_a.arrive()
    hand_a.start(run_a[...])
    wide_b.arrive()
    hand_b.start(run_b[...])
    table.high_to_far()
    attn.fourth()
    table.turn()
    table.far_to_high()
    hand_high.start(attn.finish())
    table.high_to_low()
    hand_high.arrive()
    hand_low.start(attn_run[...])
    table.low_to_near()
    sends = []

    for item in (hand_a, hand_b, hand_low):
        item.arrive()
    sums = block_out[...].astype(F32)
    sums = colsum(sums * sums)
    squares[pl.ds(p.mp, 1)] = jnp.broadcast_to(
        sums[:, 0:128] + sums[:, 128:256] + sums[:, 256:384], (8, 128)
    )[None]

    for step in range(1, p.n_y):
        sends.append(
            remote(
                squares.at[p.mp], squares.at[p.mp], square_sem.at[0, step],
                square_sem.at[1, step], (p.dp, p.along_y(step) * 2 + p.core),
            )
        )
        sends[-1].start()
    for step in range(1, p.n_y):
        source = p.along_y(p.n_y - step) * 2 + p.core
        remote(
            squares.at[p.mp], squares.at[source], square_sem.at[0, step], square_sem.at[1, step],
            (p.dp, source),
        ).wait_recv()
    mine = squares[pl.ds(p.core, 1)]
    for y in range(1, p.n_y):
        mine += squares[pl.ds(2 * y + p.core, 1)]
    squares[pl.ds(n_mp + p.core, 1)] = mine
    sends.append(
        remote(
            squares.at[n_mp + p.core], squares.at[n_mp + p.core], square_sem.at[0, 0],
            square_sem.at[1, 0], p.sibling,
        )
    )
    sends[-1].start()
    table.finish()
    remote(
        squares.at[n_mp + p.core], squares.at[n_mp + 1 - p.core], square_sem.at[0, 0],
        square_sem.at[1, 0], p.sibling,
    ).wait_recv()
    square_out[...] = squares[n_mp] + squares[n_mp + 1]
    for copy in sends:
        copy.wait_send()
    for item in (attn, wide_a, wide_b, hand_a, hand_b, hand_high, hand_low):
        item.wait_sends()


def reduce_scratch(n_dp, n_mp, rows_a, wide, feed):
    assert wide == 256
    n_lo = 2 if n_dp < 16 else 4
    n_hi = n_dp // n_lo
    dma = pltpu.SemaphoreType.DMA
    return (
        [
            pltpu.VMEM((n_mp + 2, 8, 128), F32), pltpu.VMEM((rows_a // n_lo, D), BF),
            pltpu.VMEM((feed[0], D), BF), pltpu.VMEM((feed[1], D), BF),
            dma((2, n_lo)), dma((2, n_lo)), dma((2, n_hi)), dma((2, n_hi)), dma((2, n_hi)),
            dma((2, n_lo)), dma((2, n_mp)),
        ]
        + sum_scratch(n_dp, n_mp, rows_a, True)
        + table_scratch(n_dp, n_mp, wide)
    )


def root(values):
    return values * lax.rsqrt(values)


def adam_parts(gradient, mean, square, factor):
    clipped = gradient * factor
    mean_new = BETA_ONE * mean + (1.0 - BETA_ONE) * clipped
    square_new = BETA_TWO * square + (1.0 - BETA_TWO) * clipped * clipped
    direction = (
        mean_new
        * (1.0 / (1.0 - BETA_ONE**STEP))
        / (root(square_new * (1.0 / (1.0 - BETA_TWO**STEP))) + ADAM_EPS)
    )
    return (mean_new, square_new, direction)


def fold(values):
    squares = (values * values).reshape(values.shape[0] // 8, 8, values.shape[1]).sum(0)
    width = values.shape[1]
    if width % 128:
        return jnp.broadcast_to(jnp.sum(squares, 1, keepdims=True), (8, 128)) * (1.0 / 128)
    return sum(squares[:, i : i + 128] for i in range(0, width, 128))


def total(values):
    return jnp.sum(jnp.sum(values, 0, keepdims=True), 1, keepdims=True)


def moment_sweep(factor, grad, w, m, s, u, rows):
    chunk = 32 if rows % 32 == 0 else 16

    def step(i, kept):
        at = pl.ds(pl.multiple_of(i * chunk, chunk), chunk)
        weight = w[at, :]
        mean, second, direction = adam_parts(grad(i, chunk), m[at, :], s[at, :], factor)
        m[at, :] = mean
        s[at, :] = second
        update = direction + DECAY * weight
        u[at, :] = update.astype(u.dtype)
        return (kept[0] + fold(weight), kept[1] + fold(update))

    zero = jnp.zeros((8, 128), F32)
    return lax.fori_loop(0, rows // chunk, step, (zero, zero))


def rows_from(ref, first):
    def read(i, chunk):
        at = pl.ds(pl.multiple_of(first + i * chunk, 16), chunk)
        return ref[at, :].astype(F32)

    return read


def moment_kernel(
    n_dp, block_sq, gout1, rows1, stat, aux, vec, vec_mean, vec_square, mix, mix_mean, mix_square,
    *rest,
):
    large, rest = rest[:5], rest[5:]
    state = rest[:12]
    outs = rest[12:24]
    (
        vec_out, vec_mean_out, vec_square_out, mix_out, mix_mean_out, mix_square_out,
        misc_out, sums_out,
    ) = rest[24:32]
    held = rest[32:44]
    updates = rest[44:48]
    grad_q, grad_k, grad_flip, load_sem, save_sem = rest[48:53]
    large_here = rest[53:]
    first_loads = [
        pltpu.make_async_copy(large[i], large_here[i], load_sem.at[12 + i]) for i in range(5)
    ]
    loads = [pltpu.make_async_copy(state[i], held[i], load_sem.at[i]) for i in range(12)]
    for copy in first_loads + loads:
        copy.start()
    for copy in first_loads:
        copy.wait()
    block, shared, wcls, gup1, gdown1 = large_here
    mp = lax.axis_index("mp")
    hs = state[3].shape[1]
    fs = state[9].shape[1]
    feed = pad_rows(4 * hs, n_dp)

    rows2 = shared[PIX + 208 : PIX + 224, :].astype(F32)
    rows3 = shared[PIX + 224 : PIX + 256, :].astype(F32)
    token = aux[8:9, :]
    wq = part(wcls, 0, hs)
    wk = part(wcls, hs, hs).astype(F32)
    query = nt(wq, aux[8:16, :].astype(BF))[:, 0:1].astype(BF).astype(F32)
    dkeys = jnp.concatenate(
        [jnp.broadcast_to(rows2[8 + h : 9 + h, :], (HEAD, D)) for h in range(HEADS)], 0
    )
    dquery = SCALE * jnp.sum(wk * dkeys, 1, keepdims=True)
    gq = dquery * token
    gk = (SCALE * query) * dkeys
    grad_q[...] = gq
    grad_k[...] = gk
    dtoken = rows2[6:7, :] + colsum(dquery * wq.astype(F32))
    unit, inverse = normalize(jnp.broadcast_to(vec[17:18, :], (8, D)))
    dcls = normalize_back(unit, inverse, vec[8:9, :], jnp.broadcast_to(dtoken, (8, D)))[0:1, :]
    dgain = rows2[4:5, :] + dtoken * unit[0:1, :]
    last = rows1[...]
    positions = shared[PIX : PIX + 208, :].astype(F32)
    grad_vec = jnp.concatenate(
        [
            rows3[0:4, :], rows2[0:4, :], dgain, rows2[5:6, :] + dtoken, last[2:8, :],
            colsum(positions), last[8:9, :] + dcls, last[9:11, :],
        ],
        0,
    )
    mask = head_mask()
    exact = functools.partial(
        lax.dot_general, dimension_numbers=(((1,), (1,)), ((), ())),
        preferred_element_type=F32, precision=lax.Precision.HIGHEST,
    )
    grad_mix = (exact(rows3[8:16, :], mask) * SCALE, exact(mask, rows3[16:24, :]))

    square = total(block_sq[0:1, :]) + total(stat[1:2, :]) + total(colsum(gq * gq + gk * gk))
    square += total(grad_vec * grad_vec)
    square += total(grad_mix[0] * grad_mix[0]) + total(grad_mix[1] * grad_mix[1])

    def square_rows(i, kept):
        rows = shared[pl.ds(pl.multiple_of(i * 16, 16), 16), :].astype(F32)
        return kept + fold(rows)

    square += total(lax.fori_loop(0, (PIX + 208) // 16, square_rows, jnp.zeros((8, 128), F32)))
    norm = jnp.sqrt(square)
    factor = CLIP / jnp.maximum(norm, CLIP)

    mean, second, direction = adam_parts(grad_vec, vec_mean[...], vec_square[...], factor)
    vec_mean_out[...] = mean
    vec_square_out[...] = second
    vec_out[...] = vec[...] - RATE_VECTOR * direction
    misc = []
    weight_sums = []
    for b in range(2):
        mean, second, direction = adam_parts(grad_mix[b], mix_mean[b], mix_square[b], factor)
        mix_mean_out[b] = mean
        mix_square_out[b] = second
        update = direction + DECAY * mix[b]
        weight_sq = total(mix[b] * mix[b])
        update_sq = total(update * update)
        mix_out[b] = mix[b] - RATE * jnp.sqrt(weight_sq / (update_sq + 1e-12)) * update
        weight_sums.append(weight_sq)
        misc.append(update_sq)

    def sweep(grad, w, m, s, u, rows):
        return moment_sweep(factor, grad, w, m, s, u, rows)

    saves = []

    def save(i, source):
        saves.append(pltpu.make_async_copy(source, outs[i], save_sem.at[i]))
        saves[-1].start()

    sums = []
    own_h = pl.multiple_of(mp * hs, hs)
    for kind in range(4):
        for copy in loads[3 * kind : 3 * kind + 3]:
            copy.wait()
        w, m, s = held[3 * kind : 3 * kind + 3]
        u = updates[kind]
        for b in range(2):
            views = (w.at[b], m.at[b], s.at[b], u.at[b])
            if kind == 0 and b == 0:
                sums.append(sweep(rows_from(block, 0), *views, 3 * hs))
            elif kind == 0:
                pieces = []
                for third, source in enumerate(
                    (
                        rows_from(grad_q, own_h),
                        rows_from(grad_k, own_h),
                        rows_from(block, feed + 2 * fs),
                    )
                ):
                    pieces.append(
                        sweep(
                            source, *(view.at[pl.ds(third * hs, hs)] for view in views), hs
                        )
                    )
                sums.append(
                    tuple(pieces[0][i] + pieces[1][i] + pieces[2][i] for i in range(2))
                )
            elif kind == 1:
                source = rows_from(gout1, 0) if b else rows_from(block, 3 * hs)
                sums.append(sweep(source, *views, hs))
            elif kind == 2:
                if b:
                    grad_flip[...] = gup1[...].T
                else:
                    grad_flip[...] = block[feed : feed + fs, :].astype(F32).T
                sums.append(sweep(rows_from(grad_flip, 0), *views, D))
            else:
                source = rows_from(gdown1, 0) if b else rows_from(block, feed + fs)
                sums.append(sweep(source, *views, fs))
        save(3 * kind, u)
        save(3 * kind + 1, m)
        save(3 * kind + 2, s)
    for place, pair in enumerate(sums):
        sums_out[place : place + 1, :] = colsum(pair[1])
        sums_out[8 + place : 9 + place, :] = colsum(pair[0])

    lane = lax.broadcasted_iota(jnp.int32, (1, 128), 1)
    misc_out[0:1, :] = jnp.broadcast_to(norm, (1, 128))
    weight_line = jnp.zeros((1, 128), F32)
    update_line = jnp.zeros((1, 128), F32)
    for b in range(2):
        weight_line = jnp.where(lane == 11 + b, weight_sums[b], weight_line)
        update_line = jnp.where(lane == 11 + b, misc[b], update_line)
    misc_out[1:2, :] = weight_line
    misc_out[2:3, :] = update_line
    misc_out[3:8, :] = jnp.zeros((5, 128), F32)
    for copy in saves:
        copy.wait()


def table_kernel(misc, shared, ghead, *rest):
    state, outs, misc_out = rest[:3], rest[3:6], rest[6]
    w, m, s, table_update, load_sem, save_sem = rest[7:]
    rows_all = w.shape[0]
    edge = PIX + P_SIZE - 4
    body = (rows_all - edge - 16) // 64 * 32
    middle = edge + 16 + body
    cuts = (0, PIX // 2, PIX, middle, rows_all)
    slabs = [pl.ds(low, high - low) for low, high in zip(cuts, cuts[1:])]
    loads = [
        [
            pltpu.make_async_copy(state[i].at[at], (w, m, s)[i].at[at], load_sem.at[i, place])
            for i in range(3)
        ]
        for place, at in enumerate(slabs)
    ]
    for group in loads:
        for copy in group:
            copy.start()
    factor = CLIP / jnp.maximum(misc[0:1, 0:1], CLIP)
    saves = []

    def arrive(place):
        for copy in loads[place]:
            copy.wait()

    def save(i, place):
        at = slabs[place]
        saves.append(
            pltpu.make_async_copy((w, m, s)[i].at[at], outs[i].at[at], save_sem.at[i, place])
        )
        saves[-1].start()

    def slab(first, count, grad):
        at = slice(first, first + count)
        weight = w[at, :]
        mean, second, direction = adam_parts(grad, m[at, :], s[at, :], factor)
        m[at, :] = mean
        s[at, :] = second
        update = direction + DECAY * weight
        table_update[at, :] = update
        return weight, update

    def run(first, count, source, offset):
        def at(ref, start):
            return ref.at[pl.ds(start, count)]

        return moment_sweep(
            factor, rows_from(source, offset), at(w, first), at(m, first), at(s, first),
            at(table_update, first), count,
        )

    def renew(first, count, rate):
        def step(i, _):
            at = pl.ds(pl.multiple_of(first + i * 32, 16), 32)
            w[at, :] = w[at, :] - rate * table_update[at, :]
            return 0

        lax.fori_loop(0, count // 32, step, 0)

    def rate_of(weight_sq, update_sq):
        return RATE * jnp.sqrt(weight_sq / (update_sq + 1e-12))

    def masked(values, mask):
        return total(jnp.where(mask, values * values, 0.0))

    arrive(0)
    first_half = run(0, PIX // 2, shared, 0)
    save(1, 0)
    save(2, 0)
    arrive(1)
    second_half = run(PIX // 2, PIX // 2, shared, PIX // 2)
    save(1, 1)
    save(2, 1)
    sq_w = [total(first_half[0] + second_half[0])]
    sq_u = [total(first_half[1] + second_half[1])]
    rates = [rate_of(sq_w[0], sq_u[0])]
    renew(0, PIX, rates[0])
    save(0, 0)
    save(0, 1)
    arrive(2)
    place_rows = run(PIX, P_SIZE - 4, shared, PIX)
    tile = lax.broadcasted_iota(jnp.int32, (16, 1), 0) < 4
    weight, update = slab(edge, 16, shared[edge : edge + 16, :].astype(F32) + ghead[0:16, :])
    heads = run(edge + 16, body, ghead, 16)
    save(1, 2)
    save(2, 2)
    arrive(3)
    rest_rows = (rows_all - middle) // 32 * 32
    more_heads = run(middle, rest_rows, ghead, 16 + body)
    left = middle + rest_rows
    tail_weight, tail_update = slab(
        left, rows_all - left, ghead[16 + left - edge - 16 : 16 + rows_all - edge - 16, :]
    )
    save(1, 3)
    save(2, 3)
    sq_w += [
        total(place_rows[0]) + masked(weight, tile),
        total(heads[0] + more_heads[0]) + masked(weight, ~tile) + total(tail_weight * tail_weight),
    ]
    sq_u += [
        total(place_rows[1]) + masked(update, tile),
        total(heads[1] + more_heads[1]) + masked(update, ~tile) + total(tail_update * tail_update),
    ]
    rates += [rate_of(sq_w[i], sq_u[i]) for i in (1, 2)]
    renew(PIX, P_SIZE - 4, rates[1])
    w[edge : edge + 16, :] = weight - jnp.where(tile, rates[1], rates[2]) * update
    renew(edge + 16, body, rates[2])
    save(0, 2)
    renew(middle, rest_rows, rates[2])
    w[left:rows_all, :] = tail_weight - rates[2] * tail_update
    save(0, 3)

    lane = lax.broadcasted_iota(jnp.int32, (1, 128), 1)
    weight_line = misc[1:2, :]
    update_line = misc[2:3, :]
    for place in range(3):
        weight_line = jnp.where(lane == 8 + place, sq_w[place], weight_line)
        update_line = jnp.where(lane == 8 + place, sq_u[place], update_line)
    misc_out[...] = misc[...]
    misc_out[1:2, :] = weight_line
    misc_out[2:3, :] = update_line
    for copy in saves:
        copy.wait()


def run_moments(n_dp, grads, smalls, large, state):
    outs = [
        jax.ShapeDtypeStruct(item.shape, F32 if i % 3 else BF) for i, item in enumerate(state)
    ]
    fs = state[9].shape[1]
    dma = pltpu.SemaphoreType.DMA
    return pl.pallas_call(
        functools.partial(moment_kernel, n_dp),
        in_specs=[WHOLE] * (len(grads) + len(smalls)) + [ANY] * 17,
        out_specs=[ANY] * 12 + [WHOLE] * 8,
        out_shape=outs
        + [jax.ShapeDtypeStruct(item.shape, F32) for item in smalls]
        + [shaped(8, 128), shaped(16, 128)],
        scratch_shapes=[pltpu.VMEM(item.shape, F32) for item in state]
        + [pltpu.VMEM(state[3 * kind].shape, BF) for kind in range(4)]
        + [
            pltpu.VMEM((D, D), F32), pltpu.VMEM((D, D), F32), pltpu.VMEM((D, fs), F32),
            dma((17,)), dma((12,)),
        ]
        + [pltpu.VMEM(item.shape, item.dtype) for item in large],
        compiler_params=pltpu.CompilerParams(vmem_limit_bytes=VMEM_LIMIT),
        name="moments",
    )(*grads, *smalls, *large, *state)


def run_tables(misc, shared, ghead, state):
    shape = state[0].shape
    dma = pltpu.SemaphoreType.DMA
    return pl.pallas_call(
        table_kernel,
        in_specs=[WHOLE] * 3 + [ANY] * 3,
        out_specs=[ANY] * 3 + [WHOLE],
        out_shape=[shaped(*shape)] * 3 + [shaped(8, 128)],
        scratch_shapes=[pltpu.VMEM(shape, F32)] * 4 + [dma((3, 4)), dma((3, 4))],
        cost_estimate=pl.CostEstimate(
            flops=40 * shape[0] * shape[1], bytes_accessed=28 * shape[0] * shape[1],
            transcendentals=2 * shape[0] * shape[1],
        ),
        compiler_params=pltpu.CompilerParams(vmem_limit_bytes=VMEM_LIMIT),
        name="tables",
    )(misc, shared, ghead, *state)


def renew_kernel(n_mp, misc, stat, *rest):
    theirs, rest = rest[:n_mp], rest[n_mp:]
    weights, updates = rest[:4], rest[4:8]
    new, copies = rest[8:12], rest[12:16]
    norms, norm_out, stat_out = rest[16:19]
    here, changes, lows = rest[19:23], rest[23:27], rest[27:31]
    slots, load_sem, save_sem = rest[31:]
    loads = [
        (
            pltpu.make_async_copy(weights[kind], here[kind], load_sem.at[0, kind]),
            pltpu.make_async_copy(updates[kind], changes[kind], load_sem.at[1, kind]),
        )
        for kind in range(4)
    ]
    for pair in loads[::-1]:
        for copy in pair:
            copy.start()
    mp = lax.axis_index("mp")
    for step in range(n_mp):
        slots[pl.ds(lax.rem(mp + n_mp - step, n_mp), 1)] = theirs[step][...][None]
    sums = jnp.sum(slots[...], 0)
    rates = []
    lane = lax.broadcasted_iota(jnp.int32, (1, 128), 1)
    weight_line, update_line = misc[1:2, :], misc[2:3, :]
    for place in range(8):
        update_sq = total(sums[place : place + 1, :])
        weight_sq = total(sums[8 + place : 9 + place, :])
        rates.append(RATE * jnp.sqrt(weight_sq / (update_sq + 1e-12)))
        weight_line = jnp.where(lane == place, weight_sq, weight_line)
        update_line = jnp.where(lane == place, update_sq, update_line)
    norms[...] = jnp.sqrt(jnp.concatenate([weight_line, update_line], 0))[:, :13]
    norm_out[...] = misc[0:1, 0:1]
    stat_out[...] = stat[0:1, :12]
    saves = []
    for kind in (3, 2, 1, 0):
        w, u, low = here[kind], changes[kind], lows[kind]
        rows = w.shape[1]
        chunk = 32 if rows % 32 == 0 else 16
        for copy in loads[kind]:
            copy.wait()
        for b in range(2):
            rate = rates[2 * kind + b]

            def step(i, _, b=b, w=w, u=u, low=low, rate=rate, chunk=chunk):
                at = pl.ds(pl.multiple_of(i * chunk, chunk), chunk)
                values = w[b, at, :] - rate * u[b, at, :].astype(F32)
                w[b, at, :] = values
                low[b, at, :] = values.astype(BF)
                return 0

            lax.fori_loop(0, rows // chunk, step, 0)
        saves.append(pltpu.make_async_copy(w, new[kind], save_sem.at[0, kind]))
        saves.append(pltpu.make_async_copy(low, copies[kind], save_sem.at[1, kind]))
        for copy in saves[-2:]:
            copy.start()
    for copy in saves:
        copy.wait()


def run_renew(n_mp, misc, stat, sums, weights, updates):
    dma = pltpu.SemaphoreType.DMA
    return pl.pallas_call(
        functools.partial(renew_kernel, n_mp),
        in_specs=[WHOLE] * (2 + n_mp) + [ANY] * 8,
        out_specs=[ANY] * 8 + [WHOLE] * 3,
        out_shape=[shaped(*item.shape) for item in weights]
        + [shaped(*item.shape, dtype=BF) for item in weights]
        + [shaped(2, 13), shaped(1, 1), shaped(1, 12)],
        scratch_shapes=[pltpu.VMEM(item.shape, F32) for item in weights]
        + [pltpu.VMEM(item.shape, BF) for item in weights] * 2
        + [pltpu.VMEM((n_mp, 16, 128), F32), dma((2, 4)), dma((2, 4))],
        compiler_params=pltpu.CompilerParams(vmem_limit_bytes=VMEM_LIMIT),
        name="renew",
    )(misc, stat, *sums, *weights, *updates)


def shards(
    pixels,
    token_mask,
    counts,
    labels,
    pairs,
    attn_in,
    attn_in_mean,
    attn_in_square,
    attn_out,
    attn_out_mean,
    attn_out_square,
    mlp_in,
    mlp_in_mean,
    mlp_in_square,
    mlp_out,
    mlp_out_mean,
    mlp_out_square,
    tables,
    tables_mean,
    tables_square,
    vectors,
    vectors_mean,
    vectors_square,
    talking,
    talking_mean,
    talking_square,
):
    local = pixels.shape[0]
    group = token_mask.shape[0]
    place_mp = lax.axis_index("mp")
    n_mp = lax.axis_size("mp")
    n_dp = lax.axis_size("dp")
    hs = attn_in.shape[3]
    fs = mlp_in.shape[2]

    def as_rows(item):
        return item.transpose(0, 2, 3, 1).reshape(2, 3 * hs, D)

    def from_rows(item):
        return item.reshape(2, 3, hs, D).transpose(0, 3, 1, 2)

    attn_in, attn_in_mean, attn_in_square = map(as_rows, (attn_in, attn_in_mean, attn_in_square))
    pixel_rows = pixels.transpose(1, 0, 2).reshape(P_SIZE * local, PIX)
    mask = lax.dynamic_slice_in_dim(token_mask, place_mp * local, local, 0)
    (
        wattn, mlp_rows, cls_rows, up_rows, down_rows, embed, head, t1row, t2row, cols, bias_row,
        base,
    ) = run_start(
        n_dp, n_mp, group, attn_in, attn_out, mlp_in, mlp_out, pixel_rows, tables, vectors,
        talking, mask, counts, labels, pairs,
    )
    q, k, v, prob, post, ho, raw0, middle, stat_a, wmlp = run_self_attend(
        n_dp, n_mp, embed, cols, vectors, wattn, t1row, t2row, mlp_rows
    )
    (
        patches, act, slope, raw1, aux, wcls, left, right, gv, local_rows, gout1, gup1, gdown1,
        ghead, rows1, stat,
    ) = run_feed(
        n_dp, n_mp, group, middle, cols, bias_row, base, stat_a, vectors, wmlp, cls_rows, up_rows,
        down_rows, head,
    )
    dmid, gfeed, rows2 = run_feed_back(
        n_dp, left, right, gv, local_rows, patches, middle, raw1, act, slope, vectors, wmlp
    )
    block, shared, block_sq = run_self_back(
        n_dp, n_mp, dmid, pixel_rows, embed, q, k, v, prob, post, ho, raw0, vectors, wattn,
        t1row, t2row, gfeed, rows2,
    )

    shared = shared.reshape(-1, D)
    state = (
        attn_in, attn_in_mean, attn_in_square, attn_out, attn_out_mean, attn_out_square,
        mlp_in, mlp_in_mean, mlp_in_square, mlp_out, mlp_out_mean, mlp_out_square,
    )
    smalls = (vectors, vectors_mean, vectors_square, talking, talking_mean, talking_square)
    moved = run_moments(
        n_dp, (block_sq, gout1, rows1, stat, aux), smalls, (block, shared, wcls, gup1, gdown1),
        state,
    )
    sums = [moved[19]]
    for step in range(1, n_mp):
        sums.append(lax.ppermute(moved[19], "mp", [(i, (i + step) % n_mp) for i in range(n_mp)]))
    table = run_tables(moved[18], shared, ghead, (tables, tables_mean, tables_square))
    renewed = run_renew(n_mp, table[3], stat, sums, state[0:12:3], moved[0:12:3])
    return (
        from_rows(renewed[0]),
        from_rows(moved[1]),
        from_rows(moved[2]),
        renewed[1],
        moved[4],
        moved[5],
        renewed[2],
        moved[7],
        moved[8],
        renewed[3],
        moved[10],
        moved[11],
        *table[:3],
        *moved[12:18],
        from_rows(renewed[4]),
        renewed[5],
        renewed[6],
        renewed[7],
        renewed[10].reshape(12),
        renewed[9].reshape(()),
        renewed[8],
    )


def solution(mesh):
    return jax.shard_map(
        shards,
        mesh=mesh,
        in_specs=(
            P(("dp", "mp"), None, None),
            P("dp", None),
            P("dp"),
            P(("dp", "mp")),
            P(("dp", "mp")),
            P(None, None, None, "mp"),
            P(None, None, None, "mp"),
            P(None, None, None, "mp"),
            P(None, "mp", None),
            P(None, "mp", None),
            P(None, "mp", None),
            P(None, None, "mp"),
            P(None, None, "mp"),
            P(None, None, "mp"),
            P(None, "mp", None),
            P(None, "mp", None),
            P(None, "mp", None),
            P(),
            P(),
            P(),
            P(),
            P(),
            P(),
            P(),
            P(),
            P(),
        ),
        out_specs=(
            P(None, None, None, "mp"),
            P(None, None, None, "mp"),
            P(None, None, None, "mp"),
            P(None, "mp", None),
            P(None, "mp", None),
            P(None, "mp", None),
            P(None, None, "mp"),
            P(None, None, "mp"),
            P(None, None, "mp"),
            P(None, "mp", None),
            P(None, "mp", None),
            P(None, "mp", None),
            P(),
            P(),
            P(),
            P(),
            P(),
            P(),
            P(),
            P(),
            P(),
            P(None, None, None, "mp"),
            P(None, "mp", None),
            P(None, None, "mp"),
            P(None, "mp", None),
            P(),
            P(),
            P(),
        ),
        check_vma=False,
    )
```

```python
import functools

import jax
import jax.numpy as jnp
from jax import lax
from jax.experimental import pallas as pl
from jax.experimental.pallas import tpu as pltpu
from jax.sharding import PartitionSpec as P

D = 384
HEADS = 8
HEAD = 48
PIX = 768
P_SIZE = 196
PAD = 208
WIDE = 256
STEP = 10
SCALE = HEAD**-0.5
BETA_ONE = 0.9
BETA_TWO = 0.999
ADAM_EPS = 1e-08
DECAY = 0.01
RATE = 0.5
RATE_VECTOR = 0.5
CLIP = 0.02
TEMP = 0.05
MASKED = -1000000000.0
NORM_EPS = 1e-06
F32 = jnp.float32
BF = jnp.bfloat16
VMEM_LIMIT = 58 * 2**20
ANY = pl.BlockSpec(memory_space=pl.ANY)
MESH = pl.DeviceIdType.MESH
WHOLE = pl.BlockSpec(memory_space=pltpu.VMEM)


def nn(left, right):
    return lax.dot_general(left, right, (((1,), (0,)), ((), ())), preferred_element_type=F32)


def nt(left, right):
    return lax.dot_general(left, right, (((1,), (1,)), ((), ())), preferred_element_type=F32)


def tn(left, right):
    return lax.dot_general(left, right, (((0,), (0,)), ((), ())), preferred_element_type=F32)


def colsum(values):
    return jnp.sum(values, 0, keepdims=True)


def normalize(inputs):
    center = inputs - jnp.mean(inputs, -1, keepdims=True)
    spread = jnp.mean(center * center, -1, keepdims=True)
    inverse = lax.rsqrt(spread + NORM_EPS)
    return center * inverse, inverse


def normalize_back(unit, inverse, gain, incoming):
    scaled = incoming * gain
    return inverse * (
        scaled
        - jnp.mean(scaled, -1, keepdims=True)
        - unit * jnp.mean(scaled * unit, -1, keepdims=True)
    )


def gelu_parts(inner):
    cumulative = 0.5 + 0.5 * lax.erf(inner * 0.5**0.5)
    bell = jnp.exp2(inner * inner * (-0.5 * 1.4426950408889634)) * 0.3989422804014327
    return inner * cumulative, cumulative + inner * bell


def head_mask(copies=1):
    row = lax.rem(lax.broadcasted_iota(jnp.int32, (copies * HEADS, D), 0), HEADS)
    column = lax.broadcasted_iota(jnp.int32, (copies * HEADS, D), 1)
    return ((column >= row * HEAD) & (column < row * HEAD + HEAD)).astype(F32)


def stat_lanes(parts, weight, first):
    lane = lax.broadcasted_iota(jnp.int32, (1, 128), 1)
    row = jnp.zeros((1, 128), F32)
    for place, values in enumerate(parts):
        total = jnp.sum(colsum(values * values * weight), keepdims=True)
        high = total.astype(BF).astype(F32)
        row = jnp.where(lane == first + 2 * place, high, row)
        row = jnp.where(lane == first + 2 * place + 1, total - high, row)
    return row


def part(ref, first, rows):
    shards_count = ref.shape[0]
    return ref[:, first : first + rows, :].reshape(shards_count * rows, ref.shape[2])


def pad_rows(rows, n_dp):
    return -(-rows // (16 * n_dp)) * 16 * n_dp


class Place:
    def __init__(self, n_dp, n_mp):
        self.n_dp, self.n_mp, self.n_y = n_dp, n_mp, n_mp // 2
        self.n_lo = 2 if n_dp < 16 else 4
        self.n_hi = n_dp // self.n_lo
        self.dp = lax.axis_index("dp")
        self.mp = lax.axis_index("mp")
        self.y = lax.div(self.mp, 2)
        self.core = lax.rem(self.mp, 2)
        self.high = lax.div(self.dp, self.n_lo)
        self.low = lax.rem(self.dp, self.n_lo)
        self.chunk = self.low * self.n_hi + self.high
        self.sibling = (self.dp, self.y * 2 + 1 - self.core)

    def along_y(self, step):
        return lax.rem(self.y + step, self.n_y)

    def along_lo(self, step):
        return lax.rem(self.low + step, self.n_lo)

    def along_hi(self, step):
        return lax.rem(self.high + step, self.n_hi)

    def at_lo(self, low):
        return (self.high * self.n_lo + low, self.mp)

    def at_hi(self, high):
        return (high * self.n_lo + self.low, self.mp)

    def near_partners(self):
        return [self.sibling] + [
            (self.dp, self.along_y(step) * 2 + self.core) for step in range(1, self.n_y)
        ]

    def all_partners(self):
        partners = [(lax.rem(self.dp + step, self.n_dp), self.mp) for step in range(1, self.n_dp)]
        return partners + [
            (self.dp, lax.rem(self.mp + step, self.n_mp)) for step in range(1, self.n_mp)
        ]

    def low_partners(self):
        return [self.at_lo(self.along_lo(step)) for step in range(1, self.n_lo)]

    def dp_partners(self):
        return self.low_partners() + [self.at_hi(self.along_hi(step)) for step in range(1, self.n_hi)]


def greet(partners):
    barrier = pltpu.get_barrier_semaphore()
    for partner in partners:
        pl.semaphore_signal(barrier, inc=1, device_id=partner, device_id_type=MESH)
    return lambda: pl.semaphore_wait(barrier, len(partners))


def tile_rows(ref, first, rows):
    return ref.at[pl.ds(pl.multiple_of(first, 16), rows)]


class SpreadGather:
    def __init__(self, place, rows, out, far_sem, low_sem, near_sem):
        self.place, self.rows, self.out = place, rows, out
        self.far_sem, self.low_sem, self.near_sem = far_sem, low_sem, near_sem
        self.count = rows.shape[0] // place.n_lo

    def piece(self, ref, low):
        return tile_rows(ref, low * self.count, self.count)

    def far_copy(self, step, slot):
        p = self.place
        return remote(
            self.piece(self.rows, p.low), self.piece(self.out.at[slot], p.low),
            self.far_sem.at[0, step], self.far_sem.at[1, step],
            (p.dp, p.along_y(step) * 2 + p.core),
        )

    def low_copy(self, step, turn, low):
        p = self.place
        rows = self.piece(self.out.at[self.from_y(step) + p.core], low)
        at = (step - 1) * p.n_lo + turn
        return remote(
            rows, rows, self.low_sem.at[0, at], self.low_sem.at[1, at],
            p.at_lo(p.along_lo(turn)),
        )

    def near_copy(self, step, slot):
        return remote(
            self.rows if step == 0 else self.out.at[slot], self.out.at[slot],
            self.near_sem.at[0, step], self.near_sem.at[1, step], self.place.sibling,
        )

    def own_copy(self):
        return pltpu.make_async_copy(
            self.rows, self.out.at[self.place.mp], self.far_sem.at[0, 0]
        )

    def from_y(self, step):
        p = self.place
        return p.along_y(p.n_y - step) * 2

    def start(self):
        p = self.place
        for step in range(1, p.n_y):
            self.far_copy(step, p.mp).start()
        self.near_copy(0, p.mp).start()
        self.own_copy().start()

    def spread(self):
        p = self.place
        for step in range(1, p.n_y):
            self.far_copy(step, self.from_y(step) + p.core).wait_recv()
            for turn in range(1, p.n_lo):
                self.low_copy(step, turn, p.low).start()

    def forward(self):
        p = self.place
        for step in range(1, p.n_y):
            for turn in range(1, p.n_lo):
                self.low_copy(step, turn, p.along_lo(p.n_lo - turn)).wait_recv()
            self.near_copy(step, self.from_y(step) + p.core).start()

    def finish(self):
        p = self.place
        self.own_copy().wait()
        for step in range(1, p.n_y):
            self.far_copy(step, p.mp).wait_send()
            for turn in range(1, p.n_lo):
                self.low_copy(step, turn, p.low).wait_send()
        for step in range(p.n_y):
            self.near_copy(step, self.from_y(step) + p.core if step else p.mp).wait_send()
            self.near_copy(step, self.from_y(step) + 1 - p.core).wait_recv()


def spread_scratch(n_dp, n_mp):
    n_lo = 2 if n_dp < 16 else 4
    dma = pltpu.SemaphoreType.DMA
    return [dma((2, n_mp // 2)), dma((2, n_mp // 2 * n_lo)), dma((2, n_mp // 2))]


class Gather:
    def __init__(self, place, rows, out, far_sem, near_sem):
        self.place, self.rows, self.out = place, rows, out
        self.far_sem, self.near_sem = far_sem, near_sem

    def far_copy(self, step, slot):
        p = self.place
        return remote(
            self.rows, self.out.at[slot], self.far_sem.at[0, step], self.far_sem.at[1, step],
            (p.dp, p.along_y(step) * 2 + p.core),
        )

    def near_copy(self, step, slot):
        return remote(
            self.rows if step == 0 else self.out.at[slot], self.out.at[slot],
            self.near_sem.at[0, step], self.near_sem.at[1, step], self.place.sibling,
        )

    def own_copy(self):
        return pltpu.make_async_copy(
            self.rows, self.out.at[self.place.mp], self.far_sem.at[0, 0]
        )

    def from_y(self, step):
        p = self.place
        return p.along_y(p.n_y - step) * 2

    def start(self):
        p = self.place
        for step in range(1, p.n_y):
            self.far_copy(step, p.mp).start()
        self.near_copy(0, p.mp).start()
        self.own_copy().start()

    def forward(self):
        p = self.place
        for step in range(1, p.n_y):
            slot = self.from_y(step) + p.core
            self.far_copy(step, slot).wait_recv()
            self.near_copy(step, slot).start()

    def finish(self):
        p = self.place
        self.own_copy().wait()
        for step in range(1, p.n_y):
            self.far_copy(step, p.mp).wait_send()
        for step in range(p.n_y):
            self.near_copy(step, self.from_y(step) + p.core if step else p.mp).wait_send()
            self.near_copy(step, self.from_y(step) + 1 - p.core).wait_recv()


def gather_scratch(n_mp):
    dma = pltpu.SemaphoreType.DMA
    return [dma((2, n_mp // 2)), dma((2, n_mp // 2))]


class ShardSum:
    def __init__(
        self, place, rows, first, y_first, near, far, low, half, high,
        near_sem, far_sem, low_sem, high_sem,
    ):
        self.place, self.rows, self.first, self.y_first = place, rows, first, y_first
        self.near, self.far, self.low, self.half, self.high = near, far, low, half, high
        self.near_sem, self.far_sem = near_sem, far_sem
        self.low_sem, self.high_sem = low_sem, high_sem
        self.count = near.shape[1]
        self.wide = self.count // place.n_lo
        self.chunk = self.count // place.n_dp

    def near_copy(self, step):
        p = self.place
        y = p.along_y(step)
        return remote(
            self.rows.at[y * 2 + 1 - p.core, pl.ds(self.first, self.count)], self.near.at[y],
            self.near_sem.at[0, step], self.near_sem.at[1, step], p.sibling,
        )

    def far_copy(self, step):
        p = self.place
        y = p.along_y(step)
        rows = self.near.at[y]
        if not self.y_first:
            rows = tile_rows(rows, p.low * self.wide, self.wide)
        return remote(
            rows, self.far.at[step - 1],
            self.far_sem.at[0, step], self.far_sem.at[1, step], (p.dp, y * 2 + p.core),
        )

    def low_copy(self, step):
        p = self.place
        to = p.along_lo(step)
        at = pl.ds(pl.multiple_of(to * self.wide, 16), self.wide)
        rows = self.near.at[p.y, at] if self.y_first else self.near.at[:, at]
        return remote(
            rows, self.low.at[step - 1],
            self.low_sem.at[0, step], self.low_sem.at[1, step], p.at_lo(to),
        )

    def high_copy(self, step):
        p = self.place
        to = p.along_hi(step)
        return remote(
            tile_rows(self.half, to * self.chunk, self.chunk), self.high.at[step - 1],
            self.high_sem.at[0, step], self.high_sem.at[1, step], p.at_hi(to),
        )

    def start(self):
        for step in range(1, self.place.n_y + 1):
            self.near_copy(step).start()

    def second(self):
        p = self.place
        at = slice(self.first, self.first + self.count)
        for step in range(1, p.n_y + 1):
            y = p.along_y(step)
            self.near_copy(step).wait_recv()
            self.near[pl.ds(y, 1)] = (
                self.rows[pl.ds(y * 2 + p.core, 1), at, :].astype(F32)
                + self.near[pl.ds(y, 1)].astype(F32)
            ).astype(BF)
            if self.y_first and step < p.n_y:
                self.far_copy(step).start()
        if not self.y_first:
            for step in range(1, p.n_lo):
                self.low_copy(step).start()

    def third(self):
        p = self.place
        own = pl.ds(pl.multiple_of(p.low * self.wide, 16), self.wide)
        if self.y_first:
            sums = self.near[pl.ds(p.y, 1)].astype(F32)
            for step in range(1, p.n_y):
                self.far_copy(step).wait_recv()
                sums += self.far[step - 1].astype(F32)[None]
            self.near[pl.ds(p.y, 1)] = sums.astype(BF)
            for step in range(1, p.n_lo):
                self.low_copy(step).start()
        else:
            sums = self.near[:, own, :].astype(F32)
            for step in range(1, p.n_lo):
                self.low_copy(step).wait_recv()
                sums += self.low[step - 1].astype(F32)
            self.near[:, own, :] = sums.astype(BF)
            for step in range(1, p.n_y):
                self.far_copy(step).start()

    def fourth(self):
        p = self.place
        own = pl.ds(pl.multiple_of(p.low * self.wide, 16), self.wide)
        sums = self.near[pl.ds(p.y, 1), own, :][0].astype(F32)
        if self.y_first:
            for step in range(1, p.n_lo):
                self.low_copy(step).wait_recv()
                sums += self.low[step - 1].astype(F32)
        else:
            for step in range(1, p.n_y):
                self.far_copy(step).wait_recv()
                sums += self.far[step - 1].astype(F32)
        self.half[...] = sums.astype(BF)
        for step in range(1, p.n_hi):
            self.high_copy(step).start()

    def finish(self):
        p = self.place
        at = pl.ds(pl.multiple_of(p.high * self.chunk, 16), self.chunk)
        sums = self.half[at, :].astype(F32)
        for step in range(1, p.n_hi):
            self.high_copy(step).wait_recv()
            sums += self.high[step - 1].astype(F32)
        return sums.astype(BF)

    def wait_sends(self):
        p = self.place
        for step in range(1, p.n_y + 1):
            self.near_copy(step).wait_send()
            if step < p.n_y:
                self.far_copy(step).wait_send()
        for step in range(1, p.n_lo):
            self.low_copy(step).wait_send()
        for step in range(1, p.n_hi):
            self.high_copy(step).wait_send()


def sum_scratch(n_dp, n_mp, rows, y_first):
    n_y = n_mp // 2
    n_lo = 2 if n_dp < 16 else 4
    n_hi = n_dp // n_lo
    wide = rows // n_lo
    dma = pltpu.SemaphoreType.DMA
    far = (max(n_y - 1, 1), rows, D) if y_first else (max(n_y - 1, 1), wide, D)
    low = (n_lo - 1, wide, D) if y_first else (n_lo - 1, n_y, wide, D)
    return [
        pltpu.VMEM((n_y, rows, D), BF), pltpu.VMEM(far, BF), pltpu.VMEM(low, BF),
        pltpu.VMEM((wide, D), BF), pltpu.VMEM((n_hi - 1, rows // n_dp, D), BF),
        dma((2, n_y + 1)), dma((2, n_y + 1)), dma((2, n_lo)), dma((2, n_hi)),
    ]


SUM_BUFFERS = 9


def halves(rows, n_dp):
    unit = 16 * n_dp
    first = (rows // unit + 1) // 2 * unit
    return first, rows - first


class TableSum:
    def __init__(
        self, place, rows, out, near, low, part_rows, high, last, far, near_sem, low_sem, high_sem,
        far_sem, back_sem, hand_sem,
    ):
        self.place, self.rows, self.out = place, rows, out
        self.near, self.low, self.part, self.high = near, low, part_rows, high
        self.last, self.far = last, far
        self.near_sem, self.low_sem, self.high_sem = near_sem, low_sem, high_sem
        self.far_sem, self.back_sem, self.hand_sem = far_sem, back_sem, hand_sem
        self.chunk = high.shape[2]
        self.wide = low.shape[2]
        self.slab = place.core * place.n_y + place.y
        self.first = place.core * place.n_y

    def near_copy(self):
        p = self.place
        return remote(
            self.rows.at[pl.ds((1 - p.core) * p.n_y, p.n_y)], self.near,
            self.near_sem.at[0], self.near_sem.at[1], p.sibling,
        )

    def low_copy(self, step):
        p = self.place
        to = p.along_lo(step)
        return remote(
            self.near.at[:, pl.ds(pl.multiple_of(to * self.wide, 16), self.wide)],
            self.low.at[step - 1], self.low_sem.at[0, step], self.low_sem.at[1, step], p.at_lo(to),
        )

    def high_copy(self, step):
        p = self.place
        to = p.along_hi(step)
        return remote(
            self.part.at[:, pl.ds(pl.multiple_of(to * self.chunk, 16), self.chunk)],
            self.high.at[step - 1], self.high_sem.at[0, step], self.high_sem.at[1, step],
            p.at_hi(to),
        )

    def far_copy(self, step):
        p = self.place
        to = p.along_y(step)
        return remote(
            self.last.at[to], self.far.at[step - 1], self.far_sem.at[0, step],
            self.far_sem.at[1, step], (p.dp, to * 2 + p.core),
        )

    def start(self):
        self.near_copy().start()

    def near_to_low(self):
        p = self.place
        self.near_copy().wait_recv()
        self.near[...] = (
            self.rows[pl.ds(self.first, p.n_y)].astype(F32) + self.near[...].astype(F32)
        ).astype(BF)
        for step in range(1, p.n_lo):
            self.low_copy(step).start()

    def low_to_high(self):
        p = self.place
        at = pl.ds(pl.multiple_of(p.low * self.wide, 16), self.wide)
        sums = self.near[:, at, :].astype(F32)
        for step in range(1, p.n_lo):
            self.low_copy(step).wait_recv()
            sums += self.low[step - 1].astype(F32)
        self.part[...] = sums.astype(BF)
        for step in range(1, p.n_hi):
            self.high_copy(step).start()

    def high_to_far(self):
        p = self.place
        at = pl.ds(pl.multiple_of(p.high * self.chunk, 16), self.chunk)
        sums = self.part[:, at, :].astype(F32)
        for step in range(1, p.n_hi):
            self.high_copy(step).wait_recv()
            sums += self.high[step - 1].astype(F32)
        self.last[...] = sums.astype(BF)
        for step in range(1, p.n_y):
            self.far_copy(step).start()

    def chunk_at(self, slab, chunk):
        return self.out.at[slab, pl.ds(pl.multiple_of(chunk * self.chunk, 16), self.chunk)]

    def back_far(self, step, y):
        p = self.place
        rows = self.chunk_at(self.first + y, p.chunk)
        return remote(
            rows, rows, self.back_sem.at[0, step], self.back_sem.at[1, step],
            (p.dp, p.along_y(step) * 2 + p.core),
        )

    def back_high(self, step, chunk):
        p = self.place
        rows = self.chunk_at(pl.ds(self.first, p.n_y), chunk)
        return remote(
            rows, rows, self.back_sem.at[2, step], self.back_sem.at[3, step],
            p.at_hi(p.along_hi(step)),
        )

    def back_low(self, step, low):
        p = self.place
        rows = self.out.at[
            pl.ds(self.first, p.n_y), pl.ds(pl.multiple_of(low * self.wide, 16), self.wide)
        ]
        return remote(
            rows, rows, self.back_sem.at[4, step], self.back_sem.at[5, step],
            p.at_lo(p.along_lo(step)),
        )

    def hand_copy(self, core):
        p = self.place
        rows = self.out.at[pl.ds(core * p.n_y, p.n_y)]
        return remote(rows, rows, self.hand_sem.at[0], self.hand_sem.at[1], p.sibling)

    def turn(self):
        p = self.place
        sums = self.last[pl.ds(p.y, 1)][0].astype(F32)
        for step in range(1, p.n_y):
            self.far_copy(step).wait_recv()
            sums += self.far[step - 1].astype(F32)
        at = pl.ds(pl.multiple_of(p.chunk * self.chunk, 16), self.chunk)
        self.out[pl.ds(self.slab, 1), at, :] = sums.astype(BF)[None]
        for step in range(1, p.n_y):
            self.back_far(step, p.y).start()

    def far_to_high(self):
        p = self.place
        for step in range(1, p.n_y):
            self.back_far(step, p.along_y(p.n_y - step)).wait_recv()
        for step in range(1, p.n_hi):
            self.back_high(step, p.chunk).start()

    def high_to_low(self):
        p = self.place
        for step in range(1, p.n_hi):
            self.back_high(step, p.low * p.n_hi + p.along_hi(p.n_hi - step)).wait_recv()
        for step in range(1, p.n_lo):
            self.back_low(step, p.low).start()

    def low_to_near(self):
        p = self.place
        for step in range(1, p.n_lo):
            self.back_low(step, p.along_lo(p.n_lo - step)).wait_recv()
        self.hand_copy(p.core).start()

    def finish(self):
        p = self.place
        self.hand_copy(1 - p.core).wait_recv()
        self.near_copy().wait_send()
        self.hand_copy(p.core).wait_send()
        for step in range(1, p.n_lo):
            self.low_copy(step).wait_send()
            self.back_low(step, p.low).wait_send()
        for step in range(1, p.n_hi):
            self.high_copy(step).wait_send()
            self.back_high(step, p.chunk).wait_send()
        for step in range(1, p.n_y):
            self.far_copy(step).wait_send()
            self.back_far(step, p.y).wait_send()


def table_scratch(n_dp, n_mp, rows):
    n_y = n_mp // 2
    n_lo = 2 if n_dp < 16 else 4
    n_hi = n_dp // n_lo
    wide, chunk = rows // n_lo, rows // n_dp
    dma = pltpu.SemaphoreType.DMA
    return [
        pltpu.VMEM((n_y, rows, D), BF), pltpu.VMEM((n_lo - 1, n_y, wide, D), BF),
        pltpu.VMEM((n_y, wide, D), BF), pltpu.VMEM((n_hi - 1, n_y, chunk, D), BF),
        pltpu.VMEM((n_y, chunk, D), BF), pltpu.VMEM((max(n_y - 1, 1), chunk, D), BF),
        dma((2,)), dma((2, n_lo)), dma((2, n_hi)), dma((2, n_y)),
        dma((6, max(n_y, n_lo, n_hi))), dma((2,)),
    ]


class HandHigh:
    def __init__(self, place, rows, sems):
        self.place, self.rows, self.sems = place, rows, sems
        self.chunk = rows.shape[0] // place.n_hi

    def copy(self, step, source):
        p = self.place
        rows = tile_rows(self.rows, source * self.chunk, self.chunk)
        return remote(
            rows, rows, self.sems.at[0, step], self.sems.at[1, step], p.at_hi(p.along_hi(step))
        )

    def start(self, sums):
        p = self.place
        self.rows[pl.ds(pl.multiple_of(p.high * self.chunk, 16), self.chunk), :] = sums
        for step in range(1, p.n_hi):
            self.copy(step, p.high).start()

    def arrive(self):
        p = self.place
        for step in range(1, p.n_hi):
            self.copy(step, p.along_hi(p.n_hi - step)).wait_recv()

    def wait_sends(self):
        for step in range(1, self.place.n_hi):
            self.copy(step, self.place.high).wait_send()


class HandLow:
    def __init__(self, place, rows, first, count, sems):
        self.place, self.rows, self.first, self.sems = place, rows, first, sems
        self.run = count // place.n_lo

    def copy(self, step, source):
        p = self.place
        rows = tile_rows(self.rows, self.first + source * self.run, self.run)
        return remote(
            rows, rows, self.sems.at[0, step], self.sems.at[1, step], p.at_lo(p.along_lo(step))
        )

    def start(self, sums):
        p = self.place
        self.rows[pl.ds(pl.multiple_of(self.first + p.low * self.run, 16), self.run), :] = sums
        for step in range(1, p.n_lo):
            self.copy(step, p.low).start()

    def arrive(self):
        p = self.place
        for step in range(1, p.n_lo):
            self.copy(step, p.along_lo(p.n_lo - step)).wait_recv()

    def wait_sends(self):
        for step in range(1, self.place.n_lo):
            self.copy(step, self.place.low).wait_send()


def remote(src, dst, send_sem, recv_sem, device):
    return pltpu.make_async_remote_copy(
        src_ref=src, dst_ref=dst, send_sem=send_sem, recv_sem=recv_sem,
        device_id=device, device_id_type=MESH,
    )


def stack_heads(stack, rows, gains):
    for g in range(HEADS):
        stack[g * PAD : g * PAD + P_SIZE, :] = (rows * gains[g : g + 1, :]).astype(BF)


def column(cols, index):
    lane = lax.broadcasted_iota(jnp.int32, cols.shape, 1)
    return jnp.sum(jnp.where(lane == index, cols[...], 0.0), 1, keepdims=True)


def self_attend_kernel(
    n_dp, n_mp, group, attn_in, attn_out, mlp_in, mlp_out, pixels, tables, vec, mix, mask,
    counts, labels, pairs,
    q_out, k_out, v_out, prob_out, post_out, ho_out, raw_out, mid_out, stat_out,
    wmlp_out, wattn_far, embed_far, cls_rows, up_rows, down_rows, head_out, t1row, t2row, cols,
    bias_out, base_out,
    stack, scores, embed, wattn, mlp_rows, save_sem, *rest,
):
    start_scratch, sems = rest[:-2], rest[-2:]
    shard = wattn.shape[1] // 4
    gather = Gather(Place(n_dp, n_mp), mlp_rows, wmlp_out, *sems)
    save = pltpu.make_async_copy(wattn, wattn_far, save_sem.at[0])
    images = pl.num_programs(0)
    n = pl.program_id(0)

    @pl.when(n == 0)
    def _():
        stack[...] = jnp.zeros_like(stack)
        start_part(
            n_dp, n_mp, group, attn_in, attn_out, mlp_in, mlp_out, pixels, tables, vec, mix, mask,
            counts, labels, pairs,
            wattn, mlp_rows, cls_rows, up_rows, down_rows, embed_far, head_out, t1row, t2row, cols,
            bias_out, base_out, embed, *start_scratch,
        )
        gather.start()
        save.start()

    @pl.when(n == images * 3 // 4)
    def _():
        gather.forward()

    x = embed[pl.ds(n, 1)][0]
    unit, _ = normalize(x)
    normed = (unit * vec[0:1, :] + vec[1:2, :]).astype(BF)
    q = nt(normed, part(wattn, 0, shard)).astype(BF)
    k = nt(normed, part(wattn, shard, shard)).astype(BF)
    v = nt(normed, part(wattn, 2 * shard, shard)).astype(BF)
    q_out[0] = q
    k_out[0] = k
    v_out[0] = v
    stack_heads(stack, q.astype(F32), t1row)
    scores[...] = nt(k, stack[...])
    bias = column(cols, pl.program_id(0))
    for first in range(0, HEADS * PAD, 128):
        mixed = scores[:, first : first + 128] + bias
        grown = jnp.exp(mixed - jnp.max(mixed, 0, keepdims=True))
        prob = grown * (1.0 / jnp.sum(grown, 0, keepdims=True))
        prob_out[0, :, first : first + 128] = prob.astype(BF)
    post = tn(prob_out[0], v)
    post_out[0] = post.astype(BF)
    heads_out = jnp.zeros(x.shape, F32)
    for g in range(HEADS):
        heads_out += post[g * PAD : g * PAD + P_SIZE, :] * t2row[g : g + 1, :]
    heads_out = heads_out.astype(BF)
    ho_out[0] = heads_out
    raw = nn(heads_out, part(wattn, 3 * shard, shard))
    raw_out[0] = raw.astype(BF)
    branch = vec[3:4, :] * (raw + vec[2:3, :])
    middle = x + branch
    mid_out[0] = middle
    weight = column(cols, pl.program_id(0) + cols.shape[1] // 2)
    stat_out[0] = stat_lanes((branch, middle), weight, 8)

    @pl.when(n == images - 1)
    def _():
        gather.finish()
        save.wait()


def feed_kernel(
    n_dp, n_mp, group, mid, cols, bias_row, base, stat, vec, wmlp, cls_rows, up_rows, down_rows,
    head_far,
    patch_out, act_out, slope_out, raw_out, aux_out, wcls_out, *rest,
):
    token_outs, rest = rest[:10], rest[10:]
    norm_out, cprob_out, cprob0_out, z_out, card_out, wup_out, wdown_out, wcls, head = rest[:9]
    token_scratch, (cards, slots, dp_sem, mp_sem, head_sem), sems = rest[9:13], rest[13:18], rest[18:]
    hidden = wmlp.shape[1] // 2
    shard = wcls.shape[1] // 4
    images = norm_out.shape[0]
    place = Place(n_dp, n_mp)
    load_head = pltpu.make_async_copy(head_far, head, head_sem.at[0])
    gather_cls = SpreadGather(place, cls_rows, wcls, *sems[:3])
    gather_up = SpreadGather(place, up_rows, wup_out, *sems[3:6])
    gather_down = SpreadGather(place, down_rows, wdown_out, *sems[6:])

    def beside(step, *stages):
        @pl.when(pl.program_id(0) == step)
        def _():
            for stage in stages:
                stage()

    @pl.when(pl.program_id(0) == 0)
    def _():
        norm_out[...] = jnp.zeros_like(norm_out)
        load_head.start()
        greet(place.all_partners())()
        gather_cls.start()
        gather_up.start()
        gather_down.start()

    beside(images * 3 // 8, gather_cls.spread)
    beside(images // 2, gather_up.spread)
    beside(images * 5 // 8, gather_down.spread)
    beside(images * 3 // 4, gather_cls.forward)
    beside(images - 1, gather_up.forward, gather_cls.finish)

    middle = mid[0]
    unit, _ = normalize(middle)
    normed = (unit * vec[4:5, :] + vec[5:6, :]).astype(BF)
    inner = nt(normed, part(wmlp, 0, hidden))
    active, slope = gelu_parts(inner)
    active = active.astype(BF)
    act_out[0] = active
    slope_out[0] = slope.astype(BF)
    raw = nn(active, part(wmlp, hidden, hidden))
    raw_out[0] = raw.astype(BF)
    branch = vec[7:8, :] * (raw + vec[6:7, :])
    patches = middle + branch
    patch_out[0] = patches
    card_out[pl.ds(4 * pl.program_id(0) + 3, 1), :] = (
        base[pl.ds(pl.program_id(0), 1), :]
        + stat[0]
        + stat_lanes((branch, patches), column(cols, pl.program_id(0) + images), 12)
    )
    unit, _ = normalize(patches)
    norm_out[pl.ds(pl.program_id(0), 1), :P_SIZE, :] = (
        (unit * vec[8:9, :] + vec[9:10, :]).astype(BF)[None]
    )

    @pl.when(pl.program_id(0) == images - 1)
    def _():
        unit, _ = normalize(jnp.broadcast_to(vec[17:18, :], (HEADS, D)))
        token = (unit * vec[8:9, :] + vec[9:10, :]).astype(BF)
        query = nt(token, part(wcls, 0, shard)).astype(BF).astype(F32)
        keys = nn((query * head_mask()).astype(BF), part(wcls, shard, shard)) * SCALE
        token = token.astype(F32)
        aux_out[0:8, :] = keys
        aux_out[8:16, :] = token
        aux_out[16:24, :] = query
        scores = nt(keys.astype(BF), norm_out[...].reshape(images * WIDE, D)) + bias_row[...]
        score0 = jnp.sum(keys * token, -1, keepdims=True)
        for n in range(images):
            rows = slice(n * HEADS, (n + 1) * HEADS)
            mine = scores[:, n * WIDE : (n + 1) * WIDE]
            top = jnp.maximum(jnp.max(mine, -1, keepdims=True), score0)
            grown = jnp.exp(mine - top)
            grown0 = jnp.exp(score0 - top)
            scale = 1.0 / (jnp.sum(grown, -1, keepdims=True) + grown0)
            cprob = grown * scale
            cprob0 = grown0 * scale
            cprob_out[rows, :] = cprob
            cprob0_out[rows, :] = jnp.broadcast_to(cprob0, (HEADS, 128))
            z_out[rows, :] = nn(cprob.astype(BF), norm_out[n]) + cprob0 * token
        cheads = nt(z_out[...].astype(BF), part(wcls, 2 * shard, shard)) * head_mask(images)
        cheads = cheads.reshape(images, HEADS, D).sum(1)
        for piece in range(3):
            card_out[pl.ds(piece, images, stride=4), :] = cheads[:, 128 * piece : 128 * piece + 128]
        gather_down.forward()
        share_cards(n_dp, n_mp, card_out, cards, slots, dp_sem, mp_sem)
        wcls_out[...] = wcls[...]
        gather_up.finish()
        gather_down.finish()
        load_head.wait()
        token_kernel(
            group, cards, vec, wcls, wup_out, wdown_out, head, norm_out, cprob_out, cprob0_out,
            z_out, aux_out, *token_outs, *token_scratch,
        )


def token_kernel(
    group, cards, vec, wcls, wup_rows, wdown_rows, head, norm, cprob, cprob0, z, aux,
    left_out, right_out, gv_out, local_out, gout_out, gup_out, gdown_out, ghead_out, rows_out,
    stat_out, dch_all, gout_all, gup_all, gdown_all,
):
    hidden = wup_rows.shape[1]
    shard = wcls.shape[1] // 4
    images = cards.shape[0] // 4
    cheads = jnp.concatenate(
        [cards[pl.ds(piece, images, stride=4), :] for piece in range(3)], 1
    ).astype(BF)
    card = cards[pl.ds(3, images, stride=4), :]
    labels = (card[:, 0:1] * 32.0 + card[:, 1:2]).astype(jnp.int32)
    pairs = (card[:, 2:3] * 32.0 + card[:, 3:4]).astype(jnp.int32)
    column = lax.broadcasted_iota(jnp.int32, (images, images), 1)
    row = lax.broadcasted_iota(jnp.int32, (images, images), 0)
    slot = lax.rem(lax.broadcasted_iota(jnp.int32, (images, 1), 0), group).astype(F32)
    okay = (slot >= group - card[:, 4:5]).astype(F32)
    okay_row = colsum(jnp.where(row == column, okay, 0.0))
    wo = part(wcls, 3 * shard, shard)
    wup = part(wup_rows, 0, hidden)
    wdown = part(wdown_rows, 0, hidden)
    count = jnp.sum(okay, keepdims=True)
    raw = nn(cheads, wo) + vec[10:11, :]
    branch = vec[11:12, :] * raw
    middle = vec[17:18, :] + branch
    unit2, inverse2 = normalize(middle)
    normed = (unit2 * vec[12:13, :] + vec[13:14, :]).astype(BF)
    inner = nt(normed, wup)
    active, slope = gelu_parts(inner)
    active = active.astype(BF)
    down = nn(active, wdown) + vec[14:15, :]
    mlp_branch = vec[15:16, :] * down
    token = middle + mlp_branch
    unit3, inverse3 = normalize(token)
    feature = unit3 * vec[18:19, :] + vec[19:20, :]
    feature_low = feature.astype(BF)
    logits = nt(feature_low, head[...])
    top = jnp.max(logits, -1, keepdims=True)
    grown = jnp.exp(logits - top)
    total = jnp.sum(grown, -1, keepdims=True)
    hot = lax.broadcasted_iota(jnp.int32, logits.shape, 1) == labels
    cross = jnp.log(total) + top - jnp.sum(jnp.where(hot, logits, 0.0), -1, keepdims=True)
    share = okay / count
    dlogits = (share * (grown / total - hot.astype(F32))).astype(BF)
    classes = head.shape[0]
    ghead = tn(dlogits, feature_low)
    ghead_out[0:8, :] = jnp.zeros((8, D), F32)
    ghead_out[classes:, :] = jnp.zeros((8, D), F32)
    ghead_out[4 : classes + 4, :] = ghead
    replicated_sq = colsum(ghead * ghead)
    dfeature = nn(dlogits, head[...])

    length = lax.rsqrt(jnp.sum(feature * feature, -1, keepdims=True) + NORM_EPS)
    embed = (feature * length).astype(BF)
    sims = nt(embed, embed) / TEMP
    sims = jnp.where((okay_row > 0) & (row != column), sims, MASKED)
    top = jnp.max(sims, -1, keepdims=True)
    grown = jnp.exp(sims - top)
    total = jnp.sum(grown, -1, keepdims=True)
    hot = column == pairs
    contrast = jnp.log(total) + top - jnp.sum(jnp.where(hot, sims, 0.0), -1, keepdims=True)
    dsims = share * (grown / total - hot.astype(F32))
    high = dsims.astype(BF)
    low = (dsims - high.astype(F32)).astype(BF)
    dembed = (nn(high, embed) + nn(low, embed) + tn(high, embed) + tn(low, embed)) / TEMP
    dfeature += length * dembed - feature * (
        length * length * length * jnp.sum(dembed * feature, -1, keepdims=True)
    )

    dtoken = normalize_back(unit3, inverse3, vec[18:19, :], dfeature)
    rows_out[0:1, :] = jnp.zeros((1, D), F32)
    rows_out[1:2, :] = jnp.zeros((1, D), F32)
    rows_out[7:8, :] = colsum(dtoken * down)
    rows_out[6:7, :] = vec[15:16, :] * colsum(dtoken)
    ddown = (dtoken * vec[15:16, :]).astype(BF)
    gdown = tn(active, ddown)
    own_f = pl.multiple_of(lax.axis_index("mp") * hidden, hidden)
    gdown_all[...] = gdown
    gdown_out[...] = gdown_all[pl.ds(own_f, hidden), :]
    replicated_sq += colsum(gdown * gdown)
    dinner = (nt(ddown, wdown) * slope).astype(BF)
    gup = tn(dinner, normed)
    gup_all[...] = gup
    gup_out[...] = gup_all[pl.ds(own_f, hidden), :]
    replicated_sq += colsum(gup * gup)
    dnormed = nn(dinner, wup)
    rows_out[4:5, :] = colsum(dnormed * unit2)
    rows_out[5:6, :] = colsum(dnormed)
    dmiddle = dtoken + normalize_back(unit2, inverse2, vec[12:13, :], dnormed)
    rows_out[3:4, :] = colsum(dmiddle * raw)
    rows_out[2:3, :] = vec[11:12, :] * colsum(dmiddle)
    rows_out[8:9, :] = colsum(dmiddle)
    rows_out[9:10, :] = colsum(dfeature * unit3)
    rows_out[10:11, :] = colsum(dfeature)
    dbranch = (dmiddle * vec[11:12, :]).astype(BF)
    gout = tn(cheads, dbranch)
    gout_all[...] = gout
    own_h = pl.multiple_of(lax.axis_index("mp") * shard, shard)
    gout_out[...] = gout_all[pl.ds(own_h, shard), :]
    replicated_sq += colsum(gout * gout)
    dch_all[...] = nt(dbranch, wo)
    local = norm.shape[0]
    place = lax.axis_index("dp") * lax.axis_size("mp") + lax.axis_index("mp")
    if local % 8 == 0:
        dch = dch_all[pl.ds(pl.multiple_of(place * local, local), local), :]
    else:
        share_of = 8 // local
        start = pl.multiple_of(lax.div(place, share_of) * 8, 8)
        window = dch_all[pl.ds(start, 8), :]
        pick = lax.rem(place, share_of)
        dch = sum(
            jnp.where(pick == i, window[i * local : (i + 1) * local, :], 0.0)
            for i in range(share_of)
        )

    keys = aux[0:8, :]
    class_row = aux[8:16, :]
    mask = head_mask()
    spread = jnp.concatenate([mask * dch[n : n + 1, :] for n in range(local)], 0).astype(BF)
    dz = nn(spread, part(wcls, 2 * shard, shard))
    dz_low = dz.astype(BF)
    probs = cprob[...]
    prob0 = cprob0[...][:, 0:1]
    class_rows = jnp.concatenate([class_row] * local, 0)
    dprobs = jnp.concatenate(
        [nt(dz_low[n * HEADS : (n + 1) * HEADS, :], norm[n]) for n in range(local)], 0
    )
    dprob0 = jnp.sum(dz * class_rows, -1, keepdims=True)
    inside = jnp.sum(dprobs * probs, -1, keepdims=True) + dprob0 * prob0
    dscores = (probs * (dprobs - inside)).astype(BF)
    dscore0 = prob0 * (dprob0 - inside)
    gv_out[...] = tn(spread, z[...].astype(BF))
    local_out[0:8, :] = jnp.zeros((8, D), F32)
    dkeys = jnp.zeros((HEADS, D), F32)
    from_class = jnp.zeros((1, D), F32)
    for n in range(local):
        rows = slice(n * HEADS, (n + 1) * HEADS)
        dkeys += nn(dscores[rows, :], norm[n]) + dscore0[rows, :] * class_row
        from_class += colsum(prob0[rows, :] * dz[rows, :] + dscore0[rows, :] * keys)
        left_out[n] = jnp.concatenate([probs[rows, :].astype(BF), dscores[rows, :]], 0)
        right_out[n] = jnp.concatenate([dz_low[rows, :], keys.astype(BF)], 0)
    local_out[6:7, :] = from_class
    local_out[8:16, :] = dkeys
    lane = lax.broadcasted_iota(jnp.int32, (1, 128), 1)
    self_sums = colsum(card)
    count_tokens = self_sums[:, 5:6]

    def squares(values):
        return jnp.sum(colsum(values * values * okay), keepdims=True)

    entries = [jnp.sum(okay * cross, keepdims=True), jnp.sum(okay * contrast, keepdims=True)]
    entries += [count, count_tokens]
    entries += [
        jnp.sqrt((self_sums[:, i : i + 1] + self_sums[:, i + 1 : i + 2]) / D / count_tokens)
        for i in (8, 10, 12, 14)
    ]
    entries += [
        jnp.sqrt(squares(item) / D / count) for item in (branch, middle, mlp_branch, token)
    ]
    line = jnp.zeros((1, 128), F32)
    for i, entry in enumerate(entries):
        line = jnp.where(lane == i, entry, line)
    stat_out[0:1, :] = line
    stat_out[1:8, :] = jnp.broadcast_to(
        replicated_sq[:, 0:128] + replicated_sq[:, 128:256] + replicated_sq[:, 256:384], (7, 128)
    )


def feed_back_kernel(
    left, right, gv, local_rows, patch, mid, raw, act, slope, vec, wmlp,
    dmid_out, gfeed_out, rows_out, gmlp_out,
):
    hidden = wmlp.shape[1] // 2
    count = wmlp.shape[0]
    shard = D // count

    @pl.when(pl.program_id(0) == 0)
    def _():
        gmlp_out[...] = jnp.zeros_like(gmlp_out)
        rows_out[...] = local_rows[...]

    unit, inverse = normalize(patch[0])
    dnormed = tn(left[0], right[0])[:P_SIZE, :]
    rows_out[4:5, :] += colsum(dnormed * unit)
    rows_out[5:6, :] += colsum(dnormed)
    incoming = normalize_back(unit, inverse, vec[8:9, :], dnormed)

    unit, inverse = normalize(mid[0])
    normed = (unit * vec[4:5, :] + vec[5:6, :]).astype(BF)
    rows_out[3:4, :] += colsum(incoming * (raw[0].astype(F32) + vec[6:7, :]))
    rows_out[2:3, :] += vec[7:8, :] * colsum(incoming)
    ddown = (incoming * vec[7:8, :]).astype(BF)
    gmlp_out[:, hidden:, :] += tn(act[0], ddown).reshape(count, hidden, D)
    dinner = (nt(ddown, part(wmlp, hidden, hidden)) * slope[0].astype(F32)).astype(BF)
    gmlp_out[:, :hidden, :] += tn(dinner, normed).reshape(count, hidden, D)
    dnormed = nn(dinner, part(wmlp, 0, hidden))
    rows_out[0:1, :] += colsum(dnormed * unit)
    rows_out[1:2, :] += colsum(dnormed)
    dmid_out[0] = incoming + normalize_back(unit, inverse, vec[4:5, :], dnormed)

    @pl.when(pl.program_id(0) == pl.num_programs(0) - 1)
    def _():
        used = 2 * hidden + shard
        gfeed_out[:, : 2 * hidden, :] = gmlp_out[...].astype(BF)
        gfeed_out[:, 2 * hidden : used, :] = gv[...].astype(BF).reshape(count, shard, D)
        if used < gfeed_out.shape[1]:
            gfeed_out[:, used:, :] = jnp.zeros((count, gfeed_out.shape[1] - used, D), BF)


def self_back_kernel(
    n_dp, n_mp, dmid, pixels, embed, q, k, v, prob, post, ho, raw, vec, wattn, t1row, t2row, gfeed,
    rows_feed, block_far, shared_far, square_out,
    gattn_out, gpos_out, rows_out, dx_all, dx_rows, stack_q, stack_h, slopes,
    blocks_out, commons_out, block_here, shared_here, save_sem, *sum_buffers,
):
    shard = wattn.shape[1] // 4
    count = wattn.shape[0]
    images = dx_all.shape[0]
    place = Place(n_dp, n_mp)
    rows_a, _ = halves(gfeed.shape[1], n_dp)
    sum_a = ShardSum(place, gfeed, 0, True, *sum_buffers[:SUM_BUFFERS])
    sum_b = ShardSum(
        place, gfeed, rows_a, False, *sum_buffers[SUM_BUFFERS : 2 * SUM_BUFFERS]
    )

    def beside(step, *stages):
        @pl.when(pl.program_id(0) == step)
        def _():
            for stage in stages:
                stage()

    @pl.when(pl.program_id(0) == 0)
    def _():
        gattn_out[...] = jnp.zeros_like(gattn_out)
        gpos_out[...] = jnp.zeros_like(gpos_out)
        rows_out[...] = jnp.zeros_like(rows_out)
        stack_q[...] = jnp.zeros_like(stack_q)
        stack_h[...] = jnp.zeros_like(stack_h)
        greet(place.near_partners() + place.dp_partners())()
        sum_a.start()
        sum_b.start()

    beside(1, sum_a.second, sum_b.second)
    beside(images * 3 // 8, sum_a.third, sum_b.third)
    beside(images * 5 // 8, sum_a.fourth, sum_b.fourth)

    wq = part(wattn, 0, shard)
    wk = part(wattn, shard, shard)
    wv = part(wattn, 2 * shard, shard)
    wo = part(wattn, 3 * shard, shard)
    incoming = dmid[0]
    rows_out[3:4, :] += colsum(incoming * (raw[0].astype(F32) + vec[2:3, :]))
    rows_out[2:3, :] += vec[3:4, :] * colsum(incoming)
    dbranch = (incoming * vec[3:4, :]).astype(BF)
    gattn_out[:, 3 * shard :, :] += tn(ho[0], dbranch).reshape(count, shard, D)
    dheads = nt(dbranch, wo).astype(BF).astype(F32)

    unit, inverse = normalize(embed[0])
    normed = (unit * vec[0:1, :] + vec[1:2, :]).astype(BF)
    q_wide = q[0].astype(F32)
    stack_heads(stack_q, q_wide, t1row)
    stack_heads(stack_h, dheads, t2row)
    slopes[...] = nt(v[0], stack_h[...])
    dv = nn(prob[0], stack_h[...]).astype(BF)
    for first in range(0, HEADS * PAD, 128):
        at = slice(first, first + 128)
        chance = prob[0, :, at].astype(F32)
        dprob = slopes[:, at]
        slopes[:, at] = chance * (dprob - colsum(dprob * chance))
    dmixed = slopes[...].astype(BF)
    dk = nn(dmixed, stack_q[...]).astype(BF)
    dpre = tn(dmixed, k[0])
    dq = jnp.zeros(q_wide.shape, F32)
    for g in range(HEADS):
        rows = slice(g * PAD, g * PAD + P_SIZE)
        dq += dpre[rows, :] * t1row[g : g + 1, :]
        rows_out[8 + g : 9 + g, :] += colsum(q_wide * dpre[rows, :])
        rows_out[16 + g : 17 + g, :] += colsum(dheads * post[0, rows, :].astype(F32))
    dq = dq.astype(BF)
    gattn_out[:, :shard, :] += tn(dq, normed).reshape(count, shard, D)
    gattn_out[:, shard : 2 * shard, :] += tn(dk, normed).reshape(count, shard, D)
    gattn_out[:, 2 * shard : 3 * shard, :] += tn(dv, normed).reshape(count, shard, D)
    dnormed = nn(dq, wq) + nn(dk, wk) + nn(dv, wv)
    rows_out[0:1, :] += colsum(dnormed * unit)
    rows_out[1:2, :] += colsum(dnormed)
    dx = incoming + normalize_back(unit, inverse, vec[0:1, :], dnormed)
    gpos_out[...] += dx
    dx_all[pl.program_id(0)] = dx

    @pl.when(pl.program_id(0) == pl.num_programs(0) - 1)
    def _():
        for n in range(images):
            dx_rows[:, n, :] = dx_all[n]
        gpix = tn(pixels[...], dx_rows[...].reshape(pixels.shape[0], D).astype(BF))
        used = gattn_out.shape[1]
        blocks_out[:, :used, :] = gattn_out[...].astype(BF)
        if used < blocks_out.shape[1]:
            blocks_out[:, used:, :] = jnp.zeros((count, blocks_out.shape[1] - used, D), BF)
        wide = commons_out.shape[1]
        commons_out[:3] = gpix.astype(BF).reshape(3, wide, D)
        commons_out[3] = jnp.concatenate(
            [
                gpos_out[...], jnp.zeros((12, D), F32), rows_feed[...], rows_out[...],
                jnp.zeros((8, D), F32),
            ],
            0,
        ).astype(BF)
        if count > 4:
            commons_out[4:] = jnp.zeros((count - 4, wide, D), BF)
        reduce_rows(
            place, blocks_out, commons_out, sum_a.finish(), sum_b.finish(), block_here,
            shared_here, square_out, *sum_buffers[2 * SUM_BUFFERS :],
        )
        saves = [
            pltpu.make_async_copy(block_here, block_far, save_sem.at[0]),
            pltpu.make_async_copy(shared_here, shared_far, save_sem.at[1]),
        ]
        for copy in saves:
            copy.start()
        sum_a.wait_sends()
        sum_b.wait_sends()
        for copy in saves:
            copy.wait()


def table_rows(n_dp, n_mp):
    return -(-(PIX + 256) // (16 * n_dp * n_mp)) * 16 * n_dp


def per_image(*tail):
    return pl.BlockSpec((1, *tail), lambda n: (n, *(0 for _ in tail)))


def constant(*shape):
    return pl.BlockSpec(shape, lambda n: tuple(0 for _ in shape))


def shaped(*shape, dtype=F32):
    return jax.ShapeDtypeStruct(shape, dtype)


def params():
    return pltpu.CompilerParams(vmem_limit_bytes=VMEM_LIMIT, dimension_semantics=("arbitrary",))


def remote_params(collective_id):
    return pltpu.CompilerParams(
        vmem_limit_bytes=VMEM_LIMIT, dimension_semantics=("arbitrary",),
        collective_id=collective_id, has_side_effects=True,
    )


def run_self_attend(
    n_dp, n_mp, group, attn_in, attn_out, mlp_in, mlp_out, pixels, tables, vec, mix, mask, counts,
    labels, pairs,
):
    count = labels.shape[0]
    classes = tables.shape[0] - PIX - P_SIZE
    n_y = n_mp // 2
    shard = attn_in.shape[1] + attn_out.shape[1]
    hidden = mlp_in.shape[2]
    rows = per_image(P_SIZE, D)
    low = shaped(count, P_SIZE, D, dtype=BF)
    scalars = pl.BlockSpec(memory_space=pltpu.SMEM)
    dma = pltpu.SemaphoreType.DMA
    shared = [
        shaped(shard, D, dtype=BF), shaped(hidden, D, dtype=BF), shaped(hidden, D, dtype=BF),
        shaped(classes, D, dtype=BF), shaped(HEADS, D), shaped(HEADS, D),
        shaped(P_SIZE, 2 * count), shaped(1, count * WIDE), shaped(count, 128),
    ]
    return pl.pallas_call(
        functools.partial(self_attend_kernel, n_dp, n_mp, group),
        grid=(count,),
        in_specs=[
            ANY, ANY, ANY, ANY, constant(*pixels.shape), ANY, constant(*vec.shape),
            constant(*mix.shape), constant(*mask.shape), scalars, scalars, scalars,
        ],
        out_specs=[
            rows, rows, rows, per_image(P_SIZE, HEADS * PAD), per_image(HEADS * PAD, D),
            rows, rows, rows, per_image(1, 128), ANY, ANY, ANY,
        ]
        + [constant(*item.shape) for item in shared],
        out_shape=[
            low, low, low, shaped(count, P_SIZE, HEADS * PAD, dtype=BF),
            shaped(count, HEADS * PAD, D, dtype=BF), low, low,
            shaped(count, P_SIZE, D), shaped(count, 1, 128),
            shaped(n_mp, 2 * hidden, D, dtype=BF), shaped(n_mp, shard, D, dtype=BF),
            shaped(count, P_SIZE, D),
        ]
        + shared,
        scratch_shapes=[
            pltpu.VMEM((HEADS * PAD, D), BF), pltpu.VMEM((P_SIZE, HEADS * PAD), F32),
            pltpu.VMEM((count, P_SIZE, D), F32), pltpu.VMEM((n_mp, shard, D), BF),
            pltpu.VMEM((2 * hidden, D), BF), dma((1,)),
            pltpu.VMEM((classes + 4, D), F32), pltpu.VMEM(mlp_in.shape, F32),
            pltpu.VMEM(mlp_out.shape, F32),
            pltpu.VMEM((shard, D), BF), pltpu.VMEM(attn_in.shape, F32),
            pltpu.VMEM(attn_out.shape, F32), pltpu.VMEM((PIX, D), F32),
            pltpu.VMEM((200, D), F32),
            pltpu.VMEM((P_SIZE, count, D), F32),
            dma((n_y,)), dma((n_y,)), dma((n_y,)), dma((n_y,)), dma((8,)),
        ]
        + gather_scratch(n_mp),
        compiler_params=remote_params(6),
        name="self_attend",
    )(attn_in, attn_out, mlp_in, mlp_out, pixels, tables, vec, mix, mask, counts, labels, pairs)


def run_feed(
    n_dp, n_mp, group, mid, cols, bias_row, base, stat, vec, wmlp, cls_rows, up_rows, down_rows, head
):
    count = mid.shape[0]
    shard, hidden = cls_rows.shape[0] // 4, up_rows.shape[0]
    wide = n_mp * hidden
    everyone = n_dp * n_mp * count
    wcls = (n_mp, *cls_rows.shape)
    half = (n_mp, *up_rows.shape)
    dma = pltpu.SemaphoreType.DMA
    token_outs = [
        shaped(count, 2 * HEADS, WIDE, dtype=BF), shaped(count, 2 * HEADS, D, dtype=BF),
        shaped(D, D), shaped(16, D), shaped(shard, D), shaped(hidden, D), shaped(hidden, D),
        shaped(head.shape[0] + 8, D), shaped(16, D), shaped(8, 128),
    ]
    return pl.pallas_call(
        functools.partial(feed_kernel, n_dp, n_mp, group),
        grid=(count,),
        in_specs=[
            per_image(P_SIZE, D), constant(*cols.shape), constant(1, count * WIDE),
            constant(*base.shape), per_image(1, 128), constant(*vec.shape), constant(*wmlp.shape),
            constant(*cls_rows.shape), constant(*up_rows.shape), constant(*down_rows.shape), ANY,
        ],
        out_specs=[
            per_image(P_SIZE, D), per_image(P_SIZE, wide), per_image(P_SIZE, wide),
            per_image(P_SIZE, D), constant(24, D), constant(*wcls),
        ]
        + [constant(*item.shape) for item in token_outs],
        out_shape=[
            shaped(count, P_SIZE, D), shaped(count, P_SIZE, wide, dtype=BF),
            shaped(count, P_SIZE, wide, dtype=BF), shaped(count, P_SIZE, D, dtype=BF),
            shaped(24, D), shaped(*wcls, dtype=BF),
        ]
        + token_outs,
        scratch_shapes=[
            pltpu.VMEM((count, WIDE, D), BF), pltpu.VMEM((count * HEADS, WIDE), F32),
            pltpu.VMEM((count * HEADS, 128), F32), pltpu.VMEM((count * HEADS, D), F32),
            pltpu.VMEM((4 * count, 128), F32), pltpu.VMEM(half, BF), pltpu.VMEM(half, BF),
            pltpu.VMEM(wcls, BF), pltpu.VMEM(head.shape, BF),
            pltpu.VMEM((everyone, D), F32), pltpu.VMEM((D, D), F32), pltpu.VMEM((wide, D), F32),
            pltpu.VMEM((wide, D), F32),
            pltpu.VMEM((4 * everyone, 128), F32), pltpu.VMEM((4 * everyone, 128), BF),
            dma((2, n_dp)), dma((2, n_mp)), dma((1,)),
        ]
        + spread_scratch(n_dp, n_mp) * 3,
        compiler_params=remote_params(7),
        name="feed",
    )(
        mid, cols, bias_row, base, stat, vec, wmlp, cls_rows, up_rows, down_rows, head
    )


def run_feed_back(n_dp, left, right, gv, local_rows, patch, mid, raw, act, slope, vec, wmlp):
    count = mid.shape[0]
    wide = act.shape[2]
    feed = (wmlp.shape[0], pad_rows(wmlp.shape[1] + D // wmlp.shape[0], n_dp), D)
    return pl.pallas_call(
        feed_back_kernel,
        grid=(count,),
        in_specs=[
            per_image(2 * HEADS, WIDE), per_image(2 * HEADS, D), constant(D, D), constant(16, D),
            per_image(P_SIZE, D), per_image(P_SIZE, D), per_image(P_SIZE, D),
            per_image(P_SIZE, wide), per_image(P_SIZE, wide), constant(*vec.shape),
            constant(*wmlp.shape),
        ],
        out_specs=[per_image(P_SIZE, D), constant(*feed), constant(16, D)],
        out_shape=[shaped(count, P_SIZE, D), shaped(*feed, dtype=BF), shaped(16, D)],
        scratch_shapes=[pltpu.VMEM(wmlp.shape, F32)],
        compiler_params=params(),
        name="feed_back",
    )(left, right, gv, local_rows, patch, mid, raw, act, slope, vec, wmlp)


def run_self_back(
    n_dp, n_mp, dmid, pixels, embed, q, k, v, prob, post, ho, raw, vec, wattn, t1row, t2row, gfeed,
    rows_feed,
):
    count = dmid.shape[0]
    rows_a, rows_b = halves(gfeed.shape[1], n_dp)
    blocks = (n_mp, pad_rows(wattn.shape[1], n_dp), D)
    commons = (n_mp, table_rows(n_dp, n_mp), D)
    rows = blocks[1] + rows_a + rows_b
    n_lo = 2 if n_dp < 16 else 4
    return pl.pallas_call(
        functools.partial(self_back_kernel, n_dp, n_mp),
        grid=(count,),
        in_specs=[
            per_image(P_SIZE, D), constant(*pixels.shape), per_image(P_SIZE, D),
            per_image(P_SIZE, D), per_image(P_SIZE, D), per_image(P_SIZE, D),
            per_image(P_SIZE, HEADS * PAD), per_image(HEADS * PAD, D), per_image(P_SIZE, D),
            per_image(P_SIZE, D), constant(*vec.shape), constant(*wattn.shape), constant(HEADS, D),
            constant(HEADS, D), constant(*gfeed.shape), constant(16, D),
        ],
        out_specs=[
            ANY, ANY, constant(8, 128),
        ],
        out_shape=[
            shaped(rows, D, dtype=BF), shaped(*commons, dtype=BF), shaped(8, 128),
        ],
        scratch_shapes=[
            pltpu.VMEM(wattn.shape, F32), pltpu.VMEM((P_SIZE, D), F32), pltpu.VMEM((24, D), F32),
            pltpu.VMEM((count, P_SIZE, D), F32), pltpu.VMEM((P_SIZE, count, D), F32),
            pltpu.VMEM((HEADS * PAD, D), BF), pltpu.VMEM((HEADS * PAD, D), BF),
            pltpu.VMEM((P_SIZE, HEADS * PAD), F32),
            pltpu.VMEM(blocks, BF), pltpu.VMEM(commons, BF), pltpu.VMEM((rows, D), BF),
            pltpu.VMEM(commons, BF), pltpu.SemaphoreType.DMA((2,)),
        ]
        + sum_scratch(n_dp, n_mp, rows_a, True)
        + sum_scratch(n_dp, n_mp, rows_b, False)
        + reduce_scratch(
            n_dp, n_mp, blocks[1], commons[1], (rows_a // n_lo, rows_b // n_lo)
        ),
        compiler_params=pltpu.CompilerParams(
            vmem_limit_bytes=VMEM_LIMIT, dimension_semantics=("arbitrary",), collective_id=5,
            has_side_effects=True,
        ),
        name="self_back",
    )(dmid, pixels, embed, q, k, v, prob, post, ho, raw, vec, wattn, t1row, t2row, gfeed, rows_feed)


def share_cards(n_dp, n_mp, card, out, slots, dp_sem, mp_sem):
    dp = lax.axis_index("dp")
    mp = lax.axis_index("mp")
    rows = card.shape[0]
    others_dp = [(lax.rem(dp + step, n_dp), mp) for step in range(1, n_dp)]
    others_mp = [(dp, lax.rem(mp + step, n_mp)) for step in range(1, n_mp)]
    own = tile_rows(slots, (mp * n_dp + dp) * rows, rows)
    slots[pl.ds(pl.multiple_of((mp * n_dp + dp) * rows, 16), rows), :] = card[...].astype(BF)
    sends = [
        remote(own, own, dp_sem.at[0, step], dp_sem.at[1, step], others_dp[step - 1])
        for step in range(1, n_dp)
    ]
    for copy in sends:
        copy.start()
    for step in range(1, n_dp):
        source = lax.rem(dp + n_dp - step, n_dp)
        theirs = tile_rows(slots, (mp * n_dp + source) * rows, rows)
        remote(own, theirs, dp_sem.at[0, step], dp_sem.at[1, step], (source, mp)).wait_recv()
    slab = tile_rows(slots, mp * n_dp * rows, n_dp * rows)
    for step in range(1, n_mp):
        sends.append(
            remote(slab, slab, mp_sem.at[0, step], mp_sem.at[1, step], others_mp[step - 1])
        )
        sends[-1].start()
    for step in range(1, n_mp):
        source = lax.rem(mp + n_mp - step, n_mp)
        theirs = tile_rows(slots, source * n_dp * rows, n_dp * rows)
        remote(slab, theirs, mp_sem.at[0, step], mp_sem.at[1, step], (dp, source)).wait_recv()
    for i in range(n_dp):
        for j in range(n_mp):
            to, source = (i * n_mp + j) * rows, (j * n_dp + i) * rows
            out[to : to + rows, :] = slots[source : source + rows, :].astype(F32)
    for copy in sends:
        copy.wait_send()


def start_part(
    n_dp, n_mp, group, attn_in, attn_out, mlp_in, mlp_out, pixels, tables, vec, mix, mask,
    counts, labels, pairs,
    out, mlp_rows, cls_rows, up_rows, down_rows, embed_far, head_out, t1_out, t2_out, cols_out, bias_out, base_out,
    embed_out, head_rows, wide_up, wide_down, shard, wide_in, wide_out, patch_rows, pos_rows, by_patch, near_send, near_recv, far_send, far_recv, load_sem,
):
    dp = lax.axis_index("dp")
    mp = lax.axis_index("mp")
    n_y = n_mp // 2
    y = lax.div(mp, 2)
    core = lax.rem(mp, 2)
    sibling = (dp, y * 2 + 1 - core)
    load_patch = pltpu.make_async_copy(tables.at[pl.ds(0, PIX)], patch_rows, load_sem.at[0])
    load_pos = pltpu.make_async_copy(tables.at[pl.ds(PIX, 200)], pos_rows, load_sem.at[1])
    load_in = pltpu.make_async_copy(attn_in, wide_in, load_sem.at[2])
    load_out = pltpu.make_async_copy(attn_out, wide_out, load_sem.at[3])
    load_up = pltpu.make_async_copy(mlp_in, wide_up, load_sem.at[5])
    load_down = pltpu.make_async_copy(mlp_out, wide_down, load_sem.at[6])
    load_in.start()
    load_out.start()
    load_patch.start()
    load_pos.start()
    classes = head_out.shape[0]
    load_head = pltpu.make_async_copy(
        tables.at[pl.ds(PIX + P_SIZE - 4, classes + 4)], head_rows, load_sem.at[4]
    )
    load_up.start()
    load_down.start()
    load_head.start()
    barrier = pltpu.get_barrier_semaphore()
    pl.semaphore_signal(barrier, inc=1, device_id=sibling, device_id_type=MESH)
    for step in range(1, n_y):
        pl.semaphore_signal(
            barrier, inc=1, device_id=(dp, lax.rem(y + step, n_y) * 2 + core), device_id_type=MESH
        )
    third = attn_in.shape[1]
    load_in.wait()
    load_out.wait()
    shard[:third, :] = wide_in[0].astype(BF)
    shard[third:, :] = wide_out[0].astype(BF)
    pl.semaphore_wait(barrier, n_y)
    far = [
        remote(
            shard, out.at[mp], far_send.at[step], far_recv.at[step],
            (dp, lax.rem(y + step, n_y) * 2 + core),
        )
        for step in range(1, n_y)
    ]
    for copy in far:
        copy.start()
    near = [remote(shard, out.at[mp], near_send.at[0], near_recv.at[0], sibling)]
    near[0].start()
    out[pl.ds(mp, 1)] = shard[...][None]

    cls_rows[:third, :] = wide_in[1].astype(BF)
    cls_rows[third:, :] = wide_out[1].astype(BF)
    hidden = mlp_rows.shape[0] // 2
    load_up.wait()
    load_down.wait()
    mlp_rows[:hidden, :] = wide_up[0].T.astype(BF)
    mlp_rows[hidden:, :] = wide_down[0].astype(BF)
    up_rows[...] = wide_up[1].T.astype(BF)
    down_rows[...] = wide_down[1].astype(BF)

    images = mask.shape[0]
    lane = lax.broadcasted_iota(jnp.int32, (1, 128), 1)
    keep = (mask[...] > 0).astype(F32)
    bias = (1.0 - keep) * MASKED
    count = counts[0]
    okays = []
    bias_out[...] = jnp.full(bias_out.shape, MASKED, F32)
    for n in range(images):
        okays.append((jnp.full((1, 1), mp * images + n, jnp.int32) >= group - count).astype(F32))
        bias_out[:, n * WIDE : n * WIDE + P_SIZE] = bias[n : n + 1, :]
        tokens = jnp.sum(keep[n : n + 1, :], 1, keepdims=True) * okays[n]
        entries = (
            lax.div(labels[n], 32), lax.rem(labels[n], 32), lax.div(pairs[n], 32),
            lax.rem(pairs[n], 32), count,
        )
        line = jnp.where(lane == len(entries), tokens, 0.0)
        for place, entry in enumerate(entries):
            line = jnp.where(lane == place, entry.astype(F32), line)
        base_out[n : n + 1, :] = line
    cols_out[...] = jnp.concatenate([bias, keep * jnp.concatenate(okays, 0)], 0).T
    heads = head_mask()
    exact = functools.partial(
        lax.dot_general, preferred_element_type=F32, precision=lax.Precision.HIGHEST
    )
    t1_out[...] = exact(mix[0], heads, (((1,), (0,)), ((), ()))) * SCALE
    t2_out[...] = exact(mix[1], heads, (((0,), (0,)), ((), ())))

    load_patch.wait()
    wp = patch_rows[...].astype(BF)
    local = embed_out.shape[0]
    half = P_SIZE // 2
    for place in range(2):
        rows = slice(place * half * local, (place + 1) * half * local)
        by_patch[place * half : (place + 1) * half] = nn(pixels[rows, :], wp).reshape(half, local, D)

    for step in range(1, n_y):
        source = lax.rem(y + n_y - step, n_y) * 2
        slot = source + core
        remote(
            shard, out.at[slot], far_send.at[step], far_recv.at[step], (dp, slot)
        ).wait_recv()
        copy = remote(
            out.at[slot], out.at[slot], near_send.at[step], near_recv.at[step], sibling
        )
        copy.start()
        near.append(copy)
    load_pos.wait()
    offset = pos_rows[:P_SIZE, :] + vec[16:17, :]
    for n in range(local):
        embed_out[n] = by_patch[:, n, :] + offset
    save_embed = pltpu.make_async_copy(embed_out, embed_far, load_sem.at[7])
    save_embed.start()
    load_head.wait()
    head_out[...] = head_rows[4:, :].astype(BF)
    save_embed.wait()
    for copy in far:
        copy.wait_send()
    for step in range(n_y):
        slot = lax.rem(y + n_y - step, n_y) * 2 + 1 - core
        near[step].wait_send()
        remote(
            out.at[slot], out.at[slot], near_send.at[step], near_recv.at[step], sibling
        ).wait_recv()


def reduce_rows(
    p, blocks, commons, chunk_a, chunk_b,
    block_out, shared_out, square_out,
    squares, attn_run, run_a, run_b, sem_a, sem_b, high_a, high_b, high_sem, low_sem, square_sem,
    *sum_buffers,
):
    n_mp = p.n_mp
    attn = ShardSum(p, blocks, 0, True, *sum_buffers[:SUM_BUFFERS])
    table = TableSum(p, commons, shared_out, *sum_buffers[SUM_BUFFERS:])
    rows_a = blocks.shape[1]
    rows_feed = p.n_lo * run_a.shape[0]
    hand_a = HandLow(p, block_out, rows_a, rows_feed, sem_a)
    hand_b = HandLow(p, block_out, rows_a + rows_feed, p.n_lo * run_b.shape[0], sem_b)
    wide_a = HandHigh(p, run_a, high_a)
    wide_b = HandHigh(p, run_b, high_b)
    hand_high = HandHigh(p, attn_run, high_sem)
    hand_low = HandLow(p, block_out, 0, rows_a, low_sem)

    attn.start()
    table.start()
    wide_a.start(chunk_a)
    wide_b.start(chunk_b)
    attn.second()
    table.near_to_low()
    table.low_to_high()
    attn.third()
    wide_a.arrive()
    hand_a.start(run_a[...])
    wide_b.arrive()
    hand_b.start(run_b[...])
    table.high_to_far()
    attn.fourth()
    table.turn()
    table.far_to_high()
    hand_high.start(attn.finish())
    table.high_to_low()
    hand_high.arrive()
    hand_low.start(attn_run[...])
    table.low_to_near()
    sends = []

    for item in (hand_a, hand_b, hand_low):
        item.arrive()
    sums = block_out[...].astype(F32)
    sums = colsum(sums * sums)
    squares[pl.ds(p.mp, 1)] = jnp.broadcast_to(
        sums[:, 0:128] + sums[:, 128:256] + sums[:, 256:384], (8, 128)
    )[None]

    for step in range(1, p.n_y):
        sends.append(
            remote(
                squares.at[p.mp], squares.at[p.mp], square_sem.at[0, step],
                square_sem.at[1, step], (p.dp, p.along_y(step) * 2 + p.core),
            )
        )
        sends[-1].start()
    for step in range(1, p.n_y):
        source = p.along_y(p.n_y - step) * 2 + p.core
        remote(
            squares.at[p.mp], squares.at[source], square_sem.at[0, step], square_sem.at[1, step],
            (p.dp, source),
        ).wait_recv()
    mine = squares[pl.ds(p.core, 1)]
    for y in range(1, p.n_y):
        mine += squares[pl.ds(2 * y + p.core, 1)]
    squares[pl.ds(n_mp + p.core, 1)] = mine
    sends.append(
        remote(
            squares.at[n_mp + p.core], squares.at[n_mp + p.core], square_sem.at[0, 0],
            square_sem.at[1, 0], p.sibling,
        )
    )
    sends[-1].start()
    table.finish()
    remote(
        squares.at[n_mp + p.core], squares.at[n_mp + 1 - p.core], square_sem.at[0, 0],
        square_sem.at[1, 0], p.sibling,
    ).wait_recv()
    square_out[...] = squares[n_mp] + squares[n_mp + 1]
    for copy in sends:
        copy.wait_send()
    for item in (attn, wide_a, wide_b, hand_a, hand_b, hand_high, hand_low):
        item.wait_sends()


def reduce_scratch(n_dp, n_mp, rows_a, wide, feed):
    assert wide == 256
    n_lo = 2 if n_dp < 16 else 4
    n_hi = n_dp // n_lo
    dma = pltpu.SemaphoreType.DMA
    return (
        [
            pltpu.VMEM((n_mp + 2, 8, 128), F32), pltpu.VMEM((rows_a // n_lo, D), BF),
            pltpu.VMEM((feed[0], D), BF), pltpu.VMEM((feed[1], D), BF),
            dma((2, n_lo)), dma((2, n_lo)), dma((2, n_hi)), dma((2, n_hi)), dma((2, n_hi)),
            dma((2, n_lo)), dma((2, n_mp)),
        ]
        + sum_scratch(n_dp, n_mp, rows_a, True)
        + table_scratch(n_dp, n_mp, wide)
    )


def root(values):
    return values * lax.rsqrt(values)


def adam_parts(gradient, mean, square, factor):
    clipped = gradient * factor
    mean_new = BETA_ONE * mean + (1.0 - BETA_ONE) * clipped
    square_new = BETA_TWO * square + (1.0 - BETA_TWO) * clipped * clipped
    direction = (
        mean_new
        * (1.0 / (1.0 - BETA_ONE**STEP))
        / (root(square_new * (1.0 / (1.0 - BETA_TWO**STEP))) + ADAM_EPS)
    )
    return (mean_new, square_new, direction)


def fold(values):
    squares = (values * values).reshape(values.shape[0] // 8, 8, values.shape[1]).sum(0)
    width = values.shape[1]
    if width % 128:
        return jnp.broadcast_to(jnp.sum(squares, 1, keepdims=True), (8, 128)) * (1.0 / 128)
    return sum(squares[:, i : i + 128] for i in range(0, width, 128))


def total(values):
    return jnp.sum(jnp.sum(values, 0, keepdims=True), 1, keepdims=True)


def moment_sweep(factor, grad, w, m, s, u, rows):
    chunk = 32 if rows % 32 == 0 else 16

    def step(i, kept):
        at = pl.ds(pl.multiple_of(i * chunk, chunk), chunk)
        weight = w[at, :]
        mean, second, direction = adam_parts(grad(i, chunk), m[at, :], s[at, :], factor)
        m[at, :] = mean
        s[at, :] = second
        update = direction + DECAY * weight
        u[at, :] = update.astype(u.dtype)
        return (kept[0] + fold(weight), kept[1] + fold(update))

    zero = jnp.zeros((8, 128), F32)
    return lax.fori_loop(0, rows // chunk, step, (zero, zero))


def rows_from(ref, first):
    def read(i, chunk):
        at = pl.ds(pl.multiple_of(first + i * chunk, 16), chunk)
        return ref[at, :].astype(F32)

    return read


def moment_kernel(
    n_dp, block_sq, gout1, rows1, stat, aux, vec, vec_mean, vec_square, mix, mix_mean, mix_square,
    *rest,
):
    large, rest = rest[:5], rest[5:]
    state = rest[:12]
    outs = rest[12:24]
    (
        vec_out, vec_mean_out, vec_square_out, mix_out, mix_mean_out, mix_square_out,
        misc_out, sums_out,
    ) = rest[24:32]
    held = rest[32:44]
    updates = rest[44:48]
    grad_q, grad_k, grad_flip, load_sem, save_sem = rest[48:53]
    large_here = rest[53:]
    first_loads = [
        pltpu.make_async_copy(large[i], large_here[i], load_sem.at[12 + i]) for i in range(5)
    ]
    loads = [pltpu.make_async_copy(state[i], held[i], load_sem.at[i]) for i in range(12)]
    for copy in first_loads + loads:
        copy.start()
    for copy in first_loads:
        copy.wait()
    block, shared, wcls, gup1, gdown1 = large_here
    mp = lax.axis_index("mp")
    hs = state[3].shape[1]
    fs = state[9].shape[1]
    feed = pad_rows(4 * hs, n_dp)

    rows2 = shared[PIX + 208 : PIX + 224, :].astype(F32)
    rows3 = shared[PIX + 224 : PIX + 256, :].astype(F32)
    token = aux[8:9, :]
    wq = part(wcls, 0, hs)
    wk = part(wcls, hs, hs).astype(F32)
    query = nt(wq, aux[8:16, :].astype(BF))[:, 0:1].astype(BF).astype(F32)
    dkeys = jnp.concatenate(
        [jnp.broadcast_to(rows2[8 + h : 9 + h, :], (HEAD, D)) for h in range(HEADS)], 0
    )
    dquery = SCALE * jnp.sum(wk * dkeys, 1, keepdims=True)
    gq = dquery * token
    gk = (SCALE * query) * dkeys
    grad_q[...] = gq
    grad_k[...] = gk
    dtoken = rows2[6:7, :] + colsum(dquery * wq.astype(F32))
    unit, inverse = normalize(jnp.broadcast_to(vec[17:18, :], (8, D)))
    dcls = normalize_back(unit, inverse, vec[8:9, :], jnp.broadcast_to(dtoken, (8, D)))[0:1, :]
    dgain = rows2[4:5, :] + dtoken * unit[0:1, :]
    last = rows1[...]
    positions = shared[PIX : PIX + 208, :].astype(F32)
    grad_vec = jnp.concatenate(
        [
            rows3[0:4, :], rows2[0:4, :], dgain, rows2[5:6, :] + dtoken, last[2:8, :],
            colsum(positions), last[8:9, :] + dcls, last[9:11, :],
        ],
        0,
    )
    mask = head_mask()
    exact = functools.partial(
        lax.dot_general, dimension_numbers=(((1,), (1,)), ((), ())),
        preferred_element_type=F32, precision=lax.Precision.HIGHEST,
    )
    grad_mix = (exact(rows3[8:16, :], mask) * SCALE, exact(mask, rows3[16:24, :]))

    square = total(block_sq[0:1, :]) + total(stat[1:2, :]) + total(colsum(gq * gq + gk * gk))
    square += total(grad_vec * grad_vec)
    square += total(grad_mix[0] * grad_mix[0]) + total(grad_mix[1] * grad_mix[1])

    def square_rows(i, kept):
        rows = shared[pl.ds(pl.multiple_of(i * 16, 16), 16), :].astype(F32)
        return kept + fold(rows)

    square += total(lax.fori_loop(0, (PIX + 208) // 16, square_rows, jnp.zeros((8, 128), F32)))
    norm = jnp.sqrt(square)
    factor = CLIP / jnp.maximum(norm, CLIP)

    mean, second, direction = adam_parts(grad_vec, vec_mean[...], vec_square[...], factor)
    vec_mean_out[...] = mean
    vec_square_out[...] = second
    vec_out[...] = vec[...] - RATE_VECTOR * direction
    misc = []
    weight_sums = []
    for b in range(2):
        mean, second, direction = adam_parts(grad_mix[b], mix_mean[b], mix_square[b], factor)
        mix_mean_out[b] = mean
        mix_square_out[b] = second
        update = direction + DECAY * mix[b]
        weight_sq = total(mix[b] * mix[b])
        update_sq = total(update * update)
        mix_out[b] = mix[b] - RATE * jnp.sqrt(weight_sq / (update_sq + 1e-12)) * update
        weight_sums.append(weight_sq)
        misc.append(update_sq)

    def sweep(grad, w, m, s, u, rows):
        return moment_sweep(factor, grad, w, m, s, u, rows)

    saves = []

    def save(i, source):
        saves.append(pltpu.make_async_copy(source, outs[i], save_sem.at[i]))
        saves[-1].start()

    sums = []
    own_h = pl.multiple_of(mp * hs, hs)
    for kind in range(4):
        for copy in loads[3 * kind : 3 * kind + 3]:
            copy.wait()
        w, m, s = held[3 * kind : 3 * kind + 3]
        u = updates[kind]
        for b in range(2):
            views = (w.at[b], m.at[b], s.at[b], u.at[b])
            if kind == 0 and b == 0:
                sums.append(sweep(rows_from(block, 0), *views, 3 * hs))
            elif kind == 0:
                pieces = []
                for third, source in enumerate(
                    (
                        rows_from(grad_q, own_h),
                        rows_from(grad_k, own_h),
                        rows_from(block, feed + 2 * fs),
                    )
                ):
                    pieces.append(
                        sweep(
                            source, *(view.at[pl.ds(third * hs, hs)] for view in views), hs
                        )
                    )
                sums.append(
                    tuple(pieces[0][i] + pieces[1][i] + pieces[2][i] for i in range(2))
                )
            elif kind == 1:
                source = rows_from(gout1, 0) if b else rows_from(block, 3 * hs)
                sums.append(sweep(source, *views, hs))
            elif kind == 2:
                if b:
                    grad_flip[...] = gup1[...].T
                else:
                    grad_flip[...] = block[feed : feed + fs, :].astype(F32).T
                sums.append(sweep(rows_from(grad_flip, 0), *views, D))
            else:
                source = rows_from(gdown1, 0) if b else rows_from(block, feed + fs)
                sums.append(sweep(source, *views, fs))
        save(3 * kind, u)
        save(3 * kind + 1, m)
        save(3 * kind + 2, s)
    for place, pair in enumerate(sums):
        sums_out[place : place + 1, :] = colsum(pair[1])
        sums_out[8 + place : 9 + place, :] = colsum(pair[0])

    lane = lax.broadcasted_iota(jnp.int32, (1, 128), 1)
    misc_out[0:1, :] = jnp.broadcast_to(norm, (1, 128))
    weight_line = jnp.zeros((1, 128), F32)
    update_line = jnp.zeros((1, 128), F32)
    for b in range(2):
        weight_line = jnp.where(lane == 11 + b, weight_sums[b], weight_line)
        update_line = jnp.where(lane == 11 + b, misc[b], update_line)
    misc_out[1:2, :] = weight_line
    misc_out[2:3, :] = update_line
    misc_out[3:8, :] = jnp.zeros((5, 128), F32)
    for copy in saves:
        copy.wait()


def table_kernel(misc, shared, ghead, *rest):
    state, outs, misc_out = rest[:3], rest[3:6], rest[6]
    w, m, s, table_update, load_sem, save_sem = rest[7:]
    rows_all = w.shape[0]
    edge = PIX + P_SIZE - 4
    body = (rows_all - edge - 16) // 64 * 32
    middle = edge + 16 + body
    cuts = (0, PIX // 2, PIX, middle, rows_all)
    slabs = [pl.ds(low, high - low) for low, high in zip(cuts, cuts[1:])]
    loads = [
        [
            pltpu.make_async_copy(state[i].at[at], (w, m, s)[i].at[at], load_sem.at[i, place])
            for i in range(3)
        ]
        for place, at in enumerate(slabs)
    ]
    for group in loads:
        for copy in group:
            copy.start()
    factor = CLIP / jnp.maximum(misc[0:1, 0:1], CLIP)
    saves = []

    def arrive(place):
        for copy in loads[place]:
            copy.wait()

    def save(i, place):
        at = slabs[place]
        saves.append(
            pltpu.make_async_copy((w, m, s)[i].at[at], outs[i].at[at], save_sem.at[i, place])
        )
        saves[-1].start()

    def slab(first, count, grad):
        at = slice(first, first + count)
        weight = w[at, :]
        mean, second, direction = adam_parts(grad, m[at, :], s[at, :], factor)
        m[at, :] = mean
        s[at, :] = second
        update = direction + DECAY * weight
        table_update[at, :] = update
        return weight, update

    def run(first, count, source, offset):
        def at(ref, start):
            return ref.at[pl.ds(start, count)]

        return moment_sweep(
            factor, rows_from(source, offset), at(w, first), at(m, first), at(s, first),
            at(table_update, first), count,
        )

    def renew(first, count, rate):
        def step(i, _):
            at = pl.ds(pl.multiple_of(first + i * 32, 16), 32)
            w[at, :] = w[at, :] - rate * table_update[at, :]
            return 0

        lax.fori_loop(0, count // 32, step, 0)

    def rate_of(weight_sq, update_sq):
        return RATE * jnp.sqrt(weight_sq / (update_sq + 1e-12))

    def masked(values, mask):
        return total(jnp.where(mask, values * values, 0.0))

    arrive(0)
    first_half = run(0, PIX // 2, shared, 0)
    save(1, 0)
    save(2, 0)
    arrive(1)
    second_half = run(PIX // 2, PIX // 2, shared, PIX // 2)
    save(1, 1)
    save(2, 1)
    sq_w = [total(first_half[0] + second_half[0])]
    sq_u = [total(first_half[1] + second_half[1])]
    rates = [rate_of(sq_w[0], sq_u[0])]
    renew(0, PIX, rates[0])
    save(0, 0)
    save(0, 1)
    arrive(2)
    place_rows = run(PIX, P_SIZE - 4, shared, PIX)
    tile = lax.broadcasted_iota(jnp.int32, (16, 1), 0) < 4
    weight, update = slab(edge, 16, shared[edge : edge + 16, :].astype(F32) + ghead[0:16, :])
    heads = run(edge + 16, body, ghead, 16)
    save(1, 2)
    save(2, 2)
    arrive(3)
    rest_rows = (rows_all - middle) // 32 * 32
    more_heads = run(middle, rest_rows, ghead, 16 + body)
    left = middle + rest_rows
    tail_weight, tail_update = slab(
        left, rows_all - left, ghead[16 + left - edge - 16 : 16 + rows_all - edge - 16, :]
    )
    save(1, 3)
    save(2, 3)
    sq_w += [
        total(place_rows[0]) + masked(weight, tile),
        total(heads[0] + more_heads[0]) + masked(weight, ~tile) + total(tail_weight * tail_weight),
    ]
    sq_u += [
        total(place_rows[1]) + masked(update, tile),
        total(heads[1] + more_heads[1]) + masked(update, ~tile) + total(tail_update * tail_update),
    ]
    rates += [rate_of(sq_w[i], sq_u[i]) for i in (1, 2)]
    renew(PIX, P_SIZE - 4, rates[1])
    w[edge : edge + 16, :] = weight - jnp.where(tile, rates[1], rates[2]) * update
    renew(edge + 16, body, rates[2])
    save(0, 2)
    renew(middle, rest_rows, rates[2])
    w[left:rows_all, :] = tail_weight - rates[2] * tail_update
    save(0, 3)

    lane = lax.broadcasted_iota(jnp.int32, (1, 128), 1)
    weight_line = misc[1:2, :]
    update_line = misc[2:3, :]
    for place in range(3):
        weight_line = jnp.where(lane == 8 + place, sq_w[place], weight_line)
        update_line = jnp.where(lane == 8 + place, sq_u[place], update_line)
    misc_out[...] = misc[...]
    misc_out[1:2, :] = weight_line
    misc_out[2:3, :] = update_line
    for copy in saves:
        copy.wait()


def run_moments(n_dp, grads, smalls, large, state):
    outs = [
        jax.ShapeDtypeStruct(item.shape, F32 if i % 3 else BF) for i, item in enumerate(state)
    ]
    fs = state[9].shape[1]
    dma = pltpu.SemaphoreType.DMA
    return pl.pallas_call(
        functools.partial(moment_kernel, n_dp),
        in_specs=[WHOLE] * (len(grads) + len(smalls)) + [ANY] * 17,
        out_specs=[ANY] * 12 + [WHOLE] * 8,
        out_shape=outs
        + [jax.ShapeDtypeStruct(item.shape, F32) for item in smalls]
        + [shaped(8, 128), shaped(16, 128)],
        scratch_shapes=[pltpu.VMEM(item.shape, F32) for item in state]
        + [pltpu.VMEM(state[3 * kind].shape, BF) for kind in range(4)]
        + [
            pltpu.VMEM((D, D), F32), pltpu.VMEM((D, D), F32), pltpu.VMEM((D, fs), F32),
            dma((17,)), dma((12,)),
        ]
        + [pltpu.VMEM(item.shape, item.dtype) for item in large],
        compiler_params=pltpu.CompilerParams(vmem_limit_bytes=VMEM_LIMIT),
        name="moments",
    )(*grads, *smalls, *large, *state)


def run_tables(misc, shared, ghead, state):
    shape = state[0].shape
    dma = pltpu.SemaphoreType.DMA
    return pl.pallas_call(
        table_kernel,
        in_specs=[WHOLE] * 3 + [ANY] * 3,
        out_specs=[ANY] * 3 + [WHOLE],
        out_shape=[shaped(*shape)] * 3 + [shaped(8, 128)],
        scratch_shapes=[pltpu.VMEM(shape, F32)] * 4 + [dma((3, 4)), dma((3, 4))],
        cost_estimate=pl.CostEstimate(
            flops=40 * shape[0] * shape[1], bytes_accessed=28 * shape[0] * shape[1],
            transcendentals=2 * shape[0] * shape[1],
        ),
        compiler_params=pltpu.CompilerParams(vmem_limit_bytes=VMEM_LIMIT),
        name="tables",
    )(misc, shared, ghead, *state)


def renew_kernel(n_mp, misc, stat, *rest):
    theirs, rest = rest[:n_mp], rest[n_mp:]
    weights, updates = rest[:4], rest[4:8]
    new, copies = rest[8:12], rest[12:16]
    norms, norm_out, stat_out = rest[16:19]
    here, changes, lows = rest[19:23], rest[23:27], rest[27:31]
    slots, load_sem, save_sem = rest[31:]
    loads = [
        (
            pltpu.make_async_copy(weights[kind], here[kind], load_sem.at[0, kind]),
            pltpu.make_async_copy(updates[kind], changes[kind], load_sem.at[1, kind]),
        )
        for kind in range(4)
    ]
    for pair in loads[::-1]:
        for copy in pair:
            copy.start()
    mp = lax.axis_index("mp")
    for step in range(n_mp):
        slots[pl.ds(lax.rem(mp + n_mp - step, n_mp), 1)] = theirs[step][...][None]
    sums = jnp.sum(slots[...], 0)
    rates = []
    lane = lax.broadcasted_iota(jnp.int32, (1, 128), 1)
    weight_line, update_line = misc[1:2, :], misc[2:3, :]
    for place in range(8):
        update_sq = total(sums[place : place + 1, :])
        weight_sq = total(sums[8 + place : 9 + place, :])
        rates.append(RATE * jnp.sqrt(weight_sq / (update_sq + 1e-12)))
        weight_line = jnp.where(lane == place, weight_sq, weight_line)
        update_line = jnp.where(lane == place, update_sq, update_line)
    norms[...] = jnp.sqrt(jnp.concatenate([weight_line, update_line], 0))[:, :13]
    norm_out[...] = misc[0:1, 0:1]
    stat_out[...] = stat[0:1, :12]
    saves = []
    for kind in (3, 2, 1, 0):
        w, u, low = here[kind], changes[kind], lows[kind]
        rows = w.shape[1]
        chunk = 32 if rows % 32 == 0 else 16
        for copy in loads[kind]:
            copy.wait()
        for b in range(2):
            rate = rates[2 * kind + b]

            def step(i, _, b=b, w=w, u=u, low=low, rate=rate, chunk=chunk):
                at = pl.ds(pl.multiple_of(i * chunk, chunk), chunk)
                values = w[b, at, :] - rate * u[b, at, :].astype(F32)
                w[b, at, :] = values
                low[b, at, :] = values.astype(BF)
                return 0

            lax.fori_loop(0, rows // chunk, step, 0)
        saves.append(pltpu.make_async_copy(w, new[kind], save_sem.at[0, kind]))
        saves.append(pltpu.make_async_copy(low, copies[kind], save_sem.at[1, kind]))
        for copy in saves[-2:]:
            copy.start()
    for copy in saves:
        copy.wait()


def run_renew(n_mp, misc, stat, sums, weights, updates):
    dma = pltpu.SemaphoreType.DMA
    return pl.pallas_call(
        functools.partial(renew_kernel, n_mp),
        in_specs=[WHOLE] * (2 + n_mp) + [ANY] * 8,
        out_specs=[ANY] * 8 + [WHOLE] * 3,
        out_shape=[shaped(*item.shape) for item in weights]
        + [shaped(*item.shape, dtype=BF) for item in weights]
        + [shaped(2, 13), shaped(1, 1), shaped(1, 12)],
        scratch_shapes=[pltpu.VMEM(item.shape, F32) for item in weights]
        + [pltpu.VMEM(item.shape, BF) for item in weights] * 2
        + [pltpu.VMEM((n_mp, 16, 128), F32), dma((2, 4)), dma((2, 4))],
        compiler_params=pltpu.CompilerParams(vmem_limit_bytes=VMEM_LIMIT),
        name="renew",
    )(misc, stat, *sums, *weights, *updates)


def shards(
    pixels,
    token_mask,
    counts,
    labels,
    pairs,
    attn_in,
    attn_in_mean,
    attn_in_square,
    attn_out,
    attn_out_mean,
    attn_out_square,
    mlp_in,
    mlp_in_mean,
    mlp_in_square,
    mlp_out,
    mlp_out_mean,
    mlp_out_square,
    tables,
    tables_mean,
    tables_square,
    vectors,
    vectors_mean,
    vectors_square,
    talking,
    talking_mean,
    talking_square,
):
    local = pixels.shape[0]
    group = token_mask.shape[0]
    place_mp = lax.axis_index("mp")
    n_mp = lax.axis_size("mp")
    n_dp = lax.axis_size("dp")
    hs = attn_in.shape[3]
    fs = mlp_in.shape[2]

    def as_rows(item):
        return item.transpose(0, 2, 3, 1).reshape(2, 3 * hs, D)

    def from_rows(item):
        return item.reshape(2, 3, hs, D).transpose(0, 3, 1, 2)

    attn_in, attn_in_mean, attn_in_square = map(as_rows, (attn_in, attn_in_mean, attn_in_square))
    pixel_rows = pixels.transpose(1, 0, 2).reshape(P_SIZE * local, PIX)
    mask = lax.dynamic_slice_in_dim(token_mask, place_mp * local, local, 0)
    (
        q, k, v, prob, post, ho, raw0, middle, stat_a, wmlp, wattn, embed, cls_rows, up_rows,
        down_rows, head, t1row, t2row, cols, bias_row, base,
    ) = run_self_attend(
        n_dp, n_mp, group, attn_in, attn_out, mlp_in, mlp_out, pixel_rows, tables, vectors,
        talking, mask, counts, labels, pairs,
    )
    (
        patches, act, slope, raw1, aux, wcls, left, right, gv, local_rows, gout1, gup1, gdown1,
        ghead, rows1, stat,
    ) = run_feed(
        n_dp, n_mp, group, middle, cols, bias_row, base, stat_a, vectors, wmlp, cls_rows, up_rows,
        down_rows, head,
    )
    dmid, gfeed, rows2 = run_feed_back(
        n_dp, left, right, gv, local_rows, patches, middle, raw1, act, slope, vectors, wmlp
    )
    block, shared, block_sq = run_self_back(
        n_dp, n_mp, dmid, pixel_rows, embed, q, k, v, prob, post, ho, raw0, vectors, wattn,
        t1row, t2row, gfeed, rows2,
    )

    shared = shared.reshape(-1, D)
    state = (
        attn_in, attn_in_mean, attn_in_square, attn_out, attn_out_mean, attn_out_square,
        mlp_in, mlp_in_mean, mlp_in_square, mlp_out, mlp_out_mean, mlp_out_square,
    )
    smalls = (vectors, vectors_mean, vectors_square, talking, talking_mean, talking_square)
    moved = run_moments(
        n_dp, (block_sq, gout1, rows1, stat, aux), smalls, (block, shared, wcls, gup1, gdown1),
        state,
    )
    sums = [moved[19]]
    for step in range(1, n_mp):
        sums.append(lax.ppermute(moved[19], "mp", [(i, (i + step) % n_mp) for i in range(n_mp)]))
    table = run_tables(moved[18], shared, ghead, (tables, tables_mean, tables_square))
    renewed = run_renew(n_mp, table[3], stat, sums, state[0:12:3], moved[0:12:3])
    return (
        from_rows(renewed[0]),
        from_rows(moved[1]),
        from_rows(moved[2]),
        renewed[1],
        moved[4],
        moved[5],
        renewed[2],
        moved[7],
        moved[8],
        renewed[3],
        moved[10],
        moved[11],
        *table[:3],
        *moved[12:18],
        from_rows(renewed[4]),
        renewed[5],
        renewed[6],
        renewed[7],
        renewed[10].reshape(12),
        renewed[9].reshape(()),
        renewed[8],
    )


def solution(mesh):
    return jax.shard_map(
        shards,
        mesh=mesh,
        in_specs=(
            P(("dp", "mp"), None, None),
            P("dp", None),
            P("dp"),
            P(("dp", "mp")),
            P(("dp", "mp")),
            P(None, None, None, "mp"),
            P(None, None, None, "mp"),
            P(None, None, None, "mp"),
            P(None, "mp", None),
            P(None, "mp", None),
            P(None, "mp", None),
            P(None, None, "mp"),
            P(None, None, "mp"),
            P(None, None, "mp"),
            P(None, "mp", None),
            P(None, "mp", None),
            P(None, "mp", None),
            P(),
            P(),
            P(),
            P(),
            P(),
            P(),
            P(),
            P(),
            P(),
        ),
        out_specs=(
            P(None, None, None, "mp"),
            P(None, None, None, "mp"),
            P(None, None, None, "mp"),
            P(None, "mp", None),
            P(None, "mp", None),
            P(None, "mp", None),
            P(None, None, "mp"),
            P(None, None, "mp"),
            P(None, None, "mp"),
            P(None, "mp", None),
            P(None, "mp", None),
            P(None, "mp", None),
            P(),
            P(),
            P(),
            P(),
            P(),
            P(),
            P(),
            P(),
            P(),
            P(None, None, None, "mp"),
            P(None, "mp", None),
            P(None, None, "mp"),
            P(None, "mp", None),
            P(),
            P(),
            P(),
        ),
        check_vma=False,
    )
```

```python
import functools

import jax
import jax.numpy as jnp
from jax import lax
from jax.experimental import pallas as pl
from jax.experimental.pallas import tpu as pltpu
from jax.sharding import PartitionSpec as P

D = 384
HEADS = 8
HEAD = 48
PIX = 768
P_SIZE = 196
PAD = 208
WIDE = 256
STEP = 10
SCALE = HEAD**-0.5
BETA_ONE = 0.9
BETA_TWO = 0.999
ADAM_EPS = 1e-08
DECAY = 0.01
RATE = 0.5
RATE_VECTOR = 0.5
CLIP = 0.02
TEMP = 0.05
MASKED = -1000000000.0
NORM_EPS = 1e-06
F32 = jnp.float32
BF = jnp.bfloat16
VMEM_LIMIT = 58 * 2**20
ANY = pl.BlockSpec(memory_space=pl.ANY)
MESH = pl.DeviceIdType.MESH
WHOLE = pl.BlockSpec(memory_space=pltpu.VMEM)


def nn(left, right):
    return lax.dot_general(left, right, (((1,), (0,)), ((), ())), preferred_element_type=F32)


def nt(left, right):
    return lax.dot_general(left, right, (((1,), (1,)), ((), ())), preferred_element_type=F32)


def tn(left, right):
    return lax.dot_general(left, right, (((0,), (0,)), ((), ())), preferred_element_type=F32)


def colsum(values):
    return jnp.sum(values, 0, keepdims=True)


def normalize(inputs):
    center = inputs - jnp.mean(inputs, -1, keepdims=True)
    spread = jnp.mean(center * center, -1, keepdims=True)
    inverse = lax.rsqrt(spread + NORM_EPS)
    return center * inverse, inverse


def normalize_back(unit, inverse, gain, incoming):
    scaled = incoming * gain
    return inverse * (
        scaled
        - jnp.mean(scaled, -1, keepdims=True)
        - unit * jnp.mean(scaled * unit, -1, keepdims=True)
    )


def gelu_parts(inner):
    cumulative = 0.5 + 0.5 * lax.erf(inner * 0.5**0.5)
    bell = jnp.exp2(inner * inner * (-0.5 * 1.4426950408889634)) * 0.3989422804014327
    return inner * cumulative, cumulative + inner * bell


def head_mask(copies=1):
    row = lax.rem(lax.broadcasted_iota(jnp.int32, (copies * HEADS, D), 0), HEADS)
    column = lax.broadcasted_iota(jnp.int32, (copies * HEADS, D), 1)
    return ((column >= row * HEAD) & (column < row * HEAD + HEAD)).astype(F32)


def stat_lanes(parts, weight, first):
    lane = lax.broadcasted_iota(jnp.int32, (1, 128), 1)
    row = jnp.zeros((1, 128), F32)
    for place, values in enumerate(parts):
        total = jnp.sum(colsum(values * values * weight), keepdims=True)
        high = total.astype(BF).astype(F32)
        row = jnp.where(lane == first + 2 * place, high, row)
        row = jnp.where(lane == first + 2 * place + 1, total - high, row)
    return row


def part(ref, first, rows):
    shards_count = ref.shape[0]
    return ref[:, first : first + rows, :].reshape(shards_count * rows, ref.shape[2])


def pad_rows(rows, n_dp):
    return -(-rows // (16 * n_dp)) * 16 * n_dp


class Place:
    def __init__(self, n_dp, n_mp):
        self.n_dp, self.n_mp, self.n_y = n_dp, n_mp, n_mp // 2
        self.n_lo = 2 if n_dp < 16 else 4
        self.n_hi = n_dp // self.n_lo
        self.dp = lax.axis_index("dp")
        self.mp = lax.axis_index("mp")
        self.y = lax.div(self.mp, 2)
        self.core = lax.rem(self.mp, 2)
        self.high = lax.div(self.dp, self.n_lo)
        self.low = lax.rem(self.dp, self.n_lo)
        self.chunk = self.low * self.n_hi + self.high
        self.sibling = (self.dp, self.y * 2 + 1 - self.core)

    def along_y(self, step):
        return lax.rem(self.y + step, self.n_y)

    def along_lo(self, step):
        return lax.rem(self.low + step, self.n_lo)

    def along_hi(self, step):
        return lax.rem(self.high + step, self.n_hi)

    def at_lo(self, low):
        return (self.high * self.n_lo + low, self.mp)

    def at_hi(self, high):
        return (high * self.n_lo + self.low, self.mp)

    def near_partners(self):
        return [self.sibling] + [
            (self.dp, self.along_y(step) * 2 + self.core) for step in range(1, self.n_y)
        ]

    def all_partners(self):
        partners = [(lax.rem(self.dp + step, self.n_dp), self.mp) for step in range(1, self.n_dp)]
        return partners + [
            (self.dp, lax.rem(self.mp + step, self.n_mp)) for step in range(1, self.n_mp)
        ]

    def low_partners(self):
        return [self.at_lo(self.along_lo(step)) for step in range(1, self.n_lo)]

    def dp_partners(self):
        return self.low_partners() + [self.at_hi(self.along_hi(step)) for step in range(1, self.n_hi)]


def greet(partners):
    barrier = pltpu.get_barrier_semaphore()
    for partner in partners:
        pl.semaphore_signal(barrier, inc=1, device_id=partner, device_id_type=MESH)
    return lambda: pl.semaphore_wait(barrier, len(partners))


def tile_rows(ref, first, rows):
    return ref.at[pl.ds(pl.multiple_of(first, 16), rows)]


class SpreadGather:
    def __init__(self, place, rows, out, far_sem, low_sem, near_sem):
        self.place, self.rows, self.out = place, rows, out
        self.far_sem, self.low_sem, self.near_sem = far_sem, low_sem, near_sem
        self.count = rows.shape[0] // place.n_lo

    def piece(self, ref, low):
        return tile_rows(ref, low * self.count, self.count)

    def far_copy(self, step, slot):
        p = self.place
        return remote(
            self.piece(self.rows, p.low), self.piece(self.out.at[slot], p.low),
            self.far_sem.at[0, step], self.far_sem.at[1, step],
            (p.dp, p.along_y(step) * 2 + p.core),
        )

    def low_copy(self, step, turn, low):
        p = self.place
        rows = self.piece(self.out.at[self.from_y(step) + p.core], low)
        at = (step - 1) * p.n_lo + turn
        return remote(
            rows, rows, self.low_sem.at[0, at], self.low_sem.at[1, at],
            p.at_lo(p.along_lo(turn)),
        )

    def near_copy(self, step, slot):
        return remote(
            self.rows if step == 0 else self.out.at[slot], self.out.at[slot],
            self.near_sem.at[0, step], self.near_sem.at[1, step], self.place.sibling,
        )

    def own_copy(self):
        return pltpu.make_async_copy(
            self.rows, self.out.at[self.place.mp], self.far_sem.at[0, 0]
        )

    def from_y(self, step):
        p = self.place
        return p.along_y(p.n_y - step) * 2

    def start(self):
        p = self.place
        for step in range(1, p.n_y):
            self.far_copy(step, p.mp).start()
        self.near_copy(0, p.mp).start()
        self.own_copy().start()

    def spread(self):
        p = self.place
        for step in range(1, p.n_y):
            self.far_copy(step, self.from_y(step) + p.core).wait_recv()
            for turn in range(1, p.n_lo):
                self.low_copy(step, turn, p.low).start()

    def forward(self):
        p = self.place
        for step in range(1, p.n_y):
            for turn in range(1, p.n_lo):
                self.low_copy(step, turn, p.along_lo(p.n_lo - turn)).wait_recv()
            self.near_copy(step, self.from_y(step) + p.core).start()

    def finish(self):
        p = self.place
        self.own_copy().wait()
        for step in range(1, p.n_y):
            self.far_copy(step, p.mp).wait_send()
            for turn in range(1, p.n_lo):
                self.low_copy(step, turn, p.low).wait_send()
        for step in range(p.n_y):
            self.near_copy(step, self.from_y(step) + p.core if step else p.mp).wait_send()
            self.near_copy(step, self.from_y(step) + 1 - p.core).wait_recv()


def spread_scratch(n_dp, n_mp):
    n_lo = 2 if n_dp < 16 else 4
    dma = pltpu.SemaphoreType.DMA
    return [dma((2, n_mp // 2)), dma((2, n_mp // 2 * n_lo)), dma((2, n_mp // 2))]


class Gather:
    def __init__(self, place, rows, out, far_sem, near_sem):
        self.place, self.rows, self.out = place, rows, out
        self.far_sem, self.near_sem = far_sem, near_sem

    def far_copy(self, step, slot):
        p = self.place
        return remote(
            self.rows, self.out.at[slot], self.far_sem.at[0, step], self.far_sem.at[1, step],
            (p.dp, p.along_y(step) * 2 + p.core),
        )

    def near_copy(self, step, slot):
        return remote(
            self.rows if step == 0 else self.out.at[slot], self.out.at[slot],
            self.near_sem.at[0, step], self.near_sem.at[1, step], self.place.sibling,
        )

    def own_copy(self):
        return pltpu.make_async_copy(
            self.rows, self.out.at[self.place.mp], self.far_sem.at[0, 0]
        )

    def from_y(self, step):
        p = self.place
        return p.along_y(p.n_y - step) * 2

    def start(self):
        p = self.place
        for step in range(1, p.n_y):
            self.far_copy(step, p.mp).start()
        self.near_copy(0, p.mp).start()
        self.own_copy().start()

    def forward(self):
        p = self.place
        for step in range(1, p.n_y):
            slot = self.from_y(step) + p.core
            self.far_copy(step, slot).wait_recv()
            self.near_copy(step, slot).start()

    def finish(self):
        p = self.place
        self.own_copy().wait()
        for step in range(1, p.n_y):
            self.far_copy(step, p.mp).wait_send()
        for step in range(p.n_y):
            self.near_copy(step, self.from_y(step) + p.core if step else p.mp).wait_send()
            self.near_copy(step, self.from_y(step) + 1 - p.core).wait_recv()


def gather_scratch(n_mp):
    dma = pltpu.SemaphoreType.DMA
    return [dma((2, n_mp // 2)), dma((2, n_mp // 2))]


class ShardSum:
    def __init__(
        self, place, rows, first, y_first, near, far, low, half, high,
        near_sem, far_sem, low_sem, high_sem,
    ):
        self.place, self.rows, self.first, self.y_first = place, rows, first, y_first
        self.near, self.far, self.low, self.half, self.high = near, far, low, half, high
        self.near_sem, self.far_sem = near_sem, far_sem
        self.low_sem, self.high_sem = low_sem, high_sem
        self.count = near.shape[1]
        self.wide = self.count // place.n_lo
        self.chunk = self.count // place.n_dp

    def near_copy(self, step):
        p = self.place
        y = p.along_y(step)
        return remote(
            self.rows.at[y * 2 + 1 - p.core, pl.ds(self.first, self.count)], self.near.at[y],
            self.near_sem.at[0, step], self.near_sem.at[1, step], p.sibling,
        )

    def far_copy(self, step):
        p = self.place
        y = p.along_y(step)
        rows = self.near.at[y]
        if not self.y_first:
            rows = tile_rows(rows, p.low * self.wide, self.wide)
        return remote(
            rows, self.far.at[step - 1],
            self.far_sem.at[0, step], self.far_sem.at[1, step], (p.dp, y * 2 + p.core),
        )

    def low_copy(self, step):
        p = self.place
        to = p.along_lo(step)
        at = pl.ds(pl.multiple_of(to * self.wide, 16), self.wide)
        rows = self.near.at[p.y, at] if self.y_first else self.near.at[:, at]
        return remote(
            rows, self.low.at[step - 1],
            self.low_sem.at[0, step], self.low_sem.at[1, step], p.at_lo(to),
        )

    def high_copy(self, step):
        p = self.place
        to = p.along_hi(step)
        return remote(
            tile_rows(self.half, to * self.chunk, self.chunk), self.high.at[step - 1],
            self.high_sem.at[0, step], self.high_sem.at[1, step], p.at_hi(to),
        )

    def start(self):
        for step in range(1, self.place.n_y + 1):
            self.near_copy(step).start()

    def second(self):
        p = self.place
        at = slice(self.first, self.first + self.count)
        for step in range(1, p.n_y + 1):
            y = p.along_y(step)
            self.near_copy(step).wait_recv()
            self.near[pl.ds(y, 1)] = (
                self.rows[pl.ds(y * 2 + p.core, 1), at, :].astype(F32)
                + self.near[pl.ds(y, 1)].astype(F32)
            ).astype(BF)
            if self.y_first and step < p.n_y:
                self.far_copy(step).start()
        if not self.y_first:
            for step in range(1, p.n_lo):
                self.low_copy(step).start()

    def third(self):
        p = self.place
        own = pl.ds(pl.multiple_of(p.low * self.wide, 16), self.wide)
        if self.y_first:
            sums = self.near[pl.ds(p.y, 1)].astype(F32)
            for step in range(1, p.n_y):
                self.far_copy(step).wait_recv()
                sums += self.far[step - 1].astype(F32)[None]
            self.near[pl.ds(p.y, 1)] = sums.astype(BF)
            for step in range(1, p.n_lo):
                self.low_copy(step).start()
        else:
            sums = self.near[:, own, :].astype(F32)
            for step in range(1, p.n_lo):
                self.low_copy(step).wait_recv()
                sums += self.low[step - 1].astype(F32)
            self.near[:, own, :] = sums.astype(BF)
            for step in range(1, p.n_y):
                self.far_copy(step).start()

    def fourth(self):
        p = self.place
        own = pl.ds(pl.multiple_of(p.low * self.wide, 16), self.wide)
        sums = self.near[pl.ds(p.y, 1), own, :][0].astype(F32)
        if self.y_first:
            for step in range(1, p.n_lo):
                self.low_copy(step).wait_recv()
                sums += self.low[step - 1].astype(F32)
        else:
            for step in range(1, p.n_y):
                self.far_copy(step).wait_recv()
                sums += self.far[step - 1].astype(F32)
        self.half[...] = sums.astype(BF)
        for step in range(1, p.n_hi):
            self.high_copy(step).start()

    def finish(self):
        p = self.place
        at = pl.ds(pl.multiple_of(p.high * self.chunk, 16), self.chunk)
        sums = self.half[at, :].astype(F32)
        for step in range(1, p.n_hi):
            self.high_copy(step).wait_recv()
            sums += self.high[step - 1].astype(F32)
        return sums.astype(BF)

    def wait_sends(self):
        p = self.place
        for step in range(1, p.n_y + 1):
            self.near_copy(step).wait_send()
            if step < p.n_y:
                self.far_copy(step).wait_send()
        for step in range(1, p.n_lo):
            self.low_copy(step).wait_send()
        for step in range(1, p.n_hi):
            self.high_copy(step).wait_send()


def sum_scratch(n_dp, n_mp, rows, y_first):
    n_y = n_mp // 2
    n_lo = 2 if n_dp < 16 else 4
    n_hi = n_dp // n_lo
    wide = rows // n_lo
    dma = pltpu.SemaphoreType.DMA
    far = (max(n_y - 1, 1), rows, D) if y_first else (max(n_y - 1, 1), wide, D)
    low = (n_lo - 1, wide, D) if y_first else (n_lo - 1, n_y, wide, D)
    return [
        pltpu.VMEM((n_y, rows, D), BF), pltpu.VMEM(far, BF), pltpu.VMEM(low, BF),
        pltpu.VMEM((wide, D), BF), pltpu.VMEM((n_hi - 1, rows // n_dp, D), BF),
        dma((2, n_y + 1)), dma((2, n_y + 1)), dma((2, n_lo)), dma((2, n_hi)),
    ]


SUM_BUFFERS = 9


def halves(rows, n_dp):
    unit = 16 * n_dp
    first = (rows // unit + 1) // 2 * unit
    return first, rows - first


class TableSum:
    def __init__(
        self, place, rows, out, near, low, part_rows, high, last, far, near_sem, low_sem, high_sem,
        far_sem, back_sem, hand_sem,
    ):
        self.place, self.rows, self.out = place, rows, out
        self.near, self.low, self.part, self.high = near, low, part_rows, high
        self.last, self.far = last, far
        self.near_sem, self.low_sem, self.high_sem = near_sem, low_sem, high_sem
        self.far_sem, self.back_sem, self.hand_sem = far_sem, back_sem, hand_sem
        self.chunk = high.shape[2]
        self.wide = low.shape[2]
        self.slab = place.core * place.n_y + place.y
        self.first = place.core * place.n_y

    def near_copy(self):
        p = self.place
        return remote(
            self.rows.at[pl.ds((1 - p.core) * p.n_y, p.n_y)], self.near,
            self.near_sem.at[0], self.near_sem.at[1], p.sibling,
        )

    def low_copy(self, step):
        p = self.place
        to = p.along_lo(step)
        return remote(
            self.near.at[:, pl.ds(pl.multiple_of(to * self.wide, 16), self.wide)],
            self.low.at[step - 1], self.low_sem.at[0, step], self.low_sem.at[1, step], p.at_lo(to),
        )

    def high_copy(self, step):
        p = self.place
        to = p.along_hi(step)
        return remote(
            self.part.at[:, pl.ds(pl.multiple_of(to * self.chunk, 16), self.chunk)],
            self.high.at[step - 1], self.high_sem.at[0, step], self.high_sem.at[1, step],
            p.at_hi(to),
        )

    def far_copy(self, step):
        p = self.place
        to = p.along_y(step)
        return remote(
            self.last.at[to], self.far.at[step - 1], self.far_sem.at[0, step],
            self.far_sem.at[1, step], (p.dp, to * 2 + p.core),
        )

    def start(self):
        self.near_copy().start()

    def near_to_low(self):
        p = self.place
        self.near_copy().wait_recv()
        self.near[...] = (
            self.rows[pl.ds(self.first, p.n_y)].astype(F32) + self.near[...].astype(F32)
        ).astype(BF)
        for step in range(1, p.n_lo):
            self.low_copy(step).start()

    def low_to_high(self):
        p = self.place
        at = pl.ds(pl.multiple_of(p.low * self.wide, 16), self.wide)
        sums = self.near[:, at, :].astype(F32)
        for step in range(1, p.n_lo):
            self.low_copy(step).wait_recv()
            sums += self.low[step - 1].astype(F32)
        self.part[...] = sums.astype(BF)
        for step in range(1, p.n_hi):
            self.high_copy(step).start()

    def high_to_far(self):
        p = self.place
        at = pl.ds(pl.multiple_of(p.high * self.chunk, 16), self.chunk)
        sums = self.part[:, at, :].astype(F32)
        for step in range(1, p.n_hi):
            self.high_copy(step).wait_recv()
            sums += self.high[step - 1].astype(F32)
        self.last[...] = sums.astype(BF)
        for step in range(1, p.n_y):
            self.far_copy(step).start()

    def chunk_at(self, slab, chunk):
        return self.out.at[slab, pl.ds(pl.multiple_of(chunk * self.chunk, 16), self.chunk)]

    def back_far(self, step, y):
        p = self.place
        rows = self.chunk_at(self.first + y, p.chunk)
        return remote(
            rows, rows, self.back_sem.at[0, step], self.back_sem.at[1, step],
            (p.dp, p.along_y(step) * 2 + p.core),
        )

    def back_high(self, step, chunk):
        p = self.place
        rows = self.chunk_at(pl.ds(self.first, p.n_y), chunk)
        return remote(
            rows, rows, self.back_sem.at[2, step], self.back_sem.at[3, step],
            p.at_hi(p.along_hi(step)),
        )

    def back_low(self, step, low):
        p = self.place
        rows = self.out.at[
            pl.ds(self.first, p.n_y), pl.ds(pl.multiple_of(low * self.wide, 16), self.wide)
        ]
        return remote(
            rows, rows, self.back_sem.at[4, step], self.back_sem.at[5, step],
            p.at_lo(p.along_lo(step)),
        )

    def hand_copy(self, core):
        p = self.place
        rows = self.out.at[pl.ds(core * p.n_y, p.n_y)]
        return remote(rows, rows, self.hand_sem.at[0], self.hand_sem.at[1], p.sibling)

    def turn(self):
        p = self.place
        sums = self.last[pl.ds(p.y, 1)][0].astype(F32)
        for step in range(1, p.n_y):
            self.far_copy(step).wait_recv()
            sums += self.far[step - 1].astype(F32)
        at = pl.ds(pl.multiple_of(p.chunk * self.chunk, 16), self.chunk)
        self.out[pl.ds(self.slab, 1), at, :] = sums.astype(BF)[None]
        for step in range(1, p.n_y):
            self.back_far(step, p.y).start()

    def far_to_high(self):
        p = self.place
        for step in range(1, p.n_y):
            self.back_far(step, p.along_y(p.n_y - step)).wait_recv()
        for step in range(1, p.n_hi):
            self.back_high(step, p.chunk).start()

    def high_to_low(self):
        p = self.place
        for step in range(1, p.n_hi):
            self.back_high(step, p.low * p.n_hi + p.along_hi(p.n_hi - step)).wait_recv()
        for step in range(1, p.n_lo):
            self.back_low(step, p.low).start()

    def low_to_near(self):
        p = self.place
        for step in range(1, p.n_lo):
            self.back_low(step, p.along_lo(p.n_lo - step)).wait_recv()
        self.hand_copy(p.core).start()

    def finish(self):
        p = self.place
        self.hand_copy(1 - p.core).wait_recv()
        self.near_copy().wait_send()
        self.hand_copy(p.core).wait_send()
        for step in range(1, p.n_lo):
            self.low_copy(step).wait_send()
            self.back_low(step, p.low).wait_send()
        for step in range(1, p.n_hi):
            self.high_copy(step).wait_send()
            self.back_high(step, p.chunk).wait_send()
        for step in range(1, p.n_y):
            self.far_copy(step).wait_send()
            self.back_far(step, p.y).wait_send()


def table_scratch(n_dp, n_mp, rows):
    n_y = n_mp // 2
    n_lo = 2 if n_dp < 16 else 4
    n_hi = n_dp // n_lo
    wide, chunk = rows // n_lo, rows // n_dp
    dma = pltpu.SemaphoreType.DMA
    return [
        pltpu.VMEM((n_y, rows, D), BF), pltpu.VMEM((n_lo - 1, n_y, wide, D), BF),
        pltpu.VMEM((n_y, wide, D), BF), pltpu.VMEM((n_hi - 1, n_y, chunk, D), BF),
        pltpu.VMEM((n_y, chunk, D), BF), pltpu.VMEM((max(n_y - 1, 1), chunk, D), BF),
        dma((2,)), dma((2, n_lo)), dma((2, n_hi)), dma((2, n_y)),
        dma((6, max(n_y, n_lo, n_hi))), dma((2,)),
    ]


class HandHigh:
    def __init__(self, place, rows, sems):
        self.place, self.rows, self.sems = place, rows, sems
        self.chunk = rows.shape[0] // place.n_hi

    def copy(self, step, source):
        p = self.place
        rows = tile_rows(self.rows, source * self.chunk, self.chunk)
        return remote(
            rows, rows, self.sems.at[0, step], self.sems.at[1, step], p.at_hi(p.along_hi(step))
        )

    def start(self, sums):
        p = self.place
        self.rows[pl.ds(pl.multiple_of(p.high * self.chunk, 16), self.chunk), :] = sums
        for step in range(1, p.n_hi):
            self.copy(step, p.high).start()

    def arrive(self):
        p = self.place
        for step in range(1, p.n_hi):
            self.copy(step, p.along_hi(p.n_hi - step)).wait_recv()

    def wait_sends(self):
        for step in range(1, self.place.n_hi):
            self.copy(step, self.place.high).wait_send()


class HandLow:
    def __init__(self, place, rows, first, count, sems):
        self.place, self.rows, self.first, self.sems = place, rows, first, sems
        self.run = count // place.n_lo

    def copy(self, step, source):
        p = self.place
        rows = tile_rows(self.rows, self.first + source * self.run, self.run)
        return remote(
            rows, rows, self.sems.at[0, step], self.sems.at[1, step], p.at_lo(p.along_lo(step))
        )

    def start(self, sums):
        p = self.place
        self.rows[pl.ds(pl.multiple_of(self.first + p.low * self.run, 16), self.run), :] = sums
        for step in range(1, p.n_lo):
            self.copy(step, p.low).start()

    def arrive(self):
        p = self.place
        for step in range(1, p.n_lo):
            self.copy(step, p.along_lo(p.n_lo - step)).wait_recv()

    def wait_sends(self):
        for step in range(1, self.place.n_lo):
            self.copy(step, self.place.low).wait_send()


def remote(src, dst, send_sem, recv_sem, device):
    return pltpu.make_async_remote_copy(
        src_ref=src, dst_ref=dst, send_sem=send_sem, recv_sem=recv_sem,
        device_id=device, device_id_type=MESH,
    )


def stack_heads(stack, rows, gains):
    for g in range(HEADS):
        stack[g * PAD : g * PAD + P_SIZE, :] = (rows * gains[g : g + 1, :]).astype(BF)


def column(cols, index):
    lane = lax.broadcasted_iota(jnp.int32, cols.shape, 1)
    return jnp.sum(jnp.where(lane == index, cols[...], 0.0), 1, keepdims=True)


def self_attend_kernel(
    n_dp, n_mp, group, attn_in, attn_out, mlp_in, mlp_out, pixels, tables, vec, mix, mask,
    counts, labels, pairs,
    q_out, k_out, v_out, prob_out, post_out, ho_out, raw_out, mid_out, stat_out,
    wmlp_out, wattn_far, embed_far, wcls_out, up_rows, down_rows, head_out, t1row, t2row, cols,
    bias_out, base_out,
    stack, scores, embed, wattn, mlp_rows, cls_rows, save_sem, *rest,
):
    start_scratch, sems = rest[:-4], rest[-4:]
    shard = wattn.shape[1] // 4
    gather = Gather(Place(n_dp, n_mp), mlp_rows, wmlp_out, *sems[:2])
    gather_cls = Gather(gather.place, cls_rows, wcls_out, *sems[2:])
    save = pltpu.make_async_copy(wattn, wattn_far, save_sem.at[0])
    images = pl.num_programs(0)
    n = pl.program_id(0)

    @pl.when(n == 0)
    def _():
        stack[...] = jnp.zeros_like(stack)

        def begin():
            gather.start()
            gather_cls.start()

        start_part(
            begin, n_dp, n_mp, group, attn_in, attn_out, mlp_in, mlp_out, pixels, tables, vec, mix, mask,
            counts, labels, pairs,
            wattn, mlp_rows, cls_rows, up_rows, down_rows, embed_far, head_out, t1row, t2row, cols,
            bias_out, base_out, embed, *start_scratch,
        )
        save.start()

    @pl.when(n == images * 5 // 8)
    def _():
        gather.forward()

    @pl.when(n == images - 1)
    def _():
        gather_cls.forward()

    x = embed[pl.ds(n, 1)][0]
    unit, _ = normalize(x)
    normed = (unit * vec[0:1, :] + vec[1:2, :]).astype(BF)
    q = nt(normed, part(wattn, 0, shard)).astype(BF)
    k = nt(normed, part(wattn, shard, shard)).astype(BF)
    v = nt(normed, part(wattn, 2 * shard, shard)).astype(BF)
    q_out[0] = q
    k_out[0] = k
    v_out[0] = v
    stack_heads(stack, q.astype(F32), t1row)
    scores[...] = nt(k, stack[...])
    bias = column(cols, pl.program_id(0))
    for first in range(0, HEADS * PAD, 128):
        mixed = scores[:, first : first + 128] + bias
        grown = jnp.exp(mixed - jnp.max(mixed, 0, keepdims=True))
        prob = grown * (1.0 / jnp.sum(grown, 0, keepdims=True))
        prob_out[0, :, first : first + 128] = prob.astype(BF)
    post = tn(prob_out[0], v)
    post_out[0] = post.astype(BF)
    heads_out = jnp.zeros(x.shape, F32)
    for g in range(HEADS):
        heads_out += post[g * PAD : g * PAD + P_SIZE, :] * t2row[g : g + 1, :]
    heads_out = heads_out.astype(BF)
    ho_out[0] = heads_out
    raw = nn(heads_out, part(wattn, 3 * shard, shard))
    raw_out[0] = raw.astype(BF)
    branch = vec[3:4, :] * (raw + vec[2:3, :])
    middle = x + branch
    mid_out[0] = middle
    weight = column(cols, pl.program_id(0) + cols.shape[1] // 2)
    stat_out[0] = stat_lanes((branch, middle), weight, 8)

    @pl.when(n == images - 1)
    def _():
        gather.finish()
        gather_cls.finish()
        save.wait()


def feed_kernel(
    n_dp, n_mp, group, mid, cols, bias_row, base, stat, vec, wmlp, wcls, up_rows, down_rows,
    head_far,
    patch_out, act_out, slope_out, raw_out, aux_out, *rest,
):
    token_outs, rest = rest[:10], rest[10:]
    norm_out, cprob_out, cprob0_out, z_out, card_out, wup_out, wdown_out, head = rest[:8]
    token_scratch, (cards, slots, dp_sem, mp_sem, head_sem), sems = rest[8:12], rest[12:17], rest[17:]
    hidden = wmlp.shape[1] // 2
    shard = wcls.shape[1] // 4
    images = norm_out.shape[0]
    place = Place(n_dp, n_mp)
    load_head = pltpu.make_async_copy(head_far, head, head_sem.at[0])
    gather_up = SpreadGather(place, up_rows, wup_out, *sems[:3])
    gather_down = SpreadGather(place, down_rows, wdown_out, *sems[3:])

    def beside(step, *stages):
        @pl.when(pl.program_id(0) == step)
        def _():
            for stage in stages:
                stage()

    @pl.when(pl.program_id(0) == 0)
    def _():
        norm_out[...] = jnp.zeros_like(norm_out)
        load_head.start()
        greet(place.all_partners())()
        gather_up.start()
        gather_down.start()

    beside(images * 3 // 8, gather_up.spread)
    beside(images // 2, gather_down.spread)
    beside(images * 3 // 4, gather_up.forward)
    beside(images - 1, gather_down.forward)

    middle = mid[0]
    unit, _ = normalize(middle)
    normed = (unit * vec[4:5, :] + vec[5:6, :]).astype(BF)
    inner = nt(normed, part(wmlp, 0, hidden))
    active, slope = gelu_parts(inner)
    active = active.astype(BF)
    act_out[0] = active
    slope_out[0] = slope.astype(BF)
    raw = nn(active, part(wmlp, hidden, hidden))
    raw_out[0] = raw.astype(BF)
    branch = vec[7:8, :] * (raw + vec[6:7, :])
    patches = middle + branch
    patch_out[0] = patches
    card_out[pl.ds(4 * pl.program_id(0) + 3, 1), :] = (
        base[pl.ds(pl.program_id(0), 1), :]
        + stat[0]
        + stat_lanes((branch, patches), column(cols, pl.program_id(0) + images), 12)
    )
    unit, _ = normalize(patches)
    norm_out[pl.ds(pl.program_id(0), 1), :P_SIZE, :] = (
        (unit * vec[8:9, :] + vec[9:10, :]).astype(BF)[None]
    )

    @pl.when(pl.program_id(0) == images - 1)
    def _():
        unit, _ = normalize(jnp.broadcast_to(vec[17:18, :], (HEADS, D)))
        token = (unit * vec[8:9, :] + vec[9:10, :]).astype(BF)
        query = nt(token, part(wcls, 0, shard)).astype(BF).astype(F32)
        keys = nn((query * head_mask()).astype(BF), part(wcls, shard, shard)) * SCALE
        token = token.astype(F32)
        aux_out[0:8, :] = keys
        aux_out[8:16, :] = token
        aux_out[16:24, :] = query
        scores = nt(keys.astype(BF), norm_out[...].reshape(images * WIDE, D)) + bias_row[...]
        score0 = jnp.sum(keys * token, -1, keepdims=True)
        for n in range(images):
            rows = slice(n * HEADS, (n + 1) * HEADS)
            mine = scores[:, n * WIDE : (n + 1) * WIDE]
            top = jnp.maximum(jnp.max(mine, -1, keepdims=True), score0)
            grown = jnp.exp(mine - top)
            grown0 = jnp.exp(score0 - top)
            scale = 1.0 / (jnp.sum(grown, -1, keepdims=True) + grown0)
            cprob = grown * scale
            cprob0 = grown0 * scale
            cprob_out[rows, :] = cprob
            cprob0_out[rows, :] = jnp.broadcast_to(cprob0, (HEADS, 128))
            z_out[rows, :] = nn(cprob.astype(BF), norm_out[n]) + cprob0 * token
        cheads = nt(z_out[...].astype(BF), part(wcls, 2 * shard, shard)) * head_mask(images)
        cheads = cheads.reshape(images, HEADS, D).sum(1)
        for piece in range(3):
            card_out[pl.ds(piece, images, stride=4), :] = cheads[:, 128 * piece : 128 * piece + 128]
        share_cards(n_dp, n_mp, card_out, cards, slots, dp_sem, mp_sem)
        gather_up.finish()
        gather_down.finish()
        load_head.wait()
        token_kernel(
            group, cards, vec, wcls, wup_out, wdown_out, head, norm_out, cprob_out, cprob0_out,
            z_out, aux_out, *token_outs, *token_scratch,
        )


def token_kernel(
    group, cards, vec, wcls, wup_rows, wdown_rows, head, norm, cprob, cprob0, z, aux,
    left_out, right_out, gv_out, local_out, gout_out, gup_out, gdown_out, ghead_out, rows_out,
    stat_out, dch_all, gout_all, gup_all, gdown_all,
):
    hidden = wup_rows.shape[1]
    shard = wcls.shape[1] // 4
    images = cards.shape[0] // 4
    cheads = jnp.concatenate(
        [cards[pl.ds(piece, images, stride=4), :] for piece in range(3)], 1
    ).astype(BF)
    card = cards[pl.ds(3, images, stride=4), :]
    labels = (card[:, 0:1] * 32.0 + card[:, 1:2]).astype(jnp.int32)
    pairs = (card[:, 2:3] * 32.0 + card[:, 3:4]).astype(jnp.int32)
    column = lax.broadcasted_iota(jnp.int32, (images, images), 1)
    row = lax.broadcasted_iota(jnp.int32, (images, images), 0)
    slot = lax.rem(lax.broadcasted_iota(jnp.int32, (images, 1), 0), group).astype(F32)
    okay = (slot >= group - card[:, 4:5]).astype(F32)
    okay_row = colsum(jnp.where(row == column, okay, 0.0))
    wo = part(wcls, 3 * shard, shard)
    wup = part(wup_rows, 0, hidden)
    wdown = part(wdown_rows, 0, hidden)
    count = jnp.sum(okay, keepdims=True)
    raw = nn(cheads, wo) + vec[10:11, :]
    branch = vec[11:12, :] * raw
    middle = vec[17:18, :] + branch
    unit2, inverse2 = normalize(middle)
    normed = (unit2 * vec[12:13, :] + vec[13:14, :]).astype(BF)
    inner = nt(normed, wup)
    active, slope = gelu_parts(inner)
    active = active.astype(BF)
    down = nn(active, wdown) + vec[14:15, :]
    mlp_branch = vec[15:16, :] * down
    token = middle + mlp_branch
    unit3, inverse3 = normalize(token)
    feature = unit3 * vec[18:19, :] + vec[19:20, :]
    feature_low = feature.astype(BF)
    logits = nt(feature_low, head[...])
    top = jnp.max(logits, -1, keepdims=True)
    grown = jnp.exp(logits - top)
    total = jnp.sum(grown, -1, keepdims=True)
    hot = lax.broadcasted_iota(jnp.int32, logits.shape, 1) == labels
    cross = jnp.log(total) + top - jnp.sum(jnp.where(hot, logits, 0.0), -1, keepdims=True)
    share = okay / count
    dlogits = (share * (grown / total - hot.astype(F32))).astype(BF)
    classes = head.shape[0]
    ghead = tn(dlogits, feature_low)
    ghead_out[0:8, :] = jnp.zeros((8, D), F32)
    ghead_out[classes:, :] = jnp.zeros((8, D), F32)
    ghead_out[4 : classes + 4, :] = ghead
    replicated_sq = colsum(ghead * ghead)
    dfeature = nn(dlogits, head[...])

    length = lax.rsqrt(jnp.sum(feature * feature, -1, keepdims=True) + NORM_EPS)
    embed = (feature * length).astype(BF)
    sims = nt(embed, embed) / TEMP
    sims = jnp.where((okay_row > 0) & (row != column), sims, MASKED)
    top = jnp.max(sims, -1, keepdims=True)
    grown = jnp.exp(sims - top)
    total = jnp.sum(grown, -1, keepdims=True)
    hot = column == pairs
    contrast = jnp.log(total) + top - jnp.sum(jnp.where(hot, sims, 0.0), -1, keepdims=True)
    dsims = share * (grown / total - hot.astype(F32))
    high = dsims.astype(BF)
    low = (dsims - high.astype(F32)).astype(BF)
    dembed = (nn(high, embed) + nn(low, embed) + tn(high, embed) + tn(low, embed)) / TEMP
    dfeature += length * dembed - feature * (
        length * length * length * jnp.sum(dembed * feature, -1, keepdims=True)
    )

    dtoken = normalize_back(unit3, inverse3, vec[18:19, :], dfeature)
    rows_out[0:1, :] = jnp.zeros((1, D), F32)
    rows_out[1:2, :] = jnp.zeros((1, D), F32)
    rows_out[7:8, :] = colsum(dtoken * down)
    rows_out[6:7, :] = vec[15:16, :] * colsum(dtoken)
    ddown = (dtoken * vec[15:16, :]).astype(BF)
    gdown = tn(active, ddown)
    own_f = pl.multiple_of(lax.axis_index("mp") * hidden, hidden)
    gdown_all[...] = gdown
    gdown_out[...] = gdown_all[pl.ds(own_f, hidden), :]
    replicated_sq += colsum(gdown * gdown)
    dinner = (nt(ddown, wdown) * slope).astype(BF)
    gup = tn(dinner, normed)
    gup_all[...] = gup
    gup_out[...] = gup_all[pl.ds(own_f, hidden), :]
    replicated_sq += colsum(gup * gup)
    dnormed = nn(dinner, wup)
    rows_out[4:5, :] = colsum(dnormed * unit2)
    rows_out[5:6, :] = colsum(dnormed)
    dmiddle = dtoken + normalize_back(unit2, inverse2, vec[12:13, :], dnormed)
    rows_out[3:4, :] = colsum(dmiddle * raw)
    rows_out[2:3, :] = vec[11:12, :] * colsum(dmiddle)
    rows_out[8:9, :] = colsum(dmiddle)
    rows_out[9:10, :] = colsum(dfeature * unit3)
    rows_out[10:11, :] = colsum(dfeature)
    dbranch = (dmiddle * vec[11:12, :]).astype(BF)
    gout = tn(cheads, dbranch)
    gout_all[...] = gout
    own_h = pl.multiple_of(lax.axis_index("mp") * shard, shard)
    gout_out[...] = gout_all[pl.ds(own_h, shard), :]
    replicated_sq += colsum(gout * gout)
    dch_all[...] = nt(dbranch, wo)
    local = norm.shape[0]
    place = lax.axis_index("dp") * lax.axis_size("mp") + lax.axis_index("mp")
    if local % 8 == 0:
        dch = dch_all[pl.ds(pl.multiple_of(place * local, local), local), :]
    else:
        share_of = 8 // local
        start = pl.multiple_of(lax.div(place, share_of) * 8, 8)
        window = dch_all[pl.ds(start, 8), :]
        pick = lax.rem(place, share_of)
        dch = sum(
            jnp.where(pick == i, window[i * local : (i + 1) * local, :], 0.0)
            for i in range(share_of)
        )

    keys = aux[0:8, :]
    class_row = aux[8:16, :]
    mask = head_mask()
    spread = jnp.concatenate([mask * dch[n : n + 1, :] for n in range(local)], 0).astype(BF)
    dz = nn(spread, part(wcls, 2 * shard, shard))
    dz_low = dz.astype(BF)
    probs = cprob[...]
    prob0 = cprob0[...][:, 0:1]
    class_rows = jnp.concatenate([class_row] * local, 0)
    dprobs = jnp.concatenate(
        [nt(dz_low[n * HEADS : (n + 1) * HEADS, :], norm[n]) for n in range(local)], 0
    )
    dprob0 = jnp.sum(dz * class_rows, -1, keepdims=True)
    inside = jnp.sum(dprobs * probs, -1, keepdims=True) + dprob0 * prob0
    dscores = (probs * (dprobs - inside)).astype(BF)
    dscore0 = prob0 * (dprob0 - inside)
    gv_out[...] = tn(spread, z[...].astype(BF))
    local_out[0:8, :] = jnp.zeros((8, D), F32)
    dkeys = jnp.zeros((HEADS, D), F32)
    from_class = jnp.zeros((1, D), F32)
    for n in range(local):
        rows = slice(n * HEADS, (n + 1) * HEADS)
        dkeys += nn(dscores[rows, :], norm[n]) + dscore0[rows, :] * class_row
        from_class += colsum(prob0[rows, :] * dz[rows, :] + dscore0[rows, :] * keys)
        left_out[n] = jnp.concatenate([probs[rows, :].astype(BF), dscores[rows, :]], 0)
        right_out[n] = jnp.concatenate([dz_low[rows, :], keys.astype(BF)], 0)
    local_out[6:7, :] = from_class
    local_out[8:16, :] = dkeys
    lane = lax.broadcasted_iota(jnp.int32, (1, 128), 1)
    self_sums = colsum(card)
    count_tokens = self_sums[:, 5:6]

    def squares(values):
        return jnp.sum(colsum(values * values * okay), keepdims=True)

    entries = [jnp.sum(okay * cross, keepdims=True), jnp.sum(okay * contrast, keepdims=True)]
    entries += [count, count_tokens]
    entries += [
        jnp.sqrt((self_sums[:, i : i + 1] + self_sums[:, i + 1 : i + 2]) / D / count_tokens)
        for i in (8, 10, 12, 14)
    ]
    entries += [
        jnp.sqrt(squares(item) / D / count) for item in (branch, middle, mlp_branch, token)
    ]
    line = jnp.zeros((1, 128), F32)
    for i, entry in enumerate(entries):
        line = jnp.where(lane == i, entry, line)
    stat_out[0:1, :] = line
    stat_out[1:8, :] = jnp.broadcast_to(
        replicated_sq[:, 0:128] + replicated_sq[:, 128:256] + replicated_sq[:, 256:384], (7, 128)
    )


def feed_back_kernel(
    left, right, gv, local_rows, patch, mid, raw, act, slope, vec, wmlp,
    dmid_out, gfeed_out, rows_out, gmlp_out,
):
    hidden = wmlp.shape[1] // 2
    count = wmlp.shape[0]
    shard = D // count

    @pl.when(pl.program_id(0) == 0)
    def _():
        gmlp_out[...] = jnp.zeros_like(gmlp_out)
        rows_out[...] = local_rows[...]

    unit, inverse = normalize(patch[0])
    dnormed = tn(left[0], right[0])[:P_SIZE, :]
    rows_out[4:5, :] += colsum(dnormed * unit)
    rows_out[5:6, :] += colsum(dnormed)
    incoming = normalize_back(unit, inverse, vec[8:9, :], dnormed)

    unit, inverse = normalize(mid[0])
    normed = (unit * vec[4:5, :] + vec[5:6, :]).astype(BF)
    rows_out[3:4, :] += colsum(incoming * (raw[0].astype(F32) + vec[6:7, :]))
    rows_out[2:3, :] += vec[7:8, :] * colsum(incoming)
    ddown = (incoming * vec[7:8, :]).astype(BF)
    gmlp_out[:, hidden:, :] += tn(act[0], ddown).reshape(count, hidden, D)
    dinner = (nt(ddown, part(wmlp, hidden, hidden)) * slope[0].astype(F32)).astype(BF)
    gmlp_out[:, :hidden, :] += tn(dinner, normed).reshape(count, hidden, D)
    dnormed = nn(dinner, part(wmlp, 0, hidden))
    rows_out[0:1, :] += colsum(dnormed * unit)
    rows_out[1:2, :] += colsum(dnormed)
    dmid_out[0] = incoming + normalize_back(unit, inverse, vec[4:5, :], dnormed)

    @pl.when(pl.program_id(0) == pl.num_programs(0) - 1)
    def _():
        used = 2 * hidden + shard
        gfeed_out[:, : 2 * hidden, :] = gmlp_out[...].astype(BF)
        gfeed_out[:, 2 * hidden : used, :] = gv[...].astype(BF).reshape(count, shard, D)
        if used < gfeed_out.shape[1]:
            gfeed_out[:, used:, :] = jnp.zeros((count, gfeed_out.shape[1] - used, D), BF)


def self_back_kernel(
    n_dp, n_mp, dmid, pixels, embed, q, k, v, prob, post, ho, raw, vec, wattn, t1row, t2row, gfeed,
    rows_feed, block_far, shared_far, square_out,
    gattn_out, gpos_out, rows_out, dx_all, dx_rows, stack_q, stack_h, slopes,
    blocks_out, commons_out, block_here, shared_here, save_sem, *sum_buffers,
):
    shard = wattn.shape[1] // 4
    count = wattn.shape[0]
    images = dx_all.shape[0]
    place = Place(n_dp, n_mp)
    rows_a, _ = halves(gfeed.shape[1], n_dp)
    sum_a = ShardSum(place, gfeed, 0, True, *sum_buffers[:SUM_BUFFERS])
    sum_b = ShardSum(
        place, gfeed, rows_a, False, *sum_buffers[SUM_BUFFERS : 2 * SUM_BUFFERS]
    )

    def beside(step, *stages):
        @pl.when(pl.program_id(0) == step)
        def _():
            for stage in stages:
                stage()

    @pl.when(pl.program_id(0) == 0)
    def _():
        gattn_out[...] = jnp.zeros_like(gattn_out)
        gpos_out[...] = jnp.zeros_like(gpos_out)
        rows_out[...] = jnp.zeros_like(rows_out)
        stack_q[...] = jnp.zeros_like(stack_q)
        stack_h[...] = jnp.zeros_like(stack_h)
        greet(place.near_partners() + place.dp_partners())()
        sum_a.start()
        sum_b.start()

    beside(1, sum_a.second, sum_b.second)
    beside(images * 3 // 8, sum_a.third, sum_b.third)
    beside(images * 5 // 8, sum_a.fourth, sum_b.fourth)

    wq = part(wattn, 0, shard)
    wk = part(wattn, shard, shard)
    wv = part(wattn, 2 * shard, shard)
    wo = part(wattn, 3 * shard, shard)
    incoming = dmid[0]
    rows_out[3:4, :] += colsum(incoming * (raw[0].astype(F32) + vec[2:3, :]))
    rows_out[2:3, :] += vec[3:4, :] * colsum(incoming)
    dbranch = (incoming * vec[3:4, :]).astype(BF)
    gattn_out[:, 3 * shard :, :] += tn(ho[0], dbranch).reshape(count, shard, D)
    dheads = nt(dbranch, wo).astype(BF).astype(F32)

    unit, inverse = normalize(embed[0])
    normed = (unit * vec[0:1, :] + vec[1:2, :]).astype(BF)
    q_wide = q[0].astype(F32)
    stack_heads(stack_q, q_wide, t1row)
    stack_heads(stack_h, dheads, t2row)
    slopes[...] = nt(v[0], stack_h[...])
    dv = nn(prob[0], stack_h[...]).astype(BF)
    for first in range(0, HEADS * PAD, 128):
        at = slice(first, first + 128)
        chance = prob[0, :, at].astype(F32)
        dprob = slopes[:, at]
        slopes[:, at] = chance * (dprob - colsum(dprob * chance))
    dmixed = slopes[...].astype(BF)
    dk = nn(dmixed, stack_q[...]).astype(BF)
    dpre = tn(dmixed, k[0])
    dq = jnp.zeros(q_wide.shape, F32)
    for g in range(HEADS):
        rows = slice(g * PAD, g * PAD + P_SIZE)
        dq += dpre[rows, :] * t1row[g : g + 1, :]
        rows_out[8 + g : 9 + g, :] += colsum(q_wide * dpre[rows, :])
        rows_out[16 + g : 17 + g, :] += colsum(dheads * post[0, rows, :].astype(F32))
    dq = dq.astype(BF)
    gattn_out[:, :shard, :] += tn(dq, normed).reshape(count, shard, D)
    gattn_out[:, shard : 2 * shard, :] += tn(dk, normed).reshape(count, shard, D)
    gattn_out[:, 2 * shard : 3 * shard, :] += tn(dv, normed).reshape(count, shard, D)
    dnormed = nn(dq, wq) + nn(dk, wk) + nn(dv, wv)
    rows_out[0:1, :] += colsum(dnormed * unit)
    rows_out[1:2, :] += colsum(dnormed)
    dx = incoming + normalize_back(unit, inverse, vec[0:1, :], dnormed)
    gpos_out[...] += dx
    dx_all[pl.program_id(0)] = dx

    @pl.when(pl.program_id(0) == pl.num_programs(0) - 1)
    def _():
        for n in range(images):
            dx_rows[:, n, :] = dx_all[n]
        gpix = tn(pixels[...], dx_rows[...].reshape(pixels.shape[0], D).astype(BF))
        used = gattn_out.shape[1]
        blocks_out[:, :used, :] = gattn_out[...].astype(BF)
        if used < blocks_out.shape[1]:
            blocks_out[:, used:, :] = jnp.zeros((count, blocks_out.shape[1] - used, D), BF)
        wide = commons_out.shape[1]
        commons_out[:3] = gpix.astype(BF).reshape(3, wide, D)
        commons_out[3] = jnp.concatenate(
            [
                gpos_out[...], jnp.zeros((12, D), F32), rows_feed[...], rows_out[...],
                jnp.zeros((8, D), F32),
            ],
            0,
        ).astype(BF)
        if count > 4:
            commons_out[4:] = jnp.zeros((count - 4, wide, D), BF)
        reduce_rows(
            place, blocks_out, commons_out, sum_a.finish(), sum_b.finish(), block_here,
            shared_here, square_out, *sum_buffers[2 * SUM_BUFFERS :],
        )
        saves = [
            pltpu.make_async_copy(block_here, block_far, save_sem.at[0]),
            pltpu.make_async_copy(shared_here, shared_far, save_sem.at[1]),
        ]
        for copy in saves:
            copy.start()
        sum_a.wait_sends()
        sum_b.wait_sends()
        for copy in saves:
            copy.wait()


def table_rows(n_dp, n_mp):
    return -(-(PIX + 256) // (16 * n_dp * n_mp)) * 16 * n_dp


def per_image(*tail):
    return pl.BlockSpec((1, *tail), lambda n: (n, *(0 for _ in tail)))


def constant(*shape):
    return pl.BlockSpec(shape, lambda n: tuple(0 for _ in shape))


def shaped(*shape, dtype=F32):
    return jax.ShapeDtypeStruct(shape, dtype)


def params():
    return pltpu.CompilerParams(vmem_limit_bytes=VMEM_LIMIT, dimension_semantics=("arbitrary",))


def remote_params(collective_id):
    return pltpu.CompilerParams(
        vmem_limit_bytes=VMEM_LIMIT, dimension_semantics=("arbitrary",),
        collective_id=collective_id, has_side_effects=True,
    )


def run_self_attend(
    n_dp, n_mp, group, attn_in, attn_out, mlp_in, mlp_out, pixels, tables, vec, mix, mask, counts,
    labels, pairs,
):
    count = labels.shape[0]
    classes = tables.shape[0] - PIX - P_SIZE
    n_y = n_mp // 2
    shard = attn_in.shape[1] + attn_out.shape[1]
    hidden = mlp_in.shape[2]
    rows = per_image(P_SIZE, D)
    low = shaped(count, P_SIZE, D, dtype=BF)
    scalars = pl.BlockSpec(memory_space=pltpu.SMEM)
    dma = pltpu.SemaphoreType.DMA
    shared = [
        shaped(hidden, D, dtype=BF), shaped(hidden, D, dtype=BF),
        shaped(classes, D, dtype=BF), shaped(HEADS, D), shaped(HEADS, D),
        shaped(P_SIZE, 2 * count), shaped(1, count * WIDE), shaped(count, 128),
    ]
    return pl.pallas_call(
        functools.partial(self_attend_kernel, n_dp, n_mp, group),
        grid=(count,),
        in_specs=[
            ANY, ANY, ANY, ANY, constant(*pixels.shape), ANY, constant(*vec.shape),
            constant(*mix.shape), constant(*mask.shape), scalars, scalars, scalars,
        ],
        out_specs=[
            rows, rows, rows, per_image(P_SIZE, HEADS * PAD), per_image(HEADS * PAD, D),
            rows, rows, rows, per_image(1, 128), ANY, ANY, ANY, ANY,
        ]
        + [constant(*item.shape) for item in shared],
        out_shape=[
            low, low, low, shaped(count, P_SIZE, HEADS * PAD, dtype=BF),
            shaped(count, HEADS * PAD, D, dtype=BF), low, low,
            shaped(count, P_SIZE, D), shaped(count, 1, 128),
            shaped(n_mp, 2 * hidden, D, dtype=BF), shaped(n_mp, shard, D, dtype=BF),
            shaped(count, P_SIZE, D), shaped(n_mp, shard, D, dtype=BF),
        ]
        + shared,
        scratch_shapes=[
            pltpu.VMEM((HEADS * PAD, D), BF), pltpu.VMEM((P_SIZE, HEADS * PAD), F32),
            pltpu.VMEM((count, P_SIZE, D), F32), pltpu.VMEM((n_mp, shard, D), BF),
            pltpu.VMEM((2 * hidden, D), BF), pltpu.VMEM((shard, D), BF), dma((1,)),
            pltpu.VMEM((classes + 4, D), F32), pltpu.VMEM(mlp_in.shape, F32),
            pltpu.VMEM(mlp_out.shape, F32),
            pltpu.VMEM((shard, D), BF), pltpu.VMEM(attn_in.shape, F32),
            pltpu.VMEM(attn_out.shape, F32), pltpu.VMEM((PIX, D), F32),
            pltpu.VMEM((200, D), F32),
            pltpu.VMEM((P_SIZE, count, D), F32),
            dma((n_y,)), dma((n_y,)), dma((n_y,)), dma((n_y,)), dma((8,)),
        ]
        + gather_scratch(n_mp) * 2,
        compiler_params=remote_params(6),
        name="self_attend",
    )(attn_in, attn_out, mlp_in, mlp_out, pixels, tables, vec, mix, mask, counts, labels, pairs)


def run_feed(
    n_dp, n_mp, group, mid, cols, bias_row, base, stat, vec, wmlp, wcls, up_rows, down_rows, head
):
    count = mid.shape[0]
    shard, hidden = wcls.shape[1] // 4, up_rows.shape[0]
    wide = n_mp * hidden
    everyone = n_dp * n_mp * count
    half = (n_mp, *up_rows.shape)
    dma = pltpu.SemaphoreType.DMA
    token_outs = [
        shaped(count, 2 * HEADS, WIDE, dtype=BF), shaped(count, 2 * HEADS, D, dtype=BF),
        shaped(D, D), shaped(16, D), shaped(shard, D), shaped(hidden, D), shaped(hidden, D),
        shaped(head.shape[0] + 8, D), shaped(16, D), shaped(8, 128),
    ]
    return pl.pallas_call(
        functools.partial(feed_kernel, n_dp, n_mp, group),
        grid=(count,),
        in_specs=[
            per_image(P_SIZE, D), constant(*cols.shape), constant(1, count * WIDE),
            constant(*base.shape), per_image(1, 128), constant(*vec.shape), constant(*wmlp.shape),
            constant(*wcls.shape), constant(*up_rows.shape), constant(*down_rows.shape), ANY,
        ],
        out_specs=[
            per_image(P_SIZE, D), per_image(P_SIZE, wide), per_image(P_SIZE, wide),
            per_image(P_SIZE, D), constant(24, D),
        ]
        + [constant(*item.shape) for item in token_outs],
        out_shape=[
            shaped(count, P_SIZE, D), shaped(count, P_SIZE, wide, dtype=BF),
            shaped(count, P_SIZE, wide, dtype=BF), shaped(count, P_SIZE, D, dtype=BF),
            shaped(24, D),
        ]
        + token_outs,
        scratch_shapes=[
            pltpu.VMEM((count, WIDE, D), BF), pltpu.VMEM((count * HEADS, WIDE), F32),
            pltpu.VMEM((count * HEADS, 128), F32), pltpu.VMEM((count * HEADS, D), F32),
            pltpu.VMEM((4 * count, 128), F32), pltpu.VMEM(half, BF), pltpu.VMEM(half, BF),
            pltpu.VMEM(head.shape, BF),
            pltpu.VMEM((everyone, D), F32), pltpu.VMEM((D, D), F32), pltpu.VMEM((wide, D), F32),
            pltpu.VMEM((wide, D), F32),
            pltpu.VMEM((4 * everyone, 128), F32), pltpu.VMEM((4 * everyone, 128), BF),
            dma((2, n_dp)), dma((2, n_mp)), dma((1,)),
        ]
        + spread_scratch(n_dp, n_mp) * 2,
        compiler_params=remote_params(7),
        name="feed",
    )(
        mid, cols, bias_row, base, stat, vec, wmlp, wcls, up_rows, down_rows, head
    )


def run_feed_back(n_dp, left, right, gv, local_rows, patch, mid, raw, act, slope, vec, wmlp):
    count = mid.shape[0]
    wide = act.shape[2]
    feed = (wmlp.shape[0], pad_rows(wmlp.shape[1] + D // wmlp.shape[0], n_dp), D)
    return pl.pallas_call(
        feed_back_kernel,
        grid=(count,),
        in_specs=[
            per_image(2 * HEADS, WIDE), per_image(2 * HEADS, D), constant(D, D), constant(16, D),
            per_image(P_SIZE, D), per_image(P_SIZE, D), per_image(P_SIZE, D),
            per_image(P_SIZE, wide), per_image(P_SIZE, wide), constant(*vec.shape),
            constant(*wmlp.shape),
        ],
        out_specs=[per_image(P_SIZE, D), constant(*feed), constant(16, D)],
        out_shape=[shaped(count, P_SIZE, D), shaped(*feed, dtype=BF), shaped(16, D)],
        scratch_shapes=[pltpu.VMEM(wmlp.shape, F32)],
        compiler_params=params(),
        name="feed_back",
    )(left, right, gv, local_rows, patch, mid, raw, act, slope, vec, wmlp)


def run_self_back(
    n_dp, n_mp, dmid, pixels, embed, q, k, v, prob, post, ho, raw, vec, wattn, t1row, t2row, gfeed,
    rows_feed,
):
    count = dmid.shape[0]
    rows_a, rows_b = halves(gfeed.shape[1], n_dp)
    blocks = (n_mp, pad_rows(wattn.shape[1], n_dp), D)
    commons = (n_mp, table_rows(n_dp, n_mp), D)
    rows = blocks[1] + rows_a + rows_b
    n_lo = 2 if n_dp < 16 else 4
    return pl.pallas_call(
        functools.partial(self_back_kernel, n_dp, n_mp),
        grid=(count,),
        in_specs=[
            per_image(P_SIZE, D), constant(*pixels.shape), per_image(P_SIZE, D),
            per_image(P_SIZE, D), per_image(P_SIZE, D), per_image(P_SIZE, D),
            per_image(P_SIZE, HEADS * PAD), per_image(HEADS * PAD, D), per_image(P_SIZE, D),
            per_image(P_SIZE, D), constant(*vec.shape), constant(*wattn.shape), constant(HEADS, D),
            constant(HEADS, D), constant(*gfeed.shape), constant(16, D),
        ],
        out_specs=[
            ANY, ANY, constant(8, 128),
        ],
        out_shape=[
            shaped(rows, D, dtype=BF), shaped(*commons, dtype=BF), shaped(8, 128),
        ],
        scratch_shapes=[
            pltpu.VMEM(wattn.shape, F32), pltpu.VMEM((P_SIZE, D), F32), pltpu.VMEM((24, D), F32),
            pltpu.VMEM((count, P_SIZE, D), F32), pltpu.VMEM((P_SIZE, count, D), F32),
            pltpu.VMEM((HEADS * PAD, D), BF), pltpu.VMEM((HEADS * PAD, D), BF),
            pltpu.VMEM((P_SIZE, HEADS * PAD), F32),
            pltpu.VMEM(blocks, BF), pltpu.VMEM(commons, BF), pltpu.VMEM((rows, D), BF),
            pltpu.VMEM(commons, BF), pltpu.SemaphoreType.DMA((2,)),
        ]
        + sum_scratch(n_dp, n_mp, rows_a, True)
        + sum_scratch(n_dp, n_mp, rows_b, False)
        + reduce_scratch(
            n_dp, n_mp, blocks[1], commons[1], (rows_a // n_lo, rows_b // n_lo)
        ),
        compiler_params=pltpu.CompilerParams(
            vmem_limit_bytes=VMEM_LIMIT, dimension_semantics=("arbitrary",), collective_id=5,
            has_side_effects=True,
        ),
        name="self_back",
    )(dmid, pixels, embed, q, k, v, prob, post, ho, raw, vec, wattn, t1row, t2row, gfeed, rows_feed)


def share_cards(n_dp, n_mp, card, out, slots, dp_sem, mp_sem):
    dp = lax.axis_index("dp")
    mp = lax.axis_index("mp")
    rows = card.shape[0]
    others_dp = [(lax.rem(dp + step, n_dp), mp) for step in range(1, n_dp)]
    others_mp = [(dp, lax.rem(mp + step, n_mp)) for step in range(1, n_mp)]
    own = tile_rows(slots, (mp * n_dp + dp) * rows, rows)
    slots[pl.ds(pl.multiple_of((mp * n_dp + dp) * rows, 16), rows), :] = card[...].astype(BF)
    sends = [
        remote(own, own, dp_sem.at[0, step], dp_sem.at[1, step], others_dp[step - 1])
        for step in range(1, n_dp)
    ]
    for copy in sends:
        copy.start()
    for step in range(1, n_dp):
        source = lax.rem(dp + n_dp - step, n_dp)
        theirs = tile_rows(slots, (mp * n_dp + source) * rows, rows)
        remote(own, theirs, dp_sem.at[0, step], dp_sem.at[1, step], (source, mp)).wait_recv()
    slab = tile_rows(slots, mp * n_dp * rows, n_dp * rows)
    for step in range(1, n_mp):
        sends.append(
            remote(slab, slab, mp_sem.at[0, step], mp_sem.at[1, step], others_mp[step - 1])
        )
        sends[-1].start()
    for step in range(1, n_mp):
        source = lax.rem(mp + n_mp - step, n_mp)
        theirs = tile_rows(slots, source * n_dp * rows, n_dp * rows)
        remote(slab, theirs, mp_sem.at[0, step], mp_sem.at[1, step], (dp, source)).wait_recv()
    for i in range(n_dp):
        for j in range(n_mp):
            to, source = (i * n_mp + j) * rows, (j * n_dp + i) * rows
            out[to : to + rows, :] = slots[source : source + rows, :].astype(F32)
    for copy in sends:
        copy.wait_send()


def start_part(
    begin, n_dp, n_mp, group, attn_in, attn_out, mlp_in, mlp_out, pixels, tables, vec, mix, mask,
    counts, labels, pairs,
    out, mlp_rows, cls_rows, up_rows, down_rows, embed_far, head_out, t1_out, t2_out, cols_out, bias_out, base_out,
    embed_out, head_rows, wide_up, wide_down, shard, wide_in, wide_out, patch_rows, pos_rows, by_patch, near_send, near_recv, far_send, far_recv, load_sem,
):
    dp = lax.axis_index("dp")
    mp = lax.axis_index("mp")
    n_y = n_mp // 2
    y = lax.div(mp, 2)
    core = lax.rem(mp, 2)
    sibling = (dp, y * 2 + 1 - core)
    load_patch = pltpu.make_async_copy(tables.at[pl.ds(0, PIX)], patch_rows, load_sem.at[0])
    load_pos = pltpu.make_async_copy(tables.at[pl.ds(PIX, 200)], pos_rows, load_sem.at[1])
    load_in = pltpu.make_async_copy(attn_in, wide_in, load_sem.at[2])
    load_out = pltpu.make_async_copy(attn_out, wide_out, load_sem.at[3])
    load_up = pltpu.make_async_copy(mlp_in, wide_up, load_sem.at[5])
    load_down = pltpu.make_async_copy(mlp_out, wide_down, load_sem.at[6])
    load_in.start()
    load_out.start()
    load_patch.start()
    load_pos.start()
    classes = head_out.shape[0]
    load_head = pltpu.make_async_copy(
        tables.at[pl.ds(PIX + P_SIZE - 4, classes + 4)], head_rows, load_sem.at[4]
    )
    load_up.start()
    load_down.start()
    load_head.start()
    barrier = pltpu.get_barrier_semaphore()
    pl.semaphore_signal(barrier, inc=1, device_id=sibling, device_id_type=MESH)
    for step in range(1, n_y):
        pl.semaphore_signal(
            barrier, inc=1, device_id=(dp, lax.rem(y + step, n_y) * 2 + core), device_id_type=MESH
        )
    third = attn_in.shape[1]
    load_in.wait()
    load_out.wait()
    shard[:third, :] = wide_in[0].astype(BF)
    shard[third:, :] = wide_out[0].astype(BF)
    pl.semaphore_wait(barrier, n_y)
    far = [
        remote(
            shard, out.at[mp], far_send.at[step], far_recv.at[step],
            (dp, lax.rem(y + step, n_y) * 2 + core),
        )
        for step in range(1, n_y)
    ]
    for copy in far:
        copy.start()
    near = [remote(shard, out.at[mp], near_send.at[0], near_recv.at[0], sibling)]
    near[0].start()
    out[pl.ds(mp, 1)] = shard[...][None]

    cls_rows[:third, :] = wide_in[1].astype(BF)
    cls_rows[third:, :] = wide_out[1].astype(BF)
    hidden = mlp_rows.shape[0] // 2
    load_up.wait()
    load_down.wait()
    mlp_rows[:hidden, :] = wide_up[0].T.astype(BF)
    mlp_rows[hidden:, :] = wide_down[0].astype(BF)
    begin()
    up_rows[...] = wide_up[1].T.astype(BF)
    down_rows[...] = wide_down[1].astype(BF)

    images = mask.shape[0]
    lane = lax.broadcasted_iota(jnp.int32, (1, 128), 1)
    keep = (mask[...] > 0).astype(F32)
    bias = (1.0 - keep) * MASKED
    count = counts[0]
    okays = []
    bias_out[...] = jnp.full(bias_out.shape, MASKED, F32)
    for n in range(images):
        okays.append((jnp.full((1, 1), mp * images + n, jnp.int32) >= group - count).astype(F32))
        bias_out[:, n * WIDE : n * WIDE + P_SIZE] = bias[n : n + 1, :]
        tokens = jnp.sum(keep[n : n + 1, :], 1, keepdims=True) * okays[n]
        entries = (
            lax.div(labels[n], 32), lax.rem(labels[n], 32), lax.div(pairs[n], 32),
            lax.rem(pairs[n], 32), count,
        )
        line = jnp.where(lane == len(entries), tokens, 0.0)
        for place, entry in enumerate(entries):
            line = jnp.where(lane == place, entry.astype(F32), line)
        base_out[n : n + 1, :] = line
    cols_out[...] = jnp.concatenate([bias, keep * jnp.concatenate(okays, 0)], 0).T
    heads = head_mask()
    exact = functools.partial(
        lax.dot_general, preferred_element_type=F32, precision=lax.Precision.HIGHEST
    )
    t1_out[...] = exact(mix[0], heads, (((1,), (0,)), ((), ()))) * SCALE
    t2_out[...] = exact(mix[1], heads, (((0,), (0,)), ((), ())))

    load_patch.wait()
    wp = patch_rows[...].astype(BF)
    local = embed_out.shape[0]
    half = P_SIZE // 2
    for place in range(2):
        rows = slice(place * half * local, (place + 1) * half * local)
        by_patch[place * half : (place + 1) * half] = nn(pixels[rows, :], wp).reshape(half, local, D)

    for step in range(1, n_y):
        source = lax.rem(y + n_y - step, n_y) * 2
        slot = source + core
        remote(
            shard, out.at[slot], far_send.at[step], far_recv.at[step], (dp, slot)
        ).wait_recv()
        copy = remote(
            out.at[slot], out.at[slot], near_send.at[step], near_recv.at[step], sibling
        )
        copy.start()
        near.append(copy)
    load_pos.wait()
    offset = pos_rows[:P_SIZE, :] + vec[16:17, :]
    for n in range(local):
        embed_out[n] = by_patch[:, n, :] + offset
    save_embed = pltpu.make_async_copy(embed_out, embed_far, load_sem.at[7])
    save_embed.start()
    load_head.wait()
    head_out[...] = head_rows[4:, :].astype(BF)
    save_embed.wait()
    for copy in far:
        copy.wait_send()
    for step in range(n_y):
        slot = lax.rem(y + n_y - step, n_y) * 2 + 1 - core
        near[step].wait_send()
        remote(
            out.at[slot], out.at[slot], near_send.at[step], near_recv.at[step], sibling
        ).wait_recv()


def reduce_rows(
    p, blocks, commons, chunk_a, chunk_b,
    block_out, shared_out, square_out,
    squares, attn_run, run_a, run_b, sem_a, sem_b, high_a, high_b, high_sem, low_sem, square_sem,
    *sum_buffers,
):
    n_mp = p.n_mp
    attn = ShardSum(p, blocks, 0, True, *sum_buffers[:SUM_BUFFERS])
    table = TableSum(p, commons, shared_out, *sum_buffers[SUM_BUFFERS:])
    rows_a = blocks.shape[1]
    rows_feed = p.n_lo * run_a.shape[0]
    hand_a = HandLow(p, block_out, rows_a, rows_feed, sem_a)
    hand_b = HandLow(p, block_out, rows_a + rows_feed, p.n_lo * run_b.shape[0], sem_b)
    wide_a = HandHigh(p, run_a, high_a)
    wide_b = HandHigh(p, run_b, high_b)
    hand_high = HandHigh(p, attn_run, high_sem)
    hand_low = HandLow(p, block_out, 0, rows_a, low_sem)

    attn.start()
    table.start()
    wide_a.start(chunk_a)
    wide_b.start(chunk_b)
    attn.second()
    table.near_to_low()
    table.low_to_high()
    attn.third()
    wide_a.arrive()
    hand_a.start(run_a[...])
    wide_b.arrive()
    hand_b.start(run_b[...])
    table.high_to_far()
    attn.fourth()
    table.turn()
    table.far_to_high()
    hand_high.start(attn.finish())
    table.high_to_low()
    hand_high.arrive()
    hand_low.start(attn_run[...])
    table.low_to_near()
    sends = []

    for item in (hand_a, hand_b, hand_low):
        item.arrive()
    sums = block_out[...].astype(F32)
    sums = colsum(sums * sums)
    squares[pl.ds(p.mp, 1)] = jnp.broadcast_to(
        sums[:, 0:128] + sums[:, 128:256] + sums[:, 256:384], (8, 128)
    )[None]

    for step in range(1, p.n_y):
        sends.append(
            remote(
                squares.at[p.mp], squares.at[p.mp], square_sem.at[0, step],
                square_sem.at[1, step], (p.dp, p.along_y(step) * 2 + p.core),
            )
        )
        sends[-1].start()
    for step in range(1, p.n_y):
        source = p.along_y(p.n_y - step) * 2 + p.core
        remote(
            squares.at[p.mp], squares.at[source], square_sem.at[0, step], square_sem.at[1, step],
            (p.dp, source),
        ).wait_recv()
    mine = squares[pl.ds(p.core, 1)]
    for y in range(1, p.n_y):
        mine += squares[pl.ds(2 * y + p.core, 1)]
    squares[pl.ds(n_mp + p.core, 1)] = mine
    sends.append(
        remote(
            squares.at[n_mp + p.core], squares.at[n_mp + p.core], square_sem.at[0, 0],
            square_sem.at[1, 0], p.sibling,
        )
    )
    sends[-1].start()
    table.finish()
    remote(
        squares.at[n_mp + p.core], squares.at[n_mp + 1 - p.core], square_sem.at[0, 0],
        square_sem.at[1, 0], p.sibling,
    ).wait_recv()
    square_out[...] = squares[n_mp] + squares[n_mp + 1]
    for copy in sends:
        copy.wait_send()
    for item in (attn, wide_a, wide_b, hand_a, hand_b, hand_high, hand_low):
        item.wait_sends()


def reduce_scratch(n_dp, n_mp, rows_a, wide, feed):
    assert wide == 256
    n_lo = 2 if n_dp < 16 else 4
    n_hi = n_dp // n_lo
    dma = pltpu.SemaphoreType.DMA
    return (
        [
            pltpu.VMEM((n_mp + 2, 8, 128), F32), pltpu.VMEM((rows_a // n_lo, D), BF),
            pltpu.VMEM((feed[0], D), BF), pltpu.VMEM((feed[1], D), BF),
            dma((2, n_lo)), dma((2, n_lo)), dma((2, n_hi)), dma((2, n_hi)), dma((2, n_hi)),
            dma((2, n_lo)), dma((2, n_mp)),
        ]
        + sum_scratch(n_dp, n_mp, rows_a, True)
        + table_scratch(n_dp, n_mp, wide)
    )


def root(values):
    return values * lax.rsqrt(values)


def adam_parts(gradient, mean, square, factor):
    clipped = gradient * factor
    mean_new = BETA_ONE * mean + (1.0 - BETA_ONE) * clipped
    square_new = BETA_TWO * square + (1.0 - BETA_TWO) * clipped * clipped
    direction = (
        mean_new
        * (1.0 / (1.0 - BETA_ONE**STEP))
        / (root(square_new * (1.0 / (1.0 - BETA_TWO**STEP))) + ADAM_EPS)
    )
    return (mean_new, square_new, direction)


def fold(values):
    squares = (values * values).reshape(values.shape[0] // 8, 8, values.shape[1]).sum(0)
    width = values.shape[1]
    if width % 128:
        return jnp.broadcast_to(jnp.sum(squares, 1, keepdims=True), (8, 128)) * (1.0 / 128)
    return sum(squares[:, i : i + 128] for i in range(0, width, 128))


def total(values):
    return jnp.sum(jnp.sum(values, 0, keepdims=True), 1, keepdims=True)


def moment_sweep(factor, grad, w, m, s, u, rows):
    chunk = 32 if rows % 32 == 0 else 16

    def step(i, kept):
        at = pl.ds(pl.multiple_of(i * chunk, chunk), chunk)
        weight = w[at, :]
        mean, second, direction = adam_parts(grad(i, chunk), m[at, :], s[at, :], factor)
        m[at, :] = mean
        s[at, :] = second
        update = direction + DECAY * weight
        u[at, :] = update.astype(u.dtype)
        return (kept[0] + fold(weight), kept[1] + fold(update))

    zero = jnp.zeros((8, 128), F32)
    return lax.fori_loop(0, rows // chunk, step, (zero, zero))


def rows_from(ref, first):
    def read(i, chunk):
        at = pl.ds(pl.multiple_of(first + i * chunk, 16), chunk)
        return ref[at, :].astype(F32)

    return read


def moment_kernel(
    n_dp, block_sq, gout1, rows1, stat, aux, vec, vec_mean, vec_square, mix, mix_mean, mix_square,
    *rest,
):
    large, rest = rest[:5], rest[5:]
    state = rest[:12]
    outs = rest[12:24]
    (
        vec_out, vec_mean_out, vec_square_out, mix_out, mix_mean_out, mix_square_out,
        misc_out, sums_out,
    ) = rest[24:32]
    held = rest[32:44]
    updates = rest[44:48]
    grad_q, grad_k, grad_flip, load_sem, save_sem = rest[48:53]
    large_here = rest[53:]
    first_loads = [
        pltpu.make_async_copy(large[i], large_here[i], load_sem.at[12 + i]) for i in range(5)
    ]
    loads = [pltpu.make_async_copy(state[i], held[i], load_sem.at[i]) for i in range(12)]
    for copy in first_loads + loads:
        copy.start()
    for copy in first_loads:
        copy.wait()
    block, shared, wcls, gup1, gdown1 = large_here
    mp = lax.axis_index("mp")
    hs = state[3].shape[1]
    fs = state[9].shape[1]
    feed = pad_rows(4 * hs, n_dp)

    rows2 = shared[PIX + 208 : PIX + 224, :].astype(F32)
    rows3 = shared[PIX + 224 : PIX + 256, :].astype(F32)
    token = aux[8:9, :]
    wq = part(wcls, 0, hs)
    wk = part(wcls, hs, hs).astype(F32)
    query = nt(wq, aux[8:16, :].astype(BF))[:, 0:1].astype(BF).astype(F32)
    dkeys = jnp.concatenate(
        [jnp.broadcast_to(rows2[8 + h : 9 + h, :], (HEAD, D)) for h in range(HEADS)], 0
    )
    dquery = SCALE * jnp.sum(wk * dkeys, 1, keepdims=True)
    gq = dquery * token
    gk = (SCALE * query) * dkeys
    grad_q[...] = gq
    grad_k[...] = gk
    dtoken = rows2[6:7, :] + colsum(dquery * wq.astype(F32))
    unit, inverse = normalize(jnp.broadcast_to(vec[17:18, :], (8, D)))
    dcls = normalize_back(unit, inverse, vec[8:9, :], jnp.broadcast_to(dtoken, (8, D)))[0:1, :]
    dgain = rows2[4:5, :] + dtoken * unit[0:1, :]
    last = rows1[...]
    positions = shared[PIX : PIX + 208, :].astype(F32)
    grad_vec = jnp.concatenate(
        [
            rows3[0:4, :], rows2[0:4, :], dgain, rows2[5:6, :] + dtoken, last[2:8, :],
            colsum(positions), last[8:9, :] + dcls, last[9:11, :],
        ],
        0,
    )
    mask = head_mask()
    exact = functools.partial(
        lax.dot_general, dimension_numbers=(((1,), (1,)), ((), ())),
        preferred_element_type=F32, precision=lax.Precision.HIGHEST,
    )
    grad_mix = (exact(rows3[8:16, :], mask) * SCALE, exact(mask, rows3[16:24, :]))

    square = total(block_sq[0:1, :]) + total(stat[1:2, :]) + total(colsum(gq * gq + gk * gk))
    square += total(grad_vec * grad_vec)
    square += total(grad_mix[0] * grad_mix[0]) + total(grad_mix[1] * grad_mix[1])

    def square_rows(i, kept):
        rows = shared[pl.ds(pl.multiple_of(i * 16, 16), 16), :].astype(F32)
        return kept + fold(rows)

    square += total(lax.fori_loop(0, (PIX + 208) // 16, square_rows, jnp.zeros((8, 128), F32)))
    norm = jnp.sqrt(square)
    factor = CLIP / jnp.maximum(norm, CLIP)

    mean, second, direction = adam_parts(grad_vec, vec_mean[...], vec_square[...], factor)
    vec_mean_out[...] = mean
    vec_square_out[...] = second
    vec_out[...] = vec[...] - RATE_VECTOR * direction
    misc = []
    weight_sums = []
    for b in range(2):
        mean, second, direction = adam_parts(grad_mix[b], mix_mean[b], mix_square[b], factor)
        mix_mean_out[b] = mean
        mix_square_out[b] = second
        update = direction + DECAY * mix[b]
        weight_sq = total(mix[b] * mix[b])
        update_sq = total(update * update)
        mix_out[b] = mix[b] - RATE * jnp.sqrt(weight_sq / (update_sq + 1e-12)) * update
        weight_sums.append(weight_sq)
        misc.append(update_sq)

    def sweep(grad, w, m, s, u, rows):
        return moment_sweep(factor, grad, w, m, s, u, rows)

    saves = []

    def save(i, source):
        saves.append(pltpu.make_async_copy(source, outs[i], save_sem.at[i]))
        saves[-1].start()

    sums = []
    own_h = pl.multiple_of(mp * hs, hs)
    for kind in range(4):
        for copy in loads[3 * kind : 3 * kind + 3]:
            copy.wait()
        w, m, s = held[3 * kind : 3 * kind + 3]
        u = updates[kind]
        for b in range(2):
            views = (w.at[b], m.at[b], s.at[b], u.at[b])
            if kind == 0 and b == 0:
                sums.append(sweep(rows_from(block, 0), *views, 3 * hs))
            elif kind == 0:
                pieces = []
                for third, source in enumerate(
                    (
                        rows_from(grad_q, own_h),
                        rows_from(grad_k, own_h),
                        rows_from(block, feed + 2 * fs),
                    )
                ):
                    pieces.append(
                        sweep(
                            source, *(view.at[pl.ds(third * hs, hs)] for view in views), hs
                        )
                    )
                sums.append(
                    tuple(pieces[0][i] + pieces[1][i] + pieces[2][i] for i in range(2))
                )
            elif kind == 1:
                source = rows_from(gout1, 0) if b else rows_from(block, 3 * hs)
                sums.append(sweep(source, *views, hs))
            elif kind == 2:
                if b:
                    grad_flip[...] = gup1[...].T
                else:
                    grad_flip[...] = block[feed : feed + fs, :].astype(F32).T
                sums.append(sweep(rows_from(grad_flip, 0), *views, D))
            else:
                source = rows_from(gdown1, 0) if b else rows_from(block, feed + fs)
                sums.append(sweep(source, *views, fs))
        save(3 * kind, u)
        save(3 * kind + 1, m)
        save(3 * kind + 2, s)
    for place, pair in enumerate(sums):
        sums_out[place : place + 1, :] = colsum(pair[1])
        sums_out[8 + place : 9 + place, :] = colsum(pair[0])

    lane = lax.broadcasted_iota(jnp.int32, (1, 128), 1)
    misc_out[0:1, :] = jnp.broadcast_to(norm, (1, 128))
    weight_line = jnp.zeros((1, 128), F32)
    update_line = jnp.zeros((1, 128), F32)
    for b in range(2):
        weight_line = jnp.where(lane == 11 + b, weight_sums[b], weight_line)
        update_line = jnp.where(lane == 11 + b, misc[b], update_line)
    misc_out[1:2, :] = weight_line
    misc_out[2:3, :] = update_line
    misc_out[3:8, :] = jnp.zeros((5, 128), F32)
    for copy in saves:
        copy.wait()


def table_kernel(misc, shared, ghead, *rest):
    state, outs, misc_out = rest[:3], rest[3:6], rest[6]
    w, m, s, table_update, load_sem, save_sem = rest[7:]
    rows_all = w.shape[0]
    edge = PIX + P_SIZE - 4
    body = (rows_all - edge - 16) // 64 * 32
    middle = edge + 16 + body
    cuts = (0, PIX // 2, PIX, middle, rows_all)
    slabs = [pl.ds(low, high - low) for low, high in zip(cuts, cuts[1:])]
    loads = [
        [
            pltpu.make_async_copy(state[i].at[at], (w, m, s)[i].at[at], load_sem.at[i, place])
            for i in range(3)
        ]
        for place, at in enumerate(slabs)
    ]
    for group in loads:
        for copy in group:
            copy.start()
    factor = CLIP / jnp.maximum(misc[0:1, 0:1], CLIP)
    saves = []

    def arrive(place):
        for copy in loads[place]:
            copy.wait()

    def save(i, place):
        at = slabs[place]
        saves.append(
            pltpu.make_async_copy((w, m, s)[i].at[at], outs[i].at[at], save_sem.at[i, place])
        )
        saves[-1].start()

    def slab(first, count, grad):
        at = slice(first, first + count)
        weight = w[at, :]
        mean, second, direction = adam_parts(grad, m[at, :], s[at, :], factor)
        m[at, :] = mean
        s[at, :] = second
        update = direction + DECAY * weight
        table_update[at, :] = update
        return weight, update

    def run(first, count, source, offset):
        def at(ref, start):
            return ref.at[pl.ds(start, count)]

        return moment_sweep(
            factor, rows_from(source, offset), at(w, first), at(m, first), at(s, first),
            at(table_update, first), count,
        )

    def renew(first, count, rate):
        def step(i, _):
            at = pl.ds(pl.multiple_of(first + i * 32, 16), 32)
            w[at, :] = w[at, :] - rate * table_update[at, :]
            return 0

        lax.fori_loop(0, count // 32, step, 0)

    def rate_of(weight_sq, update_sq):
        return RATE * jnp.sqrt(weight_sq / (update_sq + 1e-12))

    def masked(values, mask):
        return total(jnp.where(mask, values * values, 0.0))

    arrive(0)
    first_half = run(0, PIX // 2, shared, 0)
    save(1, 0)
    save(2, 0)
    arrive(1)
    second_half = run(PIX // 2, PIX // 2, shared, PIX // 2)
    save(1, 1)
    save(2, 1)
    sq_w = [total(first_half[0] + second_half[0])]
    sq_u = [total(first_half[1] + second_half[1])]
    rates = [rate_of(sq_w[0], sq_u[0])]
    renew(0, PIX, rates[0])
    save(0, 0)
    save(0, 1)
    arrive(2)
    place_rows = run(PIX, P_SIZE - 4, shared, PIX)
    tile = lax.broadcasted_iota(jnp.int32, (16, 1), 0) < 4
    weight, update = slab(edge, 16, shared[edge : edge + 16, :].astype(F32) + ghead[0:16, :])
    heads = run(edge + 16, body, ghead, 16)
    save(1, 2)
    save(2, 2)
    arrive(3)
    rest_rows = (rows_all - middle) // 32 * 32
    more_heads = run(middle, rest_rows, ghead, 16 + body)
    left = middle + rest_rows
    tail_weight, tail_update = slab(
        left, rows_all - left, ghead[16 + left - edge - 16 : 16 + rows_all - edge - 16, :]
    )
    save(1, 3)
    save(2, 3)
    sq_w += [
        total(place_rows[0]) + masked(weight, tile),
        total(heads[0] + more_heads[0]) + masked(weight, ~tile) + total(tail_weight * tail_weight),
    ]
    sq_u += [
        total(place_rows[1]) + masked(update, tile),
        total(heads[1] + more_heads[1]) + masked(update, ~tile) + total(tail_update * tail_update),
    ]
    rates += [rate_of(sq_w[i], sq_u[i]) for i in (1, 2)]
    renew(PIX, P_SIZE - 4, rates[1])
    w[edge : edge + 16, :] = weight - jnp.where(tile, rates[1], rates[2]) * update
    renew(edge + 16, body, rates[2])
    save(0, 2)
    renew(middle, rest_rows, rates[2])
    w[left:rows_all, :] = tail_weight - rates[2] * tail_update
    save(0, 3)

    lane = lax.broadcasted_iota(jnp.int32, (1, 128), 1)
    weight_line = misc[1:2, :]
    update_line = misc[2:3, :]
    for place in range(3):
        weight_line = jnp.where(lane == 8 + place, sq_w[place], weight_line)
        update_line = jnp.where(lane == 8 + place, sq_u[place], update_line)
    misc_out[...] = misc[...]
    misc_out[1:2, :] = weight_line
    misc_out[2:3, :] = update_line
    for copy in saves:
        copy.wait()


def run_moments(n_dp, grads, smalls, large, state):
    outs = [
        jax.ShapeDtypeStruct(item.shape, F32 if i % 3 else BF) for i, item in enumerate(state)
    ]
    fs = state[9].shape[1]
    dma = pltpu.SemaphoreType.DMA
    return pl.pallas_call(
        functools.partial(moment_kernel, n_dp),
        in_specs=[WHOLE] * (len(grads) + len(smalls)) + [ANY] * 17,
        out_specs=[ANY] * 12 + [WHOLE] * 8,
        out_shape=outs
        + [jax.ShapeDtypeStruct(item.shape, F32) for item in smalls]
        + [shaped(8, 128), shaped(16, 128)],
        scratch_shapes=[pltpu.VMEM(item.shape, F32) for item in state]
        + [pltpu.VMEM(state[3 * kind].shape, BF) for kind in range(4)]
        + [
            pltpu.VMEM((D, D), F32), pltpu.VMEM((D, D), F32), pltpu.VMEM((D, fs), F32),
            dma((17,)), dma((12,)),
        ]
        + [pltpu.VMEM(item.shape, item.dtype) for item in large],
        compiler_params=pltpu.CompilerParams(vmem_limit_bytes=VMEM_LIMIT),
        name="moments",
    )(*grads, *smalls, *large, *state)


def run_tables(misc, shared, ghead, state):
    shape = state[0].shape
    dma = pltpu.SemaphoreType.DMA
    return pl.pallas_call(
        table_kernel,
        in_specs=[WHOLE] * 3 + [ANY] * 3,
        out_specs=[ANY] * 3 + [WHOLE],
        out_shape=[shaped(*shape)] * 3 + [shaped(8, 128)],
        scratch_shapes=[pltpu.VMEM(shape, F32)] * 4 + [dma((3, 4)), dma((3, 4))],
        cost_estimate=pl.CostEstimate(
            flops=40 * shape[0] * shape[1], bytes_accessed=28 * shape[0] * shape[1],
            transcendentals=2 * shape[0] * shape[1],
        ),
        compiler_params=pltpu.CompilerParams(vmem_limit_bytes=VMEM_LIMIT),
        name="tables",
    )(misc, shared, ghead, *state)


def renew_kernel(n_mp, misc, stat, *rest):
    theirs, rest = rest[:n_mp], rest[n_mp:]
    weights, updates = rest[:4], rest[4:8]
    new, copies = rest[8:12], rest[12:16]
    norms, norm_out, stat_out = rest[16:19]
    here, changes, lows = rest[19:23], rest[23:27], rest[27:31]
    slots, load_sem, save_sem = rest[31:]
    loads = [
        (
            pltpu.make_async_copy(weights[kind], here[kind], load_sem.at[0, kind]),
            pltpu.make_async_copy(updates[kind], changes[kind], load_sem.at[1, kind]),
        )
        for kind in range(4)
    ]
    for pair in loads[::-1]:
        for copy in pair:
            copy.start()
    mp = lax.axis_index("mp")
    for step in range(n_mp):
        slots[pl.ds(lax.rem(mp + n_mp - step, n_mp), 1)] = theirs[step][...][None]
    sums = jnp.sum(slots[...], 0)
    rates = []
    lane = lax.broadcasted_iota(jnp.int32, (1, 128), 1)
    weight_line, update_line = misc[1:2, :], misc[2:3, :]
    for place in range(8):
        update_sq = total(sums[place : place + 1, :])
        weight_sq = total(sums[8 + place : 9 + place, :])
        rates.append(RATE * jnp.sqrt(weight_sq / (update_sq + 1e-12)))
        weight_line = jnp.where(lane == place, weight_sq, weight_line)
        update_line = jnp.where(lane == place, update_sq, update_line)
    norms[...] = jnp.sqrt(jnp.concatenate([weight_line, update_line], 0))[:, :13]
    norm_out[...] = misc[0:1, 0:1]
    stat_out[...] = stat[0:1, :12]
    saves = []
    for kind in (3, 2, 1, 0):
        w, u, low = here[kind], changes[kind], lows[kind]
        rows = w.shape[1]
        chunk = 32 if rows % 32 == 0 else 16
        for copy in loads[kind]:
            copy.wait()
        for b in range(2):
            rate = rates[2 * kind + b]

            def step(i, _, b=b, w=w, u=u, low=low, rate=rate, chunk=chunk):
                at = pl.ds(pl.multiple_of(i * chunk, chunk), chunk)
                values = w[b, at, :] - rate * u[b, at, :].astype(F32)
                w[b, at, :] = values
                low[b, at, :] = values.astype(BF)
                return 0

            lax.fori_loop(0, rows // chunk, step, 0)
        saves.append(pltpu.make_async_copy(w, new[kind], save_sem.at[0, kind]))
        saves.append(pltpu.make_async_copy(low, copies[kind], save_sem.at[1, kind]))
        for copy in saves[-2:]:
            copy.start()
    for copy in saves:
        copy.wait()


def run_renew(n_mp, misc, stat, sums, weights, updates):
    dma = pltpu.SemaphoreType.DMA
    return pl.pallas_call(
        functools.partial(renew_kernel, n_mp),
        in_specs=[WHOLE] * (2 + n_mp) + [ANY] * 8,
        out_specs=[ANY] * 8 + [WHOLE] * 3,
        out_shape=[shaped(*item.shape) for item in weights]
        + [shaped(*item.shape, dtype=BF) for item in weights]
        + [shaped(2, 13), shaped(1, 1), shaped(1, 12)],
        scratch_shapes=[pltpu.VMEM(item.shape, F32) for item in weights]
        + [pltpu.VMEM(item.shape, BF) for item in weights] * 2
        + [pltpu.VMEM((n_mp, 16, 128), F32), dma((2, 4)), dma((2, 4))],
        compiler_params=pltpu.CompilerParams(vmem_limit_bytes=VMEM_LIMIT),
        name="renew",
    )(misc, stat, *sums, *weights, *updates)


def shards(
    pixels,
    token_mask,
    counts,
    labels,
    pairs,
    attn_in,
    attn_in_mean,
    attn_in_square,
    attn_out,
    attn_out_mean,
    attn_out_square,
    mlp_in,
    mlp_in_mean,
    mlp_in_square,
    mlp_out,
    mlp_out_mean,
    mlp_out_square,
    tables,
    tables_mean,
    tables_square,
    vectors,
    vectors_mean,
    vectors_square,
    talking,
    talking_mean,
    talking_square,
):
    local = pixels.shape[0]
    group = token_mask.shape[0]
    place_mp = lax.axis_index("mp")
    n_mp = lax.axis_size("mp")
    n_dp = lax.axis_size("dp")
    hs = attn_in.shape[3]
    fs = mlp_in.shape[2]

    def as_rows(item):
        return item.transpose(0, 2, 3, 1).reshape(2, 3 * hs, D)

    def from_rows(item):
        return item.reshape(2, 3, hs, D).transpose(0, 3, 1, 2)

    attn_in, attn_in_mean, attn_in_square = map(as_rows, (attn_in, attn_in_mean, attn_in_square))
    pixel_rows = pixels.transpose(1, 0, 2).reshape(P_SIZE * local, PIX)
    mask = lax.dynamic_slice_in_dim(token_mask, place_mp * local, local, 0)
    (
        q, k, v, prob, post, ho, raw0, middle, stat_a, wmlp, wattn, embed, wcls, up_rows,
        down_rows, head, t1row, t2row, cols, bias_row, base,
    ) = run_self_attend(
        n_dp, n_mp, group, attn_in, attn_out, mlp_in, mlp_out, pixel_rows, tables, vectors,
        talking, mask, counts, labels, pairs,
    )
    (
        patches, act, slope, raw1, aux, left, right, gv, local_rows, gout1, gup1, gdown1,
        ghead, rows1, stat,
    ) = run_feed(
        n_dp, n_mp, group, middle, cols, bias_row, base, stat_a, vectors, wmlp, wcls, up_rows,
        down_rows, head,
    )
    dmid, gfeed, rows2 = run_feed_back(
        n_dp, left, right, gv, local_rows, patches, middle, raw1, act, slope, vectors, wmlp
    )
    block, shared, block_sq = run_self_back(
        n_dp, n_mp, dmid, pixel_rows, embed, q, k, v, prob, post, ho, raw0, vectors, wattn,
        t1row, t2row, gfeed, rows2,
    )

    shared = shared.reshape(-1, D)
    state = (
        attn_in, attn_in_mean, attn_in_square, attn_out, attn_out_mean, attn_out_square,
        mlp_in, mlp_in_mean, mlp_in_square, mlp_out, mlp_out_mean, mlp_out_square,
    )
    smalls = (vectors, vectors_mean, vectors_square, talking, talking_mean, talking_square)
    moved = run_moments(
        n_dp, (block_sq, gout1, rows1, stat, aux), smalls, (block, shared, wcls, gup1, gdown1),
        state,
    )
    sums = [moved[19]]
    for step in range(1, n_mp):
        sums.append(lax.ppermute(moved[19], "mp", [(i, (i + step) % n_mp) for i in range(n_mp)]))
    table = run_tables(moved[18], shared, ghead, (tables, tables_mean, tables_square))
    renewed = run_renew(n_mp, table[3], stat, sums, state[0:12:3], moved[0:12:3])
    return (
        from_rows(renewed[0]),
        from_rows(moved[1]),
        from_rows(moved[2]),
        renewed[1],
        moved[4],
        moved[5],
        renewed[2],
        moved[7],
        moved[8],
        renewed[3],
        moved[10],
        moved[11],
        *table[:3],
        *moved[12:18],
        from_rows(renewed[4]),
        renewed[5],
        renewed[6],
        renewed[7],
        renewed[10].reshape(12),
        renewed[9].reshape(()),
        renewed[8],
    )


def solution(mesh):
    return jax.shard_map(
        shards,
        mesh=mesh,
        in_specs=(
            P(("dp", "mp"), None, None),
            P("dp", None),
            P("dp"),
            P(("dp", "mp")),
            P(("dp", "mp")),
            P(None, None, None, "mp"),
            P(None, None, None, "mp"),
            P(None, None, None, "mp"),
            P(None, "mp", None),
            P(None, "mp", None),
            P(None, "mp", None),
            P(None, None, "mp"),
            P(None, None, "mp"),
            P(None, None, "mp"),
            P(None, "mp", None),
            P(None, "mp", None),
            P(None, "mp", None),
            P(),
            P(),
            P(),
            P(),
            P(),
            P(),
            P(),
            P(),
            P(),
        ),
        out_specs=(
            P(None, None, None, "mp"),
            P(None, None, None, "mp"),
            P(None, None, None, "mp"),
            P(None, "mp", None),
            P(None, "mp", None),
            P(None, "mp", None),
            P(None, None, "mp"),
            P(None, None, "mp"),
            P(None, None, "mp"),
            P(None, "mp", None),
            P(None, "mp", None),
            P(None, "mp", None),
            P(),
            P(),
            P(),
            P(),
            P(),
            P(),
            P(),
            P(),
            P(),
            P(None, None, None, "mp"),
            P(None, "mp", None),
            P(None, None, "mp"),
            P(None, "mp", None),
            P(),
            P(),
            P(),
        ),
        check_vma=False,
    )
```
